32 devices in a mesh: stn: 16 (over z, x, core), tm: 2 (over y).
Axes of the slice: x: 2, y: 2, z: 4, core: 2. Of those that a mesh axis runs over, the one named last changes fastest.
Arguments:
- voltage: bfloat16 [128, 64, 2, 4096], P('stn', 'tm'), may hold values from -6 to 6
- fir_taps: float32 [16, 4096], replicated, may hold values from -1.5 to 1.5
Outputs:
- visibilities: float32 [2, 128, 32, 2048], P(None, 'stn', None, 'tm')
The draws below stay inside these ranges and needn't reach their ends.
All inputs are finite; a program needn't handle non-finite values.
Results may differ from the reference program's by a relative error of at most 0.0014.
Values may be sent and summed in bfloat16 or wider, within the bound.
No kernel may reach another device: no remote copies, remote signals or barrier semaphores. Data moves between devices by JAX's collectives and lax.ppermute only.
A program may use at most 192 MiB of HBM per device.

```python
import math
import jax
import jax.numpy as jnp
from jax import lax

SIG_DEV = 8
SIGNALS = 128
NCH = 4096
CHANS = 2048
TAPS = 16
VISITS = 4
FRAMES = 64
N_STN = 16


def block_levels(own_key, dims, cuts, low, high):
    def one(position, parts):
        draws = jax.random.uniform(jax.random.fold_in(jax.random.fold_in(own_key, 6), position), (parts,), jnp.float32, low / len(cuts), high / len(cuts))
        return jnp.repeat(jnp.exp(draws), dims[position] // parts).reshape((-1,) + (1,) * (len(dims) - position - 1))

    loudness = one(*cuts[0])
    for cut in cuts[1:]:
        loudness = loudness * one(*cut)
    return loudness


def gaussian(rng, dims, deviation, reach, cuts=(), kind=jnp.bfloat16):
    drawn = deviation * jax.random.normal(rng, dims, jnp.float32)
    if cuts:
        drawn = drawn * block_levels(rng, dims, cuts, -0.22, 0.18)
    return jnp.clip(drawn, -reach, reach).astype(kind)


def setup_inputs(seed: int = 0) -> dict:
    keys = jax.random.split(jax.random.key(seed), 3)
    return {
        "voltage": gaussian(keys[0], (SIGNALS, FRAMES, 2, NCH), 1.0, 6.0, ((0, 16), (1, 2))),
        "fir_taps": gaussian(keys[1], (TAPS, NCH), 0.25, 1.5, (), jnp.float32),
    }


def channel_block(block, fir_taps):
    frames_all = block.shape[1]
    extended = jnp.pad(block.astype(jnp.float32), ((0, 0), (TAPS - 1, 0), (0, 0), (0, 0)))
    filtered = fir_taps[0] * extended[:, 0:frames_all]
    for tap_index in range(1, TAPS):
        filtered = filtered + fir_taps[tap_index] * extended[:, tap_index:tap_index + frames_all]
    complex_form = filtered[:, :, 0] + 1j * filtered[:, :, 1]
    spectrum = jnp.fft.fft(complex_form, axis=-1)[..., :CHANS] / math.sqrt(NCH)
    return jnp.stack([jnp.real(spectrum), jnp.imag(spectrum)], axis=2).astype(jnp.bfloat16)

def correlate(own_block, other_block):
    products = jnp.einsum('sfrc,tfqc->rsqtc', own_block.astype(jnp.float32), other_block.astype(jnp.float32))
    real_part = products[0, :, 0] + products[1, :, 1]
    imag_part = products[1, :, 0] - products[0, :, 1]
    return jnp.stack([real_part, imag_part], 0)

def reference(voltage, fir_taps):
    grouped = voltage.reshape(N_STN, SIG_DEV, FRAMES, 2, NCH)
    spectra = lax.map(lambda blk: channel_block(blk, fir_taps), grouped)

    def one_block(block_index):
        own_block = spectra[block_index]
        pieces = []
        for visit_index in range(VISITS):
            partner = ((block_index - visit_index) % N_STN).astype(jnp.int32)
            pieces.append(correlate(own_block, spectra[partner]))
        return jnp.concatenate(pieces, 2) / FRAMES
    blockwise = lax.map(one_block, jnp.arange(N_STN, dtype=jnp.int32))
    return jnp.transpose(blockwise, (1, 0, 2, 3, 4)).reshape(2, SIGNALS, VISITS * SIG_DEV, CHANS)
```

```python
import functools
import math

import jax
import jax.numpy as jnp
import ml_dtypes
import numpy as np
from jax import lax
from jax.experimental import pallas as pl
from jax.experimental.pallas import tpu as pltpu
from jax.sharding import PartitionSpec as P

NCH = 4096
CHANS = 2048
TAPS = 16
VISITS = 4
H = 32
LANES = 128
ROWS = 2 * H
K2 = CHANS // H
GROUP = 4
SUB = 8
BF16 = jnp.bfloat16
F32 = jnp.float32


def split(table):
    high = table.astype(ml_dtypes.bfloat16)
    low = (table - high.astype(np.float64)).astype(ml_dtypes.bfloat16)
    return high, low


def angles(rows, columns, modulus):
    turns = np.outer(rows, columns) % modulus
    return turns.astype(np.float64) * (2.0 * math.pi / modulus)


def stage_one_table():
    theta = angles(np.arange(H), np.arange(H), H)
    cosine, sine = np.cos(theta), np.sin(theta)
    table = np.zeros((2, H, H, 2))
    table[0, :, :, 0], table[0, :, :, 1] = cosine, sine
    table[1, :, :, 0], table[1, :, :, 1] = -sine, cosine
    high, low = split(table.reshape(ROWS, ROWS))
    return np.concatenate([high, high, low], axis=1)


def turn_table():
    theta = angles(np.arange(H), np.arange(LANES), NCH)
    return np.stack([np.cos(theta), np.sin(theta)]).astype(np.float32)


def stage_two_table(groups):
    per_group = K2 // groups
    row = np.arange(per_group)
    inner = per_group // 4
    k2_of_row = 4 * (row % inner) + row // inner
    k2 = (np.arange(groups)[:, None] * per_group + k2_of_row[None]).reshape(-1)
    theta = angles(k2, np.arange(LANES), LANES)
    cosine, sine = np.cos(theta) / math.sqrt(NCH), np.sin(theta) / math.sqrt(NCH)
    slots = per_group // SUB
    shape = (groups, slots, 1, SUB, LANES)
    real = np.concatenate([cosine.reshape(shape), sine.reshape(shape)], -1)
    imag = np.concatenate([-sine.reshape(shape), cosine.reshape(shape)], -1)
    table = np.concatenate([real, imag], 2).reshape(2 * K2, 2 * LANES)
    return split(table)


def halves(value):
    high = value.astype(BF16)
    return high, (value - high.astype(F32)).astype(BF16)


def dot(left, right):
    return lax.dot_general(left, right, (((1,), (0,)), ((), ())), preferred_element_type=F32)


def dot_nt(left, right):
    return lax.dot_general(left, right, (((1,), (1,)), ((), ())), preferred_element_type=F32)


def spectra_kernel(parts, out_frames, place, *refs):
    part_refs, refs = refs[: len(parts)], refs[len(parts) :]
    taps_ref, one_ref, turn_ref, high_ref, low_ref = refs[:5]
    outs, (taps, ext, filtered) = refs[5:-3], refs[-3:]

    @pl.when(pl.program_id(0) == 0)
    def _():
        for h in range(H):
            for half in range(TAPS // SUB):
                tile = taps_ref[pl.ds(half * SUB, SUB), pl.ds(h * LANES, LANES)]
                for r in range(2):
                    taps[pl.ds(half * SUB * ROWS + 2 * h + r, SUB, stride=ROWS), :] = tile

    for number, (frames, ref) in enumerate(zip(parts, part_refs)):
        start = place[3 * number + 1]
        valid = place[3 * number + 2]

        @pl.when(valid == 1)
        def _():
            for f in range(frames):
                ext[start + f] = ref[0, f].astype(F32)

        @pl.when(valid == 0)
        def _():
            for f in range(frames):
                ext[start + f] = jnp.zeros((ROWS, LANES), F32)

    def fir(q, carry):
        rows = pl.ds(pl.multiple_of(q * SUB, SUB), SUB)
        tap = [taps[pl.ds(pl.multiple_of(m * ROWS + q * SUB, SUB), SUB), :] for m in range(TAPS)]
        for f in range(out_frames):
            total = tap[0] * ext[f + 1, rows]
            for m in range(1, TAPS):
                total = total + tap[m] * ext[f + 1 + m, rows]
            filtered[f, rows] = total
        return carry

    lax.fori_loop(0, ROWS // SUB, fir, 0)

    cosine = turn_ref[0]
    sine = turn_ref[1]
    step = 2 * GROUP
    for g in range(out_frames // step):
        block = jnp.concatenate([filtered[g * step + f] for f in range(step)], axis=1)
        high, low = halves(block)
        first = dot(one_ref[...], jnp.concatenate([high, low, high], axis=0))
        turned = []
        for f in range(step):
            real = first[:H, f * LANES : (f + 1) * LANES]
            imag = first[H:, f * LANES : (f + 1) * LANES]
            turned.append(
                jnp.concatenate([real * cosine + imag * sine, imag * cosine - real * sine], axis=1)
            )
        high, low = halves(jnp.concatenate(turned, axis=0))
        spectrum = dot_nt(high_ref[...], high) + dot_nt(low_ref[...], high) + dot_nt(high_ref[...], low)
        spectrum = spectrum.astype(BF16)
        for j in range(2):
            tile = spectrum[:, j * LANES : (j + 1) * LANES]
            at = 0
            for out in outs:
                slots = out.shape[2]
                out[0, 2 * g + j] = tile[at : at + slots * 16].reshape(slots, 16, LANES)
                at += slots * 16


def spectra(parts, out_frames, fir_taps, table, group_sizes):
    signals = parts[0][0].shape[0]
    place = jnp.stack([jnp.asarray(v, jnp.int32) for part in parts for v in part[2:]])
    whole = lambda shape: pl.BlockSpec(shape, lambda s, place: (0,) * len(shape))
    in_specs = [
        pl.BlockSpec(
            (1, part[1], ROWS, LANES), functools.partial(lambda n, s, place: (s, place[3 * n], 0, 0), n)
        )
        for n, part in enumerate(parts)
    ]
    one, turn, (high, low) = stage_one_table(), turn_table(), table
    in_specs += [whole((TAPS, NCH)), whole(one.shape), whole(turn.shape), whole(high.shape), whole(low.shape)]
    groups = out_frames // GROUP
    out_specs = [
        pl.BlockSpec((1, groups, n, 16, LANES), lambda s, place: (s, 0, 0, 0, 0)) for n in group_sizes
    ]
    out_shape = [jax.ShapeDtypeStruct((signals, groups, n, 16, LANES), BF16) for n in group_sizes]
    return pl.pallas_call(
        functools.partial(spectra_body, tuple(p[1] for p in parts), out_frames),
        grid_spec=pltpu.PrefetchScalarGridSpec(
            num_scalar_prefetch=1,
            grid=(signals,),
            in_specs=in_specs,
            out_specs=out_specs,
            scratch_shapes=[
                pltpu.VMEM((TAPS * ROWS, LANES), F32),
                pltpu.VMEM((TAPS + out_frames, ROWS, LANES), F32),
                pltpu.VMEM((out_frames, ROWS, LANES), F32),
            ],
        ),
        out_shape=out_shape,
        compiler_params=pltpu.CompilerParams(vmem_limit_bytes=32 << 20),
        cost_estimate=pl.CostEstimate(
            flops=signals * out_frames * NCH * 8 * 64, bytes_accessed=signals * out_frames * NCH * 8, transcendentals=0
        ),
    )(place, *[part[0] for part in parts], fir_taps, one, turn, high, low)


def spectra_body(parts, out_frames, place, *refs):
    spectra_kernel(parts, out_frames, place, *refs)


def correlate_kernel(jobs, scale, add, place, *refs):
    refs = list(refs)
    raw = refs.pop()
    out = refs.pop()
    before = refs.pop() if add else None
    signals, slots = raw.shape[1], raw.shape[3]
    block = 4
    across = signals // block
    lane = lax.broadcasted_iota(jnp.int32, (SUB, LANES), 1)
    low_half = lane < LANES // 2
    even = lane % (LANES // 2) < LANES // 4
    for number, (own_list, other_list) in enumerate(jobs):
        pairs = [(refs[a], refs[b]) for a, b in zip(own_list, other_list)]

        def tile(index, carry):
            slot = index % slots
            rest = index // slots
            first = rest % across * block
            second = rest // across * block
            totals = tuple(jnp.zeros((SUB, LANES), F32) for _ in range(2 * block * block))
            for a_ref, b_ref in pairs:

                def frames(f, totals):
                    a = [a_ref[first + i, f, slot].astype(F32) for i in range(block)]
                    b = [b_ref[second + i, f, slot].astype(F32) for i in range(block)]
                    new = []
                    for i in range(block):
                        ar, ai = a[i][:SUB], a[i][SUB:]
                        for k in range(block):
                            br, bi = b[k][:SUB], b[k][SUB:]
                            at = 2 * (i * block + k)
                            new.append(totals[at] + (ar * br + ai * bi))
                            new.append(totals[at + 1] + (ai * br - ar * bi))
                    return tuple(new)

                totals = lax.fori_loop(0, a_ref.shape[1], frames, totals)
            for i in range(block):
                for k in range(block):
                    at = 2 * (i * block + k)
                    raw[0, first + i, second + k, slot] = totals[at]
                    raw[1, first + i, second + k, slot] = totals[at + 1]
            return carry

        lax.fori_loop(0, slots * across * across, tile, 0)
        visit = place[number]

        def finish(index, carry):
            part = index // signals
            own = index % signals
            for t in range(signals):
                value = [raw[part, own, t, s] for s in range(slots)]
                if slots == 4:
                    pair = []
                    for x, y in ((value[0], value[2]), (value[1], value[3])):
                        pair.append(
                            jnp.where(low_half, x, y)
                            + pltpu.roll(jnp.where(low_half, y, x), LANES // 2, 1)
                        )
                    merged = jnp.where(even, pair[0], pair[1]) + jnp.where(
                        even, pltpu.roll(pair[0], LANES - LANES // 4, 1), pltpu.roll(pair[1], LANES // 4, 1)
                    )
                else:
                    sums = []
                    for x in value:
                        x = x + pltpu.roll(x, LANES // 2, 1)
                        sums.append(x + pltpu.roll(x, LANES // 4, 1))
                    sums = jnp.concatenate(sums, axis=0) if slots > 1 else sums[0]
                    inner = slots * SUB // 4
                    merged = jnp.zeros((inner, LANES), F32)
                    for j in range(4):
                        mine = lane[:inner] // (LANES // 4) == j
                        merged = jnp.where(mine, sums[j * inner : (j + 1) * inner], merged)
                inner = merged.shape[0]
                rows = pl.ds(t, inner, stride=signals)
                merged = merged * scale
                if add:
                    merged = merged + before[part, own, visit, rows, :]
                out[part, own, visit, rows, :] = merged
            return carry

        lax.fori_loop(0, 2 * signals, finish, 0)


def correlate(arrays, jobs, place, scale, before=None):
    signals, _, slots = arrays[0].shape[:3]
    rows = slots * SUB // 4 * signals
    shape = (2, signals, VISITS, rows, LANES)
    operands = list(arrays) + ([] if before is None else [before])
    vmem = pl.BlockSpec(memory_space=pltpu.VMEM)
    work = sum(arrays[a].shape[1] for own, _ in jobs for a in own)
    return pl.pallas_call(
        functools.partial(correlate_body, jobs, scale, before is not None),
        grid_spec=pltpu.PrefetchScalarGridSpec(
            num_scalar_prefetch=1,
            grid=(1,),
            in_specs=[pl.BlockSpec(x.shape, functools.partial(lambda n, i, place: (0,) * n, x.ndim)) for x in operands],
            out_specs=pl.BlockSpec(shape, lambda i, place: (0,) * len(shape)),
            scratch_shapes=[pltpu.VMEM((2, signals, signals, slots, SUB, LANES), F32)],
        ),
        out_shape=jax.ShapeDtypeStruct(shape, F32),
        compiler_params=pltpu.CompilerParams(vmem_limit_bytes=48 << 20),
        input_output_aliases={} if before is None else {len(operands): 0},
        cost_estimate=pl.CostEstimate(
            flops=work * signals * signals * slots * 1024 * 64, bytes_accessed=8 << 20, transcendentals=0
        ),
    )(place, *operands)


def correlate_body(jobs, scale, add, place, *refs):
    correlate_kernel(jobs, scale, add, place, *refs)


def stacked(voltage):
    s, f = voltage.shape[:2]
    return voltage.reshape(s, f, 2, H, LANES).transpose(0, 1, 3, 2, 4).reshape(s, f, ROWS, LANES)


def natural(out, channels):
    parts, s, visits, rows, lanes = out.shape
    i = channels // lanes
    out = out.reshape(parts, s, visits, i, rows // i, lanes)
    return out.transpose(0, 1, 2, 4, 3, 5).reshape(parts, s, visits * (rows // i), channels)


def shifted(block, axis, distance):
    size = lax.axis_size(axis)
    return lax.ppermute(block, axis, [(i, (i + distance) % size) for i in range(size)])


def neighbours(block):
    size = lax.axis_size("stn")
    two = shifted(block, "stn", 2)
    swapped = lax.ppermute(two, "stn", [(i, i ^ 1) for i in range(size)])
    rest = lax.ppermute(block, "stn", [(i, (i + 1 if i % 2 == 0 else i + 3) % size) for i in range(size)])
    return [swapped, two, rest]


def local(voltage, fir_taps):
    groups = lax.axis_size("tm")
    frames = voltage.shape[1]
    volts = stacked(voltage)
    me = lax.axis_index("tm")
    history = lax.ppermute(volts[:, frames - TAPS :], "tm", [(i, i + 1) for i in range(groups - 1)])
    table = stage_two_table(groups)
    slots = K2 // groups // SUB
    first = spectra(
        [(history, TAPS, 0, 0, 1), (volts, TAPS, 0, TAPS, 1)], TAPS, fir_taps, table, [slots * groups]
    )[0]
    later = spectra(
        [(volts, TAPS, 0, 0, 1), (volts, TAPS, 1, TAPS, 1)], TAPS, fir_taps, table, [slots * groups]
    )[0]
    blocks = []
    for piece in (first, later):
        block = lax.all_to_all(piece, "tm", split_axis=2, concat_axis=1, tiled=True)
        blocks.append([block] + neighbours(block))
    even = lax.axis_index("stn") % 2 == 0
    place = jnp.where(even, jnp.array([0, 1, 2, 3]), jnp.array([0, 3, 2, 1])).astype(jnp.int32)
    arrays = [x for blk in blocks for x in blk]
    jobs = [((0, 4), (v, v + 4)) for v in range(VISITS)]
    out = correlate(arrays, jobs, place, 1.0 / (groups * frames))
    return natural(out, CHANS // groups)


def solution(mesh):
    return jax.shard_map(
        local,
        mesh=mesh,
        in_specs=(P("stn", "tm", None, None), P()),
        out_specs=P(None, "stn", None, "tm"),
        check_vma=False,
    )
```

```python
import functools
import math

import jax
import jax.numpy as jnp
import numpy as np
from jax import lax
from jax.experimental import pallas as pl
from jax.experimental.pallas import tpu as pltpu
from jax.sharding import PartitionSpec as P

NCH = 4096
CHANS = 2048
TAPS = 16
VISITS = 4
H = 32
LANES = 128
ROWS = 2 * H
K2 = CHANS // H
GROUP = 4
SUB = 8
BF16 = jnp.bfloat16
F32 = jnp.float32


def angles(rows, columns, modulus):
    turns = np.outer(rows, columns) % modulus
    return turns.astype(np.float64) * (2.0 * math.pi / modulus)


def stage_one_table():
    theta = angles(np.arange(H), np.arange(H), H)
    cosine, sine = np.cos(theta), np.sin(theta)
    table = np.zeros((2, H, H, 2))
    table[0, :, :, 0], table[0, :, :, 1] = cosine, sine
    table[1, :, :, 0], table[1, :, :, 1] = -sine, cosine
    return np.pad(table.reshape(ROWS, ROWS), ((0, 0), (0, 2 * LANES - ROWS)))


def turn_table():
    theta = angles(np.arange(H), np.arange(LANES), NCH)
    return np.concatenate([np.cos(theta), np.sin(theta)], axis=1)


def stage_two_table(groups):
    per_group = K2 // groups
    row = np.arange(per_group)
    inner = per_group // 4
    k2_of_row = 4 * (row % inner) + row // inner
    k2 = (np.arange(groups)[:, None] * per_group + k2_of_row[None]).reshape(-1)
    theta = angles(k2, np.arange(LANES), LANES)
    cosine, sine = np.cos(theta) / math.sqrt(NCH), np.sin(theta) / math.sqrt(NCH)
    shape = (groups, per_group // SUB, 1, SUB, LANES)
    real = np.concatenate([cosine.reshape(shape), sine.reshape(shape)], -1)
    imag = np.concatenate([-sine.reshape(shape), cosine.reshape(shape)], -1)
    return np.concatenate([real, imag], 2).reshape(2 * K2, 2 * LANES)


def tables(groups):
    two = stage_two_table(groups)
    rolled = np.roll(two, K2, axis=0)
    return np.concatenate([stage_one_table(), turn_table(), two, rolled]).astype(np.float32)


def halves(value):
    high = value.astype(BF16)
    return high, (value - high.astype(F32)).astype(BF16)


def dot(left, right):
    return lax.dot_general(left, right, (((1,), (0,)), ((), ())), preferred_element_type=F32)


def dot_nt(left, right):
    return lax.dot_general(left, right, (((1,), (1,)), ((), ())), preferred_element_type=F32)


def spectra_kernel(parts, out_frames, place, *refs):
    part_refs, refs = refs[: len(parts)], refs[len(parts) :]
    taps_ref, table_ref = refs[:2]
    outs, (taps, one, two, ext, filtered) = refs[2:-5], refs[-5:]

    @pl.when(pl.program_id(0) == 0)
    def _():
        for h in range(H):
            for half in range(TAPS // SUB):
                tile = taps_ref[pl.ds(half * SUB, SUB), pl.ds(h * LANES, LANES)]
                for r in range(2):
                    taps[pl.ds(half * SUB * ROWS + 2 * h + r, SUB, stride=ROWS), :] = tile
        high, low = halves(table_ref[:ROWS, :ROWS])
        one[...] = jnp.concatenate([high, high, low], axis=1)
        start = pl.multiple_of(ROWS + H + place[1] * 2 * K2, SUB)
        high, low = halves(table_ref[pl.ds(start, 2 * K2), :])
        two[0] = high
        two[1] = low

    def body():
        for number, (frames, ref) in enumerate(zip(parts, part_refs)):
            start = place[2 + 3 * number + 1]
            valid = place[2 + 3 * number + 2]

            @pl.when(valid == 1)
            def _():
                for f in range(frames):
                    ext[start + f] = ref[0, f].astype(F32)

            @pl.when(valid == 0)
            def _():
                for f in range(frames):
                    ext[start + f] = jnp.zeros((ROWS, LANES), F32)

        def fir(q, carry):
            rows = pl.ds(pl.multiple_of(q * SUB, SUB), SUB)
            tap = [taps[pl.ds(pl.multiple_of(m * ROWS + q * SUB, SUB), SUB), :] for m in range(TAPS)]
            for f in range(out_frames):
                total = tap[0] * ext[f + 1, rows]
                for m in range(1, TAPS):
                    total = total + tap[m] * ext[f + 1 + m, rows]
                filtered[f, rows] = total
            return carry

        lax.fori_loop(0, ROWS // SUB, fir, 0)

        cosine = table_ref[ROWS : ROWS + H, :LANES]
        sine = table_ref[ROWS : ROWS + H, LANES:]
        step = 2 * GROUP
        for g in range(out_frames // step):
            block = jnp.concatenate([filtered[g * step + f] for f in range(step)], axis=1)
            high, low = halves(block)
            first = dot(one[...], jnp.concatenate([high, low, high], axis=0))
            turned = []
            for f in range(step):
                real = first[:H, f * LANES : (f + 1) * LANES]
                imag = first[H:, f * LANES : (f + 1) * LANES]
                turned.append(
                    jnp.concatenate([real * cosine + imag * sine, imag * cosine - real * sine], axis=1)
                )
            high, low = halves(jnp.concatenate(turned, axis=0))
            spectrum = dot_nt(two[0], high) + dot_nt(two[1], high) + dot_nt(two[0], low)
            spectrum = spectrum.astype(BF16)
            for j in range(2):
                tile = spectrum[:, j * LANES : (j + 1) * LANES]
                at = 0
                for out in outs:
                    slots = out.shape[2]
                    out[0, 2 * g + j] = tile[at : at + slots * 16].reshape(slots, 16, LANES)
                    at += slots * 16

    pl.when(place[0] == 1)(body)


def spectra(parts, out_frames, fir_taps, groups, group_sizes, run=1, order=0):
    signals = parts[0][0].shape[0]
    numbers = [run, order] + [v for part in parts for v in part[2:]]
    place = jnp.stack([jnp.asarray(v, jnp.int32) for v in numbers])
    table = tables(groups)
    whole = lambda shape: pl.BlockSpec(shape, lambda s, place: (0,) * len(shape))
    in_specs = [
        pl.BlockSpec(
            (1, part[1], ROWS, LANES), functools.partial(lambda n, s, place: (s, place[2 + 3 * n], 0, 0), n)
        )
        for n, part in enumerate(parts)
    ]
    in_specs += [whole((TAPS, NCH)), whole(table.shape)]
    tiles = out_frames // GROUP
    out_specs = [pl.BlockSpec((1, tiles, n, 16, LANES), lambda s, place: (s, 0, 0, 0, 0)) for n in group_sizes]
    out_shape = [jax.ShapeDtypeStruct((signals, tiles, n, 16, LANES), BF16) for n in group_sizes]
    return pl.pallas_call(
        functools.partial(spectra_kernel, tuple(p[1] for p in parts), out_frames),
        grid_spec=pltpu.PrefetchScalarGridSpec(
            num_scalar_prefetch=1,
            grid=(signals,),
            in_specs=in_specs,
            out_specs=out_specs,
            scratch_shapes=[
                pltpu.VMEM((TAPS * ROWS, LANES), F32),
                pltpu.VMEM((ROWS, 3 * ROWS), BF16),
                pltpu.VMEM((2, 2 * K2, 2 * LANES), BF16),
                pltpu.VMEM((TAPS + out_frames, ROWS, LANES), F32),
                pltpu.VMEM((out_frames, ROWS, LANES), F32),
            ],
        ),
        out_shape=out_shape,
        compiler_params=pltpu.CompilerParams(vmem_limit_bytes=32 << 20),
        cost_estimate=pl.CostEstimate(
            flops=signals * out_frames * NCH * 8 * 64, bytes_accessed=signals * out_frames * NCH * 8, transcendentals=0
        ),
    )(place, *[part[0] for part in parts], fir_taps, table)


def correlate_kernel(jobs, scale, add, place, *refs):
    refs = list(refs)
    raw = refs.pop()
    out = refs.pop()
    before = refs.pop() if add else None
    signals, slots = raw.shape[1], raw.shape[3]
    block = 4
    across = signals // block
    lane = lax.broadcasted_iota(jnp.int32, (SUB, LANES), 1)
    low_half = lane < LANES // 2
    even = lane % (LANES // 2) < LANES // 4
    for number, (own_list, other_list) in enumerate(jobs):
        pairs = [(refs[a], refs[b]) for a, b in zip(own_list, other_list)]

        def tile(index, carry):
            slot = index % slots
            rest = index // slots
            first = rest % across * block
            second = rest // across * block
            totals = tuple(jnp.zeros((SUB, LANES), F32) for _ in range(2 * block * block))
            for a_ref, b_ref in pairs:

                def frames(f, totals):
                    a = [a_ref[first + i, f, slot].astype(F32) for i in range(block)]
                    b = [b_ref[second + i, f, slot].astype(F32) for i in range(block)]
                    new = []
                    for i in range(block):
                        ar, ai = a[i][:SUB], a[i][SUB:]
                        for k in range(block):
                            br, bi = b[k][:SUB], b[k][SUB:]
                            at = 2 * (i * block + k)
                            new.append(totals[at] + (ar * br + ai * bi))
                            new.append(totals[at + 1] + (ai * br - ar * bi))
                    return tuple(new)

                totals = lax.fori_loop(0, a_ref.shape[1], frames, totals, unroll=4)
            for i in range(block):
                for k in range(block):
                    at = 2 * (i * block + k)
                    raw[0, first + i, second + k, slot] = totals[at]
                    raw[1, first + i, second + k, slot] = totals[at + 1]
            return carry

        lax.fori_loop(0, slots * across * across, tile, 0)
        visit = place[number]

        def finish(index, carry):
            part = index // signals
            own = index % signals
            for t in range(signals):
                value = [raw[part, own, t, s] for s in range(slots)]
                if slots == 4:
                    pair = []
                    for x, y in ((value[0], value[2]), (value[1], value[3])):
                        pair.append(
                            jnp.where(low_half, x, y)
                            + pltpu.roll(jnp.where(low_half, y, x), LANES // 2, 1)
                        )
                    merged = jnp.where(even, pair[0], pair[1]) + jnp.where(
                        even, pltpu.roll(pair[0], LANES - LANES // 4, 1), pltpu.roll(pair[1], LANES // 4, 1)
                    )
                else:
                    sums = []
                    for x in value:
                        x = x + pltpu.roll(x, LANES // 2, 1)
                        sums.append(x + pltpu.roll(x, LANES // 4, 1))
                    sums = jnp.concatenate(sums, axis=0) if slots > 1 else sums[0]
                    inner = slots * SUB // 4
                    merged = jnp.zeros((inner, LANES), F32)
                    for j in range(4):
                        mine = lane[:inner] // (LANES // 4) == j
                        merged = jnp.where(mine, sums[j * inner : (j + 1) * inner], merged)
                inner = merged.shape[0]
                rows = pl.ds(t, inner, stride=signals)
                merged = merged * scale
                if add:
                    merged = merged + before[part, own, visit, rows, :]
                out[part, own, visit, rows, :] = merged
            return carry

        lax.fori_loop(0, 2 * signals, finish, 0)


def correlate(arrays, jobs, place, scale, before=None):
    signals, _, slots = arrays[0].shape[:3]
    rows = slots * SUB // 4 * signals
    shape = (2, signals, VISITS, rows, LANES)
    operands = list(arrays) + ([] if before is None else [before])
    vmem = pl.BlockSpec(memory_space=pltpu.VMEM)
    work = sum(arrays[a].shape[1] for own, _ in jobs for a in own)
    return pl.pallas_call(
        functools.partial(correlate_kernel, jobs, scale, before is not None),
        grid_spec=pltpu.PrefetchScalarGridSpec(
            num_scalar_prefetch=1,
            grid=(1,),
            in_specs=[pl.BlockSpec(x.shape, functools.partial(lambda n, i, place: (0,) * n, x.ndim)) for x in operands],
            out_specs=pl.BlockSpec(shape, lambda i, place: (0,) * len(shape)),
            scratch_shapes=[pltpu.VMEM((2, signals, signals, slots, SUB, LANES), F32)],
        ),
        out_shape=jax.ShapeDtypeStruct(shape, F32),
        compiler_params=pltpu.CompilerParams(vmem_limit_bytes=48 << 20),
        input_output_aliases={} if before is None else {len(operands): 0},
        cost_estimate=pl.CostEstimate(
            flops=work * signals * signals * slots * 1024 * 64, bytes_accessed=8 << 20, transcendentals=0
        ),
    )(place, *operands)


def stacked(voltage):
    s, f = voltage.shape[:2]
    return voltage.reshape(s, f, 2, H, LANES).transpose(0, 1, 3, 2, 4).reshape(s, f, ROWS, LANES)


def natural(out, channels):
    parts, s, visits, rows, lanes = out.shape
    i = channels // lanes
    out = out.reshape(parts, s, visits, i, rows // i, lanes)
    return out.transpose(0, 1, 2, 4, 3, 5).reshape(parts, s, visits * (rows // i), channels)


def shifted(block, axis, distance):
    size = lax.axis_size(axis)
    return lax.ppermute(block, axis, [(i, (i + distance) % size) for i in range(size)])


def neighbours(block):
    size = lax.axis_size("stn")
    two = shifted(block, "stn", 2)
    swapped = lax.ppermute(two, "stn", [(i, i ^ 1) for i in range(size)])
    rest = lax.ppermute(block, "stn", [(i, (i + 1 if i % 2 == 0 else i + 3) % size) for i in range(size)])
    return [block, swapped, two, rest]


def general(volts, fir_taps):
    groups = lax.axis_size("tm")
    frames = volts.shape[1]
    slots = K2 // groups // SUB
    history = lax.ppermute(volts[:, frames - TAPS :], "tm", [(i, i + 1) for i in range(groups - 1)])
    pieces = []
    for block in range(frames // TAPS):
        if block:
            before = (volts, TAPS, block - 1, 0, 1)
        else:
            before = (history, TAPS, 0, 0, 1)
        piece = spectra([before, (volts, TAPS, block, TAPS, 1)], TAPS, fir_taps, groups, [slots * groups])[0]
        pieces.append(lax.all_to_all(piece, "tm", split_axis=2, concat_axis=1, tiled=True))
    return [[piece] for piece in pieces]


def paired(volts, fir_taps):
    frames = volts.shape[1]
    me = lax.axis_index("tm")
    slots = K2 // 2 // SUB
    sizes = [slots, slots]
    swap = [(0, 1), (1, 0)]
    edge = TAPS // 2
    last = frames // edge
    edge_frames = lax.dynamic_slice_in_dim(volts, jnp.where(me == 0, frames - edge, 0), edge, 1)
    visiting = lax.ppermute(edge_frames, "tm", swap)
    own_a, away_a = spectra(
        [(volts, TAPS, 0, 0, me), (volts, TAPS, me, TAPS, 1)], TAPS, fir_taps, 2, sizes, 1, me
    )
    own_b, away_b = spectra(
        [(volts, TAPS, 0, 0, 1), (volts, TAPS, 1, TAPS, 1)], TAPS, fir_taps, 2, sizes, 1 - me, me
    )
    own_c, away_c = spectra(
        [
            (volts, edge, jnp.where(me == 0, last - 2, 0), edge * me, 1),
            (volts, edge, jnp.where(me == 0, last - 1, 1), edge * me + edge, 1),
            (visiting, edge, 0, 2 * edge * (1 - me), 1),
        ],
        edge, fir_taps, 2, sizes, 1, me,
    )
    got_a = lax.ppermute(away_a, "tm", swap)
    got_b = lax.ppermute(away_b, "tm", [(0, 1)])
    got_c = lax.ppermute(away_c, "tm", swap)
    return [[own_a, got_a], [jnp.where(me == 0, own_b, got_b)], [own_c, got_c]]


def local(voltage, fir_taps):
    groups = lax.axis_size("tm")
    volts = stacked(voltage)
    stages = paired(volts, fir_taps) if groups == 2 else general(volts, fir_taps)
    even = lax.axis_index("stn") % 2 == 0
    place = jnp.where(even, jnp.array([0, 1, 2, 3]), jnp.array([0, 3, 2, 1])).astype(jnp.int32)
    out = None
    for pieces in stages:
        arrays = [x for piece in pieces for x in neighbours(piece)]
        own = tuple(range(0, len(arrays), VISITS))
        jobs = [(own, tuple(v + o for o in own)) for v in range(VISITS)]
        out = correlate(arrays, jobs, place, 1.0 / (groups * voltage.shape[1]), out)
    return natural(out, CHANS // groups)


def solution(mesh):
    return jax.shard_map(
        local,
        mesh=mesh,
        in_specs=(P("stn", "tm", None, None), P()),
        out_specs=P(None, "stn", None, "tm"),
        check_vma=False,
    )
```

```python
import functools
import math

import jax
import jax.numpy as jnp
import numpy as np
from jax import lax
from jax.experimental import pallas as pl
from jax.experimental.pallas import tpu as pltpu
from jax.sharding import PartitionSpec as P

NCH = 4096
CHANS = 2048
TAPS = 16
VISITS = 4
H = 32
LANES = 128
ROWS = 2 * H
K2 = CHANS // H
STEP = 8
TILE = 16
SUB = 8
BF16 = jnp.bfloat16
F32 = jnp.float32


def angles(rows, columns, modulus):
    turns = np.outer(rows, columns) % modulus
    return turns.astype(np.float64) * (2.0 * math.pi / modulus)


def stage_one_table():
    theta = angles(np.arange(H), np.arange(H), H)
    cosine, sine = np.cos(theta), np.sin(theta)
    table = np.zeros((2, H, H, 2))
    table[0, :, :, 0], table[0, :, :, 1] = cosine, sine
    table[1, :, :, 0], table[1, :, :, 1] = -sine, cosine
    return np.pad(table.reshape(ROWS, ROWS), ((0, 0), (0, 2 * LANES - ROWS)))


def turn_table():
    theta = angles(np.arange(H), np.arange(LANES), NCH)
    return np.concatenate([np.cos(theta), np.sin(theta)], axis=1)


def stage_two_table(groups):
    theta = angles(np.arange(K2), np.arange(LANES), LANES)
    cosine, sine = np.cos(theta) / math.sqrt(NCH), np.sin(theta) / math.sqrt(NCH)
    real = np.concatenate([cosine, sine], 1).reshape(groups, 1, K2 // groups, 2 * LANES)
    imag = np.concatenate([-sine, cosine], 1).reshape(groups, 1, K2 // groups, 2 * LANES)
    return np.concatenate([real, imag], 1).reshape(2 * K2, 2 * LANES)


def tables(groups):
    two = stage_two_table(groups)
    rolled = np.roll(two, K2, axis=0)
    return np.concatenate([stage_one_table(), turn_table(), two, rolled]).astype(np.float32)


def halves(value):
    high = value.astype(BF16)
    return high, (value - high.astype(F32)).astype(BF16)


def dot(left, right):
    return lax.dot_general(left, right, (((1,), (0,)), ((), ())), preferred_element_type=F32)


def dot_nt(left, right):
    return lax.dot_general(left, right, (((1,), (1,)), ((), ())), preferred_element_type=F32)


def spectra_kernel(groups, parts, out_frames, place, *refs):
    part_refs, refs = refs[: len(parts)], refs[len(parts) :]
    taps_ref, table_ref = refs[:2]
    outs, (taps, one, two, ext, filtered, turned, staged) = refs[2:-7], refs[-7:]
    signal, signals = pl.program_id(0), pl.num_programs(0)
    per_group = K2 // groups
    share = LANES // out_frames
    tiles = H // share

    @pl.when(signal == 0)
    def _():
        for h in range(H):
            for half in range(TAPS // SUB):
                tile = taps_ref[pl.ds(half * SUB, SUB), pl.ds(h * LANES, LANES)]
                for r in range(2):
                    taps[pl.ds(half * SUB * ROWS + 2 * h + r, SUB, stride=ROWS), :] = tile
        high, low = halves(table_ref[:ROWS, :ROWS])
        one[...] = jnp.concatenate([high, high, low], axis=1)
        start = pl.multiple_of(ROWS + H + place[1] * 2 * K2, SUB)
        high, low = halves(table_ref[pl.ds(start, 2 * K2), :])
        two[0] = high
        two[1] = low

    def body():
        for number, (frames, ref) in enumerate(zip(parts, part_refs)):
            start = place[2 + 3 * number + 1]
            valid = place[2 + 3 * number + 2]

            @pl.when(valid == 1)
            def _():
                for f in range(frames):
                    ext[start + f] = ref[0, f].astype(F32)

            @pl.when(valid == 0)
            def _():
                for f in range(frames):
                    ext[start + f] = jnp.zeros((ROWS, LANES), F32)

        def fir(q, carry):
            rows = pl.ds(pl.multiple_of(q * SUB, SUB), SUB)
            tap = [taps[pl.ds(pl.multiple_of(m * ROWS + q * SUB, SUB), SUB), :] for m in range(TAPS)]
            for f in range(out_frames):
                total = tap[0] * ext[f + 1, rows]
                for m in range(1, TAPS):
                    total = total + tap[m] * ext[f + 1 + m, rows]
                filtered[f, rows] = total
            return carry

        lax.fori_loop(0, ROWS // SUB, fir, 0)

        cosine = table_ref[ROWS : ROWS + H, :LANES]
        sine = table_ref[ROWS : ROWS + H, LANES:]
        for g in range(out_frames // STEP):
            block = jnp.concatenate([filtered[g * STEP + f] for f in range(STEP)], axis=1)
            high, low = halves(block)
            first = dot(one[...], jnp.concatenate([high, low, high], axis=0))
            for f in range(STEP):
                real = first[:H, f * LANES : (f + 1) * LANES]
                imag = first[H:, f * LANES : (f + 1) * LANES]
                at = (g * STEP + f) * ROWS
                turned[at : at + H, :] = real * cosine + imag * sine
                turned[at + H : at + ROWS, :] = imag * cosine - real * sine
        for pair in range(tiles // 2):
            rows = []
            for k1 in range(2 * pair * share, 2 * (pair + 1) * share):
                for f in range(0, out_frames, SUB):
                    rows.append(
                        jnp.concatenate(
                            [turned[pl.ds(f * ROWS + p * H + k1, SUB, stride=ROWS), :] for p in range(2)], axis=1
                        )
                    )
            high, low = halves(jnp.concatenate(rows, axis=0))
            spectrum = dot_nt(two[0], high) + dot_nt(two[1], high) + dot_nt(two[0], low)
            for k in range(2):
                for t in range(groups):
                    for p in range(2):
                        for k2 in range(0, per_group, SUB):
                            row = (t * 2 + p) * per_group + k2
                            start = ((t * per_group + k2) * tiles + 2 * pair + k) * TILE + p * SUB
                            staged[pl.ds(start + signal, SUB, stride=tiles * TILE), :] = spectrum[
                                row : row + SUB, k * LANES : (k + 1) * LANES
                            ]

        @pl.when(signal == signals - 1)
        def _():
            at = 0
            for out in outs:

                def write(k2, carry):
                    for k in range(tiles):
                        start = pl.multiple_of((at + k2) * tiles * TILE + k * TILE, TILE)
                        out[k2, k] = staged[pl.ds(start, TILE), :].astype(BF16)
                    return carry

                lax.fori_loop(0, out.shape[0], write, 0)
                at += out.shape[0]

    pl.when(place[0] == 1)(body)


def spectra(parts, out_frames, fir_taps, groups, sizes, run=1, order=0):
    signals = parts[0][0].shape[0]
    numbers = [run, order] + [v for part in parts for v in part[2:]]
    place = jnp.stack([jnp.asarray(v, jnp.int32) for v in numbers])
    table = tables(groups)
    tiles = H * out_frames // LANES
    whole = lambda shape: pl.BlockSpec(shape, lambda s, place: (0,) * len(shape))
    in_specs = [
        pl.BlockSpec(
            (1, part[1], ROWS, LANES), functools.partial(lambda n, s, place: (s, place[2 + 3 * n], 0, 0), n)
        )
        for n, part in enumerate(parts)
    ]
    in_specs += [whole((TAPS, NCH)), whole(table.shape)]
    shapes = [(n, tiles, TILE, LANES) for n in sizes]
    return pl.pallas_call(
        functools.partial(spectra_kernel, groups, tuple(p[1] for p in parts), out_frames),
        grid_spec=pltpu.PrefetchScalarGridSpec(
            num_scalar_prefetch=1,
            grid=(signals,),
            in_specs=in_specs,
            out_specs=[whole(shape) for shape in shapes],
            scratch_shapes=[
                pltpu.VMEM((TAPS * ROWS, LANES), F32),
                pltpu.VMEM((ROWS, 3 * ROWS), BF16),
                pltpu.VMEM((2, 2 * K2, 2 * LANES), BF16),
                pltpu.VMEM((TAPS + out_frames, ROWS, LANES), F32),
                pltpu.VMEM((out_frames, ROWS, LANES), F32),
                pltpu.VMEM((out_frames * ROWS, LANES), F32),
                pltpu.VMEM((K2 * tiles * TILE, LANES), F32),
            ],
        ),
        out_shape=[jax.ShapeDtypeStruct(shape, BF16) for shape in shapes],
        compiler_params=pltpu.CompilerParams(vmem_limit_bytes=32 << 20),
        cost_estimate=pl.CostEstimate(
            flops=signals * out_frames * NCH * 8 * 64, bytes_accessed=signals * out_frames * NCH * 8, transcendentals=0
        ),
    )(place, *[part[0] for part in parts], fir_taps, table)


def correlate_kernel(pieces, per_group, scale, add, last, place, *refs):
    refs = list(refs)
    sums = refs.pop() if last else None
    out = refs.pop()
    before = refs.pop() if add else None
    if not last:
        sums = out
    half = per_group // 2
    lane = lax.broadcasted_iota(jnp.int32, (SUB, LANES), 1)
    first_tile = lane < LANES // 2
    real_lane = lane % TILE < SUB
    sign = jnp.where(real_lane, 1.0, -1.0).astype(F32)
    for number, piece in enumerate(pieces):
        tiles = refs[piece[0][0][0]].shape[1]
        share = H // tiles
        where = lax.broadcasted_iota(jnp.int32, (TILE, LANES), 1) // (LANES // share)

        def pair(index, carry):
            k2 = index // tiles
            k1 = index % tiles
            own, other = [], []
            for position in range(len(piece[0])):
                rows = []
                for tile in range(2):
                    array, start = piece[0][position]
                    a = refs[array][start + tile * half + k2, k1]
                    rows += [jnp.where(where == c, a, jnp.zeros_like(a)) for c in range(share)]
                own.append(jnp.concatenate(rows, axis=0))
                rows = []
                for tile in range(2):
                    for visit in range(VISITS):
                        array, start = piece[visit][position]
                        rows.append(refs[array][start + tile * half + k2, k1])
                other.append(jnp.concatenate(rows, axis=0))
            product = dot_nt(jnp.concatenate(own, axis=1), jnp.concatenate(other, axis=1))
            for c in range(share):
                value = []
                for p in range(2):
                    at = [((tile * share + c) * 2 + p) * SUB for tile in range(2)]
                    value.append(
                        jnp.where(first_tile, product[at[0] : at[0] + SUB], product[at[1] : at[1] + SUB])
                    )
                turned = jnp.where(
                    real_lane, pltpu.roll(value[1], LANES - SUB, 1), pltpu.roll(value[1], SUB, 1)
                )
                total = value[0] * sign + turned
                channel = k2 // 4 * LANES + k2 % 4 * H + k1 * share + c
                rows = pl.ds(pl.multiple_of(channel * SUB, SUB), SUB)
                if number:
                    total = total + sums[rows, :]
                elif add:
                    total = total + before[rows, :]
                sums[rows, :] = total
            return carry

        lax.fori_loop(0, half * tiles, pair, 0, unroll=2)
    if not last:
        return

    def finish(index, carry):
        block = index // SUB
        signal = index % SUB
        value = sums[pl.ds(block * LANES * SUB + signal, LANES, stride=SUB), :]
        value = jnp.transpose(value * scale)
        at = 0
        for tile in range(2):
            for visit in range(VISITS):
                for part in range(2):
                    out[part, signal, place[visit], tile * (half // 4) + block] = value[at : at + SUB]
                    at += SUB
        return carry

    lax.fori_loop(0, half // 4 * SUB, finish, 0)


def correlate(arrays, pieces, per_group, place, scale, before, last):
    signals = TILE // 2
    rows = per_group // 2 * H * SUB
    shape = (2, signals, VISITS, per_group // 4, SUB, LANES) if last else (rows, LANES)
    operands = list(arrays) + ([] if before is None else [before])
    whole = lambda shape: pl.BlockSpec(shape, lambda i, place: (0,) * len(shape))
    return pl.pallas_call(
        functools.partial(correlate_kernel, pieces, per_group, scale, before is not None, last),
        grid_spec=pltpu.PrefetchScalarGridSpec(
            num_scalar_prefetch=1,
            grid=(1,),
            in_specs=[whole(x.shape) for x in operands],
            out_specs=whole(shape),
            scratch_shapes=[pltpu.VMEM((rows, LANES), F32)] if last else [],
        ),
        out_shape=jax.ShapeDtypeStruct(shape, F32),
        compiler_params=pltpu.CompilerParams(vmem_limit_bytes=48 << 20),
        input_output_aliases={} if before is None or last else {len(operands): 0},
        cost_estimate=pl.CostEstimate(flops=8 << 30, bytes_accessed=8 << 20, transcendentals=0),
    )(place, *operands)


def stacked(voltage):
    s, f = voltage.shape[:2]
    return voltage.reshape(s, f, 2, H, LANES).transpose(0, 1, 3, 2, 4).reshape(s, f, ROWS, LANES)


def natural(out):
    parts, s, visits, i, t, lanes = out.shape
    return out.transpose(0, 1, 2, 4, 3, 5).reshape(parts, s, visits * t, i * lanes)


def shifted(block, axis, distance):
    size = lax.axis_size(axis)
    return lax.ppermute(block, axis, [(i, (i + distance) % size) for i in range(size)])


def neighbours(block):
    size = lax.axis_size("stn")
    two = shifted(block, "stn", 2)
    swapped = lax.ppermute(two, "stn", [(i, i ^ 1) for i in range(size)])
    rest = lax.ppermute(block, "stn", [(i, (i + 1 if i % 2 == 0 else i + 3) % size) for i in range(size)])
    return [block, swapped, two, rest]


def general(volts, fir_taps):
    groups = lax.axis_size("tm")
    frames = volts.shape[1]
    history = lax.ppermute(volts[:, frames - TAPS :], "tm", [(i, i + 1) for i in range(groups - 1)])
    parts = [(history, TAPS, 0, 0, 1)] + [(volts, TAPS, i, TAPS * (i + 1), 1) for i in range(frames // TAPS)]
    spectrum = spectra(parts, frames, fir_taps, groups, [K2])[0]
    return [[lax.all_to_all(spectrum, "tm", split_axis=0, concat_axis=0, tiled=True)]]


def paired(volts, fir_taps):
    frames = volts.shape[1]
    me = lax.axis_index("tm")
    sizes = [K2 // 2, K2 // 2]
    swap = [(0, 1), (1, 0)]
    edge = TAPS // 2
    last = frames // edge
    edge_frames = lax.dynamic_slice_in_dim(volts, jnp.where(me == 0, frames - edge, 0), edge, 1)
    visiting = lax.ppermute(edge_frames, "tm", swap)
    own_a, away_a = spectra(
        [(volts, TAPS, 0, 0, me), (volts, TAPS, me, TAPS, 1)], TAPS, fir_taps, 2, sizes, 1, me
    )
    own_b, away_b = spectra(
        [(volts, TAPS, 0, 0, 1), (volts, TAPS, 1, TAPS, 1)], TAPS, fir_taps, 2, sizes, 1 - me, me
    )
    own_c, away_c = spectra(
        [
            (volts, edge, jnp.where(me == 0, last - 2, 0), edge * me, 1),
            (volts, edge, jnp.where(me == 0, last - 1, 1), edge * me + edge, 1),
            (visiting, edge, 0, 2 * edge * (1 - me), 1),
        ],
        edge, fir_taps, 2, sizes, 1, me,
    )
    got_a = lax.ppermute(away_a, "tm", swap)
    got_b = lax.ppermute(away_b, "tm", [(0, 1)])
    got_c = lax.ppermute(away_c, "tm", swap)
    return [[own_a, got_a], [jnp.where(me == 0, own_b, got_b)], [own_c, got_c]]


def local(voltage, fir_taps):
    groups = lax.axis_size("tm")
    per_group = K2 // groups
    volts = stacked(voltage)
    stages = paired(volts, fir_taps) if groups == 2 else general(volts, fir_taps)
    even = lax.axis_index("stn") % 2 == 0
    place = jnp.where(even, jnp.array([0, 1, 2, 3]), jnp.array([0, 3, 2, 1])).astype(jnp.int32)
    scale = 1.0 / (groups * voltage.shape[1])
    out = None
    for number, pieces in enumerate(stages):
        arrays = [x for piece in pieces for x in neighbours(piece)]
        starts = range(0, arrays[0].shape[0], per_group)
        laid = tuple(
            tuple((VISITS * n + visit, start) for n in range(len(pieces)) for start in starts)
            for visit in range(VISITS)
        )
        out = correlate(arrays, [laid], per_group, place, scale, out, number == len(stages) - 1)
    return natural(out)


def solution(mesh):
    return jax.shard_map(
        local,
        mesh=mesh,
        in_specs=(P("stn", "tm", None, None), P()),
        out_specs=P(None, "stn", None, "tm"),
        check_vma=False,
    )
```

```python
import functools
import math

import jax
import jax.numpy as jnp
import numpy as np
from jax import lax
from jax.experimental import pallas as pl
from jax.experimental.pallas import tpu as pltpu
from jax.sharding import PartitionSpec as P

NCH = 4096
CHANS = 2048
TAPS = 16
VISITS = 4
H = 32
LANES = 128
ROWS = 2 * H
K2 = CHANS // H
STEP = 8
TILE = 16
MEMBERS = 4
PAD = 8
SUB = 8
BF16 = jnp.bfloat16
F32 = jnp.float32


def angles(rows, columns, modulus):
    turns = np.outer(rows, columns) % modulus
    return turns.astype(np.float64) * (2.0 * math.pi / modulus)


def stage_one_table():
    theta = angles(np.arange(H), np.arange(H), H)
    cosine, sine = np.cos(theta), np.sin(theta)
    table = np.zeros((2, H, H, 2))
    table[0, :, :, 0], table[0, :, :, 1] = cosine, sine
    table[1, :, :, 0], table[1, :, :, 1] = -sine, cosine
    return np.pad(table.reshape(ROWS, ROWS), ((0, 0), (0, 2 * LANES - ROWS)))


def turn_table():
    theta = angles(np.arange(H), np.arange(LANES), NCH)
    return np.concatenate([np.cos(theta), np.sin(theta)], axis=1)


def stage_two_table(groups):
    theta = angles(np.arange(K2), np.arange(LANES), LANES)
    cosine, sine = np.cos(theta) / math.sqrt(NCH), np.sin(theta) / math.sqrt(NCH)
    real = np.concatenate([cosine, sine], 1).reshape(groups, 1, K2 // groups, 2 * LANES)
    imag = np.concatenate([-sine, cosine], 1).reshape(groups, 1, K2 // groups, 2 * LANES)
    return np.concatenate([real, imag], 1).reshape(2 * K2, 2 * LANES)


def tables(groups):
    two = stage_two_table(groups)
    rolled = np.roll(two, K2, axis=0)
    return np.concatenate([stage_one_table(), turn_table(), two, rolled]).astype(np.float32)


def halves(value):
    high = value.astype(BF16)
    return high, (value - high.astype(F32)).astype(BF16)


def dot(left, right):
    return lax.dot_general(left, right, (((1,), (0,)), ((), ())), preferred_element_type=F32)


def dot_nt(left, right):
    return lax.dot_general(left, right, (((1,), (1,)), ((), ())), preferred_element_type=F32)


def spectra_kernel(groups, parts, out_frames, place, *refs):
    part_refs, refs = refs[: len(parts)], refs[len(parts) :]
    taps_ref, table_ref = refs[:2]
    outs, (taps, one, two, ext, filtered, turned, staged) = refs[2:-7], refs[-7:]
    step, steps, members = pl.program_id(0), pl.num_programs(0), part_refs[0].shape[0]
    per_group = K2 // groups
    share = LANES // out_frames
    tiles = H // share
    pairs = tiles // 2
    frame_rows, row_rows = ROWS + PAD, tiles * TILE + PAD

    @pl.when(step == 0)
    def _():
        for h in range(H):
            for half in range(TAPS // SUB):
                tile = taps_ref[pl.ds(half * SUB, SUB), pl.ds(h * LANES, LANES)]
                for r in range(2):
                    taps[pl.ds(half * SUB * ROWS + 2 * h + r, SUB, stride=ROWS), :] = tile
        high, low = halves(table_ref[:ROWS, :ROWS])
        one[...] = jnp.concatenate([high, high, low], axis=1)
        start = pl.multiple_of(ROWS + H + place[1] * 2 * K2, SUB)
        high, low = halves(table_ref[pl.ds(start, 2 * K2), :])
        two[0] = high
        two[1] = low

    def load(member):
        for number, (frames, ref) in enumerate(zip(parts, part_refs)):
            start = place[2 + 3 * number + 1]
            valid = place[2 + 3 * number + 2]

            @pl.when(valid == 1)
            def _():
                for f in range(frames):
                    ext[member, start + f] = ref[member, f].astype(F32)

            @pl.when(valid == 0)
            def _():
                for f in range(frames):
                    ext[member, start + f] = jnp.zeros((ROWS, LANES), F32)

    def filter_rows(member, q):
        rows = pl.ds(pl.multiple_of(q * SUB, SUB), SUB)
        tap = [taps[pl.ds(pl.multiple_of(m * ROWS + q * SUB, SUB), SUB), :] for m in range(TAPS)]
        for f in range(out_frames):
            total = tap[0] * ext[member, f + 1, rows]
            for m in range(1, TAPS):
                total = total + tap[m] * ext[member, f + 1 + m, rows]
            filtered[member, f, rows] = total

    def first_stage(member):
        cosine = table_ref[ROWS : ROWS + H, :LANES]
        sine = table_ref[ROWS : ROWS + H, LANES:]
        for g in range(out_frames // STEP):
            block = jnp.concatenate([filtered[member, g * STEP + f] for f in range(STEP)], axis=1)
            high, low = halves(block)
            first = dot(one[...], jnp.concatenate([high, low, high], axis=0))
            for f in range(STEP):
                real = first[:H, f * LANES : (f + 1) * LANES]
                imag = first[H:, f * LANES : (f + 1) * LANES]
                at = (g * STEP + f) * frame_rows
                turned[member, at : at + H, :] = real * cosine + imag * sine
                turned[member, at + H : at + ROWS, :] = imag * cosine - real * sine

    def second_stage(member, pair):
        rows = []
        for k1 in range(2 * pair * share, 2 * (pair + 1) * share):
            for f in range(0, out_frames, SUB):
                rows.append(
                    jnp.concatenate(
                        [turned[member, pl.ds(f * frame_rows + p * H + k1, SUB, stride=frame_rows), :] for p in range(2)],
                        axis=1,
                    )
                )
        high, low = halves(jnp.concatenate(rows, axis=0))
        spectrum = dot_nt(two[0], high) + dot_nt(two[1], high) + dot_nt(two[0], low)
        for k in range(2):
            for t in range(groups):
                for p in range(2):
                    for k2 in range(0, per_group, SUB):
                        row = (t * 2 + p) * per_group + k2
                        start = (t * per_group + k2) * row_rows + (2 * pair + k) * TILE + p * SUB
                        staged[pl.ds(start + step * members + member, SUB, stride=row_rows), :] = spectrum[
                            row : row + SUB, k * LANES : (k + 1) * LANES
                        ]

    def write():
        at = 0
        for out in outs:

            def write_row(k2, carry):
                for k in range(tiles):
                    start = pl.multiple_of((at + k2) * row_rows + k * TILE, PAD)
                    out[k2, k] = staged[pl.ds(start, TILE), :].astype(BF16)
                return carry

            lax.fori_loop(0, out.shape[0], write_row, 0, unroll=2)
            at += out.shape[0]

    @pl.when(place[0] == 1)
    def _():
        for member in range(members):
            load(member)

        def filter_one(index, carry):
            filter_rows(index // (ROWS // SUB), index % (ROWS // SUB))
            return carry

        lax.fori_loop(0, members * (ROWS // SUB), filter_one, 0)
        for member in range(members):
            first_stage(member)
        for member in range(members):
            for pair in range(pairs):
                second_stage(member, pair)

        @pl.when(step == steps - 1)
        def _():
            write()


def after(value, *others):
    return lax.optimization_barrier((value, *others))[0]


def spectra(parts, out_frames, fir_taps, groups, sizes, run=1, order=0, wait=(), cost=10**6):
    signals = parts[0][0].shape[0]
    numbers = [run, order] + [v for part in parts for v in part[2:]]
    place = jnp.stack([jnp.asarray(v, jnp.int32) for v in numbers])
    place = after(place, *wait)
    table = tables(groups)
    tiles = H * out_frames // LANES
    whole = lambda shape: pl.BlockSpec(shape, lambda s, place: (0,) * len(shape))
    in_specs = [
        pl.BlockSpec(
            (MEMBERS, part[1], ROWS, LANES), functools.partial(lambda n, s, place: (s, place[2 + 3 * n], 0, 0), n)
        )
        for n, part in enumerate(parts)
    ]
    in_specs += [whole((TAPS, NCH)), whole(table.shape)]
    shapes = [(n, tiles, TILE, LANES) for n in sizes]
    return pl.pallas_call(
        functools.partial(spectra_kernel, groups, tuple(p[1] for p in parts), out_frames),
        grid_spec=pltpu.PrefetchScalarGridSpec(
            num_scalar_prefetch=1,
            grid=(signals // MEMBERS,),
            in_specs=in_specs,
            out_specs=[whole(shape) for shape in shapes],
            scratch_shapes=[
                pltpu.VMEM((TAPS * ROWS, LANES), F32),
                pltpu.VMEM((ROWS, 3 * ROWS), BF16),
                pltpu.VMEM((2, 2 * K2, 2 * LANES), BF16),
                pltpu.VMEM((MEMBERS, TAPS + out_frames, ROWS, LANES), F32),
                pltpu.VMEM((MEMBERS, out_frames, ROWS, LANES), F32),
                pltpu.VMEM((MEMBERS, out_frames * (ROWS + PAD), LANES), F32),
                pltpu.VMEM((K2 * (tiles * TILE + PAD), LANES), F32),
            ],
        ),
        out_shape=[jax.ShapeDtypeStruct(shape, BF16) for shape in shapes],
        compiler_params=pltpu.CompilerParams(vmem_limit_bytes=32 << 20),
        cost_estimate=pl.CostEstimate(
            flops=cost, bytes_accessed=0, transcendentals=0
        ),
    )(place, *[part[0] for part in parts], fir_taps, table)


def correlate_kernel(pieces, per_group, scale, add, last, place, *refs):
    refs = list(refs)
    sums = refs.pop() if last else None
    out = refs.pop()
    before = refs.pop() if add else None
    if not last:
        sums = out
    half = per_group // 2
    lane = lax.broadcasted_iota(jnp.int32, (SUB, LANES), 1)
    first_tile = lane < LANES // 2
    real_lane = lane % TILE < SUB
    sign = jnp.where(real_lane, 1.0, -1.0).astype(F32)
    for number, piece in enumerate(pieces):
        tiles, piece = piece
        share = H // tiles
        where = lax.broadcasted_iota(jnp.int32, (TILE, LANES), 1) // (LANES // share)

        def pair(index, carry):
            k2 = index // tiles
            k1 = index % tiles
            own, other = [], []
            for position in range(len(piece[0])):
                rows = []
                for tile in range(2):
                    array, row, column = piece[0][position]
                    a = refs[array][row + tile * half + k2, column + k1]
                    rows += [jnp.where(where == c, a, jnp.zeros_like(a)) for c in range(share)]
                own.append(jnp.concatenate(rows, axis=0))
                rows = []
                for tile in range(2):
                    for visit in range(VISITS):
                        array, row, column = piece[visit][position]
                        rows.append(refs[array][row + tile * half + k2, column + k1])
                other.append(jnp.concatenate(rows, axis=0))
            product = dot_nt(jnp.concatenate(own, axis=1), jnp.concatenate(other, axis=1))
            for c in range(share):
                value = []
                for p in range(2):
                    at = [((tile * share + c) * 2 + p) * SUB for tile in range(2)]
                    value.append(
                        jnp.where(first_tile, product[at[0] : at[0] + SUB], product[at[1] : at[1] + SUB])
                    )
                turned = jnp.where(
                    real_lane, pltpu.roll(value[1], LANES - SUB, 1), pltpu.roll(value[1], SUB, 1)
                )
                total = value[0] * sign + turned
                channel = k2 // 4 * LANES + k2 % 4 * H + k1 * share + c
                rows = pl.ds(pl.multiple_of(channel * SUB, SUB), SUB)
                if number:
                    total = total + sums[rows, :]
                elif add:
                    total = total + before[rows, :]
                sums[rows, :] = total
            return carry

        lax.fori_loop(0, half * tiles, pair, 0, unroll=16)
    if not last:
        return

    def finish(index, carry):
        block = index // SUB
        signal = index % SUB
        value = sums[pl.ds(block * LANES * SUB + signal, LANES, stride=SUB), :]
        value = jnp.transpose(value * scale)
        at = 0
        for tile in range(2):
            for visit in range(VISITS):
                for part in range(2):
                    out[part, signal, place[visit], tile * (half // 4) + block] = value[at : at + SUB]
                    at += SUB
        return carry

    lax.fori_loop(0, half // 4 * SUB, finish, 0)


def correlate(arrays, pieces, per_group, place, scale, before, last, wait=()):
    signals = TILE // 2
    rows = per_group // 2 * H * SUB
    place = after(place, *wait)
    shape = (2, signals, VISITS, per_group // 4, SUB, LANES) if last else (rows, LANES)
    operands = list(arrays) + ([] if before is None else [before])
    whole = lambda shape: pl.BlockSpec(shape, lambda i, place: (0,) * len(shape))
    return pl.pallas_call(
        functools.partial(correlate_kernel, pieces, per_group, scale, before is not None, last),
        grid_spec=pltpu.PrefetchScalarGridSpec(
            num_scalar_prefetch=1,
            grid=(1,),
            in_specs=[whole(x.shape) for x in operands],
            out_specs=whole(shape),
            scratch_shapes=[pltpu.VMEM((rows, LANES), F32)] if last else [],
        ),
        out_shape=jax.ShapeDtypeStruct(shape, F32),
        compiler_params=pltpu.CompilerParams(vmem_limit_bytes=48 << 20),
        input_output_aliases={} if before is None or last else {len(operands): 0},
        cost_estimate=pl.CostEstimate(flops=6 * 10**9, bytes_accessed=0, transcendentals=0),
    )(place, *operands)


def stacked(voltage):
    s, f = voltage.shape[:2]
    return voltage.reshape(s, f, 2, H, LANES).transpose(0, 1, 3, 2, 4).reshape(s, f, ROWS, LANES)


def natural(out):
    parts, s, visits, i, t, lanes = out.shape
    return out.transpose(0, 1, 2, 4, 3, 5).reshape(parts, s, visits * t, i * lanes)


def shifted(block, axis, distance):
    size = lax.axis_size(axis)
    return lax.ppermute(block, axis, [(i, (i + distance) % size) for i in range(size)])


def farther(block):
    size = lax.axis_size("stn")
    rest = lax.ppermute(block, "stn", [(i, (i + 1 if i % 2 == 0 else i + 3) % size) for i in range(size)])
    return shifted(block, "stn", 2), rest


def exchanged(block):
    return lax.ppermute(block, "stn", [(i, i ^ 1) for i in range(lax.axis_size("stn"))])


def general(volts, fir_taps):
    groups = lax.axis_size("tm")
    frames = volts.shape[1]
    history = lax.ppermute(volts[:, frames - TAPS :], "tm", [(i, i + 1) for i in range(groups - 1)])
    parts = [(history, TAPS, 0, 0, 1)] + [(volts, TAPS, i, TAPS * (i + 1), 1) for i in range(frames // TAPS)]
    spectrum = spectra(parts, frames, fir_taps, groups, [K2])[0]
    spectrum = lax.all_to_all(spectrum, "tm", split_axis=0, concat_axis=0, tiled=True)
    tiles = spectrum.shape[1]
    return [([spectrum], [(tiles, [(0, K2 // groups * t, 0) for t in range(groups)])])]


def paired(volts, fir_taps, correlated):
    frames = volts.shape[1]
    me = lax.axis_index("tm")
    sizes = [K2 // 2, K2 // 2]
    swap = [(0, 1), (1, 0)]
    edge = TAPS // 2
    last = frames // edge
    edge_frames = lax.dynamic_slice_in_dim(volts, jnp.where(me == 0, frames - edge, 0), edge, 1)
    visiting = lax.ppermute(edge_frames, "tm", swap)
    own_a, away_a = spectra(
        [(volts, TAPS, 0, 0, me), (volts, TAPS, me, TAPS, 1)], TAPS, fir_taps, 2, sizes, 1, me, (edge_frames,)
    )
    got_a = lax.ppermute(away_a, "tm", swap)
    two_a, rest_a = farther(own_a)
    own_b, away_b = spectra(
        [(volts, TAPS, 0, 0, 1), (volts, TAPS, 1, TAPS, 1)], TAPS, fir_taps, 2, sizes, 1 - me, me, (own_a,)
    )
    got_b = lax.ppermute(away_b, "tm", [(0, 1)])
    pair_a = exchanged(two_a)
    own_c, away_c = spectra(
        [
            (volts, edge, jnp.where(me == 0, last - 2, 0), edge * me, 1),
            (volts, edge, jnp.where(me == 0, last - 1, 1), edge * me + edge, 1),
            (visiting, edge, 0, 2 * edge * (1 - me), 1),
        ],
        edge, fir_taps, 2, sizes, 1, me, (own_b, two_a, got_a), 9 * 10**9,
    )
    got_c = lax.ppermute(away_c, "tm", swap)
    two_g, rest_g = farther(got_a)
    pair_g = exchanged(two_g)
    own_c = after(own_c, two_g, pair_a, rest_a)
    rest = jnp.concatenate([jnp.where(me == 0, own_b, got_b), own_c, got_c], axis=1)
    two_r, rest_r = farther(rest)
    pair_r = exchanged(two_r)
    many, few = own_a.shape[1], own_c.shape[1]
    sums = correlated(
        [own_a, pair_a, two_a, rest_a, got_a, pair_g, two_g, rest_g], [(many, [(0, 0, 0), (1, 0, 0)])], None, False
    )
    return correlated(
        [rest, pair_r, two_r, rest_r], [(many, [(0, 0, 0)]), (few, [(0, 0, many), (0, 0, many + few)])], sums, True
    )


def general(volts, fir_taps, correlated):
    groups = lax.axis_size("tm")
    frames = volts.shape[1]
    history = lax.ppermute(volts[:, frames - TAPS :], "tm", [(i, i + 1) for i in range(groups - 1)])
    parts = [(history, TAPS, 0, 0, 1)] + [(volts, TAPS, i, TAPS * (i + 1), 1) for i in range(frames // TAPS)]
    spectrum = spectra(parts, frames, fir_taps, groups, [K2])[0]
    spectrum = lax.all_to_all(spectrum, "tm", split_axis=0, concat_axis=0, tiled=True)
    two, rest = farther(spectrum)
    spots = [(0, K2 // groups * t, 0) for t in range(groups)]
    return correlated([spectrum, exchanged(two), two, rest], [(spectrum.shape[1], spots)], None, True)


def local(voltage, fir_taps):
    groups = lax.axis_size("tm")
    even = lax.axis_index("stn") % 2 == 0
    place = jnp.where(even, jnp.array([0, 1, 2, 3]), jnp.array([0, 3, 2, 1])).astype(jnp.int32)
    scale = 1.0 / (groups * voltage.shape[1])

    def correlated(arrays, pieces, before, last, wait=()):
        laid = [
            (tiles, [[(VISITS * n + visit, row, column) for n, row, column in spots] for visit in range(VISITS)])
            for tiles, spots in pieces
        ]
        return correlate(arrays, laid, K2 // groups, place, scale, before, last, wait)

    run = paired if groups == 2 else general
    return natural(run(stacked(voltage), fir_taps, correlated))


def solution(mesh):
    return jax.shard_map(
        local,
        mesh=mesh,
        in_specs=(P("stn", "tm", None, None), P()),
        out_specs=P(None, "stn", None, "tm"),
        check_vma=False,
    )
```

```python
import functools
import math

import jax
import jax.numpy as jnp
import numpy as np
from jax import lax
from jax.experimental import pallas as pl
from jax.experimental.pallas import tpu as pltpu
from jax.sharding import PartitionSpec as P

NCH = 4096
CHANS = 2048
TAPS = 16
VISITS = 4
H = 32
LANES = 128
ROWS = 2 * H
K2 = CHANS // H
STEP = 8
TILE = 16
MEMBERS = 4
PAD = 8
SUB = 8
BF16 = jnp.bfloat16
F32 = jnp.float32


def angles(rows, columns, modulus):
    turns = np.outer(rows, columns) % modulus
    return turns.astype(np.float64) * (2.0 * math.pi / modulus)


def stage_one_table():
    theta = angles(np.arange(H), np.arange(H), H)
    cosine, sine = np.cos(theta), np.sin(theta)
    table = np.zeros((2, H, H, 2))
    table[0, :, :, 0], table[0, :, :, 1] = cosine, sine
    table[1, :, :, 0], table[1, :, :, 1] = -sine, cosine
    return np.pad(table.reshape(ROWS, ROWS), ((0, 0), (0, 2 * LANES - ROWS)))


def turn_table():
    theta = angles(np.arange(H), np.arange(LANES), NCH)
    return np.concatenate([np.cos(theta), np.sin(theta)], axis=1)


def stage_two_table(groups):
    theta = angles(np.arange(K2), np.arange(LANES), LANES)
    cosine, sine = np.cos(theta) / math.sqrt(NCH), np.sin(theta) / math.sqrt(NCH)
    real = np.concatenate([cosine, sine], 1).reshape(groups, 1, K2 // groups, 2 * LANES)
    imag = np.concatenate([-sine, cosine], 1).reshape(groups, 1, K2 // groups, 2 * LANES)
    return np.concatenate([real, imag], 1).reshape(2 * K2, 2 * LANES)


def tables(groups):
    two = stage_two_table(groups)
    rolled = np.roll(two, K2, axis=0)
    return np.concatenate([stage_one_table(), turn_table(), two, rolled]).astype(np.float32)


def halves(value):
    high = value.astype(BF16)
    return high, (value - high.astype(F32)).astype(BF16)


def dot(left, right):
    return lax.dot_general(left, right, (((1,), (0,)), ((), ())), preferred_element_type=F32)


def dot_nt(left, right):
    return lax.dot_general(left, right, (((1,), (1,)), ((), ())), preferred_element_type=F32)


def spectra_kernel(groups, parts, out_frames, place, *refs):
    sources, refs = refs[: len(parts)], refs[len(parts) :]
    taps_source, table_source = refs[:2]
    buffers, refs = refs[-len(parts) - 2 :], refs[2 : -len(parts) - 2]
    outs, (taps, one, two, ext, filtered, turned, staged, arrived, fixed) = refs[:-9], refs[-9:]
    taps_ref, table_ref, part_refs = buffers[0], buffers[1], buffers[2:]
    step, steps, members = pl.program_id(0), pl.num_programs(0), MEMBERS
    per_group = K2 // groups
    share = LANES // out_frames
    tiles = H // share
    pairs = tiles // 2
    frame_rows, row_rows = ROWS + PAD, tiles * TILE + PAD
    signals = part_refs[0].shape[0]

    def fixed_copies():
        return [
            pltpu.make_async_copy(taps_source, taps_ref, fixed.at[0]),
            pltpu.make_async_copy(table_source, table_ref, fixed.at[1]),
        ]

    def copy(number, signal):
        frames = parts[number]
        start = pl.multiple_of(place[2 + 3 * number] * frames, frames)
        return pltpu.make_async_copy(
            sources[number].at[signal, pl.ds(start, frames)],
            part_refs[number].at[signal],
            arrived.at[number, signal],
        )

    @pl.when((step == 0) & (place[0] == 1))
    def _():
        for one_copy in fixed_copies():
            one_copy.start()
        for signal in range(signals):
            for number in range(len(parts)):
                copy(number, signal).start()
        for one_copy in fixed_copies():
            one_copy.wait()

        for h in range(H):
            for half in range(TAPS // SUB):
                tile = taps_ref[pl.ds(half * SUB, SUB), pl.ds(h * LANES, LANES)]
                for r in range(2):
                    taps[pl.ds(half * SUB * ROWS + 2 * h + r, SUB, stride=ROWS), :] = tile
        high, low = halves(table_ref[:ROWS, :ROWS])
        one[...] = jnp.concatenate([high, high, low], axis=1)
        start = pl.multiple_of(ROWS + H + place[1] * 2 * K2, SUB)
        high, low = halves(table_ref[pl.ds(start, 2 * K2), :])
        two[0] = high
        two[1] = low

    def load(member):
        signal = step * members + member
        for number, (frames, ref) in enumerate(zip(parts, part_refs)):
            start = place[2 + 3 * number + 1]
            valid = place[2 + 3 * number + 2]
            copy(number, signal).wait()

            @pl.when(valid == 1)
            def _():
                for f in range(frames):
                    ext[member, start + f] = ref[signal, f].astype(F32)

            @pl.when(valid == 0)
            def _():
                for f in range(frames):
                    ext[member, start + f] = jnp.zeros((ROWS, LANES), F32)

    def filter_rows(member, q):
        rows = pl.ds(pl.multiple_of(q * SUB, SUB), SUB)
        tap = [taps[pl.ds(pl.multiple_of(m * ROWS + q * SUB, SUB), SUB), :] for m in range(TAPS)]
        for f in range(out_frames):
            total = tap[0] * ext[member, f + 1, rows]
            for m in range(1, TAPS):
                total = total + tap[m] * ext[member, f + 1 + m, rows]
            filtered[member, f, rows] = total

    def first_stage(member):
        cosine = table_ref[ROWS : ROWS + H, :LANES]
        sine = table_ref[ROWS : ROWS + H, LANES:]
        for g in range(out_frames // STEP):
            block = jnp.concatenate([filtered[member, g * STEP + f] for f in range(STEP)], axis=1)
            high, low = halves(block)
            first = dot(one[...], jnp.concatenate([high, low, high], axis=0))
            for f in range(STEP):
                real = first[:H, f * LANES : (f + 1) * LANES]
                imag = first[H:, f * LANES : (f + 1) * LANES]
                at = (g * STEP + f) * frame_rows
                turned[member, at : at + H, :] = real * cosine + imag * sine
                turned[member, at + H : at + ROWS, :] = imag * cosine - real * sine

    def second_stage(member, pair):
        rows = []
        for k1 in range(2 * pair * share, 2 * (pair + 1) * share):
            for f in range(0, out_frames, SUB):
                rows.append(
                    jnp.concatenate(
                        [turned[member, pl.ds(f * frame_rows + p * H + k1, SUB, stride=frame_rows), :] for p in range(2)],
                        axis=1,
                    )
                )
        high, low = halves(jnp.concatenate(rows, axis=0))
        spectrum = dot_nt(two[0], high) + dot_nt(two[1], high) + dot_nt(two[0], low)
        for k in range(2):
            for t in range(groups):
                for p in range(2):
                    for k2 in range(0, per_group, SUB):
                        row = (t * 2 + p) * per_group + k2
                        start = (t * per_group + k2) * row_rows + (2 * pair + k) * TILE + p * SUB
                        staged[pl.ds(start + step * members + member, SUB, stride=row_rows), :] = spectrum[
                            row : row + SUB, k * LANES : (k + 1) * LANES
                        ]

    def write():
        at = 0
        for out in outs:

            def write_row(k2, carry):
                for k in range(tiles):
                    start = pl.multiple_of((at + k2) * row_rows + k * TILE, PAD)
                    out[k2, k] = staged[pl.ds(start, TILE), :].astype(BF16)
                return carry

            lax.fori_loop(0, out.shape[0], write_row, 0, unroll=2)
            at += out.shape[0]

    @pl.when(place[0] == 1)
    def _():
        for member in range(members):
            load(member)

        def filter_one(index, carry):
            filter_rows(index // (ROWS // SUB), index % (ROWS // SUB))
            return carry

        lax.fori_loop(0, members * (ROWS // SUB), filter_one, 0)
        for member in range(members):
            first_stage(member)
        for member in range(members):
            for pair in range(pairs):
                second_stage(member, pair)

        @pl.when(step == steps - 1)
        def _():
            write()


def in_hbm(array):
    return pltpu.with_memory_space_constraint(array, pltpu.HBM)


def cut_kernel(place, source, out, done):
    count = out.shape[1]
    start = pl.multiple_of(place[0], count)
    copy = pltpu.make_async_copy(source.at[:, pl.ds(start, count)], out, done)
    copy.start()
    copy.wait()


def cut(volts, start, count):
    return pl.pallas_call(
        cut_kernel,
        grid_spec=pltpu.PrefetchScalarGridSpec(
            num_scalar_prefetch=1,
            grid=(1,),
            in_specs=[pl.BlockSpec(memory_space=pl.ANY)],
            out_specs=pl.BlockSpec(memory_space=pl.ANY),
            scratch_shapes=[pltpu.SemaphoreType.DMA],
        ),
        out_shape=jax.ShapeDtypeStruct((volts.shape[0], count, ROWS, LANES), BF16),
    )(jnp.reshape(start, (1,)).astype(jnp.int32), volts)


def after(value, *others):
    return lax.optimization_barrier((value, *others))[0]


def spectra(parts, out_frames, fir_taps, groups, sizes, run=1, order=0, wait=(), cost=10**6):
    signals = parts[0][0].shape[0]
    numbers = [run, order] + [v for part in parts for v in part[2:]]
    place = jnp.stack([jnp.asarray(v, jnp.int32) for v in numbers])
    place = after(place, *wait)
    table = jnp.asarray(tables(groups))
    tiles = H * out_frames // LANES
    whole = lambda shape: pl.BlockSpec(shape, lambda s, place: (0,) * len(shape))
    in_specs = [pl.BlockSpec(memory_space=pl.ANY)] * (len(parts) + 2)
    shapes = [(n, tiles, TILE, LANES) for n in sizes]
    return pl.pallas_call(
        functools.partial(spectra_kernel, groups, tuple(p[1] for p in parts), out_frames),
        grid_spec=pltpu.PrefetchScalarGridSpec(
            num_scalar_prefetch=1,
            grid=(signals // MEMBERS,),
            in_specs=in_specs,
            out_specs=[whole(shape) for shape in shapes],
            scratch_shapes=[
                pltpu.VMEM((TAPS * ROWS, LANES), F32),
                pltpu.VMEM((ROWS, 3 * ROWS), BF16),
                pltpu.VMEM((2, 2 * K2, 2 * LANES), BF16),
                pltpu.VMEM((MEMBERS, TAPS + out_frames, ROWS, LANES), F32),
                pltpu.VMEM((MEMBERS, out_frames, ROWS, LANES), F32),
                pltpu.VMEM((MEMBERS, out_frames * (ROWS + PAD), LANES), F32),
                pltpu.VMEM((K2 * (tiles * TILE + PAD), LANES), F32),
                pltpu.SemaphoreType.DMA((len(parts), signals)),
                pltpu.SemaphoreType.DMA((2,)),
                pltpu.VMEM((TAPS, NCH), F32),
                pltpu.VMEM(table.shape, F32),
            ]
            + [pltpu.VMEM((signals, part[1], ROWS, LANES), BF16) for part in parts],
        ),
        out_shape=[jax.ShapeDtypeStruct(shape, BF16) for shape in shapes],
        compiler_params=pltpu.CompilerParams(vmem_limit_bytes=32 << 20),
        cost_estimate=pl.CostEstimate(
            flops=cost, bytes_accessed=0, transcendentals=0
        ),
    )(place, *[part[0] for part in parts], fir_taps, in_hbm(table))


def correlate_kernel(pieces, per_group, scale, add, last, place, *refs):
    refs = list(refs)
    sums = refs.pop() if last else None
    out = refs.pop()
    before = refs.pop() if add else None
    if not last:
        sums = out
    half = per_group // 2
    lane = lax.broadcasted_iota(jnp.int32, (SUB, LANES), 1)
    first_tile = lane < LANES // 2
    real_lane = lane % TILE < SUB
    sign = jnp.where(real_lane, 1.0, -1.0).astype(F32)
    for number, piece in enumerate(pieces):
        tiles, piece = piece
        share = H // tiles
        where = lax.broadcasted_iota(jnp.int32, (TILE, LANES), 1) // (LANES // share)

        def pair(index, carry):
            k2 = index // tiles
            k1 = index % tiles
            own, other = [], []
            for position in range(len(piece[0])):
                rows = []
                for tile in range(2):
                    array, row, column = piece[0][position]
                    a = refs[array][row + tile * half + k2, column + k1]
                    rows += [jnp.where(where == c, a, jnp.zeros_like(a)) for c in range(share)]
                own.append(jnp.concatenate(rows, axis=0))
                rows = []
                for tile in range(2):
                    for visit in range(VISITS):
                        array, row, column = piece[visit][position]
                        rows.append(refs[array][row + tile * half + k2, column + k1])
                other.append(jnp.concatenate(rows, axis=0))
            product = dot_nt(jnp.concatenate(own, axis=1), jnp.concatenate(other, axis=1))
            for c in range(share):
                value = []
                for p in range(2):
                    at = [((tile * share + c) * 2 + p) * SUB for tile in range(2)]
                    value.append(
                        jnp.where(first_tile, product[at[0] : at[0] + SUB], product[at[1] : at[1] + SUB])
                    )
                turned = jnp.where(
                    real_lane, pltpu.roll(value[1], LANES - SUB, 1), pltpu.roll(value[1], SUB, 1)
                )
                total = value[0] * sign + turned
                channel = k2 // 4 * LANES + k2 % 4 * H + k1 * share + c
                rows = pl.ds(pl.multiple_of(channel * SUB, SUB), SUB)
                if number:
                    total = total + sums[rows, :]
                elif add:
                    total = total + before[rows, :]
                sums[rows, :] = total
            return carry

        lax.fori_loop(0, half * tiles, pair, 0, unroll=16)
    if not last:
        return

    def finish(index, carry):
        block = index // SUB
        signal = index % SUB
        value = sums[pl.ds(block * LANES * SUB + signal, LANES, stride=SUB), :]
        value = jnp.transpose(value * scale)
        at = 0
        for tile in range(2):
            for visit in range(VISITS):
                for part in range(2):
                    out[part, signal, place[visit], tile * (half // 4) + block] = value[at : at + SUB]
                    at += SUB
        return carry

    lax.fori_loop(0, half // 4 * SUB, finish, 0)


def correlate(arrays, pieces, per_group, place, scale, before, last, wait=()):
    signals = TILE // 2
    rows = per_group // 2 * H * SUB
    place = after(place, *wait)
    shape = (2, signals, VISITS, per_group // 4, SUB, LANES) if last else (rows, LANES)
    operands = list(arrays) + ([] if before is None else [before])
    whole = lambda shape: pl.BlockSpec(shape, lambda i, place: (0,) * len(shape))
    return pl.pallas_call(
        functools.partial(correlate_kernel, pieces, per_group, scale, before is not None, last),
        grid_spec=pltpu.PrefetchScalarGridSpec(
            num_scalar_prefetch=1,
            grid=(1,),
            in_specs=[whole(x.shape) for x in operands],
            out_specs=whole(shape),
            scratch_shapes=[pltpu.VMEM((rows, LANES), F32)] if last else [],
        ),
        out_shape=jax.ShapeDtypeStruct(shape, F32),
        compiler_params=pltpu.CompilerParams(vmem_limit_bytes=48 << 20),
        input_output_aliases={} if before is None or last else {len(operands): 0},
        cost_estimate=pl.CostEstimate(flops=6 * 10**9, bytes_accessed=0, transcendentals=0),
    )(place, *operands)


def stacked(voltage):
    s, f = voltage.shape[:2]
    return voltage.reshape(s, f, 2, H, LANES).transpose(0, 1, 3, 2, 4).reshape(s, f, ROWS, LANES)


def natural(out):
    parts, s, visits, i, t, lanes = out.shape
    return out.transpose(0, 1, 2, 4, 3, 5).reshape(parts, s, visits * t, i * lanes)


def shifted(block, axis, distance):
    size = lax.axis_size(axis)
    return lax.ppermute(block, axis, [(i, (i + distance) % size) for i in range(size)])


def farther(block):
    size = lax.axis_size("stn")
    rest = lax.ppermute(block, "stn", [(i, (i + 1 if i % 2 == 0 else i + 3) % size) for i in range(size)])
    return shifted(block, "stn", 2), rest


def exchanged(block):
    return lax.ppermute(block, "stn", [(i, i ^ 1) for i in range(lax.axis_size("stn"))])


def general(volts, fir_taps):
    groups = lax.axis_size("tm")
    frames = volts.shape[1]
    history = lax.ppermute(cut(volts, jnp.int32(frames - TAPS), TAPS), "tm", [(i, i + 1) for i in range(groups - 1)])
    parts = [(history, TAPS, 0, 0, 1)] + [(volts, TAPS, i, TAPS * (i + 1), 1) for i in range(frames // TAPS)]
    spectrum = spectra(parts, frames, fir_taps, groups, [K2])[0]
    spectrum = lax.all_to_all(spectrum, "tm", split_axis=0, concat_axis=0, tiled=True)
    tiles = spectrum.shape[1]
    return [([spectrum], [(tiles, [(0, K2 // groups * t, 0) for t in range(groups)])])]


def paired(volts, fir_taps, correlated):
    frames = volts.shape[1]
    me = lax.axis_index("tm")
    sizes = [K2 // 2, K2 // 2]
    swap = [(0, 1), (1, 0)]
    edge = TAPS // 2
    last = frames // edge
    edge_frames = cut(volts, jnp.where(me == 0, frames - edge, 0), edge)
    visiting = lax.ppermute(edge_frames, "tm", swap)
    own_a, away_a = spectra(
        [(volts, TAPS, 0, 0, me), (volts, TAPS, me, TAPS, 1)], TAPS, fir_taps, 2, sizes, 1, me, (edge_frames,)
    )
    got_a = lax.ppermute(away_a, "tm", swap)
    two_a, rest_a = farther(own_a)
    own_b, away_b = spectra(
        [(volts, TAPS, 0, 0, 1), (volts, TAPS, 1, TAPS, 1)], TAPS, fir_taps, 2, sizes, 1 - me, me, (own_a,)
    )
    got_b = lax.ppermute(away_b, "tm", [(0, 1)])
    pair_a = exchanged(two_a)
    own_c, away_c = spectra(
        [
            (volts, edge, jnp.where(me == 0, last - 2, 0), edge * me, 1),
            (volts, edge, jnp.where(me == 0, last - 1, 1), edge * me + edge, 1),
            (visiting, edge, 0, 2 * edge * (1 - me), 1),
        ],
        edge, fir_taps, 2, sizes, 1, me, (own_b, two_a, got_a), 9 * 10**9,
    )
    got_c = lax.ppermute(away_c, "tm", swap)
    two_g, rest_g = farther(got_a)
    pair_g = exchanged(two_g)
    own_c = after(own_c, two_g, pair_a, rest_a)
    rest = jnp.concatenate([jnp.where(me == 0, own_b, got_b), own_c, got_c], axis=1)
    two_r, rest_r = farther(rest)
    many, few = own_a.shape[1], own_c.shape[1]
    sums = correlated(
        [own_a, pair_a, two_a, rest_a, got_a, pair_g, two_g, rest_g], [(many, [(0, 0, 0), (1, 0, 0)])], None, False
    )
    pair_r = exchanged(after(two_r, sums))
    return correlated(
        [rest, pair_r, two_r, rest_r], [(many, [(0, 0, 0)]), (few, [(0, 0, many), (0, 0, many + few)])], sums, True
    )


def general(volts, fir_taps, correlated):
    groups = lax.axis_size("tm")
    frames = volts.shape[1]
    history = lax.ppermute(cut(volts, jnp.int32(frames - TAPS), TAPS), "tm", [(i, i + 1) for i in range(groups - 1)])
    parts = [(history, TAPS, 0, 0, 1)] + [(volts, TAPS, i, TAPS * (i + 1), 1) for i in range(frames // TAPS)]
    spectrum = spectra(parts, frames, fir_taps, groups, [K2])[0]
    spectrum = lax.all_to_all(spectrum, "tm", split_axis=0, concat_axis=0, tiled=True)
    two, rest = farther(spectrum)
    spots = [(0, K2 // groups * t, 0) for t in range(groups)]
    return correlated([spectrum, exchanged(two), two, rest], [(spectrum.shape[1], spots)], None, True)


def local(voltage, fir_taps):
    groups = lax.axis_size("tm")
    even = lax.axis_index("stn") % 2 == 0
    place = jnp.where(even, jnp.array([0, 1, 2, 3]), jnp.array([0, 3, 2, 1])).astype(jnp.int32)
    scale = 1.0 / (groups * voltage.shape[1])

    def correlated(arrays, pieces, before, last, wait=()):
        laid = [
            (tiles, [[(VISITS * n + visit, row, column) for n, row, column in spots] for visit in range(VISITS)])
            for tiles, spots in pieces
        ]
        return correlate(arrays, laid, K2 // groups, place, scale, before, last, wait)

    run = paired if groups == 2 else general
    return natural(run(in_hbm(stacked(voltage)), in_hbm(fir_taps), correlated))


def solution(mesh):
    return jax.shard_map(
        local,
        mesh=mesh,
        in_specs=(P("stn", "tm", None, None), P()),
        out_specs=P(None, "stn", None, "tm"),
        check_vma=False,
    )
```

```python
import functools
import math

import jax
import jax.numpy as jnp
import numpy as np
from jax import lax
from jax.experimental import pallas as pl
from jax.experimental.pallas import tpu as pltpu
from jax.sharding import PartitionSpec as P

NCH = 4096
CHANS = 2048
TAPS = 16
VISITS = 4
H = 32
LANES = 128
ROWS = 2 * H
K2 = CHANS // H
STEP = 8
TILE = 16
MEMBERS = 4
PAD = 8
SUB = 8
BF16 = jnp.bfloat16
F32 = jnp.float32


def angles(rows, columns, modulus):
    turns = np.outer(rows, columns) % modulus
    return turns.astype(np.float64) * (2.0 * math.pi / modulus)


def stage_one_table():
    theta = angles(np.arange(H), np.arange(H), H)
    cosine, sine = np.cos(theta), np.sin(theta)
    table = np.zeros((2, H, H, 2))
    table[0, :, :, 0], table[0, :, :, 1] = cosine, sine
    table[1, :, :, 0], table[1, :, :, 1] = -sine, cosine
    return np.pad(table.reshape(ROWS, ROWS), ((0, 0), (0, 2 * LANES - ROWS)))


def turn_table():
    theta = angles(np.arange(H), np.arange(LANES), NCH)
    return np.concatenate([np.cos(theta), np.sin(theta)], axis=1)


def stage_two_table(groups):
    theta = angles(np.arange(K2), np.arange(LANES), LANES)
    cosine, sine = np.cos(theta) / math.sqrt(NCH), np.sin(theta) / math.sqrt(NCH)
    real = np.concatenate([cosine, sine], 1).reshape(groups, 1, K2 // groups, 2 * LANES)
    imag = np.concatenate([-sine, cosine], 1).reshape(groups, 1, K2 // groups, 2 * LANES)
    return np.concatenate([real, imag], 1).reshape(2 * K2, 2 * LANES)


def halves(value):
    high = value.astype(BF16)
    return high, (value - high.astype(F32)).astype(BF16)


def dot(left, right):
    return lax.dot_general(left, right, (((1,), (0,)), ((), ())), preferred_element_type=F32)


def dot_nt(left, right):
    return lax.dot_general(left, right, (((1,), (1,)), ((), ())), preferred_element_type=F32)


def prepare_kernel(place, volts_source, taps_source, table_source, volts, edge, taps, one, two, done, taps_ref, table_ref):
    count = edge.shape[1]
    start = pl.multiple_of(place[1] * count, count)
    copies = [
        pltpu.make_async_copy(taps_source, taps_ref, done.at[0]),
        pltpu.make_async_copy(table_source, table_ref, done.at[1]),
        pltpu.make_async_copy(volts_source.at[:, pl.ds(start, count)], edge, done.at[2]),
        pltpu.make_async_copy(volts_source, volts, done.at[3]),
    ]
    for copy in copies:
        copy.start()
    copies[0].wait()
    copies[1].wait()
    for h in range(H):
        for half in range(TAPS // SUB):
            tile = taps_ref[pl.ds(half * SUB, SUB), pl.ds(h * LANES, LANES)]
            for r in range(2):
                taps[pl.ds(half * SUB * ROWS + 2 * h + r, SUB, stride=ROWS), :] = tile
    high, low = halves(table_ref[:ROWS, :ROWS])
    one[...] = jnp.concatenate([high, high, low], axis=1)
    start = pl.multiple_of(ROWS + place[0] * 2 * K2, SUB)
    high, low = halves(table_ref[pl.ds(start, 2 * K2), :])
    two[0] = high
    two[1] = low
    copies[2].wait()
    copies[3].wait()


def prepare(volts, fir_taps, groups, order, edge_block, edge_frames):
    signals, frames = volts.shape[:2]
    two = stage_two_table(groups)
    table = np.concatenate([stage_one_table(), two, np.roll(two, K2, axis=0)]).astype(np.float32)
    vmem = pl.BlockSpec(memory_space=pltpu.VMEM)
    return pl.pallas_call(
        prepare_kernel,
        grid_spec=pltpu.PrefetchScalarGridSpec(
            num_scalar_prefetch=1,
            grid=(),
            in_specs=[pl.BlockSpec(memory_space=pl.ANY)] * 3,
            out_specs=[vmem] * 5,
            scratch_shapes=[
                pltpu.SemaphoreType.DMA((4,)),
                pltpu.VMEM(fir_taps.shape, F32),
                pltpu.VMEM(table.shape, F32),
            ],
        ),
        out_shape=[
            jax.ShapeDtypeStruct((signals, frames, ROWS, LANES), BF16),
            jax.ShapeDtypeStruct((signals, edge_frames, ROWS, LANES), BF16),
            jax.ShapeDtypeStruct((TAPS * ROWS, LANES), F32),
            jax.ShapeDtypeStruct((ROWS, 3 * ROWS), BF16),
            jax.ShapeDtypeStruct((2, 2 * K2, 2 * LANES), BF16),
        ],
        compiler_params=pltpu.CompilerParams(vmem_limit_bytes=24 << 20),
    )(
        jnp.stack([jnp.asarray(v, jnp.int32) for v in (order, edge_block)]),
        *[pltpu.with_memory_space_constraint(x, pltpu.HBM) for x in (volts, fir_taps, jnp.asarray(table))],
    )


def spectra_kernel(groups, parts, out_frames, place, *refs):
    part_refs, refs = refs[: len(parts)], refs[len(parts) :]
    taps, one, two, turn = refs[:4]
    outs, (ext, filtered, turned, staged) = refs[4:-4], refs[-4:]
    step, steps, members = pl.program_id(0), pl.num_programs(0), MEMBERS
    per_group = K2 // groups
    share = LANES // out_frames
    tiles = H // share
    pairs = tiles // 2
    frame_rows, row_rows = ROWS + PAD, tiles * TILE + PAD

    def load(member):
        signal = step * members + member
        for number, (frames, ref) in enumerate(zip(parts, part_refs)):
            first = place[1 + 3 * number] * frames
            start = place[1 + 3 * number + 1]
            valid = place[1 + 3 * number + 2]

            @pl.when(valid == 1)
            def _():
                for f in range(frames):
                    ext[member, start + f] = ref[signal, first + f].astype(F32)

            @pl.when(valid == 0)
            def _():
                for f in range(frames):
                    ext[member, start + f] = jnp.zeros((ROWS, LANES), F32)

    def filter_rows(member, q):
        rows = pl.ds(pl.multiple_of(q * SUB, SUB), SUB)
        tap = [taps[pl.ds(pl.multiple_of(m * ROWS + q * SUB, SUB), SUB), :] for m in range(TAPS)]
        for f in range(out_frames):
            total = tap[0] * ext[member, f + 1, rows]
            for m in range(1, TAPS):
                total = total + tap[m] * ext[member, f + 1 + m, rows]
            filtered[member, f, rows] = total

    def first_stage(member):
        cosine = turn[:, :LANES]
        sine = turn[:, LANES:]
        for g in range(out_frames // STEP):
            block = jnp.concatenate([filtered[member, g * STEP + f] for f in range(STEP)], axis=1)
            high, low = halves(block)
            first = dot(one[...], jnp.concatenate([high, low, high], axis=0))
            for f in range(STEP):
                real = first[:H, f * LANES : (f + 1) * LANES]
                imag = first[H:, f * LANES : (f + 1) * LANES]
                at = (g * STEP + f) * frame_rows
                turned[member, at : at + H, :] = real * cosine + imag * sine
                turned[member, at + H : at + ROWS, :] = imag * cosine - real * sine

    def second_stage(member, pair):
        rows = []
        for k1 in range(2 * pair * share, 2 * (pair + 1) * share):
            for f in range(0, out_frames, SUB):
                rows.append(
                    jnp.concatenate(
                        [turned[member, pl.ds(f * frame_rows + p * H + k1, SUB, stride=frame_rows), :] for p in range(2)],
                        axis=1,
                    )
                )
        high, low = halves(jnp.concatenate(rows, axis=0))
        spectrum = dot_nt(two[0], high) + dot_nt(two[1], high) + dot_nt(two[0], low)
        for k in range(2):
            for t in range(groups):
                for p in range(2):
                    for k2 in range(0, per_group, SUB):
                        row = (t * 2 + p) * per_group + k2
                        start = (t * per_group + k2) * row_rows + (2 * pair + k) * TILE + p * SUB
                        staged[pl.ds(start + step * members + member, SUB, stride=row_rows), :] = spectrum[
                            row : row + SUB, k * LANES : (k + 1) * LANES
                        ]

    def write():
        at = 0
        for out in outs:

            def write_row(k2, carry):
                for k in range(tiles):
                    start = pl.multiple_of((at + k2) * row_rows + k * TILE, PAD)
                    out[k2, k] = staged[pl.ds(start, TILE), :].astype(BF16)
                return carry

            lax.fori_loop(0, out.shape[0], write_row, 0, unroll=2)
            at += out.shape[0]

    @pl.when(place[0] == 1)
    def _():
        for member in range(members):
            load(member)

        def filter_one(index, carry):
            filter_rows(index // (ROWS // SUB), index % (ROWS // SUB))
            return carry

        lax.fori_loop(0, members * (ROWS // SUB), filter_one, 0)
        for member in range(members):
            first_stage(member)
        for member in range(members):
            for pair in range(pairs):
                second_stage(member, pair)

        @pl.when(step == steps - 1)
        def _():
            write()


def after(value, *others):
    return lax.optimization_barrier((value, *others))[0]


def spectra(parts, out_frames, fixed, groups, sizes, run=1, wait=(), cost=10**6):
    signals = parts[0][0].shape[0]
    numbers = [run] + [v for part in parts for v in part[2:]]
    place = jnp.stack([jnp.asarray(v, jnp.int32) for v in numbers])
    place = after(place, *wait)
    tiles = H * out_frames // LANES
    shapes = [(n, tiles, TILE, LANES) for n in sizes]
    return pl.pallas_call(
        functools.partial(spectra_kernel, groups, tuple(p[1] for p in parts), out_frames),
        grid_spec=pltpu.PrefetchScalarGridSpec(
            num_scalar_prefetch=1,
            grid=(signals // MEMBERS,),
            in_specs=[pl.BlockSpec(memory_space=pltpu.VMEM)] * (len(parts) + 4),
            out_specs=[pl.BlockSpec(shape, lambda s, place: (0, 0, 0, 0)) for shape in shapes],
            scratch_shapes=[
                pltpu.VMEM((MEMBERS, TAPS + out_frames, ROWS, LANES), F32),
                pltpu.VMEM((MEMBERS, out_frames, ROWS, LANES), F32),
                pltpu.VMEM((MEMBERS, out_frames * (ROWS + PAD), LANES), F32),
                pltpu.VMEM((K2 * (tiles * TILE + PAD), LANES), F32),
            ],
        ),
        out_shape=[jax.ShapeDtypeStruct(shape, BF16) for shape in shapes],
        compiler_params=pltpu.CompilerParams(vmem_limit_bytes=32 << 20),
        cost_estimate=pl.CostEstimate(flops=cost, bytes_accessed=0, transcendentals=0),
    )(place, *[part[0] for part in parts], *fixed, jnp.asarray(turn_table(), F32))


def after(value, *others):
    return lax.optimization_barrier((value, *others))[0]


def correlate_kernel(pieces, per_group, scale, add, last, place, *refs):
    refs = list(refs)
    sums = refs.pop() if last else None
    out = refs.pop()
    before = refs.pop() if add else None
    if not last:
        sums = out
    half = per_group // 2
    lane = lax.broadcasted_iota(jnp.int32, (SUB, LANES), 1)
    first_tile = lane < LANES // 2
    real_lane = lane % TILE < SUB
    sign = jnp.where(real_lane, 1.0, -1.0).astype(F32)
    for number, piece in enumerate(pieces):
        tiles, piece = piece
        share = H // tiles
        where = lax.broadcasted_iota(jnp.int32, (TILE, LANES), 1) // (LANES // share)

        def pair(index, carry):
            k2 = index // tiles
            k1 = index % tiles
            own, other = [], []
            for position in range(len(piece[0])):
                rows = []
                for tile in range(2):
                    array, row, column = piece[0][position]
                    a = refs[array][row + tile * half + k2, column + k1]
                    rows += [jnp.where(where == c, a, jnp.zeros_like(a)) for c in range(share)]
                own.append(jnp.concatenate(rows, axis=0))
                rows = []
                for tile in range(2):
                    for visit in range(VISITS):
                        array, row, column = piece[visit][position]
                        rows.append(refs[array][row + tile * half + k2, column + k1])
                other.append(jnp.concatenate(rows, axis=0))
            product = dot_nt(jnp.concatenate(own, axis=1), jnp.concatenate(other, axis=1))
            for c in range(share):
                value = []
                for p in range(2):
                    at = [((tile * share + c) * 2 + p) * SUB for tile in range(2)]
                    value.append(
                        jnp.where(first_tile, product[at[0] : at[0] + SUB], product[at[1] : at[1] + SUB])
                    )
                turned = jnp.where(
                    real_lane, pltpu.roll(value[1], LANES - SUB, 1), pltpu.roll(value[1], SUB, 1)
                )
                total = value[0] * sign + turned
                channel = k2 // 4 * LANES + k2 % 4 * H + k1 * share + c
                rows = pl.ds(pl.multiple_of(channel * SUB, SUB), SUB)
                if number:
                    total = total + sums[rows, :]
                elif add:
                    total = total + before[rows, :]
                sums[rows, :] = total
            return carry

        lax.fori_loop(0, half * tiles, pair, 0, unroll=16)
    if not last:
        return

    def finish(index, carry):
        block = index // SUB
        signal = index % SUB
        value = sums[pl.ds(block * LANES * SUB + signal, LANES, stride=SUB), :]
        value = jnp.transpose(value * scale)
        at = 0
        for tile in range(2):
            for visit in range(VISITS):
                for part in range(2):
                    out[part, signal, place[visit], tile * (half // 4) + block] = value[at : at + SUB]
                    at += SUB
        return carry

    lax.fori_loop(0, half // 4 * SUB, finish, 0)


def correlate(arrays, pieces, per_group, place, scale, before, last, wait=()):
    signals = TILE // 2
    rows = per_group // 2 * H * SUB
    place = after(place, *wait)
    shape = (2, signals, VISITS, per_group // 4, SUB, LANES) if last else (rows, LANES)
    operands = list(arrays) + ([] if before is None else [before])
    whole = lambda shape: pl.BlockSpec(shape, lambda i, place: (0,) * len(shape))
    return pl.pallas_call(
        functools.partial(correlate_kernel, pieces, per_group, scale, before is not None, last),
        grid_spec=pltpu.PrefetchScalarGridSpec(
            num_scalar_prefetch=1,
            grid=(1,),
            in_specs=[whole(x.shape) for x in operands],
            out_specs=whole(shape),
            scratch_shapes=[pltpu.VMEM((rows, LANES), F32)] if last else [],
        ),
        out_shape=jax.ShapeDtypeStruct(shape, F32),
        compiler_params=pltpu.CompilerParams(vmem_limit_bytes=48 << 20),
        input_output_aliases={} if before is None or last else {len(operands): 0},
        cost_estimate=pl.CostEstimate(flops=6 * 10**9, bytes_accessed=0, transcendentals=0),
    )(place, *operands)


def stacked(voltage):
    s, f = voltage.shape[:2]
    return voltage.reshape(s, f, 2, H, LANES).transpose(0, 1, 3, 2, 4).reshape(s, f, ROWS, LANES)


def natural(out):
    parts, s, visits, i, t, lanes = out.shape
    return out.transpose(0, 1, 2, 4, 3, 5).reshape(parts, s, visits * t, i * lanes)


def shifted(block, axis, distance):
    size = lax.axis_size(axis)
    return lax.ppermute(block, axis, [(i, (i + distance) % size) for i in range(size)])


def farther(block):
    size = lax.axis_size("stn")
    rest = lax.ppermute(block, "stn", [(i, (i + 1 if i % 2 == 0 else i + 3) % size) for i in range(size)])
    return shifted(block, "stn", 2), rest


def exchanged(block):
    return lax.ppermute(block, "stn", [(i, i ^ 1) for i in range(lax.axis_size("stn"))])


def general(volts, fir_taps):
    groups = lax.axis_size("tm")
    frames = volts.shape[1]
    volts, edge_frames, *fixed = prepare(volts, fir_taps, groups, 0, frames // TAPS - 1, TAPS)
    history = lax.ppermute(edge_frames, "tm", [(i, i + 1) for i in range(groups - 1)])
    parts = [(history, TAPS, 0, 0, 1)] + [(volts, TAPS, i, TAPS * (i + 1), 1) for i in range(frames // TAPS)]
    spectrum = spectra(parts, frames, fixed, groups, [K2])[0]
    spectrum = lax.all_to_all(spectrum, "tm", split_axis=0, concat_axis=0, tiled=True)
    tiles = spectrum.shape[1]
    return [([spectrum], [(tiles, [(0, K2 // groups * t, 0) for t in range(groups)])])]


def paired(volts, fir_taps, correlated):
    frames = volts.shape[1]
    me = lax.axis_index("tm")
    sizes = [K2 // 2, K2 // 2]
    swap = [(0, 1), (1, 0)]
    edge = TAPS // 2
    last = frames // edge
    volts, edge_frames, *fixed = prepare(volts, fir_taps, 2, me, jnp.where(me == 0, frames // edge - 1, 0), edge)
    visiting = lax.ppermute(edge_frames, "tm", swap)
    own_a, away_a = spectra(
        [(volts, TAPS, 0, 0, me), (volts, TAPS, me, TAPS, 1)], TAPS, fixed, 2, sizes
    )
    got_a = lax.ppermute(away_a, "tm", swap)
    two_a, rest_a = farther(own_a)
    own_b, away_b = spectra(
        [(volts, TAPS, 0, 0, 1), (volts, TAPS, 1, TAPS, 1)], TAPS, fixed, 2, sizes, 1 - me, (own_a,)
    )
    got_b = lax.ppermute(away_b, "tm", [(0, 1)])
    pair_a = exchanged(two_a)
    own_c, away_c = spectra(
        [
            (volts, edge, jnp.where(me == 0, last - 2, 0), edge * me, 1),
            (volts, edge, jnp.where(me == 0, last - 1, 1), edge * me + edge, 1),
            (visiting, edge, 0, 2 * edge * (1 - me), 1),
        ],
        edge, fixed, 2, sizes, 1, (own_b, two_a, got_a), 9 * 10**9,
    )
    got_c = lax.ppermute(away_c, "tm", swap)
    two_g, rest_g = farther(got_a)
    pair_g = exchanged(two_g)
    own_c = after(own_c, two_g, pair_a, rest_a)
    rest = jnp.concatenate([jnp.where(me == 0, own_b, got_b), own_c, got_c], axis=1)
    two_r, rest_r = farther(rest)
    many, few = own_a.shape[1], own_c.shape[1]
    sums = correlated(
        [own_a, pair_a, two_a, rest_a, got_a, pair_g, two_g, rest_g], [(many, [(0, 0, 0), (1, 0, 0)])], None, False
    )
    pair_r = exchanged(after(two_r, sums))
    return correlated(
        [rest, pair_r, two_r, rest_r], [(many, [(0, 0, 0)]), (few, [(0, 0, many), (0, 0, many + few)])], sums, True
    )


def general(volts, fir_taps, correlated):
    groups = lax.axis_size("tm")
    frames = volts.shape[1]
    volts, edge_frames, *fixed = prepare(volts, fir_taps, groups, 0, frames // TAPS - 1, TAPS)
    history = lax.ppermute(edge_frames, "tm", [(i, i + 1) for i in range(groups - 1)])
    parts = [(history, TAPS, 0, 0, 1)] + [(volts, TAPS, i, TAPS * (i + 1), 1) for i in range(frames // TAPS)]
    spectrum = spectra(parts, frames, fixed, groups, [K2])[0]
    spectrum = lax.all_to_all(spectrum, "tm", split_axis=0, concat_axis=0, tiled=True)
    two, rest = farther(spectrum)
    spots = [(0, K2 // groups * t, 0) for t in range(groups)]
    return correlated([spectrum, exchanged(two), two, rest], [(spectrum.shape[1], spots)], None, True)


def local(voltage, fir_taps):
    groups = lax.axis_size("tm")
    even = lax.axis_index("stn") % 2 == 0
    place = jnp.where(even, jnp.array([0, 1, 2, 3]), jnp.array([0, 3, 2, 1])).astype(jnp.int32)
    scale = 1.0 / (groups * voltage.shape[1])

    def correlated(arrays, pieces, before, last, wait=()):
        laid = [
            (tiles, [[(VISITS * n + visit, row, column) for n, row, column in spots] for visit in range(VISITS)])
            for tiles, spots in pieces
        ]
        return correlate(arrays, laid, K2 // groups, place, scale, before, last, wait)

    run = paired if groups == 2 else general
    return natural(run(stacked(voltage), fir_taps, correlated))


def solution(mesh):
    return jax.shard_map(
        local,
        mesh=mesh,
        in_specs=(P("stn", "tm", None, None), P()),
        out_specs=P(None, "stn", None, "tm"),
        check_vma=False,
    )
```

```python
import functools
import math

import jax
import jax.numpy as jnp
import numpy as np
from jax import lax
from jax.experimental import pallas as pl
from jax.experimental.pallas import tpu as pltpu
from jax.sharding import PartitionSpec as P

NCH = 4096
CHANS = 2048
TAPS = 16
VISITS = 4
H = 32
LANES = 128
ROWS = 2 * H
K2 = CHANS // H
STEP = 8
TILE = 16
PLACES = (0, (1, 3), 2, (3, 1))
MEMBERS = 4
PAD = 8
SUB = 8
BF16 = jnp.bfloat16
F32 = jnp.float32


def angles(rows, columns, modulus):
    turns = np.outer(rows, columns) % modulus
    return turns.astype(np.float64) * (2.0 * math.pi / modulus)


def stage_one_table():
    theta = angles(np.arange(H), np.arange(H), H)
    cosine, sine = np.cos(theta), np.sin(theta)
    table = np.zeros((2, H, H, 2))
    table[0, :, :, 0], table[0, :, :, 1] = cosine, sine
    table[1, :, :, 0], table[1, :, :, 1] = -sine, cosine
    return np.pad(table.reshape(ROWS, ROWS), ((0, 0), (0, 2 * LANES - ROWS)))


def turn_table():
    theta = angles(np.arange(H), np.arange(LANES), NCH)
    return np.concatenate([np.cos(theta), np.sin(theta)], axis=1)


def stage_two_table(groups):
    theta = angles(np.arange(K2), np.arange(LANES), LANES)
    cosine, sine = np.cos(theta) / math.sqrt(NCH), np.sin(theta) / math.sqrt(NCH)
    real = np.concatenate([cosine, sine], 1).reshape(groups, 1, K2 // groups, 2 * LANES)
    imag = np.concatenate([-sine, cosine], 1).reshape(groups, 1, K2 // groups, 2 * LANES)
    return np.concatenate([real, imag], 1).reshape(2 * K2, 2 * LANES)


def halves(value):
    high = value.astype(BF16)
    return high, (value - high.astype(F32)).astype(BF16)


def dot(left, right):
    return lax.dot_general(left, right, (((1,), (0,)), ((), ())), preferred_element_type=F32)


def dot_nt(left, right):
    return lax.dot_general(left, right, (((1,), (1,)), ((), ())), preferred_element_type=F32)


def value_of(number, group):
    if isinstance(number, int):
        return number
    return number[0] + (number[1] - number[0]) * group


def prepare_kernel(edge_block, swapped, place, volts_source, taps_source, table_source, turn_source, volts, edge, taps, one, two, turn, done, taps_ref, table_ref):
    count = edge.shape[1]
    start = pl.multiple_of(value_of(edge_block, place[0]) * count, count)
    copies = [
        pltpu.make_async_copy(taps_source, taps_ref, done.at[0]),
        pltpu.make_async_copy(table_source, table_ref, done.at[1]),
        pltpu.make_async_copy(volts_source.at[:, pl.ds(start, count)], edge, done.at[2]),
        pltpu.make_async_copy(volts_source, volts, done.at[3]),
        pltpu.make_async_copy(turn_source, turn, done.at[4]),
    ]
    for copy in copies:
        copy.start()
    copies[0].wait()
    copies[1].wait()
    for h in range(H):
        for half in range(TAPS // SUB):
            tile = taps_ref[pl.ds(half * SUB, SUB), pl.ds(h * LANES, LANES)]
            for r in range(2):
                taps[pl.ds(half * SUB * ROWS + 2 * h + r, SUB, stride=ROWS), :] = tile
    high, low = halves(table_ref[:ROWS, :ROWS])
    one[...] = jnp.concatenate([high, high, low], axis=1)
    start = pl.multiple_of(ROWS + place[0] * (2 * K2 * swapped), SUB)
    high, low = halves(table_ref[pl.ds(start, 2 * K2), :])
    two[0] = high
    two[1] = low
    for copy in copies[2:]:
        copy.wait()


def prepare(volts, fir_taps, place, groups, edge_block, edge_frames):
    signals, frames = volts.shape[:2]
    two = stage_two_table(groups)
    table = np.concatenate([stage_one_table(), two, np.roll(two, K2, axis=0)]).astype(np.float32)
    vmem = pl.BlockSpec(memory_space=pltpu.VMEM)
    return pl.pallas_call(
        functools.partial(prepare_kernel, edge_block, int(groups == 2)),
        grid_spec=pltpu.PrefetchScalarGridSpec(
            num_scalar_prefetch=1,
            grid=(),
            in_specs=[pl.BlockSpec(memory_space=pl.ANY)] * 4,
            out_specs=[vmem] * 6,
            scratch_shapes=[
                pltpu.SemaphoreType.DMA((5,)),
                pltpu.VMEM(fir_taps.shape, F32),
                pltpu.VMEM(table.shape, F32),
            ],
        ),
        out_shape=[
            jax.ShapeDtypeStruct((signals, frames, ROWS, LANES), BF16),
            jax.ShapeDtypeStruct((signals, edge_frames, ROWS, LANES), BF16),
            jax.ShapeDtypeStruct((TAPS * ROWS, LANES), F32),
            jax.ShapeDtypeStruct((ROWS, 3 * ROWS), BF16),
            jax.ShapeDtypeStruct((2, 2 * K2, 2 * LANES), BF16),
            jax.ShapeDtypeStruct((H, 2 * LANES), F32),
        ],
        compiler_params=pltpu.CompilerParams(vmem_limit_bytes=24 << 20),
    )(
        place,
        *[
            pltpu.with_memory_space_constraint(x, pltpu.HBM)
            for x in (volts, fir_taps, jnp.asarray(table), jnp.asarray(turn_table(), F32))
        ],
    )


def spectra_kernel(groups, parts, out_frames, run, place, *refs):
    part_refs, refs = refs[: len(parts)], refs[len(parts) :]
    taps, one, two, turn = refs[:4]
    outs, (ext, filtered, turned, staged) = refs[4:-4], refs[-4:]
    step, steps, members = pl.program_id(0), pl.num_programs(0), MEMBERS
    per_group = K2 // groups
    share = LANES // out_frames
    tiles = H // share
    pairs = tiles // 2
    frame_rows, row_rows = ROWS + PAD, tiles * TILE + PAD

    def load(member):
        signal = step * members + member
        for (frames, block, start, valid), ref in zip(parts, part_refs):
            first = value_of(block, place[0]) * frames
            start = value_of(start, place[0])
            valid = value_of(valid, place[0])

            def fill(ref=ref, frames=frames, first=first, start=start):
                for f in range(frames):
                    ext[member, start + f] = ref[signal, first + f].astype(F32)

            def clear(frames=frames, start=start):
                for f in range(frames):
                    ext[member, start + f] = jnp.zeros((ROWS, LANES), F32)

            if isinstance(valid, int):
                fill() if valid else clear()
            else:
                pl.when(valid == 1)(fill)
                pl.when(valid == 0)(clear)

    def filter_rows(member, q):
        rows = pl.ds(pl.multiple_of(q * SUB, SUB), SUB)
        tap = [taps[pl.ds(pl.multiple_of(m * ROWS + q * SUB, SUB), SUB), :] for m in range(TAPS)]
        for f in range(out_frames):
            total = tap[0] * ext[member, f + 1, rows]
            for m in range(1, TAPS):
                total = total + tap[m] * ext[member, f + 1 + m, rows]
            filtered[member, f, rows] = total

    def first_stage(member):
        cosine = turn[:, :LANES]
        sine = turn[:, LANES:]
        for g in range(out_frames // STEP):
            block = jnp.concatenate([filtered[member, g * STEP + f] for f in range(STEP)], axis=1)
            high, low = halves(block)
            first = dot(one[...], jnp.concatenate([high, low, high], axis=0))
            for f in range(STEP):
                real = first[:H, f * LANES : (f + 1) * LANES]
                imag = first[H:, f * LANES : (f + 1) * LANES]
                at = (g * STEP + f) * frame_rows
                turned[member, at : at + H, :] = real * cosine + imag * sine
                turned[member, at + H : at + ROWS, :] = imag * cosine - real * sine

    def second_stage(member, pair):
        rows = []
        for k1 in range(2 * pair * share, 2 * (pair + 1) * share):
            for f in range(0, out_frames, SUB):
                rows.append(
                    jnp.concatenate(
                        [turned[member, pl.ds(f * frame_rows + p * H + k1, SUB, stride=frame_rows), :] for p in range(2)],
                        axis=1,
                    )
                )
        high, low = halves(jnp.concatenate(rows, axis=0))
        spectrum = dot_nt(two[0], high) + dot_nt(two[1], high) + dot_nt(two[0], low)
        for k in range(2):
            for t in range(groups):
                for p in range(2):
                    for k2 in range(0, per_group, SUB):
                        row = (t * 2 + p) * per_group + k2
                        start = (t * per_group + k2) * row_rows + (2 * pair + k) * TILE + p * SUB
                        staged[pl.ds(start + step * members + member, SUB, stride=row_rows), :] = spectrum[
                            row : row + SUB, k * LANES : (k + 1) * LANES
                        ]

    def write():
        at = 0
        for out in outs:

            def write_row(k2, carry):
                for k in range(tiles):
                    start = pl.multiple_of((at + k2) * row_rows + k * TILE, PAD)
                    out[k2, k] = staged[pl.ds(start, TILE), :].astype(BF16)
                return carry

            lax.fori_loop(0, out.shape[0], write_row, 0, unroll=2)
            at += out.shape[0]

    def body():
        for member in range(members):
            load(member)

        def filter_one(index, carry):
            filter_rows(index // (ROWS // SUB), index % (ROWS // SUB))
            return carry

        lax.fori_loop(0, members * (ROWS // SUB), filter_one, 0)
        for member in range(members):
            first_stage(member)
        for member in range(members):
            for pair in range(pairs):
                second_stage(member, pair)

        pl.when(step == steps - 1)(write)

    if isinstance(run, int):
        body()
    else:
        pl.when(value_of(run, place[0]) == 1)(body)


def after(value, *others):
    return lax.optimization_barrier((value, *others))[0]


def spectra(parts, out_frames, fixed, place, groups, sizes, run=1, wait=(), cost=10**6):
    signals = parts[0][0].shape[0]
    place = after(place, *wait)
    tiles = H * out_frames // LANES
    shapes = [(n, tiles, TILE, LANES) for n in sizes]
    return pl.pallas_call(
        functools.partial(spectra_kernel, groups, tuple(part[1:] for part in parts), out_frames, run),
        grid_spec=pltpu.PrefetchScalarGridSpec(
            num_scalar_prefetch=1,
            grid=(signals // MEMBERS,),
            in_specs=[pl.BlockSpec(memory_space=pltpu.VMEM)] * (len(parts) + 4),
            out_specs=[pl.BlockSpec(shape, lambda s, place: (0, 0, 0, 0)) for shape in shapes],
            scratch_shapes=[
                pltpu.VMEM((MEMBERS, TAPS + out_frames, ROWS, LANES), F32),
                pltpu.VMEM((MEMBERS, out_frames, ROWS, LANES), F32),
                pltpu.VMEM((MEMBERS, out_frames * (ROWS + PAD), LANES), F32),
                pltpu.VMEM((K2 * (tiles * TILE + PAD), LANES), F32),
            ],
        ),
        out_shape=[jax.ShapeDtypeStruct(shape, BF16) for shape in shapes],
        compiler_params=pltpu.CompilerParams(vmem_limit_bytes=32 << 20),
        cost_estimate=pl.CostEstimate(flops=cost, bytes_accessed=0, transcendentals=0),
    )(place, *[part[0] for part in parts], *fixed)


def after(value, *others):
    return lax.optimization_barrier((value, *others))[0]


def correlate_kernel(pieces, per_group, scale, add, last, place, *refs):
    refs = list(refs)
    sums = refs.pop() if last else None
    out = refs.pop()
    before = refs.pop() if add else None
    if not last:
        sums = out
    half = per_group // 2
    lane = lax.broadcasted_iota(jnp.int32, (SUB, LANES), 1)
    first_tile = lane < LANES // 2
    real_lane = lane % TILE < SUB
    sign = jnp.where(real_lane, 1.0, -1.0).astype(F32)
    for number, piece in enumerate(pieces):
        tiles, piece = piece
        share = H // tiles
        where = lax.broadcasted_iota(jnp.int32, (TILE, LANES), 1) // (LANES // share)

        def pair(index, carry):
            k2 = index // tiles
            k1 = index % tiles
            own, other = [], []
            for position in range(len(piece[0])):
                rows = []
                for tile in range(2):
                    array, row, column = piece[0][position]
                    a = refs[array][row + tile * half + k2, column + k1]
                    rows += [jnp.where(where == c, a, jnp.zeros_like(a)) for c in range(share)]
                own.append(jnp.concatenate(rows, axis=0))
                rows = []
                for tile in range(2):
                    for visit in range(VISITS):
                        array, row, column = piece[visit][position]
                        rows.append(refs[array][row + tile * half + k2, column + k1])
                other.append(jnp.concatenate(rows, axis=0))
            product = dot_nt(jnp.concatenate(own, axis=1), jnp.concatenate(other, axis=1))
            for c in range(share):
                value = []
                for p in range(2):
                    at = [((tile * share + c) * 2 + p) * SUB for tile in range(2)]
                    value.append(
                        jnp.where(first_tile, product[at[0] : at[0] + SUB], product[at[1] : at[1] + SUB])
                    )
                turned = jnp.where(
                    real_lane, pltpu.roll(value[1], LANES - SUB, 1), pltpu.roll(value[1], SUB, 1)
                )
                total = value[0] * sign + turned
                channel = k2 // 4 * LANES + k2 % 4 * H + k1 * share + c
                rows = pl.ds(pl.multiple_of(channel * SUB, SUB), SUB)
                if number:
                    total = total + sums[rows, :]
                elif add:
                    total = total + before[rows, :]
                sums[rows, :] = total
            return carry

        lax.fori_loop(0, half * tiles, pair, 0, unroll=16)
    if not last:
        return

    def finish(index, carry):
        block = index // SUB
        signal = index % SUB
        value = sums[pl.ds(block * LANES * SUB + signal, LANES, stride=SUB), :]
        value = jnp.transpose(value * scale)
        at = 0
        for tile in range(2):
            for visit in range(VISITS):
                for part in range(2):
                    out[part, signal, value_of(PLACES[visit], place[1]), tile * (half // 4) + block] = value[at : at + SUB]
                    at += SUB
        return carry

    lax.fori_loop(0, half // 4 * SUB, finish, 0)


def correlate(arrays, pieces, per_group, place, scale, before, last, wait=()):
    signals = TILE // 2
    rows = per_group // 2 * H * SUB
    place = after(place, *wait)
    shape = (2, signals, VISITS, per_group // 4, SUB, LANES) if last else (rows, LANES)
    operands = list(arrays) + ([] if before is None else [before])
    whole = lambda shape: pl.BlockSpec(shape, lambda i, place: (0,) * len(shape))
    return pl.pallas_call(
        functools.partial(correlate_kernel, pieces, per_group, scale, before is not None, last),
        grid_spec=pltpu.PrefetchScalarGridSpec(
            num_scalar_prefetch=1,
            grid=(1,),
            in_specs=[whole(x.shape) for x in operands],
            out_specs=whole(shape),
            scratch_shapes=[pltpu.VMEM((rows, LANES), F32)] if last else [],
        ),
        out_shape=jax.ShapeDtypeStruct(shape, F32),
        compiler_params=pltpu.CompilerParams(vmem_limit_bytes=48 << 20),
        input_output_aliases={} if before is None or last else {len(operands): 0},
        cost_estimate=pl.CostEstimate(flops=6 * 10**9, bytes_accessed=0, transcendentals=0),
    )(place, *operands)


def stacked(voltage):
    s, f = voltage.shape[:2]
    return voltage.reshape(s, f, 2, H, LANES).transpose(0, 1, 3, 2, 4).reshape(s, f, ROWS, LANES)


def natural(out):
    parts, s, visits, i, t, lanes = out.shape
    return out.transpose(0, 1, 2, 4, 3, 5).reshape(parts, s, visits * t, i * lanes)


def shifted(block, axis, distance):
    size = lax.axis_size(axis)
    return lax.ppermute(block, axis, [(i, (i + distance) % size) for i in range(size)])


def farther(block):
    size = lax.axis_size("stn")
    rest = lax.ppermute(block, "stn", [(i, (i + 1 if i % 2 == 0 else i + 3) % size) for i in range(size)])
    return shifted(block, "stn", 2), rest


def exchanged(block):
    return lax.ppermute(block, "stn", [(i, i ^ 1) for i in range(lax.axis_size("stn"))])


def general(volts, fir_taps):
    groups = lax.axis_size("tm")
    frames = volts.shape[1]
    volts, edge_frames, *fixed = prepare(volts, fir_taps, place, groups, frames // TAPS - 1, TAPS)
    history = lax.ppermute(edge_frames, "tm", [(i, i + 1) for i in range(groups - 1)])
    parts = [(history, TAPS, 0, 0, 1)] + [(volts, TAPS, i, TAPS * (i + 1), 1) for i in range(frames // TAPS)]
    spectrum = spectra(parts, frames, fixed, place, groups, [K2])[0]
    spectrum = lax.all_to_all(spectrum, "tm", split_axis=0, concat_axis=0, tiled=True)
    tiles = spectrum.shape[1]
    return [([spectrum], [(tiles, [(0, K2 // groups * t, 0) for t in range(groups)])])]


def paired(volts, fir_taps, place, correlated):
    frames = volts.shape[1]
    me = lax.axis_index("tm")
    sizes = [K2 // 2, K2 // 2]
    swap = [(0, 1), (1, 0)]
    edge = TAPS // 2
    last = frames // edge
    volts, edge_frames, *fixed = prepare(volts, fir_taps, place, 2, (last - 1, 0), edge)
    visiting = lax.ppermute(edge_frames, "tm", swap)
    own_a, away_a = spectra(
        [(volts, TAPS, 0, 0, (0, 1)), (volts, TAPS, (0, 1), TAPS, 1)], TAPS, fixed, place, 2, sizes
    )
    got_a = lax.ppermute(away_a, "tm", swap)
    two_a, rest_a = farther(own_a)
    own_b, away_b = spectra(
        [(volts, TAPS, 0, 0, 1), (volts, TAPS, 1, TAPS, 1)], TAPS, fixed, place, 2, sizes, (1, 0), (own_a,)
    )
    got_b = lax.ppermute(away_b, "tm", [(0, 1)])
    pair_a = exchanged(two_a)
    own_c, away_c = spectra(
        [
            (volts, edge, (last - 2, 0), (0, edge), 1),
            (volts, edge, (last - 1, 1), (edge, 2 * edge), 1),
            (visiting, edge, 0, (2 * edge, 0), 1),
        ],
        edge, fixed, place, 2, sizes, 1, (own_b, two_a, got_a), 9 * 10**9,
    )
    got_c = lax.ppermute(away_c, "tm", swap)
    two_g, rest_g = farther(got_a)
    pair_g = exchanged(two_g)
    own_c = after(own_c, two_g, pair_a, rest_a)
    rest = jnp.concatenate([jnp.where(me == 0, own_b, got_b), own_c, got_c], axis=1)
    two_r, rest_r = farther(rest)
    many, few = own_a.shape[1], own_c.shape[1]
    sums = correlated(
        [own_a, pair_a, two_a, rest_a, got_a, pair_g, two_g, rest_g], [(many, [(0, 0, 0), (1, 0, 0)])], None, False
    )
    pair_r = exchanged(after(two_r, sums))
    return correlated(
        [rest, pair_r, two_r, rest_r], [(many, [(0, 0, 0)]), (few, [(0, 0, many), (0, 0, many + few)])], sums, True
    )


def general(volts, fir_taps, place, correlated):
    groups = lax.axis_size("tm")
    frames = volts.shape[1]
    volts, edge_frames, *fixed = prepare(volts, fir_taps, place, groups, frames // TAPS - 1, TAPS)
    history = lax.ppermute(edge_frames, "tm", [(i, i + 1) for i in range(groups - 1)])
    parts = [(history, TAPS, 0, 0, 1)] + [(volts, TAPS, i, TAPS * (i + 1), 1) for i in range(frames // TAPS)]
    spectrum = spectra(parts, frames, fixed, place, groups, [K2])[0]
    spectrum = lax.all_to_all(spectrum, "tm", split_axis=0, concat_axis=0, tiled=True)
    two, rest = farther(spectrum)
    spots = [(0, K2 // groups * t, 0) for t in range(groups)]
    return correlated([spectrum, exchanged(two), two, rest], [(spectrum.shape[1], spots)], None, True)


def local(voltage, fir_taps):
    groups = lax.axis_size("tm")
    place = jnp.stack([lax.axis_index("tm"), lax.axis_index("stn") % 2]).astype(jnp.int32)
    scale = 1.0 / (groups * voltage.shape[1])

    def correlated(arrays, pieces, before, last, wait=()):
        laid = [
            (tiles, [[(VISITS * n + visit, row, column) for n, row, column in spots] for visit in range(VISITS)])
            for tiles, spots in pieces
        ]
        return correlate(arrays, laid, K2 // groups, place, scale, before, last, wait)

    run = paired if groups == 2 else general
    return natural(run(stacked(voltage), fir_taps, place, correlated))


def solution(mesh):
    return jax.shard_map(
        local,
        mesh=mesh,
        in_specs=(P("stn", "tm", None, None), P()),
        out_specs=P(None, "stn", None, "tm"),
        check_vma=False,
    )
```

```python
import functools
import math

import jax
import jax.numpy as jnp
import numpy as np
from jax import lax
from jax.experimental import pallas as pl
from jax.experimental.pallas import tpu as pltpu
from jax.sharding import PartitionSpec as P

NCH = 4096
CHANS = 2048
TAPS = 16
VISITS = 4
H = 32
LANES = 128
ROWS = 2 * H
K2 = CHANS // H
STEP = 8
TILE = 16
PLACES = (0, (1, 3), 2, (3, 1))
MEMBERS = 4
PAD = 8
SUB = 8
BF16 = jnp.bfloat16
F32 = jnp.float32


def angles(rows, columns, modulus):
    turns = np.outer(rows, columns) % modulus
    return turns.astype(np.float64) * (2.0 * math.pi / modulus)


def stage_one_table():
    theta = angles(np.arange(H), np.arange(H), H)
    cosine, sine = np.cos(theta), np.sin(theta)
    table = np.zeros((2, H, H, 2))
    table[0, :, :, 0], table[0, :, :, 1] = cosine, sine
    table[1, :, :, 0], table[1, :, :, 1] = -sine, cosine
    return np.pad(table.reshape(ROWS, ROWS), ((0, 0), (0, 2 * LANES - ROWS)))


def turn_table():
    theta = angles(np.arange(H), np.arange(LANES), NCH)
    return np.concatenate([np.cos(theta), np.sin(theta)], axis=1)


def stage_two_table(groups):
    theta = angles(np.arange(K2), np.arange(LANES), LANES)
    cosine, sine = np.cos(theta) / math.sqrt(NCH), np.sin(theta) / math.sqrt(NCH)
    real = np.concatenate([cosine, sine], 1).reshape(groups, 1, K2 // groups, 2 * LANES)
    imag = np.concatenate([-sine, cosine], 1).reshape(groups, 1, K2 // groups, 2 * LANES)
    return np.concatenate([real, imag], 1).reshape(2 * K2, 2 * LANES)


def halves(value):
    high = value.astype(BF16)
    return high, (value - high.astype(F32)).astype(BF16)


def dot(left, right):
    return lax.dot_general(left, right, (((1,), (0,)), ((), ())), preferred_element_type=F32)


def dot_nt(left, right):
    return lax.dot_general(left, right, (((1,), (1,)), ((), ())), preferred_element_type=F32)


def value_of(number, group):
    if isinstance(number, int):
        return number
    return number[0] + (number[1] - number[0]) * group


def prepare_kernel(edge_block, swapped, place, volts_source, taps_source, table_source, turn_source, volts, edge, taps, one, two, turn, done, taps_ref, table_ref):
    count = edge.shape[1]
    start = pl.multiple_of(value_of(edge_block, place[0]) * count, count)
    copies = [
        pltpu.make_async_copy(taps_source, taps_ref, done.at[0]),
        pltpu.make_async_copy(table_source, table_ref, done.at[1]),
        pltpu.make_async_copy(volts_source.at[:, pl.ds(start, count)], edge, done.at[2]),
        pltpu.make_async_copy(volts_source, volts, done.at[3]),
        pltpu.make_async_copy(turn_source, turn, done.at[4]),
    ]
    for copy in copies:
        copy.start()
    copies[0].wait()
    copies[1].wait()
    for h in range(H):
        for half in range(TAPS // SUB):
            tile = taps_ref[pl.ds(half * SUB, SUB), pl.ds(h * LANES, LANES)]
            for r in range(2):
                taps[pl.ds(half * SUB * ROWS + 2 * h + r, SUB, stride=ROWS), :] = tile
    high, low = halves(table_ref[:ROWS, :ROWS])
    one[...] = jnp.concatenate([high, high, low], axis=1)
    start = pl.multiple_of(ROWS + place[0] * (2 * K2 * swapped), SUB)
    high, low = halves(table_ref[pl.ds(start, 2 * K2), :])
    two[0] = high
    two[1] = low
    for copy in copies[2:]:
        copy.wait()


def prepare(volts, fir_taps, place, groups, edge_block, edge_frames):
    signals, frames = volts.shape[:2]
    two = stage_two_table(groups)
    table = np.concatenate([stage_one_table(), two, np.roll(two, K2, axis=0)]).astype(np.float32)
    vmem = pl.BlockSpec(memory_space=pltpu.VMEM)
    return pl.pallas_call(
        functools.partial(prepare_kernel, edge_block, int(groups == 2)),
        grid_spec=pltpu.PrefetchScalarGridSpec(
            num_scalar_prefetch=1,
            grid=(),
            in_specs=[pl.BlockSpec(memory_space=pl.ANY)] * 4,
            out_specs=[vmem] * 6,
            scratch_shapes=[
                pltpu.SemaphoreType.DMA((5,)),
                pltpu.VMEM(fir_taps.shape, F32),
                pltpu.VMEM(table.shape, F32),
            ],
        ),
        out_shape=[
            jax.ShapeDtypeStruct((signals, frames, ROWS, LANES), BF16),
            jax.ShapeDtypeStruct((signals, edge_frames, ROWS, LANES), BF16),
            jax.ShapeDtypeStruct((TAPS * ROWS, LANES), F32),
            jax.ShapeDtypeStruct((ROWS, 3 * ROWS), BF16),
            jax.ShapeDtypeStruct((2, 2 * K2, 2 * LANES), BF16),
            jax.ShapeDtypeStruct((H, 2 * LANES), F32),
        ],
        compiler_params=pltpu.CompilerParams(vmem_limit_bytes=24 << 20),
    )(
        place,
        *[
            pltpu.with_memory_space_constraint(x, pltpu.HBM)
            for x in (volts, fir_taps, jnp.asarray(table), jnp.asarray(turn_table(), F32))
        ],
    )


def spectra_kernel(groups, parts, out_frames, run, place, *refs):
    part_refs, refs = refs[: len(parts)], refs[len(parts) :]
    taps, one, two, turn = refs[:4]
    outs, (ext, filtered, turned, staged) = refs[4:-4], refs[-4:]
    step, steps, members = pl.program_id(0), pl.num_programs(0), MEMBERS
    per_group = K2 // groups
    share = LANES // out_frames
    tiles = H // share
    pairs = tiles // 2
    frame_rows, row_rows = ROWS + PAD, tiles * TILE + PAD

    def load(member):
        signal = step * members + member
        for (frames, block, start, valid), ref in zip(parts, part_refs):
            first = value_of(block, place[0]) * frames
            start = value_of(start, place[0])
            valid = value_of(valid, place[0])

            def fill(ref=ref, frames=frames, first=first, start=start):
                for f in range(frames):
                    ext[member, start + f] = ref[signal, first + f].astype(F32)

            def clear(frames=frames, start=start):
                for f in range(frames):
                    ext[member, start + f] = jnp.zeros((ROWS, LANES), F32)

            if isinstance(valid, int):
                fill() if valid else clear()
            else:
                pl.when(valid == 1)(fill)
                pl.when(valid == 0)(clear)

    def filter_rows(member, q):
        rows = pl.ds(pl.multiple_of(q * SUB, SUB), SUB)
        tap = [taps[pl.ds(pl.multiple_of(m * ROWS + q * SUB, SUB), SUB), :] for m in range(TAPS)]
        for f in range(out_frames):
            total = tap[0] * ext[member, f + 1, rows]
            for m in range(1, TAPS):
                total = total + tap[m] * ext[member, f + 1 + m, rows]
            filtered[member, f, rows] = total

    def first_stage(member):
        cosine = turn[:, :LANES]
        sine = turn[:, LANES:]
        for g in range(out_frames // STEP):
            block = jnp.concatenate([filtered[member, g * STEP + f] for f in range(STEP)], axis=1)
            high, low = halves(block)
            first = dot(one[...], jnp.concatenate([high, low, high], axis=0))
            for f in range(STEP):
                real = first[:H, f * LANES : (f + 1) * LANES]
                imag = first[H:, f * LANES : (f + 1) * LANES]
                at = (g * STEP + f) * frame_rows
                turned[member, at : at + H, :] = real * cosine + imag * sine
                turned[member, at + H : at + ROWS, :] = imag * cosine - real * sine

    def second_stage(member, pair):
        rows = []
        for k1 in range(2 * pair * share, 2 * (pair + 1) * share):
            for f in range(0, out_frames, SUB):
                rows.append(
                    jnp.concatenate(
                        [turned[member, pl.ds(f * frame_rows + p * H + k1, SUB, stride=frame_rows), :] for p in range(2)],
                        axis=1,
                    )
                )
        high, low = halves(jnp.concatenate(rows, axis=0))
        spectrum = dot_nt(two[0], high) + dot_nt(two[1], high) + dot_nt(two[0], low)
        for k in range(2):
            for t in range(groups):
                for p in range(2):
                    for k2 in range(0, per_group, SUB):
                        row = (t * 2 + p) * per_group + k2
                        start = (t * per_group + k2) * row_rows + (2 * pair + k) * TILE + p * SUB
                        staged[pl.ds(start + step * members + member, SUB, stride=row_rows), :] = spectrum[
                            row : row + SUB, k * LANES : (k + 1) * LANES
                        ]

    def write():
        at = 0
        for out in outs:

            def write_row(k2, carry):
                for k in range(tiles):
                    start = pl.multiple_of((at + k2) * row_rows + k * TILE, PAD)
                    out[k2, k] = staged[pl.ds(start, TILE), :].astype(BF16)
                return carry

            lax.fori_loop(0, out.shape[0], write_row, 0, unroll=2)
            at += out.shape[0]

    def body():
        for member in range(members):
            load(member)

        def filter_one(index, carry):
            filter_rows(index // (ROWS // SUB), index % (ROWS // SUB))
            return carry

        lax.fori_loop(0, members * (ROWS // SUB), filter_one, 0)
        for member in range(members):
            first_stage(member)
        for member in range(members):
            for pair in range(pairs):
                second_stage(member, pair)

        pl.when(step == steps - 1)(write)

    if isinstance(run, int):
        body()
    else:
        pl.when(value_of(run, place[0]) == 1)(body)


def after(value, *others):
    return lax.optimization_barrier((value, *others))[0]


def spectra(parts, out_frames, fixed, place, groups, sizes, run=1, wait=(), cost=10**6):
    signals = parts[0][0].shape[0]
    place = after(place, *wait)
    tiles = H * out_frames // LANES
    shapes = [(n, tiles, TILE, LANES) for n in sizes]
    return pl.pallas_call(
        functools.partial(spectra_kernel, groups, tuple(part[1:] for part in parts), out_frames, run),
        grid_spec=pltpu.PrefetchScalarGridSpec(
            num_scalar_prefetch=1,
            grid=(signals // MEMBERS,),
            in_specs=[pl.BlockSpec(memory_space=pltpu.VMEM)] * (len(parts) + 4),
            out_specs=[pl.BlockSpec(shape, lambda s, place: (0, 0, 0, 0)) for shape in shapes],
            scratch_shapes=[
                pltpu.VMEM((MEMBERS, TAPS + out_frames, ROWS, LANES), F32),
                pltpu.VMEM((MEMBERS, out_frames, ROWS, LANES), F32),
                pltpu.VMEM((MEMBERS, out_frames * (ROWS + PAD), LANES), F32),
                pltpu.VMEM((K2 * (tiles * TILE + PAD), LANES), F32),
            ],
        ),
        out_shape=[jax.ShapeDtypeStruct(shape, BF16) for shape in shapes],
        compiler_params=pltpu.CompilerParams(vmem_limit_bytes=32 << 20),
        cost_estimate=pl.CostEstimate(flops=cost, bytes_accessed=0, transcendentals=0),
    )(place, *[part[0] for part in parts], *fixed)


def after(value, *others):
    return lax.optimization_barrier((value, *others))[0]


def correlate_kernel(pieces, per_group, scale, add, last, place, *refs):
    refs = list(refs)
    sums = refs.pop() if last else None
    out = refs.pop()
    before = refs.pop() if add else None
    if not last:
        sums = out
    half = per_group // 2
    lane = lax.broadcasted_iota(jnp.int32, (SUB, LANES), 1)
    first_tile = lane < LANES // 2
    real_lane = lane % TILE < SUB
    sign = jnp.where(real_lane, 1.0, -1.0).astype(F32)

    def fetch(spot, tile, k2, k1):
        arrays, row, column = spot
        values = [refs[array][row + tile * half + k2, column + k1] for array in arrays]
        return values[0] if len(values) == 1 else values[0] + values[1]

    for number, piece in enumerate(pieces):
        tiles, piece = piece
        share = H // tiles
        where = lax.broadcasted_iota(jnp.int32, (TILE, LANES), 1) // (LANES // share)

        def pair(index, carry):
            k2 = index // tiles
            k1 = index % tiles
            own, other = [], []
            for position in range(len(piece[0])):
                rows = []
                for tile in range(2):
                    a = fetch(piece[0][position], tile, k2, k1)
                    rows += [jnp.where(where == c, a, jnp.zeros_like(a)) for c in range(share)]
                own.append(jnp.concatenate(rows, axis=0))
                rows = []
                for tile in range(2):
                    for visit in range(VISITS):
                        rows.append(fetch(piece[visit][position], tile, k2, k1))
                other.append(jnp.concatenate(rows, axis=0))
            product = dot_nt(jnp.concatenate(own, axis=1), jnp.concatenate(other, axis=1))
            for c in range(share):
                value = []
                for p in range(2):
                    at = [((tile * share + c) * 2 + p) * SUB for tile in range(2)]
                    value.append(
                        jnp.where(first_tile, product[at[0] : at[0] + SUB], product[at[1] : at[1] + SUB])
                    )
                turned = jnp.where(
                    real_lane, pltpu.roll(value[1], LANES - SUB, 1), pltpu.roll(value[1], SUB, 1)
                )
                total = value[0] * sign + turned
                channel = k2 // 4 * LANES + k2 % 4 * H + k1 * share + c
                rows = pl.ds(pl.multiple_of(channel * SUB, SUB), SUB)
                if number:
                    total = total + sums[rows, :]
                elif add:
                    total = total + before[rows, :]
                sums[rows, :] = total
            return carry

        lax.fori_loop(0, half * tiles, pair, 0, unroll=16)
    if not last:
        return

    def finish(index, carry):
        block = index // SUB
        signal = index % SUB
        value = sums[pl.ds(block * LANES * SUB + signal, LANES, stride=SUB), :]
        value = jnp.transpose(value * scale)
        at = 0
        for tile in range(2):
            for visit in range(VISITS):
                for part in range(2):
                    out[part, signal, value_of(PLACES[visit], place[1]), tile * (half // 4) + block] = value[at : at + SUB]
                    at += SUB
        return carry

    lax.fori_loop(0, half // 4 * SUB, finish, 0)


def correlate(arrays, pieces, per_group, place, scale, before, last, wait=()):
    signals = TILE // 2
    rows = per_group // 2 * H * SUB
    place = after(place, *wait)
    shape = (2, signals, VISITS, per_group // 4, SUB, LANES) if last else (rows, LANES)
    operands = list(arrays) + ([] if before is None else [before])
    whole = lambda shape: pl.BlockSpec(shape, lambda i, place: (0,) * len(shape))
    return pl.pallas_call(
        functools.partial(correlate_kernel, pieces, per_group, scale, before is not None, last),
        grid_spec=pltpu.PrefetchScalarGridSpec(
            num_scalar_prefetch=1,
            grid=(1,),
            in_specs=[whole(x.shape) for x in operands],
            out_specs=whole(shape),
            scratch_shapes=[pltpu.VMEM((rows, LANES), F32)] if last else [],
        ),
        out_shape=jax.ShapeDtypeStruct(shape, F32),
        compiler_params=pltpu.CompilerParams(vmem_limit_bytes=48 << 20),
        input_output_aliases={} if before is None or last else {len(operands): 0},
        cost_estimate=pl.CostEstimate(flops=6 * 10**9, bytes_accessed=0, transcendentals=0),
    )(place, *operands)


def stacked(voltage):
    s, f = voltage.shape[:2]
    return voltage.reshape(s, f, 2, H, LANES).transpose(0, 1, 3, 2, 4).reshape(s, f, ROWS, LANES)


def natural(out):
    parts, s, visits, i, t, lanes = out.shape
    return out.transpose(0, 1, 2, 4, 3, 5).reshape(parts, s, visits * t, i * lanes)


VISIT_ARRAYS = ((0,), (4, 5), (1, 3), (2,))


def sent(block, way):
    size = lax.axis_size("stn")
    pairs = [(i, way(i)) for i in range(size)]
    return lax.ppermute(block, "stn", [(i, j % size) for i, j in pairs if j is not None])


def direct(block):
    two = sent(block, lambda i: i + 2 if i % 4 < 3 else None)
    return two, sent(block, lambda i: i + 1 if i % 2 == 0 else i + 3)


def relayed(rest):
    return sent(rest, lambda i: i - 1 if i % 4 == 2 else None)


def across(two):
    return sent(two, lambda i: i ^ 1 if i % 4 != 1 else None)


def across_relayed(relay):
    return sent(relay, lambda i: i - 1 if i % 4 == 1 else None)


def paired(volts, fir_taps, place, correlated):
    frames = volts.shape[1]
    me = lax.axis_index("tm")
    sizes = [K2 // 2, K2 // 2]
    swap = [(0, 1), (1, 0)]
    edge = TAPS // 2
    last = frames // edge
    volts, edge_frames, *fixed = prepare(volts, fir_taps, place, 2, (last - 1, 0), edge)
    visiting = lax.ppermute(edge_frames, "tm", swap)
    own_a, away_a = spectra(
        [(volts, TAPS, 0, 0, (0, 1)), (volts, TAPS, (0, 1), TAPS, 1)], TAPS, fixed, place, 2, sizes
    )
    got_a = lax.ppermute(away_a, "tm", swap)
    two_a, rest_a = direct(own_a)
    own_b, away_b = spectra(
        [(volts, TAPS, 0, 0, 1), (volts, TAPS, 1, TAPS, 1)], TAPS, fixed, place, 2, sizes, (1, 0), (own_a,)
    )
    got_a = after(got_a, own_b)
    got_b = lax.ppermute(away_b, "tm", [(0, 1)])
    relay_a, pair_a = relayed(rest_a), across(two_a)
    own_c, away_c = spectra(
        [
            (volts, edge, (last - 2, 0), (0, edge), 1),
            (volts, edge, (last - 1, 1), (edge, 2 * edge), 1),
            (visiting, edge, 0, (2 * edge, 0), 1),
        ],
        edge, fixed, place, 2, sizes, 1, (own_b, two_a, rest_a, got_a), 9 * 10**9,
    )
    got_c = lax.ppermute(away_c, "tm", swap)
    two_g, rest_g = direct(got_a)
    own_c, got_c, pair_a, relay_a, two_g, rest_g = lax.optimization_barrier(
        (own_c, got_c, pair_a, relay_a, two_g, rest_g)
    )
    rest = jnp.concatenate([jnp.where(me == 0, own_b, got_b), own_c, got_c], axis=1)
    two_r, rest_r = direct(rest)
    relay_g, pair_g = relayed(rest_g), across(two_g)
    last_a, last_g = across_relayed(after(relay_a, rest)), across_relayed(after(relay_g, rest))
    many, few = own_a.shape[1], own_c.shape[1]
    sums = correlated(
        [own_a, two_a, rest_a, relay_a, pair_a, last_a, got_a, two_g, rest_g, relay_g, pair_g, last_g],
        [(many, [(0, 0, 0), (1, 0, 0)])],
        None,
        False,
    )
    relay_r, pair_r = relayed(after(rest_r, sums)), across(after(two_r, sums))
    last_r = across_relayed(relay_r)
    return correlated(
        [rest, two_r, rest_r, relay_r, pair_r, last_r],
        [(many, [(0, 0, 0)]), (few, [(0, 0, many), (0, 0, many + few)])],
        sums,
        True,
    )


def general(volts, fir_taps, place, correlated):
    groups = lax.axis_size("tm")
    frames = volts.shape[1]
    volts, edge_frames, *fixed = prepare(volts, fir_taps, place, groups, frames // TAPS - 1, TAPS)
    history = lax.ppermute(edge_frames, "tm", [(i, i + 1) for i in range(groups - 1)])
    parts = [(history, TAPS, 0, 0, 1)] + [(volts, TAPS, i, TAPS * (i + 1), 1) for i in range(frames // TAPS)]
    spectrum = spectra(parts, frames, fixed, place, groups, [K2])[0]
    spectrum = lax.all_to_all(spectrum, "tm", split_axis=0, concat_axis=0, tiled=True)
    two, rest = direct(spectrum)
    relay = relayed(rest)
    spots = [(0, K2 // groups * t, 0) for t in range(groups)]
    return correlated(
        [spectrum, two, rest, relay, across(two), across_relayed(relay)], [(spectrum.shape[1], spots)], None, True
    )


def local(voltage, fir_taps):
    groups = lax.axis_size("tm")
    place = jnp.stack([lax.axis_index("tm"), lax.axis_index("stn") % 2]).astype(jnp.int32)
    scale = 1.0 / (groups * voltage.shape[1])

    def correlated(arrays, pieces, before, last, wait=()):
        laid = [
            (tiles, [[([6 * n + k for k in visit], row, column) for n, row, column in spots] for visit in VISIT_ARRAYS])
            for tiles, spots in pieces
        ]
        return correlate(arrays, laid, K2 // groups, place, scale, before, last, wait)

    run = paired if groups == 2 else general
    return natural(run(stacked(voltage), fir_taps, place, correlated))


def solution(mesh):
    return jax.shard_map(
        local,
        mesh=mesh,
        in_specs=(P("stn", "tm", None, None), P()),
        out_specs=P(None, "stn", None, "tm"),
        check_vma=False,
    )
```

```python
import functools
import math

import jax
import jax.numpy as jnp
import numpy as np
from jax import lax
from jax.experimental import pallas as pl
from jax.experimental.pallas import tpu as pltpu
from jax.sharding import PartitionSpec as P

NCH = 4096
CHANS = 2048
TAPS = 16
VISITS = 4
H = 32
LANES = 128
ROWS = 2 * H
K2 = CHANS // H
STEP = 8
TILE = 16
PLACES = (0, (1, 3), 2, (3, 1))
MEMBERS = 4
PAD = 8
SUB = 8
BF16 = jnp.bfloat16
F32 = jnp.float32


def angles(rows, columns, modulus):
    turns = np.outer(rows, columns) % modulus
    return turns.astype(np.float64) * (2.0 * math.pi / modulus)


def stage_one_table():
    theta = angles(np.arange(H), np.arange(H), H)
    cosine, sine = np.cos(theta), np.sin(theta)
    table = np.zeros((2, H, H, 2))
    table[0, :, :, 0], table[0, :, :, 1] = cosine, sine
    table[1, :, :, 0], table[1, :, :, 1] = -sine, cosine
    return np.pad(table.reshape(ROWS, ROWS), ((0, 0), (0, 2 * LANES - ROWS)))


def turn_table():
    theta = angles(np.arange(H), np.arange(LANES), NCH)
    return np.concatenate([np.cos(theta), np.sin(theta)], axis=1)


def stage_two_table(groups):
    theta = angles(np.arange(K2), np.arange(LANES), LANES)
    cosine, sine = np.cos(theta) / math.sqrt(NCH), np.sin(theta) / math.sqrt(NCH)
    real = np.concatenate([cosine, sine], 1).reshape(groups, 1, K2 // groups, 2 * LANES)
    imag = np.concatenate([-sine, cosine], 1).reshape(groups, 1, K2 // groups, 2 * LANES)
    return np.concatenate([real, imag], 1).reshape(2 * K2, 2 * LANES)


def halves(value):
    high = value.astype(BF16)
    return high, (value - high.astype(F32)).astype(BF16)


def dot(left, right):
    return lax.dot_general(left, right, (((1,), (0,)), ((), ())), preferred_element_type=F32)


def dot_nt(left, right):
    return lax.dot_general(left, right, (((1,), (1,)), ((), ())), preferred_element_type=F32)


def value_of(number, group):
    if isinstance(number, int):
        return number
    return number[0] + (number[1] - number[0]) * group


def prepare_kernel(edge_block, swapped, place, volts_source, taps_source, table_source, turn_source, volts, edge, taps, one, two, turn, done, taps_ref, table_ref):
    count = edge.shape[1]
    start = pl.multiple_of(value_of(edge_block, place[0]) * count, count)
    copies = [
        pltpu.make_async_copy(taps_source, taps_ref, done.at[0]),
        pltpu.make_async_copy(table_source, table_ref, done.at[1]),
        pltpu.make_async_copy(volts_source.at[:, pl.ds(start, count)], edge, done.at[2]),
        pltpu.make_async_copy(volts_source, volts, done.at[3]),
        pltpu.make_async_copy(turn_source, turn, done.at[4]),
    ]
    for copy in copies:
        copy.start()
    copies[0].wait()
    copies[1].wait()
    for h in range(H):
        for half in range(TAPS // SUB):
            tile = taps_ref[pl.ds(half * SUB, SUB), pl.ds(h * LANES, LANES)]
            for r in range(2):
                taps[pl.ds(half * SUB * ROWS + 2 * h + r, SUB, stride=ROWS), :] = tile
    high, low = halves(table_ref[:ROWS, :ROWS])
    one[...] = jnp.concatenate([high, high, low], axis=1)
    start = pl.multiple_of(ROWS + place[0] * (2 * K2 * swapped), SUB)
    high, low = halves(table_ref[pl.ds(start, 2 * K2), :])
    two[0] = high
    two[1] = low
    for copy in copies[2:]:
        copy.wait()


def prepare(volts, fir_taps, place, groups, edge_block, edge_frames):
    signals, frames = volts.shape[:2]
    two = stage_two_table(groups)
    table = np.concatenate([stage_one_table(), two, np.roll(two, K2, axis=0)]).astype(np.float32)
    vmem = pl.BlockSpec(memory_space=pltpu.VMEM)
    return pl.pallas_call(
        functools.partial(prepare_kernel, edge_block, int(groups == 2)),
        grid_spec=pltpu.PrefetchScalarGridSpec(
            num_scalar_prefetch=1,
            grid=(),
            in_specs=[pl.BlockSpec(memory_space=pl.ANY)] * 4,
            out_specs=[vmem] * 6,
            scratch_shapes=[
                pltpu.SemaphoreType.DMA((5,)),
                pltpu.VMEM(fir_taps.shape, F32),
                pltpu.VMEM(table.shape, F32),
            ],
        ),
        out_shape=[
            jax.ShapeDtypeStruct((signals, frames, ROWS, LANES), BF16),
            jax.ShapeDtypeStruct((signals, edge_frames, ROWS, LANES), BF16),
            jax.ShapeDtypeStruct((TAPS * ROWS, LANES), F32),
            jax.ShapeDtypeStruct((ROWS, 3 * ROWS), BF16),
            jax.ShapeDtypeStruct((2, 2 * K2, 2 * LANES), BF16),
            jax.ShapeDtypeStruct((H, 2 * LANES), F32),
        ],
        compiler_params=pltpu.CompilerParams(vmem_limit_bytes=24 << 20),
    )(
        place,
        *[
            pltpu.with_memory_space_constraint(x, pltpu.HBM)
            for x in (volts, fir_taps, jnp.asarray(table), jnp.asarray(turn_table(), F32))
        ],
    )


def spectra_kernel(groups, parts, out_frames, run, place, *refs):
    part_refs, refs = refs[: len(parts)], refs[len(parts) :]
    taps, one, two, turn = refs[:4]
    outs, (ext, filtered, turned, staged) = refs[4:-4], refs[-4:]
    step, steps, members = pl.program_id(0), pl.num_programs(0), MEMBERS
    per_group = K2 // groups
    share = LANES // out_frames
    tiles = H // share
    pairs = tiles // 2
    frame_rows, row_rows = ROWS + PAD, tiles * TILE + PAD

    def load(member):
        signal = step * members + member
        for (frames, block, start, valid), ref in zip(parts, part_refs):
            first = value_of(block, place[0]) * frames
            start = value_of(start, place[0])
            valid = value_of(valid, place[0])

            def fill(ref=ref, frames=frames, first=first, start=start):
                for f in range(frames):
                    ext[member, start + f] = ref[signal, first + f].astype(F32)

            def clear(frames=frames, start=start):
                for f in range(frames):
                    ext[member, start + f] = jnp.zeros((ROWS, LANES), F32)

            if isinstance(valid, int):
                fill() if valid else clear()
            else:
                pl.when(valid == 1)(fill)
                pl.when(valid == 0)(clear)

    def filter_rows(member, q):
        rows = pl.ds(pl.multiple_of(q * SUB, SUB), SUB)
        tap = [taps[pl.ds(pl.multiple_of(m * ROWS + q * SUB, SUB), SUB), :] for m in range(TAPS)]
        for f in range(out_frames):
            total = tap[0] * ext[member, f + 1, rows]
            for m in range(1, TAPS):
                total = total + tap[m] * ext[member, f + 1 + m, rows]
            filtered[member, f, rows] = total

    def first_stage(member):
        cosine = turn[:, :LANES]
        sine = turn[:, LANES:]
        for g in range(out_frames // STEP):
            block = jnp.concatenate([filtered[member, g * STEP + f] for f in range(STEP)], axis=1)
            high, low = halves(block)
            first = dot(one[...], jnp.concatenate([high, low, high], axis=0))
            for f in range(STEP):
                real = first[:H, f * LANES : (f + 1) * LANES]
                imag = first[H:, f * LANES : (f + 1) * LANES]
                at = (g * STEP + f) * frame_rows
                turned[member, at : at + H, :] = real * cosine + imag * sine
                turned[member, at + H : at + ROWS, :] = imag * cosine - real * sine

    def second_stage(member, pair):
        rows = []
        for k1 in range(2 * pair * share, 2 * (pair + 1) * share):
            for f in range(0, out_frames, SUB):
                rows.append(
                    jnp.concatenate(
                        [turned[member, pl.ds(f * frame_rows + p * H + k1, SUB, stride=frame_rows), :] for p in range(2)],
                        axis=1,
                    )
                )
        high, low = halves(jnp.concatenate(rows, axis=0))
        spectrum = dot_nt(two[0], high) + dot_nt(two[1], high) + dot_nt(two[0], low)
        for k in range(2):
            for t in range(groups):
                for p in range(2):
                    for k2 in range(0, per_group, SUB):
                        row = (t * 2 + p) * per_group + k2
                        start = (t * per_group + k2) * row_rows + (2 * pair + k) * TILE + p * SUB
                        staged[pl.ds(start + step * members + member, SUB, stride=row_rows), :] = spectrum[
                            row : row + SUB, k * LANES : (k + 1) * LANES
                        ]

    def write():
        at = 0
        for out in outs:

            def write_row(k2, carry):
                for k in range(tiles):
                    start = pl.multiple_of((at + k2) * row_rows + k * TILE, PAD)
                    out[k2, k] = staged[pl.ds(start, TILE), :].astype(BF16)
                return carry

            lax.fori_loop(0, out.shape[0], write_row, 0, unroll=2)
            at += out.shape[0]

    def body():
        for member in range(members):
            load(member)

        def filter_one(index, carry):
            filter_rows(index // (ROWS // SUB), index % (ROWS // SUB))
            return carry

        lax.fori_loop(0, members * (ROWS // SUB), filter_one, 0)
        for member in range(members):
            first_stage(member)
        for member in range(members):
            for pair in range(pairs):
                second_stage(member, pair)

        pl.when(step == steps - 1)(write)

    if isinstance(run, int):
        body()
    else:
        pl.when(value_of(run, place[0]) == 1)(body)


def after(value, *others):
    return lax.optimization_barrier((value, *others))[0]


def spectra(parts, out_frames, fixed, place, groups, sizes, run=1, wait=(), cost=10**6):
    signals = parts[0][0].shape[0]
    place = after(place, *wait)
    tiles = H * out_frames // LANES
    shapes = [(n, tiles, TILE, LANES) for n in sizes]
    return pl.pallas_call(
        functools.partial(spectra_kernel, groups, tuple(part[1:] for part in parts), out_frames, run),
        grid_spec=pltpu.PrefetchScalarGridSpec(
            num_scalar_prefetch=1,
            grid=(signals // MEMBERS,),
            in_specs=[pl.BlockSpec(memory_space=pltpu.VMEM)] * (len(parts) + 4),
            out_specs=[pl.BlockSpec(shape, lambda s, place: (0, 0, 0, 0)) for shape in shapes],
            scratch_shapes=[
                pltpu.VMEM((MEMBERS, TAPS + out_frames, ROWS, LANES), F32),
                pltpu.VMEM((MEMBERS, out_frames, ROWS, LANES), F32),
                pltpu.VMEM((MEMBERS, out_frames * (ROWS + PAD), LANES), F32),
                pltpu.VMEM((K2 * (tiles * TILE + PAD), LANES), F32),
            ],
        ),
        out_shape=[jax.ShapeDtypeStruct(shape, BF16) for shape in shapes],
        compiler_params=pltpu.CompilerParams(vmem_limit_bytes=32 << 20),
        cost_estimate=pl.CostEstimate(flops=cost, bytes_accessed=0, transcendentals=0),
    )(place, *[part[0] for part in parts], *fixed)


def after(value, *others):
    return lax.optimization_barrier((value, *others))[0]


def correlate_kernel(pieces, per_group, scale, add, last, place, *refs):
    refs = list(refs)
    sums = refs.pop() if last else None
    out = refs.pop()
    before = refs.pop() if add else None
    if not last:
        sums = out
    half = per_group // 2
    lane = lax.broadcasted_iota(jnp.int32, (SUB, LANES), 1)
    first_tile = lane < LANES // 2
    real_lane = lane % TILE < SUB
    sign = jnp.where(real_lane, 1.0, -1.0).astype(F32)
    for number, piece in enumerate(pieces):
        tiles, piece = piece
        share = H // tiles
        where = lax.broadcasted_iota(jnp.int32, (TILE, LANES), 1) // (LANES // share)

        def pair(index, carry):
            k2 = index // tiles
            k1 = index % tiles
            own, other = [], []
            for position in range(len(piece[0])):
                rows = []
                for tile in range(2):
                    array, row, column = piece[0][position]
                    a = refs[array][row + tile * half + k2, column + k1]
                    rows += [jnp.where(where == c, a, jnp.zeros_like(a)) for c in range(share)]
                own.append(jnp.concatenate(rows, axis=0))
                rows = []
                for tile in range(2):
                    for visit in range(VISITS):
                        array, row, column = piece[visit][position]
                        rows.append(refs[array][row + tile * half + k2, column + k1])
                other.append(jnp.concatenate(rows, axis=0))
            product = dot_nt(jnp.concatenate(own, axis=1), jnp.concatenate(other, axis=1))
            for c in range(share):
                value = []
                for p in range(2):
                    at = [((tile * share + c) * 2 + p) * SUB for tile in range(2)]
                    value.append(
                        jnp.where(first_tile, product[at[0] : at[0] + SUB], product[at[1] : at[1] + SUB])
                    )
                turned = jnp.where(
                    real_lane, pltpu.roll(value[1], LANES - SUB, 1), pltpu.roll(value[1], SUB, 1)
                )
                total = value[0] * sign + turned
                channel = k2 // 4 * LANES + k2 % 4 * H + k1 * share + c
                rows = pl.ds(pl.multiple_of(channel * SUB, SUB), SUB)
                if number:
                    total = total + sums[rows, :]
                elif add:
                    total = total + before[rows, :]
                sums[rows, :] = total
            return carry

        lax.fori_loop(0, half * tiles, pair, 0, unroll=16)
    if not last:
        return

    def finish(index, carry):
        block = index // SUB
        signal = index % SUB
        value = sums[pl.ds(block * LANES * SUB + signal, LANES, stride=SUB), :]
        value = jnp.transpose(value * scale)
        at = 0
        for tile in range(2):
            for visit in range(VISITS):
                for part in range(2):
                    out[part, signal, value_of(PLACES[visit], place[1]), tile * (half // 4) + block] = value[at : at + SUB]
                    at += SUB
        return carry

    lax.fori_loop(0, half // 4 * SUB, finish, 0)


def correlate(arrays, pieces, per_group, place, scale, before, last, wait=(), cost=6 * 10**9):
    signals = TILE // 2
    rows = per_group // 2 * H * SUB
    place = after(place, *wait)
    shape = (2, signals, VISITS, per_group // 4, SUB, LANES) if last else (rows, LANES)
    operands = list(arrays) + ([] if before is None else [before])
    vmem = pl.BlockSpec(memory_space=pltpu.VMEM)
    return pl.pallas_call(
        functools.partial(correlate_kernel, pieces, per_group, scale, before is not None, last),
        grid_spec=pltpu.PrefetchScalarGridSpec(
            num_scalar_prefetch=1,
            grid=(),
            in_specs=[vmem] * len(operands),
            out_specs=vmem,
            scratch_shapes=[pltpu.VMEM((rows, LANES), F32)] if last else [],
        ),
        out_shape=jax.ShapeDtypeStruct(shape, F32),
        compiler_params=pltpu.CompilerParams(vmem_limit_bytes=24 << 20),
        input_output_aliases={} if before is None or last else {len(operands): 0},
        cost_estimate=pl.CostEstimate(flops=cost, bytes_accessed=0, transcendentals=0),
    )(place, *operands)


def stacked(voltage):
    s, f = voltage.shape[:2]
    return voltage.reshape(s, f, 2, H, LANES).transpose(0, 1, 3, 2, 4).reshape(s, f, ROWS, LANES)


def natural(out):
    parts, s, visits, i, t, lanes = out.shape
    return out.transpose(0, 1, 2, 4, 3, 5).reshape(parts, s, visits * t, i * lanes)


def shifted(block, axis, distance):
    size = lax.axis_size(axis)
    return lax.ppermute(block, axis, [(i, (i + distance) % size) for i in range(size)])


def farther(block):
    size = lax.axis_size("stn")
    rest = lax.ppermute(block, "stn", [(i, (i + 1 if i % 2 == 0 else i + 3) % size) for i in range(size)])
    return shifted(block, "stn", 2), rest


def exchanged(block):
    return lax.ppermute(block, "stn", [(i, i ^ 1) for i in range(lax.axis_size("stn"))])


def paired(volts, fir_taps, place, correlated):
    frames = volts.shape[1]
    me = lax.axis_index("tm")
    sizes = [K2 // 2, K2 // 2]
    swap = [(0, 1), (1, 0)]
    edge = TAPS // 2
    last = frames // edge
    volts, edge_frames, *fixed = prepare(volts, fir_taps, place, 2, (last - 1, 0), edge)
    visiting = lax.ppermute(edge_frames, "tm", swap)
    own_a, away_a = spectra(
        [(volts, TAPS, 0, 0, (0, 1)), (volts, TAPS, (0, 1), TAPS, 1)], TAPS, fixed, place, 2, sizes
    )
    got_a = lax.ppermute(away_a, "tm", swap)
    two_a, rest_a = farther(own_a)
    own_b, away_b = spectra(
        [(volts, TAPS, 0, 0, 1), (volts, TAPS, 1, TAPS, 1)], TAPS, fixed, place, 2, sizes, (1, 0), (own_a,)
    )
    got_b = lax.ppermute(away_b, "tm", [(0, 1)])
    pair_a = exchanged(two_a)
    own_c, away_c = spectra(
        [
            (volts, edge, (last - 2, 0), (0, edge), 1),
            (volts, edge, (last - 1, 1), (edge, 2 * edge), 1),
            (visiting, edge, 0, (2 * edge, 0), 1),
        ],
        edge, fixed, place, 2, sizes, 1, (own_b, two_a, got_a), 9 * 10**9,
    )
    got_c = lax.ppermute(away_c, "tm", swap)
    two_g, rest_g = farther(got_a)
    pair_g = exchanged(two_g)
    own_c = after(own_c, two_g, pair_a, rest_a)
    rest = jnp.concatenate([jnp.where(me == 0, own_b, got_b), own_c, got_c], axis=1)
    two_r, rest_r = farther(rest)
    many, few = own_a.shape[1], own_c.shape[1]
    sums = correlated(
        [own_a, pair_a, two_a, rest_a, got_a, pair_g, two_g, rest_g], [(many, [(0, 0, 0), (1, 0, 0)])], None, False
    )
    pair_r = exchanged(after(two_r, sums))
    return correlated(
        [rest, pair_r, two_r, rest_r], [(many, [(0, 0, 0)]), (few, [(0, 0, many), (0, 0, many + few)])], sums, True
    )


def general(volts, fir_taps, place, correlated):
    groups = lax.axis_size("tm")
    frames = volts.shape[1]
    volts, edge_frames, *fixed = prepare(volts, fir_taps, place, groups, frames // TAPS - 1, TAPS)
    history = lax.ppermute(edge_frames, "tm", [(i, i + 1) for i in range(groups - 1)])
    parts = [(history, TAPS, 0, 0, 1)] + [(volts, TAPS, i, TAPS * (i + 1), 1) for i in range(frames // TAPS)]
    spectrum = spectra(parts, frames, fixed, place, groups, [K2])[0]
    spectrum = lax.all_to_all(spectrum, "tm", split_axis=0, concat_axis=0, tiled=True)
    two, rest = farther(spectrum)
    spots = [(0, K2 // groups * t, 0) for t in range(groups)]
    return correlated([spectrum, exchanged(two), two, rest], [(spectrum.shape[1], spots)], None, True)


def local(voltage, fir_taps):
    groups = lax.axis_size("tm")
    place = jnp.stack([lax.axis_index("tm"), lax.axis_index("stn") % 2]).astype(jnp.int32)
    scale = 1.0 / (groups * voltage.shape[1])

    def correlated(arrays, pieces, before, last, wait=()):
        laid = [
            (tiles, [[(VISITS * n + visit, row, column) for n, row, column in spots] for visit in range(VISITS)])
            for tiles, spots in pieces
        ]
        return correlate(arrays, laid, K2 // groups, place, scale, before, last, wait)

    run = paired if groups == 2 else general
    return natural(run(stacked(voltage), fir_taps, place, correlated))


def solution(mesh):
    return jax.shard_map(
        local,
        mesh=mesh,
        in_specs=(P("stn", "tm", None, None), P()),
        out_specs=P(None, "stn", None, "tm"),
        check_vma=False,
    )
```

```python
import functools
import math

import jax
import jax.numpy as jnp
import numpy as np
from jax import lax
from jax.experimental import pallas as pl
from jax.experimental.pallas import tpu as pltpu
from jax.sharding import PartitionSpec as P

NCH = 4096
CHANS = 2048
TAPS = 16
VISITS = 4
H = 32
LANES = 128
ROWS = 2 * H
K2 = CHANS // H
STEP = 8
TILE = 16
PLACES = (0, (1, 3), 2, (3, 1))
MEMBERS = 4
PAD = 8
SUB = 8
BF16 = jnp.bfloat16
F32 = jnp.float32


def angles(rows, columns, modulus):
    turns = np.outer(rows, columns) % modulus
    return turns.astype(np.float64) * (2.0 * math.pi / modulus)


def stage_one_table():
    theta = angles(np.arange(H), np.arange(H), H)
    cosine, sine = np.cos(theta), np.sin(theta)
    table = np.zeros((2, H, H, 2))
    table[0, :, :, 0], table[0, :, :, 1] = cosine, sine
    table[1, :, :, 0], table[1, :, :, 1] = -sine, cosine
    return np.pad(table.reshape(ROWS, ROWS), ((0, 0), (0, 2 * LANES - ROWS)))


def turn_table():
    theta = angles(np.arange(H), np.arange(LANES), NCH)
    return np.concatenate([np.cos(theta), np.sin(theta)], axis=1)


def stage_two_table(groups):
    theta = angles(np.arange(K2), np.arange(LANES), LANES)
    cosine, sine = np.cos(theta) / math.sqrt(NCH), np.sin(theta) / math.sqrt(NCH)
    real = np.concatenate([cosine, sine], 1).reshape(groups, 1, K2 // groups, 2 * LANES)
    imag = np.concatenate([-sine, cosine], 1).reshape(groups, 1, K2 // groups, 2 * LANES)
    return np.concatenate([real, imag], 1).reshape(2 * K2, 2 * LANES)


def halves(value):
    high = value.astype(BF16)
    return high, (value - high.astype(F32)).astype(BF16)


def dot(left, right):
    return lax.dot_general(left, right, (((1,), (0,)), ((), ())), preferred_element_type=F32)


def dot_nt(left, right):
    return lax.dot_general(left, right, (((1,), (1,)), ((), ())), preferred_element_type=F32)


def value_of(number, group):
    if isinstance(number, int):
        return number
    return number[0] + (number[1] - number[0]) * group


def prepare_kernel(edge_block, swapped, place, volts_source, taps_source, table_source, turn_source, volts, edge, taps, one, two, turn, done, taps_ref, table_ref):
    count = edge.shape[1]
    start = pl.multiple_of(value_of(edge_block, place[0]) * count, count)
    copies = [
        pltpu.make_async_copy(taps_source, taps_ref, done.at[0]),
        pltpu.make_async_copy(table_source, table_ref, done.at[1]),
        pltpu.make_async_copy(volts_source.at[:, pl.ds(start, count)], edge, done.at[2]),
        pltpu.make_async_copy(volts_source, volts, done.at[3]),
        pltpu.make_async_copy(turn_source, turn, done.at[4]),
    ]
    for copy in copies:
        copy.start()
    copies[0].wait()
    copies[1].wait()
    for h in range(H):
        for half in range(TAPS // SUB):
            tile = taps_ref[pl.ds(half * SUB, SUB), pl.ds(h * LANES, LANES)]
            for r in range(2):
                taps[pl.ds(half * SUB * ROWS + 2 * h + r, SUB, stride=ROWS), :] = tile
    high, low = halves(table_ref[:ROWS, :ROWS])
    one[...] = jnp.concatenate([high, high, low], axis=1)
    start = pl.multiple_of(ROWS + place[0] * (2 * K2 * swapped), SUB)
    high, low = halves(table_ref[pl.ds(start, 2 * K2), :])
    two[0] = high
    two[1] = low
    for copy in copies[2:]:
        copy.wait()


def prepare(volts, fir_taps, place, groups, edge_block, edge_frames):
    signals, frames = volts.shape[:2]
    two = stage_two_table(groups)
    table = np.concatenate([stage_one_table(), two, np.roll(two, K2, axis=0)]).astype(np.float32)
    vmem = pl.BlockSpec(memory_space=pltpu.VMEM)
    return pl.pallas_call(
        functools.partial(prepare_kernel, edge_block, int(groups == 2)),
        grid_spec=pltpu.PrefetchScalarGridSpec(
            num_scalar_prefetch=1,
            grid=(),
            in_specs=[pl.BlockSpec(memory_space=pl.ANY)] * 4,
            out_specs=[vmem] * 6,
            scratch_shapes=[
                pltpu.SemaphoreType.DMA((5,)),
                pltpu.VMEM(fir_taps.shape, F32),
                pltpu.VMEM(table.shape, F32),
            ],
        ),
        out_shape=[
            jax.ShapeDtypeStruct((signals, frames, ROWS, LANES), BF16),
            jax.ShapeDtypeStruct((signals, edge_frames, ROWS, LANES), BF16),
            jax.ShapeDtypeStruct((TAPS * ROWS, LANES), F32),
            jax.ShapeDtypeStruct((ROWS, 3 * ROWS), BF16),
            jax.ShapeDtypeStruct((2, 2 * K2, 2 * LANES), BF16),
            jax.ShapeDtypeStruct((H, 2 * LANES), F32),
        ],
        compiler_params=pltpu.CompilerParams(vmem_limit_bytes=24 << 20),
    )(
        place,
        *[
            pltpu.with_memory_space_constraint(x, pltpu.HBM)
            for x in (volts, fir_taps, jnp.asarray(table), jnp.asarray(turn_table(), F32))
        ],
    )


def spectra_kernel(groups, parts, out_frames, run, place, *refs):
    part_refs, refs = refs[: len(parts)], refs[len(parts) :]
    taps, one, two, turn = refs[:4]
    outs, (ext, filtered, turned, staged) = refs[4:-4], refs[-4:]
    step, steps, members = pl.program_id(0), pl.num_programs(0), MEMBERS
    per_group = K2 // groups
    share = LANES // out_frames
    tiles = H // share
    pairs = tiles // 2
    frame_rows, row_rows = ROWS + PAD, tiles * TILE + PAD

    def load(member):
        signal = step * members + member
        for (frames, block, start, valid), ref in zip(parts, part_refs):
            first = value_of(block, place[0]) * frames
            start = value_of(start, place[0])
            valid = value_of(valid, place[0])

            def fill(ref=ref, frames=frames, first=first, start=start):
                for f in range(frames):
                    ext[member, start + f] = ref[signal, first + f].astype(F32)

            def clear(frames=frames, start=start):
                for f in range(frames):
                    ext[member, start + f] = jnp.zeros((ROWS, LANES), F32)

            if isinstance(valid, int):
                fill() if valid else clear()
            else:
                pl.when(valid == 1)(fill)
                pl.when(valid == 0)(clear)

    def filter_rows(member, q):
        rows = pl.ds(pl.multiple_of(q * SUB, SUB), SUB)
        tap = [taps[pl.ds(pl.multiple_of(m * ROWS + q * SUB, SUB), SUB), :] for m in range(TAPS)]
        for f in range(out_frames):
            total = tap[0] * ext[member, f + 1, rows]
            for m in range(1, TAPS):
                total = total + tap[m] * ext[member, f + 1 + m, rows]
            filtered[member, f, rows] = total

    def first_stage(member):
        cosine = turn[:, :LANES]
        sine = turn[:, LANES:]
        for g in range(out_frames // STEP):
            block = jnp.concatenate([filtered[member, g * STEP + f] for f in range(STEP)], axis=1)
            high, low = halves(block)
            first = dot(one[...], jnp.concatenate([high, low, high], axis=0))
            for f in range(STEP):
                real = first[:H, f * LANES : (f + 1) * LANES]
                imag = first[H:, f * LANES : (f + 1) * LANES]
                at = (g * STEP + f) * frame_rows
                turned[member, at : at + H, :] = real * cosine + imag * sine
                turned[member, at + H : at + ROWS, :] = imag * cosine - real * sine

    def second_stage(member, pair):
        rows = []
        for k1 in range(2 * pair * share, 2 * (pair + 1) * share):
            for f in range(0, out_frames, SUB):
                rows.append(
                    jnp.concatenate(
                        [turned[member, pl.ds(f * frame_rows + p * H + k1, SUB, stride=frame_rows), :] for p in range(2)],
                        axis=1,
                    )
                )
        high, low = halves(jnp.concatenate(rows, axis=0))
        spectrum = dot_nt(two[0], high) + dot_nt(two[1], high) + dot_nt(two[0], low)
        for k in range(2):
            for t in range(groups):
                for p in range(2):
                    for k2 in range(0, per_group, SUB):
                        row = (t * 2 + p) * per_group + k2
                        start = (t * per_group + k2) * row_rows + (2 * pair + k) * TILE + p * SUB
                        staged[pl.ds(start + step * members + member, SUB, stride=row_rows), :] = spectrum[
                            row : row + SUB, k * LANES : (k + 1) * LANES
                        ]

    def write():
        at = 0
        for out in outs:

            def write_row(k2, carry):
                for k in range(tiles):
                    start = pl.multiple_of((at + k2) * row_rows + k * TILE, PAD)
                    out[k2, k] = staged[pl.ds(start, TILE), :].astype(BF16)
                return carry

            lax.fori_loop(0, out.shape[0], write_row, 0, unroll=2)
            at += out.shape[0]

    def body():
        for member in range(members):
            load(member)

        def filter_one(index, carry):
            filter_rows(index // (ROWS // SUB), index % (ROWS // SUB))
            return carry

        lax.fori_loop(0, members * (ROWS // SUB), filter_one, 0)
        for member in range(members):
            first_stage(member)
        for member in range(members):
            for pair in range(pairs):
                second_stage(member, pair)

        pl.when(step == steps - 1)(write)

    if isinstance(run, int):
        body()
    else:
        pl.when(value_of(run, place[0]) == 1)(body)


def after(value, *others):
    return lax.optimization_barrier((value, *others))[0]


def spectra(parts, out_frames, fixed, place, groups, sizes, run=1, wait=(), cost=10**6):
    signals = parts[0][0].shape[0]
    place = after(place, *wait)
    tiles = H * out_frames // LANES
    shapes = [(n, tiles, TILE, LANES) for n in sizes]
    return pl.pallas_call(
        functools.partial(spectra_kernel, groups, tuple(part[1:] for part in parts), out_frames, run),
        grid_spec=pltpu.PrefetchScalarGridSpec(
            num_scalar_prefetch=1,
            grid=(signals // MEMBERS,),
            in_specs=[pl.BlockSpec(memory_space=pltpu.VMEM)] * (len(parts) + 4),
            out_specs=[pl.BlockSpec(shape, lambda s, place: (0, 0, 0, 0)) for shape in shapes],
            scratch_shapes=[
                pltpu.VMEM((MEMBERS, TAPS + out_frames, ROWS, LANES), F32),
                pltpu.VMEM((MEMBERS, out_frames, ROWS, LANES), F32),
                pltpu.VMEM((MEMBERS, out_frames * (ROWS + PAD), LANES), F32),
                pltpu.VMEM((K2 * (tiles * TILE + PAD), LANES), F32),
            ],
        ),
        out_shape=[jax.ShapeDtypeStruct(shape, BF16) for shape in shapes],
        compiler_params=pltpu.CompilerParams(vmem_limit_bytes=32 << 20),
        cost_estimate=pl.CostEstimate(flops=cost, bytes_accessed=0, transcendentals=0),
    )(place, *[part[0] for part in parts], *fixed)


def after(value, *others):
    return lax.optimization_barrier((value, *others))[0]


def correlate_kernel(pieces, per_group, scale, add, last, place, *refs):
    refs = list(refs)
    sums = refs.pop() if last else None
    out = refs.pop()
    before = refs.pop() if add else None
    if not last:
        sums = out
    half = per_group // 2
    lane = lax.broadcasted_iota(jnp.int32, (SUB, LANES), 1)
    first_tile = lane < LANES // 2
    real_lane = lane % TILE < SUB
    sign = jnp.where(real_lane, 1.0, -1.0).astype(F32)
    for number, piece in enumerate(pieces):
        tiles, piece = piece
        share = H // tiles
        where = lax.broadcasted_iota(jnp.int32, (TILE, LANES), 1) // (LANES // share)

        def pair(index, carry):
            k2 = index // tiles
            k1 = index % tiles
            own, other = [], []
            for position in range(len(piece[0])):
                rows = []
                for tile in range(2):
                    array, row, column = piece[0][position]
                    a = refs[array][row + tile * half + k2, column + k1]
                    rows += [jnp.where(where == c, a, jnp.zeros_like(a)) for c in range(share)]
                own.append(jnp.concatenate(rows, axis=0))
                rows = []
                for tile in range(2):
                    for visit in range(VISITS):
                        array, row, column = piece[visit][position]
                        rows.append(refs[array][row + tile * half + k2, column + k1])
                other.append(jnp.concatenate(rows, axis=0))
            product = dot_nt(jnp.concatenate(own, axis=1), jnp.concatenate(other, axis=1))
            for c in range(share):
                value = []
                for p in range(2):
                    at = [((tile * share + c) * 2 + p) * SUB for tile in range(2)]
                    value.append(
                        jnp.where(first_tile, product[at[0] : at[0] + SUB], product[at[1] : at[1] + SUB])
                    )
                turned = jnp.where(
                    real_lane, pltpu.roll(value[1], LANES - SUB, 1), pltpu.roll(value[1], SUB, 1)
                )
                total = value[0] * sign + turned
                channel = k2 // 4 * LANES + k2 % 4 * H + k1 * share + c
                rows = pl.ds(pl.multiple_of(channel * SUB, SUB), SUB)
                if number:
                    total = total + sums[rows, :]
                elif add:
                    total = total + before[rows, :]
                sums[rows, :] = total
            return carry

        lax.fori_loop(0, half * tiles, pair, 0, unroll=16)
    if not last:
        return

    def finish(index, carry):
        block = index // SUB
        signal = index % SUB
        value = sums[pl.ds(block * LANES * SUB + signal, LANES, stride=SUB), :]
        value = jnp.transpose(value * scale)
        at = 0
        for tile in range(2):
            for visit in range(VISITS):
                for part in range(2):
                    out[part, signal, value_of(PLACES[visit], place[1]), tile * (half // 4) + block] = value[at : at + SUB]
                    at += SUB
        return carry

    lax.fori_loop(0, half // 4 * SUB, finish, 0)


def correlate(arrays, pieces, per_group, place, scale, before, last, wait=(), cost=10**3):
    signals = TILE // 2
    rows = per_group // 2 * H * SUB
    place = after(place, *wait)
    shape = (2, signals, VISITS, per_group // 4, SUB, LANES) if last else (rows, LANES)
    operands = list(arrays) + ([] if before is None else [before])
    vmem = pl.BlockSpec(memory_space=pltpu.VMEM)
    return pl.pallas_call(
        functools.partial(correlate_kernel, pieces, per_group, scale, before is not None, last),
        grid_spec=pltpu.PrefetchScalarGridSpec(
            num_scalar_prefetch=1,
            grid=(),
            in_specs=[vmem] * len(operands),
            out_specs=vmem,
            scratch_shapes=[pltpu.VMEM((rows, LANES), F32)] if last else [],
        ),
        out_shape=jax.ShapeDtypeStruct(shape, F32),
        compiler_params=pltpu.CompilerParams(vmem_limit_bytes=24 << 20),
        input_output_aliases={} if before is None or last else {len(operands): 0},
        cost_estimate=pl.CostEstimate(flops=cost, bytes_accessed=0, transcendentals=0),
    )(place, *operands)


def stacked(voltage):
    s, f = voltage.shape[:2]
    return voltage.reshape(s, f, 2, H, LANES).transpose(0, 1, 3, 2, 4).reshape(s, f, ROWS, LANES)


def natural(out):
    parts, s, visits, i, t, lanes = out.shape
    return out.transpose(0, 1, 2, 4, 3, 5).reshape(parts, s, visits * t, i * lanes)


def shifted(block, axis, distance):
    size = lax.axis_size(axis)
    return lax.ppermute(block, axis, [(i, (i + distance) % size) for i in range(size)])


def farther(block):
    size = lax.axis_size("stn")
    rest = lax.ppermute(block, "stn", [(i, (i + 1 if i % 2 == 0 else i + 3) % size) for i in range(size)])
    return shifted(block, "stn", 2), rest


def exchanged(block):
    return lax.ppermute(block, "stn", [(i, i ^ 1) for i in range(lax.axis_size("stn"))])


def paired(volts, fir_taps, place, correlated):
    frames = volts.shape[1]
    me = lax.axis_index("tm")
    sizes = [K2 // 2, K2 // 2]
    swap = [(0, 1), (1, 0)]
    edge = TAPS // 2
    last = frames // edge
    many, few = TAPS * H // LANES, edge * H // LANES
    volts, edge_frames, *fixed = prepare(volts, fir_taps, place, 2, (last - 1, 0), edge)
    own_a, away_a = spectra(
        [(volts, TAPS, 0, 0, (0, 1)), (volts, TAPS, (0, 1), TAPS, 1)], TAPS, fixed, place, 2, sizes
    )
    got_a = lax.ppermute(away_a, "tm", swap)
    two_a, rest_a = farther(own_a)
    own_b, away_b = spectra(
        [(volts, TAPS, 0, 0, 1), (volts, TAPS, 1, TAPS, 1)], TAPS, fixed, place, 2, sizes, (1, 0), (own_a,)
    )
    got_a, own_b, away_b, edge_frames, two_a = lax.optimization_barrier((got_a, own_b, away_b, edge_frames, two_a))
    two_g, rest_g = farther(got_a)
    got_b = lax.ppermute(away_b, "tm", [(0, 1)])
    visiting = lax.ppermute(edge_frames, "tm", swap)
    pair_a = exchanged(two_a)
    first = [(many, [(0, 0, 0)])]
    sums = correlated([own_a, pair_a, two_a, rest_a], first, None, False)
    two_g, rest_g, got_b, sums = lax.optimization_barrier((two_g, rest_g, got_b, sums))
    piece_b = jnp.where(me == 0, own_b, got_b)
    two_b, rest_b = farther(piece_b)
    pair_g = exchanged(two_g)
    own_c, away_c = spectra(
        [
            (volts, edge, (last - 2, 0), (0, edge), 1),
            (volts, edge, (last - 1, 1), (edge, 2 * edge), 1),
            (visiting, edge, 0, (2 * edge, 0), 1),
        ],
        edge, fixed, place, 2, sizes, 1, (piece_b, pair_g), 9 * 10**9,
    )
    got_c = lax.ppermute(away_c, "tm", swap)
    piece_c = jnp.concatenate([own_c, got_c], axis=1)
    two_c, rest_c = farther(piece_c)
    sums = correlated([got_a, pair_g, two_g, rest_g], first, sums, False, (piece_c, two_b), 6 * 10**9)
    pair_b = exchanged(two_b)
    sums = correlated([piece_b, pair_b, two_b, rest_b], first, sums, False)
    pair_c = exchanged(after(two_c, sums))
    return correlated([piece_c, pair_c, two_c, rest_c], [(few, [(0, 0, 0), (0, 0, few)])], sums, True)


def general(volts, fir_taps, place, correlated):
    groups = lax.axis_size("tm")
    frames = volts.shape[1]
    volts, edge_frames, *fixed = prepare(volts, fir_taps, place, groups, frames // TAPS - 1, TAPS)
    history = lax.ppermute(edge_frames, "tm", [(i, i + 1) for i in range(groups - 1)])
    parts = [(history, TAPS, 0, 0, 1)] + [(volts, TAPS, i, TAPS * (i + 1), 1) for i in range(frames // TAPS)]
    spectrum = spectra(parts, frames, fixed, place, groups, [K2])[0]
    spectrum = lax.all_to_all(spectrum, "tm", split_axis=0, concat_axis=0, tiled=True)
    two, rest = farther(spectrum)
    spots = [(0, K2 // groups * t, 0) for t in range(groups)]
    return correlated([spectrum, exchanged(two), two, rest], [(spectrum.shape[1], spots)], None, True)


def local(voltage, fir_taps):
    groups = lax.axis_size("tm")
    place = jnp.stack([lax.axis_index("tm"), lax.axis_index("stn") % 2]).astype(jnp.int32)
    scale = 1.0 / (groups * voltage.shape[1])

    def correlated(arrays, pieces, before, last, wait=(), cost=10**3):
        laid = [
            (tiles, [[(VISITS * n + visit, row, column) for n, row, column in spots] for visit in range(VISITS)])
            for tiles, spots in pieces
        ]
        return correlate(arrays, laid, K2 // groups, place, scale, before, last, wait, cost)

    run = paired if groups == 2 else general
    return natural(run(stacked(voltage), fir_taps, place, correlated))


def solution(mesh):
    return jax.shard_map(
        local,
        mesh=mesh,
        in_specs=(P("stn", "tm", None, None), P()),
        out_specs=P(None, "stn", None, "tm"),
        check_vma=False,
    )
```

```python
import functools
import math

import jax
import jax.numpy as jnp
import numpy as np
from jax import lax
from jax.experimental import pallas as pl
from jax.experimental.pallas import tpu as pltpu
from jax.sharding import PartitionSpec as P

NCH = 4096
CHANS = 2048
TAPS = 16
VISITS = 4
H = 32
LANES = 128
ROWS = 2 * H
K2 = CHANS // H
STEP = 8
TILE = 16
PLACES = (0, (1, 3), 2, (3, 1))
MEMBERS = 4
PAD = 8
SUB = 8
BF16 = jnp.bfloat16
F32 = jnp.float32


def angles(rows, columns, modulus):
    turns = np.outer(rows, columns) % modulus
    return turns.astype(np.float64) * (2.0 * math.pi / modulus)


def stage_one_table():
    theta = angles(np.arange(H), np.arange(H), H)
    cosine, sine = np.cos(theta), np.sin(theta)
    table = np.zeros((2, H, H, 2))
    table[0, :, :, 0], table[0, :, :, 1] = cosine, sine
    table[1, :, :, 0], table[1, :, :, 1] = -sine, cosine
    return np.pad(table.reshape(ROWS, ROWS), ((0, 0), (0, 2 * LANES - ROWS)))


def turn_table():
    theta = angles(np.arange(H), np.arange(LANES), NCH)
    return np.concatenate([np.cos(theta), np.sin(theta)], axis=1)


def stage_two_table(groups):
    theta = angles(np.arange(K2), np.arange(LANES), LANES)
    cosine, sine = np.cos(theta) / math.sqrt(NCH), np.sin(theta) / math.sqrt(NCH)
    real = np.concatenate([cosine, sine], 1).reshape(groups, 1, K2 // groups, 2 * LANES)
    imag = np.concatenate([-sine, cosine], 1).reshape(groups, 1, K2 // groups, 2 * LANES)
    return np.concatenate([real, imag], 1).reshape(2 * K2, 2 * LANES)


def halves(value):
    high = value.astype(BF16)
    return high, (value - high.astype(F32)).astype(BF16)


def dot(left, right):
    return lax.dot_general(left, right, (((1,), (0,)), ((), ())), preferred_element_type=F32)


def dot_nt(left, right):
    return lax.dot_general(left, right, (((1,), (1,)), ((), ())), preferred_element_type=F32)


def value_of(number, group):
    if isinstance(number, int):
        return number
    return number[0] + (number[1] - number[0]) * group


def prepare_kernel(edge_block, swapped, place, volts_source, taps_source, table_source, turn_source, volts, edge, taps, one, two, turn, done, taps_ref, table_ref):
    count = edge.shape[1]
    start = pl.multiple_of(value_of(edge_block, place[0]) * count, count)
    copies = [
        pltpu.make_async_copy(taps_source, taps_ref, done.at[0]),
        pltpu.make_async_copy(table_source, table_ref, done.at[1]),
        pltpu.make_async_copy(volts_source.at[:, pl.ds(start, count)], edge, done.at[2]),
        pltpu.make_async_copy(volts_source, volts, done.at[3]),
        pltpu.make_async_copy(turn_source, turn, done.at[4]),
    ]
    for copy in copies:
        copy.start()
    copies[0].wait()
    copies[1].wait()
    for h in range(H):
        for half in range(TAPS // SUB):
            tile = taps_ref[pl.ds(half * SUB, SUB), pl.ds(h * LANES, LANES)]
            for r in range(2):
                taps[pl.ds(half * SUB * ROWS + 2 * h + r, SUB, stride=ROWS), :] = tile
    high, low = halves(table_ref[:ROWS, :ROWS])
    one[...] = jnp.concatenate([high, high, low], axis=1)
    start = pl.multiple_of(ROWS + place[0] * (2 * K2 * swapped), SUB)
    high, low = halves(table_ref[pl.ds(start, 2 * K2), :])
    two[0] = high
    two[1] = low
    for copy in copies[2:]:
        copy.wait()


def prepare(volts, fir_taps, place, groups, edge_block, edge_frames):
    signals, frames = volts.shape[:2]
    two = stage_two_table(groups)
    table = np.concatenate([stage_one_table(), two, np.roll(two, K2, axis=0)]).astype(np.float32)
    vmem = pl.BlockSpec(memory_space=pltpu.VMEM)
    return pl.pallas_call(
        functools.partial(prepare_kernel, edge_block, int(groups == 2)),
        grid_spec=pltpu.PrefetchScalarGridSpec(
            num_scalar_prefetch=1,
            grid=(),
            in_specs=[pl.BlockSpec(memory_space=pl.ANY)] * 4,
            out_specs=[vmem] * 6,
            scratch_shapes=[
                pltpu.SemaphoreType.DMA((5,)),
                pltpu.VMEM(fir_taps.shape, F32),
                pltpu.VMEM(table.shape, F32),
            ],
        ),
        out_shape=[
            jax.ShapeDtypeStruct((signals, frames, ROWS, LANES), BF16),
            jax.ShapeDtypeStruct((signals, edge_frames, ROWS, LANES), BF16),
            jax.ShapeDtypeStruct((TAPS * ROWS, LANES), F32),
            jax.ShapeDtypeStruct((ROWS, 3 * ROWS), BF16),
            jax.ShapeDtypeStruct((2, 2 * K2, 2 * LANES), BF16),
            jax.ShapeDtypeStruct((H, 2 * LANES), F32),
        ],
        compiler_params=pltpu.CompilerParams(vmem_limit_bytes=24 << 20),
    )(
        place,
        *[
            pltpu.with_memory_space_constraint(x, pltpu.HBM)
            for x in (volts, fir_taps, jnp.asarray(table), jnp.asarray(turn_table(), F32))
        ],
    )


def spectra_kernel(groups, parts, out_frames, run, place, *refs):
    part_refs, refs = refs[: len(parts)], refs[len(parts) :]
    taps, one, two, turn = refs[:4]
    outs, (ext, filtered, turned, staged) = refs[4:-4], refs[-4:]
    step, steps, members = pl.program_id(0), pl.num_programs(0), MEMBERS
    per_group = K2 // groups
    share = LANES // out_frames
    tiles = H // share
    pairs = tiles // 2
    frame_rows, row_rows = ROWS + PAD, tiles * TILE + PAD

    def load(member):
        signal = step * members + member
        for (frames, block, start, valid), ref in zip(parts, part_refs):
            first = value_of(block, place[0]) * frames
            start = value_of(start, place[0])
            valid = value_of(valid, place[0])

            def fill(ref=ref, frames=frames, first=first, start=start):
                for f in range(frames):
                    ext[member, start + f] = ref[signal, first + f].astype(F32)

            def clear(frames=frames, start=start):
                for f in range(frames):
                    ext[member, start + f] = jnp.zeros((ROWS, LANES), F32)

            if isinstance(valid, int):
                fill() if valid else clear()
            else:
                pl.when(valid == 1)(fill)
                pl.when(valid == 0)(clear)

    def filter_rows(member, q):
        rows = pl.ds(pl.multiple_of(q * SUB, SUB), SUB)
        tap = [taps[pl.ds(pl.multiple_of(m * ROWS + q * SUB, SUB), SUB), :] for m in range(TAPS)]
        for f in range(out_frames):
            total = tap[0] * ext[member, f + 1, rows]
            for m in range(1, TAPS):
                total = total + tap[m] * ext[member, f + 1 + m, rows]
            filtered[member, f, rows] = total

    def first_stage(member):
        cosine = turn[:, :LANES]
        sine = turn[:, LANES:]
        for g in range(out_frames // STEP):
            block = jnp.concatenate([filtered[member, g * STEP + f] for f in range(STEP)], axis=1)
            high, low = halves(block)
            first = dot(one[...], jnp.concatenate([high, low, high], axis=0))
            for f in range(STEP):
                real = first[:H, f * LANES : (f + 1) * LANES]
                imag = first[H:, f * LANES : (f + 1) * LANES]
                at = (g * STEP + f) * frame_rows
                turned[member, at : at + H, :] = real * cosine + imag * sine
                turned[member, at + H : at + ROWS, :] = imag * cosine - real * sine

    def second_stage(member, pair):
        rows = []
        for k1 in range(2 * pair * share, 2 * (pair + 1) * share):
            for f in range(0, out_frames, SUB):
                rows.append(
                    jnp.concatenate(
                        [turned[member, pl.ds(f * frame_rows + p * H + k1, SUB, stride=frame_rows), :] for p in range(2)],
                        axis=1,
                    )
                )
        high, low = halves(jnp.concatenate(rows, axis=0))
        spectrum = dot_nt(two[0], high) + dot_nt(two[1], high) + dot_nt(two[0], low)
        for k in range(2):
            for t in range(groups):
                for p in range(2):
                    for k2 in range(0, per_group, SUB):
                        row = (t * 2 + p) * per_group + k2
                        start = (t * per_group + k2) * row_rows + (2 * pair + k) * TILE + p * SUB
                        staged[pl.ds(start + step * members + member, SUB, stride=row_rows), :] = spectrum[
                            row : row + SUB, k * LANES : (k + 1) * LANES
                        ]

    def write():
        at = 0
        for out in outs:

            def write_row(k2, carry):
                for k in range(tiles):
                    start = pl.multiple_of((at + k2) * row_rows + k * TILE, PAD)
                    out[k2, k] = staged[pl.ds(start, TILE), :].astype(BF16)
                return carry

            lax.fori_loop(0, out.shape[0], write_row, 0, unroll=2)
            at += out.shape[0]

    def body():
        for member in range(members):
            load(member)

        def filter_one(index, carry):
            filter_rows(index // (ROWS // SUB), index % (ROWS // SUB))
            return carry

        lax.fori_loop(0, members * (ROWS // SUB), filter_one, 0)
        for member in range(members):
            first_stage(member)
        for member in range(members):
            for pair in range(pairs):
                second_stage(member, pair)

        pl.when(step == steps - 1)(write)

    if isinstance(run, int):
        body()
    else:
        pl.when(value_of(run, place[0]) == 1)(body)


def after(value, *others):
    return lax.optimization_barrier((value, *others))[0]


def spectra(parts, out_frames, fixed, place, groups, sizes, run=1, wait=(), cost=10**6):
    signals = parts[0][0].shape[0]
    place = after(place, *wait)
    tiles = H * out_frames // LANES
    shapes = [(n, tiles, TILE, LANES) for n in sizes]
    return pl.pallas_call(
        functools.partial(spectra_kernel, groups, tuple(part[1:] for part in parts), out_frames, run),
        grid_spec=pltpu.PrefetchScalarGridSpec(
            num_scalar_prefetch=1,
            grid=(signals // MEMBERS,),
            in_specs=[pl.BlockSpec(memory_space=pltpu.VMEM)] * (len(parts) + 4),
            out_specs=[pl.BlockSpec(shape, lambda s, place: (0, 0, 0, 0)) for shape in shapes],
            scratch_shapes=[
                pltpu.VMEM((MEMBERS, TAPS + out_frames, ROWS, LANES), F32),
                pltpu.VMEM((MEMBERS, out_frames, ROWS, LANES), F32),
                pltpu.VMEM((MEMBERS, out_frames * (ROWS + PAD), LANES), F32),
                pltpu.VMEM((K2 * (tiles * TILE + PAD), LANES), F32),
            ],
        ),
        out_shape=[jax.ShapeDtypeStruct(shape, BF16) for shape in shapes],
        compiler_params=pltpu.CompilerParams(vmem_limit_bytes=32 << 20),
        cost_estimate=pl.CostEstimate(flops=cost, bytes_accessed=0, transcendentals=0),
    )(place, *[part[0] for part in parts], *fixed)


def after(value, *others):
    return lax.optimization_barrier((value, *others))[0]


def correlate_kernel(pieces, per_group, scale, add, last, place, *refs):
    refs = list(refs)
    sums = refs.pop() if last else None
    out = refs.pop()
    before = refs.pop() if add else None
    if not last:
        sums = out
    half = per_group // 2
    lane = lax.broadcasted_iota(jnp.int32, (SUB, LANES), 1)
    first_tile = lane < LANES // 2
    real_lane = lane % TILE < SUB
    sign = jnp.where(real_lane, 1.0, -1.0).astype(F32)
    for number, piece in enumerate(pieces):
        tiles, piece = piece
        share = H // tiles
        where = lax.broadcasted_iota(jnp.int32, (TILE, LANES), 1) // (LANES // share)

        def pair(index, carry):
            k2 = index // tiles
            k1 = index % tiles
            own, other = [], []
            for position in range(len(piece[0])):
                rows = []
                for tile in range(2):
                    array, row, column = piece[0][position]
                    a = refs[array][row + tile * half + k2, column + k1]
                    rows += [jnp.where(where == c, a, jnp.zeros_like(a)) for c in range(share)]
                own.append(jnp.concatenate(rows, axis=0))
                rows = []
                for tile in range(2):
                    for visit in range(VISITS):
                        array, row, column = piece[visit][position]
                        rows.append(refs[array][row + tile * half + k2, column + k1])
                other.append(jnp.concatenate(rows, axis=0))
            product = dot_nt(jnp.concatenate(own, axis=1), jnp.concatenate(other, axis=1))
            for c in range(share):
                value = []
                for p in range(2):
                    at = [((tile * share + c) * 2 + p) * SUB for tile in range(2)]
                    value.append(
                        jnp.where(first_tile, product[at[0] : at[0] + SUB], product[at[1] : at[1] + SUB])
                    )
                turned = jnp.where(
                    real_lane, pltpu.roll(value[1], LANES - SUB, 1), pltpu.roll(value[1], SUB, 1)
                )
                total = value[0] * sign + turned
                channel = k2 // 4 * LANES + k2 % 4 * H + k1 * share + c
                rows = pl.ds(pl.multiple_of(channel * SUB, SUB), SUB)
                if number:
                    total = total + sums[rows, :]
                elif add:
                    total = total + before[rows, :]
                sums[rows, :] = total
            return carry

        lax.fori_loop(0, half * tiles, pair, 0, unroll=16)
    if not last:
        return

    def finish(index, carry):
        block = index // SUB
        signal = index % SUB
        value = sums[pl.ds(block * LANES * SUB + signal, LANES, stride=SUB), :]
        value = jnp.transpose(value * scale)
        at = 0
        for tile in range(2):
            for visit in range(VISITS):
                for part in range(2):
                    out[part, signal, value_of(PLACES[visit], place[1]), tile * (half // 4) + block] = value[at : at + SUB]
                    at += SUB
        return carry

    lax.fori_loop(0, half // 4 * SUB, finish, 0)


def correlate(arrays, pieces, per_group, place, scale, before, last, wait=(), cost=10**3):
    signals = TILE // 2
    rows = per_group // 2 * H * SUB
    place = after(place, *wait)
    shape = (2, signals, VISITS, per_group // 4, SUB, LANES) if last else (rows, LANES)
    operands = list(arrays) + ([] if before is None else [before])
    vmem = pl.BlockSpec(memory_space=pltpu.VMEM)
    return pl.pallas_call(
        functools.partial(correlate_kernel, pieces, per_group, scale, before is not None, last),
        grid_spec=pltpu.PrefetchScalarGridSpec(
            num_scalar_prefetch=1,
            grid=(),
            in_specs=[vmem] * len(operands),
            out_specs=vmem,
            scratch_shapes=[pltpu.VMEM((rows, LANES), F32)] if last else [],
        ),
        out_shape=jax.ShapeDtypeStruct(shape, F32),
        compiler_params=pltpu.CompilerParams(vmem_limit_bytes=24 << 20),
        input_output_aliases={} if before is None or last else {len(operands): 0},
        cost_estimate=pl.CostEstimate(flops=cost, bytes_accessed=0, transcendentals=0),
    )(place, *operands)


def stacked(voltage):
    s, f = voltage.shape[:2]
    return voltage.reshape(s, f, 2, H, LANES).transpose(0, 1, 3, 2, 4).reshape(s, f, ROWS, LANES)


def natural(out):
    parts, s, visits, i, t, lanes = out.shape
    return out.transpose(0, 1, 2, 4, 3, 5).reshape(parts, s, visits * t, i * lanes)


def shifted(block, axis, distance):
    size = lax.axis_size(axis)
    return lax.ppermute(block, axis, [(i, (i + distance) % size) for i in range(size)])


def farther(block):
    size = lax.axis_size("stn")
    rest = lax.ppermute(block, "stn", [(i, (i + 1 if i % 2 == 0 else i + 3) % size) for i in range(size)])
    return shifted(block, "stn", 2), rest


def exchanged(block):
    return lax.ppermute(block, "stn", [(i, i ^ 1) for i in range(lax.axis_size("stn"))])


def paired(volts, fir_taps, place, correlated):
    frames = volts.shape[1]
    me = lax.axis_index("tm")
    sizes = [K2 // 2, K2 // 2]
    swap = [(0, 1), (1, 0)]
    edge = TAPS // 2
    last = frames // edge
    many, few = TAPS * H // LANES, edge * H // LANES
    volts, edge_frames, *fixed = prepare(volts, fir_taps, place, 2, (last - 1, 0), edge)
    visiting = lax.ppermute(edge_frames, "tm", swap)
    own_a, away_a = spectra(
        [(volts, TAPS, 0, 0, (0, 1)), (volts, TAPS, (0, 1), TAPS, 1)], TAPS, fixed, place, 2, sizes
    )
    got_a = lax.ppermute(away_a, "tm", swap)
    two_a, rest_a = farther(own_a)
    own_b, away_b = spectra(
        [(volts, TAPS, 0, 0, 1), (volts, TAPS, 1, TAPS, 1)], TAPS, fixed, place, 2, sizes, (1, 0), (own_a,)
    )
    own_c, away_c = spectra(
        [
            (volts, edge, (last - 2, 0), (0, edge), 1),
            (volts, edge, (last - 1, 1), (edge, 2 * edge), 1),
            (visiting, edge, 0, (2 * edge, 0), 1),
        ],
        edge, fixed, place, 2, sizes, 1, (own_b, two_a),
    )
    got_a, own_c, away_b, away_c, two_a = lax.optimization_barrier((got_a, own_c, away_b, away_c, two_a))
    two_g, rest_g = farther(got_a)
    got_b = lax.ppermute(away_b, "tm", [(0, 1)])
    got_c = lax.ppermute(away_c, "tm", swap)
    pair_a = exchanged(two_a)
    first = [(many, [(0, 0, 0)])]
    sums = correlated([own_a, pair_a, two_a, rest_a], first, None, False)
    got_b, got_c, sums = lax.optimization_barrier((got_b, got_c, sums))
    piece_b = jnp.where(me == 0, own_b, got_b)
    two_b, rest_b = farther(piece_b)
    piece_c = jnp.concatenate([own_c, got_c], axis=1)
    two_c, rest_c = farther(piece_c)
    pair_g = exchanged(after(two_g, piece_b))
    sums = correlated([got_a, pair_g, two_g, rest_g], first, sums, False, (piece_c,), 6 * 10**9)
    pair_b = exchanged(two_b)
    sums = correlated([piece_b, pair_b, two_b, rest_b], first, sums, False)
    pair_c = exchanged(after(two_c, sums))
    return correlated([piece_c, pair_c, two_c, rest_c], [(few, [(0, 0, 0), (0, 0, few)])], sums, True)


def general(volts, fir_taps, place, correlated):
    groups = lax.axis_size("tm")
    frames = volts.shape[1]
    volts, edge_frames, *fixed = prepare(volts, fir_taps, place, groups, frames // TAPS - 1, TAPS)
    history = lax.ppermute(edge_frames, "tm", [(i, i + 1) for i in range(groups - 1)])
    parts = [(history, TAPS, 0, 0, 1)] + [(volts, TAPS, i, TAPS * (i + 1), 1) for i in range(frames // TAPS)]
    spectrum = spectra(parts, frames, fixed, place, groups, [K2])[0]
    spectrum = lax.all_to_all(spectrum, "tm", split_axis=0, concat_axis=0, tiled=True)
    two, rest = farther(spectrum)
    spots = [(0, K2 // groups * t, 0) for t in range(groups)]
    return correlated([spectrum, exchanged(two), two, rest], [(spectrum.shape[1], spots)], None, True)


def local(voltage, fir_taps):
    groups = lax.axis_size("tm")
    place = jnp.stack([lax.axis_index("tm"), lax.axis_index("stn") % 2]).astype(jnp.int32)
    scale = 1.0 / (groups * voltage.shape[1])

    def correlated(arrays, pieces, before, last, wait=(), cost=10**3):
        laid = [
            (tiles, [[(VISITS * n + visit, row, column) for n, row, column in spots] for visit in range(VISITS)])
            for tiles, spots in pieces
        ]
        return correlate(arrays, laid, K2 // groups, place, scale, before, last, wait, cost)

    run = paired if groups == 2 else general
    return natural(run(stacked(voltage), fir_taps, place, correlated))


def solution(mesh):
    return jax.shard_map(
        local,
        mesh=mesh,
        in_specs=(P("stn", "tm", None, None), P()),
        out_specs=P(None, "stn", None, "tm"),
        check_vma=False,
    )
```

```python
import functools
import math

import jax
import jax.numpy as jnp
import numpy as np
from jax import lax
from jax.experimental import pallas as pl
from jax.experimental.pallas import tpu as pltpu
from jax.sharding import PartitionSpec as P

NCH = 4096
CHANS = 2048
TAPS = 16
VISITS = 4
H = 32
LANES = 128
ROWS = 2 * H
K2 = CHANS // H
STEP = 8
TILE = 16
PLACES = (0, (1, 3), 2, (3, 1))
MEMBERS = 4
PAD = 8
SUB = 8
BF16 = jnp.bfloat16
F32 = jnp.float32


def angles(rows, columns, modulus):
    turns = np.outer(rows, columns) % modulus
    return turns.astype(np.float64) * (2.0 * math.pi / modulus)


def stage_one_table():
    theta = angles(np.arange(H), np.arange(H), H)
    cosine, sine = np.cos(theta), np.sin(theta)
    table = np.zeros((2, H, H, 2))
    table[0, :, :, 0], table[0, :, :, 1] = cosine, sine
    table[1, :, :, 0], table[1, :, :, 1] = -sine, cosine
    return np.pad(table.reshape(ROWS, ROWS), ((0, 0), (0, 2 * LANES - ROWS)))


def turn_table():
    theta = angles(np.arange(H), np.arange(LANES), NCH)
    return np.concatenate([np.cos(theta), np.sin(theta)], axis=1)


def stage_two_table(groups):
    theta = angles(np.arange(K2), np.arange(LANES), LANES)
    cosine, sine = np.cos(theta) / math.sqrt(NCH), np.sin(theta) / math.sqrt(NCH)
    real = np.concatenate([cosine, sine], 1).reshape(groups, 1, K2 // groups, 2 * LANES)
    imag = np.concatenate([-sine, cosine], 1).reshape(groups, 1, K2 // groups, 2 * LANES)
    return np.concatenate([real, imag], 1).reshape(2 * K2, 2 * LANES)


def halves(value):
    high = value.astype(BF16)
    return high, (value - high.astype(F32)).astype(BF16)


def dot(left, right):
    return lax.dot_general(left, right, (((1,), (0,)), ((), ())), preferred_element_type=F32)


def dot_nt(left, right):
    return lax.dot_general(left, right, (((1,), (1,)), ((), ())), preferred_element_type=F32)


def value_of(number, group):
    if isinstance(number, int):
        return number
    return number[0] + (number[1] - number[0]) * group


def prepare_kernel(edge_block, swapped, place, volts_source, taps_source, table_source, turn_source, volts, edge, taps, one, two, turn, done, taps_ref, table_ref):
    count = edge.shape[1]
    start = pl.multiple_of(value_of(edge_block, place[0]) * count, count)
    copies = [
        pltpu.make_async_copy(taps_source, taps_ref, done.at[0]),
        pltpu.make_async_copy(table_source, table_ref, done.at[1]),
        pltpu.make_async_copy(volts_source.at[:, pl.ds(start, count)], edge, done.at[2]),
        pltpu.make_async_copy(volts_source, volts, done.at[3]),
        pltpu.make_async_copy(turn_source, turn, done.at[4]),
    ]
    for copy in copies:
        copy.start()
    copies[0].wait()
    copies[1].wait()
    for h in range(H):
        for half in range(TAPS // SUB):
            tile = taps_ref[pl.ds(half * SUB, SUB), pl.ds(h * LANES, LANES)]
            for r in range(2):
                taps[pl.ds(half * SUB * ROWS + 2 * h + r, SUB, stride=ROWS), :] = tile
    high, low = halves(table_ref[:ROWS, :ROWS])
    one[...] = jnp.concatenate([high, high, low], axis=1)
    start = pl.multiple_of(ROWS + place[0] * (2 * K2 * swapped), SUB)
    high, low = halves(table_ref[pl.ds(start, 2 * K2), :])
    two[0] = high
    two[1] = low
    for copy in copies[2:]:
        copy.wait()


def prepare(volts, fir_taps, place, groups, edge_block, edge_frames):
    signals, frames = volts.shape[:2]
    two = stage_two_table(groups)
    table = np.concatenate([stage_one_table(), two, np.roll(two, K2, axis=0)]).astype(np.float32)
    vmem = pl.BlockSpec(memory_space=pltpu.VMEM)
    return pl.pallas_call(
        functools.partial(prepare_kernel, edge_block, int(groups == 2)),
        grid_spec=pltpu.PrefetchScalarGridSpec(
            num_scalar_prefetch=1,
            grid=(),
            in_specs=[pl.BlockSpec(memory_space=pl.ANY)] * 4,
            out_specs=[vmem] * 6,
            scratch_shapes=[
                pltpu.SemaphoreType.DMA((5,)),
                pltpu.VMEM(fir_taps.shape, F32),
                pltpu.VMEM(table.shape, F32),
            ],
        ),
        out_shape=[
            jax.ShapeDtypeStruct((signals, frames, ROWS, LANES), BF16),
            jax.ShapeDtypeStruct((signals, edge_frames, ROWS, LANES), BF16),
            jax.ShapeDtypeStruct((TAPS * ROWS, LANES), F32),
            jax.ShapeDtypeStruct((ROWS, 3 * ROWS), BF16),
            jax.ShapeDtypeStruct((2, 2 * K2, 2 * LANES), BF16),
            jax.ShapeDtypeStruct((H, 2 * LANES), F32),
        ],
        compiler_params=pltpu.CompilerParams(vmem_limit_bytes=24 << 20),
    )(
        place,
        *[
            pltpu.with_memory_space_constraint(x, pltpu.HBM)
            for x in (volts, fir_taps, jnp.asarray(table), jnp.asarray(turn_table(), F32))
        ],
    )


def spectra_kernel(groups, parts, out_frames, run, place, *refs):
    part_refs, refs = refs[: len(parts)], refs[len(parts) :]
    taps, one, two, turn = refs[:4]
    outs, (ext, filtered, turned, staged) = refs[4:-4], refs[-4:]
    step, steps, members = pl.program_id(0), pl.num_programs(0), MEMBERS
    per_group = K2 // groups
    share = LANES // out_frames
    tiles = H // share
    pairs = tiles // 2
    frame_rows, row_rows = ROWS + PAD, tiles * TILE + PAD

    def load(member):
        signal = step * members + member
        for (frames, block, start, valid), ref in zip(parts, part_refs):
            first = value_of(block, place[0]) * frames
            start = value_of(start, place[0])
            valid = value_of(valid, place[0])

            def fill(ref=ref, frames=frames, first=first, start=start):
                for f in range(frames):
                    ext[member, start + f] = ref[signal, first + f].astype(F32)

            def clear(frames=frames, start=start):
                for f in range(frames):
                    ext[member, start + f] = jnp.zeros((ROWS, LANES), F32)

            if isinstance(valid, int):
                fill() if valid else clear()
            else:
                pl.when(valid == 1)(fill)
                pl.when(valid == 0)(clear)

    def filter_rows(member, q):
        rows = pl.ds(pl.multiple_of(q * SUB, SUB), SUB)
        tap = [taps[pl.ds(pl.multiple_of(m * ROWS + q * SUB, SUB), SUB), :] for m in range(TAPS)]
        for f in range(out_frames):
            total = tap[0] * ext[member, f + 1, rows]
            for m in range(1, TAPS):
                total = total + tap[m] * ext[member, f + 1 + m, rows]
            filtered[member, f, rows] = total

    def first_stage(member):
        cosine = turn[:, :LANES]
        sine = turn[:, LANES:]
        for g in range(out_frames // STEP):
            block = jnp.concatenate([filtered[member, g * STEP + f] for f in range(STEP)], axis=1)
            high, low = halves(block)
            first = dot(one[...], jnp.concatenate([high, low, high], axis=0))
            for f in range(STEP):
                real = first[:H, f * LANES : (f + 1) * LANES]
                imag = first[H:, f * LANES : (f + 1) * LANES]
                at = (g * STEP + f) * frame_rows
                turned[member, at : at + H, :] = real * cosine + imag * sine
                turned[member, at + H : at + ROWS, :] = imag * cosine - real * sine

    def second_stage(member, pair):
        rows = []
        for k1 in range(2 * pair * share, 2 * (pair + 1) * share):
            for f in range(0, out_frames, SUB):
                rows.append(
                    jnp.concatenate(
                        [turned[member, pl.ds(f * frame_rows + p * H + k1, SUB, stride=frame_rows), :] for p in range(2)],
                        axis=1,
                    )
                )
        high, low = halves(jnp.concatenate(rows, axis=0))
        spectrum = dot_nt(two[0], high) + dot_nt(two[1], high) + dot_nt(two[0], low)
        for k in range(2):
            for t in range(groups):
                for p in range(2):
                    for k2 in range(0, per_group, SUB):
                        row = (t * 2 + p) * per_group + k2
                        start = (t * per_group + k2) * row_rows + (2 * pair + k) * TILE + p * SUB
                        staged[pl.ds(start + step * members + member, SUB, stride=row_rows), :] = spectrum[
                            row : row + SUB, k * LANES : (k + 1) * LANES
                        ]

    def write():
        at = 0
        for out in outs:

            def write_row(k2, carry):
                for k in range(tiles):
                    start = pl.multiple_of((at + k2) * row_rows + k * TILE, PAD)
                    out[k2, k] = staged[pl.ds(start, TILE), :].astype(BF16)
                return carry

            lax.fori_loop(0, out.shape[0], write_row, 0, unroll=2)
            at += out.shape[0]

    def body():
        for member in range(members):
            load(member)

        def filter_one(index, carry):
            filter_rows(index // (ROWS // SUB), index % (ROWS // SUB))
            return carry

        lax.fori_loop(0, members * (ROWS // SUB), filter_one, 0)
        for member in range(members):
            first_stage(member)
        for member in range(members):
            for pair in range(pairs):
                second_stage(member, pair)

        pl.when(step == steps - 1)(write)

    if isinstance(run, int):
        body()
    else:
        pl.when(value_of(run, place[0]) == 1)(body)


def after(value, *others):
    return lax.optimization_barrier((value, *others))[0]


def spectra(parts, out_frames, fixed, place, groups, sizes, run=1, wait=(), cost=10**6):
    signals = parts[0][0].shape[0]
    place = after(place, *wait)
    tiles = H * out_frames // LANES
    shapes = [(n, tiles, TILE, LANES) for n in sizes]
    return pl.pallas_call(
        functools.partial(spectra_kernel, groups, tuple(part[1:] for part in parts), out_frames, run),
        grid_spec=pltpu.PrefetchScalarGridSpec(
            num_scalar_prefetch=1,
            grid=(signals // MEMBERS,),
            in_specs=[pl.BlockSpec(memory_space=pltpu.VMEM)] * (len(parts) + 4),
            out_specs=[pl.BlockSpec(shape, lambda s, place: (0, 0, 0, 0)) for shape in shapes],
            scratch_shapes=[
                pltpu.VMEM((MEMBERS, TAPS + out_frames, ROWS, LANES), F32),
                pltpu.VMEM((MEMBERS, out_frames, ROWS, LANES), F32),
                pltpu.VMEM((MEMBERS, out_frames * (ROWS + PAD), LANES), F32),
                pltpu.VMEM((K2 * (tiles * TILE + PAD), LANES), F32),
            ],
        ),
        out_shape=[jax.ShapeDtypeStruct(shape, BF16) for shape in shapes],
        compiler_params=pltpu.CompilerParams(vmem_limit_bytes=32 << 20),
        cost_estimate=pl.CostEstimate(flops=cost, bytes_accessed=0, transcendentals=0),
    )(place, *[part[0] for part in parts], *fixed)


def after(value, *others):
    return lax.optimization_barrier((value, *others))[0]


def correlate_kernel(pieces, per_group, scale, add, last, place, *refs):
    refs = list(refs)
    sums = refs.pop() if last else None
    out = refs.pop()
    before = refs.pop() if add else None
    if not last:
        sums = out
    half = per_group // 2
    lane = lax.broadcasted_iota(jnp.int32, (SUB, LANES), 1)
    first_tile = lane < LANES // 2
    real_lane = lane % TILE < SUB
    sign = jnp.where(real_lane, 1.0, -1.0).astype(F32)
    for number, piece in enumerate(pieces):
        tiles, piece = piece
        share = H // tiles
        where = lax.broadcasted_iota(jnp.int32, (TILE, LANES), 1) // (LANES // share)

        def pair(index, carry):
            k2 = index // tiles
            k1 = index % tiles
            own, other = [], []
            for position in range(len(piece[0])):
                rows = []
                for tile in range(2):
                    array, row, column = piece[0][position]
                    a = refs[array][row + tile * half + k2, column + k1]
                    rows += [jnp.where(where == c, a, jnp.zeros_like(a)) for c in range(share)]
                own.append(jnp.concatenate(rows, axis=0))
                rows = []
                for tile in range(2):
                    for visit in range(VISITS):
                        array, row, column = piece[visit][position]
                        rows.append(refs[array][row + tile * half + k2, column + k1])
                other.append(jnp.concatenate(rows, axis=0))
            product = dot_nt(jnp.concatenate(own, axis=1), jnp.concatenate(other, axis=1))
            for c in range(share):
                value = []
                for p in range(2):
                    at = [((tile * share + c) * 2 + p) * SUB for tile in range(2)]
                    value.append(
                        jnp.where(first_tile, product[at[0] : at[0] + SUB], product[at[1] : at[1] + SUB])
                    )
                turned = jnp.where(
                    real_lane, pltpu.roll(value[1], LANES - SUB, 1), pltpu.roll(value[1], SUB, 1)
                )
                total = value[0] * sign + turned
                channel = k2 // 4 * LANES + k2 % 4 * H + k1 * share + c
                rows = pl.ds(pl.multiple_of(channel * SUB, SUB), SUB)
                if number:
                    total = total + sums[rows, :]
                elif add:
                    total = total + before[rows, :]
                sums[rows, :] = total
            return carry

        lax.fori_loop(0, half * tiles, pair, 0, unroll=16)
    if not last:
        return

    def finish(index, carry):
        block = index // SUB
        signal = index % SUB
        value = sums[pl.ds(block * LANES * SUB + signal, LANES, stride=SUB), :]
        value = jnp.transpose(value * scale)
        at = 0
        for tile in range(2):
            for visit in range(VISITS):
                for part in range(2):
                    out[part, signal, value_of(PLACES[visit], place[1]), tile * (half // 4) + block] = value[at : at + SUB]
                    at += SUB
        return carry

    lax.fori_loop(0, half // 4 * SUB, finish, 0)


def correlate(arrays, pieces, per_group, place, scale, before, last, wait=(), cost=6 * 10**9):
    signals = TILE // 2
    rows = per_group // 2 * H * SUB
    place = after(place, *wait)
    shape = (2, signals, VISITS, per_group // 4, SUB, LANES) if last else (rows, LANES)
    operands = list(arrays) + ([] if before is None else [before])
    vmem = pl.BlockSpec(memory_space=pltpu.VMEM)
    return pl.pallas_call(
        functools.partial(correlate_kernel, pieces, per_group, scale, before is not None, last),
        grid_spec=pltpu.PrefetchScalarGridSpec(
            num_scalar_prefetch=1,
            grid=(),
            in_specs=[vmem] * len(operands),
            out_specs=vmem,
            scratch_shapes=[pltpu.VMEM((rows, LANES), F32)] if last else [],
        ),
        out_shape=jax.ShapeDtypeStruct(shape, F32),
        compiler_params=pltpu.CompilerParams(vmem_limit_bytes=24 << 20),
        input_output_aliases={} if before is None or last else {len(operands): 0},
        cost_estimate=pl.CostEstimate(flops=cost, bytes_accessed=0, transcendentals=0),
    )(place, *operands)


def stacked(voltage):
    s, f = voltage.shape[:2]
    return voltage.reshape(s, f, 2, H, LANES).transpose(0, 1, 3, 2, 4).reshape(s, f, ROWS, LANES)


def natural(out):
    parts, s, visits, i, t, lanes = out.shape
    return out.transpose(0, 1, 2, 4, 3, 5).reshape(parts, s, visits * t, i * lanes)


def shifted(block, axis, distance):
    size = lax.axis_size(axis)
    return lax.ppermute(block, axis, [(i, (i + distance) % size) for i in range(size)])


def farther(block):
    size = lax.axis_size("stn")
    rest = lax.ppermute(block, "stn", [(i, (i + 1 if i % 2 == 0 else i + 3) % size) for i in range(size)])
    return shifted(block, "stn", 2), rest


def evenly(block):
    size = lax.axis_size("stn")
    rest = lax.ppermute(block, "stn", [(i, (i + 1 if i % 2 == 0 else i + 3) % size) for i in range(size)])
    return lax.ppermute(block, "stn", [(i, (i + 2) % size) for i in range(size) if i % 4 < 3]), rest


def relayed(rest):
    return lax.ppermute(rest, "stn", [(i, i - 1) for i in range(lax.axis_size("stn")) if i % 4 == 2])


def exchanged(block):
    return lax.ppermute(block, "stn", [(i, i ^ 1) for i in range(lax.axis_size("stn"))])


def paired(volts, fir_taps, place, correlated):
    frames = volts.shape[1]
    me = lax.axis_index("tm")
    sizes = [K2 // 2, K2 // 2]
    swap = [(0, 1), (1, 0)]
    edge = TAPS // 2
    last = frames // edge
    volts, edge_frames, *fixed = prepare(volts, fir_taps, place, 2, (last - 1, 0), edge)
    visiting = lax.ppermute(edge_frames, "tm", swap)
    own_a, away_a = spectra(
        [(volts, TAPS, 0, 0, (0, 1)), (volts, TAPS, (0, 1), TAPS, 1)], TAPS, fixed, place, 2, sizes
    )
    got_a = lax.ppermute(away_a, "tm", swap)
    two_a, rest_a = farther(own_a)
    own_b, away_b = spectra(
        [(volts, TAPS, 0, 0, 1), (volts, TAPS, 1, TAPS, 1)], TAPS, fixed, place, 2, sizes, (1, 0), (own_a,)
    )
    got_b = lax.ppermute(away_b, "tm", [(0, 1)])
    pair_a = exchanged(two_a)
    own_c, away_c = spectra(
        [
            (volts, edge, (last - 2, 0), (0, edge), 1),
            (volts, edge, (last - 1, 1), (edge, 2 * edge), 1),
            (visiting, edge, 0, (2 * edge, 0), 1),
        ],
        edge, fixed, place, 2, sizes, 1, (own_b, two_a, got_a), 9 * 10**9,
    )
    got_c = lax.ppermute(away_c, "tm", swap)
    two_g, rest_g = farther(got_a)
    pair_g = exchanged(two_g)
    own_c = after(own_c, two_g, pair_a, rest_a)
    rest = jnp.concatenate([jnp.where(me == 0, own_b, got_b), own_c, got_c], axis=1)
    two_r, rest_r = evenly(rest)
    many, few = own_a.shape[1], own_c.shape[1]
    sums = correlated(
        [own_a, pair_a, two_a, rest_a, got_a, pair_g, two_g, rest_g], [(many, [(0, 0, 0), (1, 0, 0)])], None, False
    )
    two_r = two_r + relayed(after(rest_r, sums))
    pair_r = exchanged(two_r)
    return correlated(
        [rest, pair_r, two_r, rest_r], [(many, [(0, 0, 0)]), (few, [(0, 0, many), (0, 0, many + few)])], sums, True
    )


def general(volts, fir_taps, place, correlated):
    groups = lax.axis_size("tm")
    frames = volts.shape[1]
    volts, edge_frames, *fixed = prepare(volts, fir_taps, place, groups, frames // TAPS - 1, TAPS)
    history = lax.ppermute(edge_frames, "tm", [(i, i + 1) for i in range(groups - 1)])
    parts = [(history, TAPS, 0, 0, 1)] + [(volts, TAPS, i, TAPS * (i + 1), 1) for i in range(frames // TAPS)]
    spectrum = spectra(parts, frames, fixed, place, groups, [K2])[0]
    spectrum = lax.all_to_all(spectrum, "tm", split_axis=0, concat_axis=0, tiled=True)
    two, rest = farther(spectrum)
    spots = [(0, K2 // groups * t, 0) for t in range(groups)]
    return correlated([spectrum, exchanged(two), two, rest], [(spectrum.shape[1], spots)], None, True)


def local(voltage, fir_taps):
    groups = lax.axis_size("tm")
    place = jnp.stack([lax.axis_index("tm"), lax.axis_index("stn") % 2]).astype(jnp.int32)
    scale = 1.0 / (groups * voltage.shape[1])

    def correlated(arrays, pieces, before, last, wait=()):
        laid = [
            (tiles, [[(VISITS * n + visit, row, column) for n, row, column in spots] for visit in range(VISITS)])
            for tiles, spots in pieces
        ]
        return correlate(arrays, laid, K2 // groups, place, scale, before, last, wait)

    run = paired if groups == 2 else general
    return natural(run(stacked(voltage), fir_taps, place, correlated))


def solution(mesh):
    return jax.shard_map(
        local,
        mesh=mesh,
        in_specs=(P("stn", "tm", None, None), P()),
        out_specs=P(None, "stn", None, "tm"),
        check_vma=False,
    )
```

```python
import functools
import math

import jax
import jax.numpy as jnp
import numpy as np
from jax import lax
from jax.experimental import pallas as pl
from jax.experimental.pallas import tpu as pltpu
from jax.sharding import PartitionSpec as P

NCH = 4096
CHANS = 2048
TAPS = 16
VISITS = 4
H = 32
LANES = 128
ROWS = 2 * H
K2 = CHANS // H
STEP = 8
TILE = 16
PLACES = (0, (1, 3), 2, (3, 1))
MEMBERS = 4
PAD = 8
SUB = 8
BF16 = jnp.bfloat16
F32 = jnp.float32


def angles(rows, columns, modulus):
    turns = np.outer(rows, columns) % modulus
    return turns.astype(np.float64) * (2.0 * math.pi / modulus)


def stage_one_table():
    theta = angles(np.arange(H), np.arange(H), H)
    cosine, sine = np.cos(theta), np.sin(theta)
    table = np.zeros((2, H, H, 2))
    table[0, :, :, 0], table[0, :, :, 1] = cosine, sine
    table[1, :, :, 0], table[1, :, :, 1] = -sine, cosine
    return np.pad(table.reshape(ROWS, ROWS), ((0, 0), (0, 2 * LANES - ROWS)))


def turn_table():
    theta = angles(np.arange(H), np.arange(LANES), NCH)
    return np.concatenate([np.cos(theta), np.sin(theta)], axis=1)


def stage_two_table(groups):
    theta = angles(np.arange(K2), np.arange(LANES), LANES)
    cosine, sine = np.cos(theta) / math.sqrt(NCH), np.sin(theta) / math.sqrt(NCH)
    real = np.concatenate([cosine, sine], 1).reshape(groups, 1, K2 // groups, 2 * LANES)
    imag = np.concatenate([-sine, cosine], 1).reshape(groups, 1, K2 // groups, 2 * LANES)
    return np.concatenate([real, imag], 1).reshape(2 * K2, 2 * LANES)


def halves(value):
    high = value.astype(BF16)
    return high, (value - high.astype(F32)).astype(BF16)


def dot(left, right):
    return lax.dot_general(left, right, (((1,), (0,)), ((), ())), preferred_element_type=F32)


def dot_nt(left, right):
    return lax.dot_general(left, right, (((1,), (1,)), ((), ())), preferred_element_type=F32)


def value_of(number, group):
    if isinstance(number, int):
        return number
    return number[0] + (number[1] - number[0]) * group


def prepare_kernel(edge_block, swapped, place, volts_source, taps_source, table_source, turn_source, volts, edge, taps, one, two, turn, done, taps_ref, table_ref):
    count = edge.shape[1]
    start = pl.multiple_of(value_of(edge_block, place[0]) * count, count)
    copies = [
        pltpu.make_async_copy(taps_source, taps_ref, done.at[0]),
        pltpu.make_async_copy(table_source, table_ref, done.at[1]),
        pltpu.make_async_copy(volts_source.at[:, pl.ds(start, count)], edge, done.at[2]),
        pltpu.make_async_copy(volts_source, volts, done.at[3]),
        pltpu.make_async_copy(turn_source, turn, done.at[4]),
    ]
    for copy in copies:
        copy.start()
    copies[0].wait()
    copies[1].wait()
    for h in range(H):
        for half in range(TAPS // SUB):
            tile = taps_ref[pl.ds(half * SUB, SUB), pl.ds(h * LANES, LANES)]
            for r in range(2):
                taps[pl.ds(half * SUB * ROWS + 2 * h + r, SUB, stride=ROWS), :] = tile
    high, low = halves(table_ref[:ROWS, :ROWS])
    one[...] = jnp.concatenate([high, high, low], axis=1)
    start = pl.multiple_of(ROWS + place[0] * (2 * K2 * swapped), SUB)
    high, low = halves(table_ref[pl.ds(start, 2 * K2), :])
    two[0] = high
    two[1] = low
    for copy in copies[2:]:
        copy.wait()


def prepare(volts, fir_taps, place, groups, edge_block, edge_frames):
    signals, frames = volts.shape[:2]
    two = stage_two_table(groups)
    table = np.concatenate([stage_one_table(), two, np.roll(two, K2, axis=0)]).astype(np.float32)
    vmem = pl.BlockSpec(memory_space=pltpu.VMEM)
    return pl.pallas_call(
        functools.partial(prepare_kernel, edge_block, int(groups == 2)),
        grid_spec=pltpu.PrefetchScalarGridSpec(
            num_scalar_prefetch=1,
            grid=(),
            in_specs=[pl.BlockSpec(memory_space=pl.ANY)] * 4,
            out_specs=[vmem] * 6,
            scratch_shapes=[
                pltpu.SemaphoreType.DMA((5,)),
                pltpu.VMEM(fir_taps.shape, F32),
                pltpu.VMEM(table.shape, F32),
            ],
        ),
        out_shape=[
            jax.ShapeDtypeStruct((signals, frames, ROWS, LANES), BF16),
            jax.ShapeDtypeStruct((signals, edge_frames, ROWS, LANES), BF16),
            jax.ShapeDtypeStruct((TAPS * ROWS, LANES), F32),
            jax.ShapeDtypeStruct((ROWS, 3 * ROWS), BF16),
            jax.ShapeDtypeStruct((2, 2 * K2, 2 * LANES), BF16),
            jax.ShapeDtypeStruct((H, 2 * LANES), F32),
        ],
        compiler_params=pltpu.CompilerParams(vmem_limit_bytes=24 << 20),
    )(
        place,
        *[
            pltpu.with_memory_space_constraint(x, pltpu.HBM)
            for x in (volts, fir_taps, jnp.asarray(table), jnp.asarray(turn_table(), F32))
        ],
    )


def spectra_kernel(groups, parts, out_frames, run, place, *refs):
    part_refs, refs = refs[: len(parts)], refs[len(parts) :]
    taps, one, two, turn = refs[:4]
    outs, (ext, filtered, turned, staged) = refs[4:-4], refs[-4:]
    step, steps, members = pl.program_id(0), pl.num_programs(0), MEMBERS
    per_group = K2 // groups
    share = LANES // out_frames
    tiles = H // share
    pairs = tiles // 2
    frame_rows, row_rows = ROWS + PAD, tiles * TILE + PAD

    def load(member):
        signal = step * members + member
        for (frames, block, start, valid), ref in zip(parts, part_refs):
            first = value_of(block, place[0]) * frames
            start = value_of(start, place[0])
            valid = value_of(valid, place[0])

            def fill(ref=ref, frames=frames, first=first, start=start):
                for f in range(frames):
                    ext[member, start + f] = ref[signal, first + f].astype(F32)

            def clear(frames=frames, start=start):
                for f in range(frames):
                    ext[member, start + f] = jnp.zeros((ROWS, LANES), F32)

            if isinstance(valid, int):
                fill() if valid else clear()
            else:
                pl.when(valid == 1)(fill)
                pl.when(valid == 0)(clear)

    def filter_rows(member, q):
        rows = pl.ds(pl.multiple_of(q * SUB, SUB), SUB)
        tap = [taps[pl.ds(pl.multiple_of(m * ROWS + q * SUB, SUB), SUB), :] for m in range(TAPS)]
        for f in range(out_frames):
            total = tap[0] * ext[member, f + 1, rows]
            for m in range(1, TAPS):
                total = total + tap[m] * ext[member, f + 1 + m, rows]
            filtered[member, f, rows] = total

    def first_stage(member):
        cosine = turn[:, :LANES]
        sine = turn[:, LANES:]
        for g in range(out_frames // STEP):
            block = jnp.concatenate([filtered[member, g * STEP + f] for f in range(STEP)], axis=1)
            high, low = halves(block)
            first = dot(one[...], jnp.concatenate([high, low, high], axis=0))
            for f in range(STEP):
                real = first[:H, f * LANES : (f + 1) * LANES]
                imag = first[H:, f * LANES : (f + 1) * LANES]
                at = (g * STEP + f) * frame_rows
                turned[member, at : at + H, :] = real * cosine + imag * sine
                turned[member, at + H : at + ROWS, :] = imag * cosine - real * sine

    def second_stage(member, pair):
        rows = []
        for k1 in range(2 * pair * share, 2 * (pair + 1) * share):
            for f in range(0, out_frames, SUB):
                rows.append(
                    jnp.concatenate(
                        [turned[member, pl.ds(f * frame_rows + p * H + k1, SUB, stride=frame_rows), :] for p in range(2)],
                        axis=1,
                    )
                )
        high, low = halves(jnp.concatenate(rows, axis=0))
        spectrum = dot_nt(two[0], high) + dot_nt(two[1], high) + dot_nt(two[0], low)
        for k in range(2):
            for t in range(groups):
                for p in range(2):
                    for k2 in range(0, per_group, SUB):
                        row = (t * 2 + p) * per_group + k2
                        start = (t * per_group + k2) * row_rows + (2 * pair + k) * TILE + p * SUB
                        staged[pl.ds(start + step * members + member, SUB, stride=row_rows), :] = spectrum[
                            row : row + SUB, k * LANES : (k + 1) * LANES
                        ]

    def write():
        at = 0
        for out in outs:

            def write_row(k2, carry):
                for k in range(tiles):
                    start = pl.multiple_of((at + k2) * row_rows + k * TILE, PAD)
                    out[k2, k] = staged[pl.ds(start, TILE), :].astype(BF16)
                return carry

            lax.fori_loop(0, out.shape[0], write_row, 0, unroll=2)
            at += out.shape[0]

    def body():
        for member in range(members):
            load(member)

        def filter_one(index, carry):
            filter_rows(index // (ROWS // SUB), index % (ROWS // SUB))
            return carry

        lax.fori_loop(0, members * (ROWS // SUB), filter_one, 0)
        for member in range(members):
            first_stage(member)
        for member in range(members):
            for pair in range(pairs):
                second_stage(member, pair)

        pl.when(step == steps - 1)(write)

    if isinstance(run, int):
        body()
    else:
        pl.when(value_of(run, place[0]) == 1)(body)


def after(value, *others):
    return lax.optimization_barrier((value, *others))[0]


def spectra(parts, out_frames, fixed, place, groups, sizes, run=1, wait=(), cost=10**6):
    signals = parts[0][0].shape[0]
    place = after(place, *wait)
    tiles = H * out_frames // LANES
    shapes = [(n, tiles, TILE, LANES) for n in sizes]
    return pl.pallas_call(
        functools.partial(spectra_kernel, groups, tuple(part[1:] for part in parts), out_frames, run),
        grid_spec=pltpu.PrefetchScalarGridSpec(
            num_scalar_prefetch=1,
            grid=(signals // MEMBERS,),
            in_specs=[pl.BlockSpec(memory_space=pltpu.VMEM)] * (len(parts) + 4),
            out_specs=[pl.BlockSpec(shape, lambda s, place: (0, 0, 0, 0)) for shape in shapes],
            scratch_shapes=[
                pltpu.VMEM((MEMBERS, TAPS + out_frames, ROWS, LANES), F32),
                pltpu.VMEM((MEMBERS, out_frames, ROWS, LANES), F32),
                pltpu.VMEM((MEMBERS, out_frames * (ROWS + PAD), LANES), F32),
                pltpu.VMEM((K2 * (tiles * TILE + PAD), LANES), F32),
            ],
        ),
        out_shape=[jax.ShapeDtypeStruct(shape, BF16) for shape in shapes],
        compiler_params=pltpu.CompilerParams(vmem_limit_bytes=32 << 20),
        cost_estimate=pl.CostEstimate(flops=cost, bytes_accessed=0, transcendentals=0),
    )(place, *[part[0] for part in parts], *fixed)


def after(value, *others):
    return lax.optimization_barrier((value, *others))[0]


def correlate_kernel(pieces, per_group, scale, add, last, place, *refs):
    refs = list(refs)
    sums = refs.pop() if last else None
    out = refs.pop()
    before = refs.pop() if add else None
    if not last:
        sums = out
    half = per_group // 2
    lane = lax.broadcasted_iota(jnp.int32, (SUB, LANES), 1)
    first_tile = lane < LANES // 2
    real_lane = lane % TILE < SUB
    sign = jnp.where(real_lane, 1.0, -1.0).astype(F32)
    for number, piece in enumerate(pieces):
        tiles, piece = piece
        share = H // tiles
        where = lax.broadcasted_iota(jnp.int32, (TILE, LANES), 1) // (LANES // share)

        def pair(index, carry):
            k2 = index // tiles
            k1 = index % tiles
            own, other = [], []
            for position in range(len(piece[0])):
                rows = []
                for tile in range(2):
                    array, row, column = piece[0][position]
                    a = refs[array][row + tile * half + k2, column + k1]
                    rows += [jnp.where(where == c, a, jnp.zeros_like(a)) for c in range(share)]
                own.append(jnp.concatenate(rows, axis=0))
                rows = []
                for tile in range(2):
                    for visit in range(VISITS):
                        array, row, column = piece[visit][position]
                        rows.append(refs[array][row + tile * half + k2, column + k1])
                other.append(jnp.concatenate(rows, axis=0))
            product = dot_nt(jnp.concatenate(own, axis=1), jnp.concatenate(other, axis=1))
            for c in range(share):
                value = []
                for p in range(2):
                    at = [((tile * share + c) * 2 + p) * SUB for tile in range(2)]
                    value.append(
                        jnp.where(first_tile, product[at[0] : at[0] + SUB], product[at[1] : at[1] + SUB])
                    )
                turned = jnp.where(
                    real_lane, pltpu.roll(value[1], LANES - SUB, 1), pltpu.roll(value[1], SUB, 1)
                )
                total = value[0] * sign + turned
                channel = k2 // 4 * LANES + k2 % 4 * H + k1 * share + c
                rows = pl.ds(pl.multiple_of(channel * SUB, SUB), SUB)
                if number:
                    total = total + sums[rows, :]
                elif add:
                    total = total + before[rows, :]
                sums[rows, :] = total
            return carry

        lax.fori_loop(0, half * tiles, pair, 0, unroll=16)
    if not last:
        return

    def finish(index, carry):
        block = index // SUB
        signal = index % SUB
        value = sums[pl.ds(block * LANES * SUB + signal, LANES, stride=SUB), :]
        value = jnp.transpose(value * scale)
        at = 0
        for tile in range(2):
            for visit in range(VISITS):
                for part in range(2):
                    out[part, signal, value_of(PLACES[visit], place[1]), tile * (half // 4) + block] = value[at : at + SUB]
                    at += SUB
        return carry

    lax.fori_loop(0, half // 4 * SUB, finish, 0)


def correlate(arrays, pieces, per_group, place, scale, before, last, wait=(), cost=10**3):
    signals = TILE // 2
    rows = per_group // 2 * H * SUB
    place = after(place, *wait)
    shape = (2, signals, VISITS, per_group // 4, SUB, LANES) if last else (rows, LANES)
    operands = list(arrays) + ([] if before is None else [before])
    vmem = pl.BlockSpec(memory_space=pltpu.VMEM)
    return pl.pallas_call(
        functools.partial(correlate_kernel, pieces, per_group, scale, before is not None, last),
        grid_spec=pltpu.PrefetchScalarGridSpec(
            num_scalar_prefetch=1,
            grid=(),
            in_specs=[vmem] * len(operands),
            out_specs=vmem,
            scratch_shapes=[pltpu.VMEM((rows, LANES), F32)] if last else [],
        ),
        out_shape=jax.ShapeDtypeStruct(shape, F32),
        compiler_params=pltpu.CompilerParams(vmem_limit_bytes=24 << 20),
        input_output_aliases={} if before is None or last else {len(operands): 0},
        cost_estimate=pl.CostEstimate(flops=cost, bytes_accessed=0, transcendentals=0),
    )(place, *operands)


def stacked(voltage):
    s, f = voltage.shape[:2]
    return voltage.reshape(s, f, 2, H, LANES).transpose(0, 1, 3, 2, 4).reshape(s, f, ROWS, LANES)


def natural(out):
    parts, s, visits, i, t, lanes = out.shape
    return out.transpose(0, 1, 2, 4, 3, 5).reshape(parts, s, visits * t, i * lanes)


def shifted(block, axis, distance):
    size = lax.axis_size(axis)
    return lax.ppermute(block, axis, [(i, (i + distance) % size) for i in range(size)])


def farther(block):
    size = lax.axis_size("stn")
    rest = lax.ppermute(block, "stn", [(i, (i + 1 if i % 2 == 0 else i + 3) % size) for i in range(size)])
    return shifted(block, "stn", 2), rest


def evenly(block):
    size = lax.axis_size("stn")
    rest = lax.ppermute(block, "stn", [(i, (i + 1 if i % 2 == 0 else i + 3) % size) for i in range(size)])
    return lax.ppermute(block, "stn", [(i, (i + 2) % size) for i in range(size) if i % 4 < 3]), rest


def relayed(rest):
    return lax.ppermute(rest, "stn", [(i, i - 1) for i in range(lax.axis_size("stn")) if i % 4 == 2])


def exchanged(block):
    return lax.ppermute(block, "stn", [(i, i ^ 1) for i in range(lax.axis_size("stn"))])


def paired(volts, fir_taps, place, correlated):
    frames = volts.shape[1]
    me = lax.axis_index("tm")
    sizes = [K2 // 2, K2 // 2]
    swap = [(0, 1), (1, 0)]
    edge = TAPS // 2
    last = frames // edge
    many, few = TAPS * H // LANES, edge * H // LANES
    volts, edge_frames, *fixed = prepare(volts, fir_taps, place, 2, (last - 1, 0), edge)
    visiting = lax.ppermute(edge_frames, "tm", swap)
    own_a, away_a = spectra(
        [(volts, TAPS, 0, 0, (0, 1)), (volts, TAPS, (0, 1), TAPS, 1)], TAPS, fixed, place, 2, sizes
    )
    got_a = lax.ppermute(away_a, "tm", swap)
    two_a, rest_a = farther(own_a)
    own_b, away_b = spectra(
        [(volts, TAPS, 0, 0, 1), (volts, TAPS, 1, TAPS, 1)], TAPS, fixed, place, 2, sizes, (1, 0), (own_a,)
    )
    own_c, away_c = spectra(
        [
            (volts, edge, (last - 2, 0), (0, edge), 1),
            (volts, edge, (last - 1, 1), (edge, 2 * edge), 1),
            (visiting, edge, 0, (2 * edge, 0), 1),
        ],
        edge, fixed, place, 2, sizes, 1, (own_b, two_a),
    )
    got_a, own_c, away_b, away_c, two_a = lax.optimization_barrier((got_a, own_c, away_b, away_c, two_a))
    two_g, rest_g = evenly(got_a)
    got_b = lax.ppermute(away_b, "tm", [(0, 1)])
    pair_a = exchanged(two_a)
    first = [(many, [(0, 0, 0)])]
    sums = correlated([own_a, pair_a, two_a, rest_a], first, None, False)
    two_g = two_g + relayed(after(rest_g, two_g, sums))
    got_b, away_c, sums = lax.optimization_barrier((got_b, away_c, sums))
    got_c = lax.ppermute(away_c, "tm", swap)
    piece_b = jnp.where(me == 0, own_b, got_b)
    two_b, rest_b = farther(piece_b)
    pair_g = exchanged(after(two_g, piece_b))
    sums = correlated([got_a, pair_g, two_g, rest_g], first, sums, False)
    piece_c = jnp.concatenate([own_c, got_c], axis=1)
    two_c, rest_c = farther(piece_c)
    pair_b = exchanged(two_b)
    sums = correlated([piece_b, pair_b, two_b, rest_b], first, sums, False)
    pair_c = exchanged(after(two_c, sums))
    return correlated([piece_c, pair_c, two_c, rest_c], [(few, [(0, 0, 0), (0, 0, few)])], sums, True)


def general(volts, fir_taps, place, correlated):
    groups = lax.axis_size("tm")
    frames = volts.shape[1]
    volts, edge_frames, *fixed = prepare(volts, fir_taps, place, groups, frames // TAPS - 1, TAPS)
    history = lax.ppermute(edge_frames, "tm", [(i, i + 1) for i in range(groups - 1)])
    parts = [(history, TAPS, 0, 0, 1)] + [(volts, TAPS, i, TAPS * (i + 1), 1) for i in range(frames // TAPS)]
    spectrum = spectra(parts, frames, fixed, place, groups, [K2])[0]
    spectrum = lax.all_to_all(spectrum, "tm", split_axis=0, concat_axis=0, tiled=True)
    two, rest = farther(spectrum)
    spots = [(0, K2 // groups * t, 0) for t in range(groups)]
    return correlated([spectrum, exchanged(two), two, rest], [(spectrum.shape[1], spots)], None, True)


def local(voltage, fir_taps):
    groups = lax.axis_size("tm")
    place = jnp.stack([lax.axis_index("tm"), lax.axis_index("stn") % 2]).astype(jnp.int32)
    scale = 1.0 / (groups * voltage.shape[1])

    def correlated(arrays, pieces, before, last, wait=(), cost=10**3):
        laid = [
            (tiles, [[(VISITS * n + visit, row, column) for n, row, column in spots] for visit in range(VISITS)])
            for tiles, spots in pieces
        ]
        return correlate(arrays, laid, K2 // groups, place, scale, before, last, wait, cost)

    run = paired if groups == 2 else general
    return natural(run(stacked(voltage), fir_taps, place, correlated))


def solution(mesh):
    return jax.shard_map(
        local,
        mesh=mesh,
        in_specs=(P("stn", "tm", None, None), P()),
        out_specs=P(None, "stn", None, "tm"),
        check_vma=False,
    )
```

```python
import functools
import math

import jax
import jax.numpy as jnp
import numpy as np
from jax import lax
from jax.experimental import pallas as pl
from jax.experimental.pallas import tpu as pltpu
from jax.sharding import PartitionSpec as P

NCH = 4096
CHANS = 2048
TAPS = 16
VISITS = 4
H = 32
LANES = 128
ROWS = 2 * H
K2 = CHANS // H
STEP = 8
TILE = 16
PLACES = (0, (1, 3), 2, (3, 1))
MEMBERS = 4
PAD = 8
SUB = 8
BF16 = jnp.bfloat16
F32 = jnp.float32


def angles(rows, columns, modulus):
    turns = np.outer(rows, columns) % modulus
    return turns.astype(np.float64) * (2.0 * math.pi / modulus)


def stage_one_table():
    theta = angles(np.arange(H), np.arange(H), H)
    cosine, sine = np.cos(theta), np.sin(theta)
    table = np.zeros((2, H, H, 2))
    table[0, :, :, 0], table[0, :, :, 1] = cosine, sine
    table[1, :, :, 0], table[1, :, :, 1] = -sine, cosine
    return np.pad(table.reshape(ROWS, ROWS), ((0, 0), (0, 2 * LANES - ROWS)))


def turn_table():
    theta = angles(np.arange(H), np.arange(LANES), NCH)
    return np.concatenate([np.cos(theta), np.sin(theta)], axis=1)


def stage_two_table(groups):
    theta = angles(np.arange(K2), np.arange(LANES), LANES)
    cosine, sine = np.cos(theta) / math.sqrt(NCH), np.sin(theta) / math.sqrt(NCH)
    real = np.concatenate([cosine, sine], 1).reshape(groups, 1, K2 // groups, 2 * LANES)
    imag = np.concatenate([-sine, cosine], 1).reshape(groups, 1, K2 // groups, 2 * LANES)
    return np.concatenate([real, imag], 1).reshape(2 * K2, 2 * LANES)


def halves(value):
    high = value.astype(BF16)
    return high, (value - high.astype(F32)).astype(BF16)


def dot(left, right):
    return lax.dot_general(left, right, (((1,), (0,)), ((), ())), preferred_element_type=F32)


def dot_nt(left, right):
    return lax.dot_general(left, right, (((1,), (1,)), ((), ())), preferred_element_type=F32)


def value_of(number, group):
    if isinstance(number, int):
        return number
    return number[0] + (number[1] - number[0]) * group


def prepare_kernel(edge_block, swapped, place, volts_source, taps_source, table_source, turn_source, volts, edge, taps, one, two, turn, done, taps_ref, table_ref):
    count = edge.shape[1]
    start = pl.multiple_of(value_of(edge_block, place[0]) * count, count)
    copies = [
        pltpu.make_async_copy(taps_source, taps_ref, done.at[0]),
        pltpu.make_async_copy(table_source, table_ref, done.at[1]),
        pltpu.make_async_copy(volts_source.at[:, pl.ds(start, count)], edge, done.at[2]),
        pltpu.make_async_copy(volts_source, volts, done.at[3]),
        pltpu.make_async_copy(turn_source, turn, done.at[4]),
    ]
    for copy in copies:
        copy.start()
    copies[0].wait()
    copies[1].wait()
    for h in range(H):
        for half in range(TAPS // SUB):
            tile = taps_ref[pl.ds(half * SUB, SUB), pl.ds(h * LANES, LANES)]
            for r in range(2):
                taps[pl.ds(half * SUB * ROWS + 2 * h + r, SUB, stride=ROWS), :] = tile
    high, low = halves(table_ref[:ROWS, :ROWS])
    one[...] = jnp.concatenate([high, high, low], axis=1)
    start = pl.multiple_of(ROWS + place[0] * (2 * K2 * swapped), SUB)
    high, low = halves(table_ref[pl.ds(start, 2 * K2), :])
    two[0] = high
    two[1] = low
    for copy in copies[2:]:
        copy.wait()


def prepare(volts, fir_taps, place, groups, edge_block, edge_frames):
    signals, frames = volts.shape[:2]
    two = stage_two_table(groups)
    table = np.concatenate([stage_one_table(), two, np.roll(two, K2, axis=0)]).astype(np.float32)
    vmem = pl.BlockSpec(memory_space=pltpu.VMEM)
    return pl.pallas_call(
        functools.partial(prepare_kernel, edge_block, int(groups == 2)),
        grid_spec=pltpu.PrefetchScalarGridSpec(
            num_scalar_prefetch=1,
            grid=(),
            in_specs=[pl.BlockSpec(memory_space=pl.ANY)] * 4,
            out_specs=[vmem] * 6,
            scratch_shapes=[
                pltpu.SemaphoreType.DMA((5,)),
                pltpu.VMEM(fir_taps.shape, F32),
                pltpu.VMEM(table.shape, F32),
            ],
        ),
        out_shape=[
            jax.ShapeDtypeStruct((signals, frames, ROWS, LANES), BF16),
            jax.ShapeDtypeStruct((signals, edge_frames, ROWS, LANES), BF16),
            jax.ShapeDtypeStruct((TAPS * ROWS, LANES), F32),
            jax.ShapeDtypeStruct((ROWS, 3 * ROWS), BF16),
            jax.ShapeDtypeStruct((2, 2 * K2, 2 * LANES), BF16),
            jax.ShapeDtypeStruct((H, 2 * LANES), F32),
        ],
        compiler_params=pltpu.CompilerParams(vmem_limit_bytes=24 << 20),
    )(
        place,
        *[
            pltpu.with_memory_space_constraint(x, pltpu.HBM)
            for x in (volts, fir_taps, jnp.asarray(table), jnp.asarray(turn_table(), F32))
        ],
    )


def spectra_kernel(groups, parts, out_frames, run, place, *refs):
    part_refs, refs = refs[: len(parts)], refs[len(parts) :]
    taps, one, two, turn = refs[:4]
    outs, (ext, filtered, turned, staged) = refs[4:-4], refs[-4:]
    step, steps, members = pl.program_id(0), pl.num_programs(0), MEMBERS
    per_group = K2 // groups
    share = LANES // out_frames
    tiles = H // share
    pairs = tiles // 2
    frame_rows, row_rows = ROWS + PAD, tiles * TILE + PAD

    def load(member):
        signal = step * members + member
        for (frames, block, start, valid), ref in zip(parts, part_refs):
            first = value_of(block, place[0]) * frames
            start = value_of(start, place[0])
            valid = value_of(valid, place[0])

            def fill(ref=ref, frames=frames, first=first, start=start):
                for f in range(frames):
                    ext[member, start + f] = ref[signal, first + f].astype(F32)

            def clear(frames=frames, start=start):
                for f in range(frames):
                    ext[member, start + f] = jnp.zeros((ROWS, LANES), F32)

            if isinstance(valid, int):
                fill() if valid else clear()
            else:
                pl.when(valid == 1)(fill)
                pl.when(valid == 0)(clear)

    def filter_rows(member, q):
        rows = pl.ds(pl.multiple_of(q * SUB, SUB), SUB)
        tap = [taps[pl.ds(pl.multiple_of(m * ROWS + q * SUB, SUB), SUB), :] for m in range(TAPS)]
        for f in range(out_frames):
            total = tap[0] * ext[member, f + 1, rows]
            for m in range(1, TAPS):
                total = total + tap[m] * ext[member, f + 1 + m, rows]
            filtered[member, f, rows] = total

    def first_stage(member):
        cosine = turn[:, :LANES]
        sine = turn[:, LANES:]
        for g in range(out_frames // STEP):
            block = jnp.concatenate([filtered[member, g * STEP + f] for f in range(STEP)], axis=1)
            high, low = halves(block)
            first = dot(one[...], jnp.concatenate([high, low, high], axis=0))
            for f in range(STEP):
                real = first[:H, f * LANES : (f + 1) * LANES]
                imag = first[H:, f * LANES : (f + 1) * LANES]
                at = (g * STEP + f) * frame_rows
                turned[member, at : at + H, :] = real * cosine + imag * sine
                turned[member, at + H : at + ROWS, :] = imag * cosine - real * sine

    def second_stage(member, pair):
        rows = []
        for k1 in range(2 * pair * share, 2 * (pair + 1) * share):
            for f in range(0, out_frames, SUB):
                rows.append(
                    jnp.concatenate(
                        [turned[member, pl.ds(f * frame_rows + p * H + k1, SUB, stride=frame_rows), :] for p in range(2)],
                        axis=1,
                    )
                )
        high, low = halves(jnp.concatenate(rows, axis=0))
        spectrum = dot_nt(two[0], high) + dot_nt(two[1], high) + dot_nt(two[0], low)
        for k in range(2):
            for t in range(groups):
                for p in range(2):
                    for k2 in range(0, per_group, SUB):
                        row = (t * 2 + p) * per_group + k2
                        start = (t * per_group + k2) * row_rows + (2 * pair + k) * TILE + p * SUB
                        staged[pl.ds(start + step * members + member, SUB, stride=row_rows), :] = spectrum[
                            row : row + SUB, k * LANES : (k + 1) * LANES
                        ]

    def write():
        at = 0
        for out in outs:

            def write_row(k2, carry):
                for k in range(tiles):
                    start = pl.multiple_of((at + k2) * row_rows + k * TILE, PAD)
                    out[k2, k] = staged[pl.ds(start, TILE), :].astype(BF16)
                return carry

            lax.fori_loop(0, out.shape[0], write_row, 0, unroll=2)
            at += out.shape[0]

    def body():
        for member in range(members):
            load(member)

        def filter_one(index, carry):
            filter_rows(index // (ROWS // SUB), index % (ROWS // SUB))
            return carry

        lax.fori_loop(0, members * (ROWS // SUB), filter_one, 0)
        for member in range(members):
            first_stage(member)
        for member in range(members):
            for pair in range(pairs):
                second_stage(member, pair)

        pl.when(step == steps - 1)(write)

    if isinstance(run, int):
        body()
    else:
        pl.when(value_of(run, place[0]) == 1)(body)


def after(value, *others):
    return lax.optimization_barrier((value, *others))[0]


def spectra(parts, out_frames, fixed, place, groups, sizes, run=1, wait=(), cost=10**6):
    signals = parts[0][0].shape[0]
    place = after(place, *wait)
    tiles = H * out_frames // LANES
    shapes = [(n, tiles, TILE, LANES) for n in sizes]
    return pl.pallas_call(
        functools.partial(spectra_kernel, groups, tuple(part[1:] for part in parts), out_frames, run),
        grid_spec=pltpu.PrefetchScalarGridSpec(
            num_scalar_prefetch=1,
            grid=(signals // MEMBERS,),
            in_specs=[pl.BlockSpec(memory_space=pltpu.VMEM)] * (len(parts) + 4),
            out_specs=[pl.BlockSpec(shape, lambda s, place: (0, 0, 0, 0)) for shape in shapes],
            scratch_shapes=[
                pltpu.VMEM((MEMBERS, TAPS + out_frames, ROWS, LANES), F32),
                pltpu.VMEM((MEMBERS, out_frames, ROWS, LANES), F32),
                pltpu.VMEM((MEMBERS, out_frames * (ROWS + PAD), LANES), F32),
                pltpu.VMEM((K2 * (tiles * TILE + PAD), LANES), F32),
            ],
        ),
        out_shape=[jax.ShapeDtypeStruct(shape, BF16) for shape in shapes],
        compiler_params=pltpu.CompilerParams(vmem_limit_bytes=32 << 20),
        cost_estimate=pl.CostEstimate(flops=cost, bytes_accessed=0, transcendentals=0),
    )(place, *[part[0] for part in parts], *fixed)


def after(value, *others):
    return lax.optimization_barrier((value, *others))[0]


def correlate_kernel(pieces, per_group, scale, add, last, place, *refs):
    refs = list(refs)
    sums = refs.pop() if last else None
    out = refs.pop()
    before = refs.pop() if add else None
    if not last:
        sums = out
    half = per_group // 2
    lane = lax.broadcasted_iota(jnp.int32, (SUB, LANES), 1)
    first_tile = lane < LANES // 2
    real_lane = lane % TILE < SUB
    sign = jnp.where(real_lane, 1.0, -1.0).astype(F32)

    def fetch(spot, tile, k2, k1):
        arrays, row, column = spot
        values = [refs[array][row + tile * half + k2, column + k1] for array in arrays]
        return values[0] if len(values) == 1 else values[0] + values[1]

    for number, piece in enumerate(pieces):
        tiles, piece = piece
        share = H // tiles
        where = lax.broadcasted_iota(jnp.int32, (TILE, LANES), 1) // (LANES // share)

        def pair(index, carry):
            k2 = index // tiles
            k1 = index % tiles
            own, other = [], []
            for position in range(len(piece[0])):
                rows = []
                for tile in range(2):
                    a = fetch(piece[0][position], tile, k2, k1)
                    rows += [jnp.where(where == c, a, jnp.zeros_like(a)) for c in range(share)]
                own.append(jnp.concatenate(rows, axis=0))
                rows = []
                for tile in range(2):
                    for visit in range(VISITS):
                        rows.append(fetch(piece[visit][position], tile, k2, k1))
                other.append(jnp.concatenate(rows, axis=0))
            product = dot_nt(jnp.concatenate(own, axis=1), jnp.concatenate(other, axis=1))
            for c in range(share):
                value = []
                for p in range(2):
                    at = [((tile * share + c) * 2 + p) * SUB for tile in range(2)]
                    value.append(
                        jnp.where(first_tile, product[at[0] : at[0] + SUB], product[at[1] : at[1] + SUB])
                    )
                turned = jnp.where(
                    real_lane, pltpu.roll(value[1], LANES - SUB, 1), pltpu.roll(value[1], SUB, 1)
                )
                total = value[0] * sign + turned
                channel = k2 // 4 * LANES + k2 % 4 * H + k1 * share + c
                rows = pl.ds(pl.multiple_of(channel * SUB, SUB), SUB)
                if number:
                    total = total + sums[rows, :]
                elif add:
                    total = total + before[rows, :]
                sums[rows, :] = total
            return carry

        lax.fori_loop(0, half * tiles, pair, 0, unroll=16)
    if not last:
        return

    def finish(index, carry):
        block = index // SUB
        signal = index % SUB
        value = sums[pl.ds(block * LANES * SUB + signal, LANES, stride=SUB), :]
        value = jnp.transpose(value * scale)
        at = 0
        for tile in range(2):
            for visit in range(VISITS):
                for part in range(2):
                    out[part, signal, value_of(PLACES[visit], place[1]), tile * (half // 4) + block] = value[at : at + SUB]
                    at += SUB
        return carry

    lax.fori_loop(0, half // 4 * SUB, finish, 0)


def correlate(arrays, pieces, per_group, place, scale, before, last, wait=(), cost=10**3):
    signals = TILE // 2
    rows = per_group // 2 * H * SUB
    place = after(place, *wait)
    shape = (2, signals, VISITS, per_group // 4, SUB, LANES) if last else (rows, LANES)
    operands = list(arrays) + ([] if before is None else [before])
    vmem = pl.BlockSpec(memory_space=pltpu.VMEM)
    return pl.pallas_call(
        functools.partial(correlate_kernel, pieces, per_group, scale, before is not None, last),
        grid_spec=pltpu.PrefetchScalarGridSpec(
            num_scalar_prefetch=1,
            grid=(),
            in_specs=[vmem] * len(operands),
            out_specs=vmem,
            scratch_shapes=[pltpu.VMEM((rows, LANES), F32)] if last else [],
        ),
        out_shape=jax.ShapeDtypeStruct(shape, F32),
        compiler_params=pltpu.CompilerParams(vmem_limit_bytes=24 << 20),
        input_output_aliases={} if before is None or last else {len(operands): 0},
        cost_estimate=pl.CostEstimate(flops=cost, bytes_accessed=0, transcendentals=0),
    )(place, *operands)


def stacked(voltage):
    s, f = voltage.shape[:2]
    return voltage.reshape(s, f, 2, H, LANES).transpose(0, 1, 3, 2, 4).reshape(s, f, ROWS, LANES)


def natural(out):
    parts, s, visits, i, t, lanes = out.shape
    return out.transpose(0, 1, 2, 4, 3, 5).reshape(parts, s, visits * t, i * lanes)


def shifted(block, axis, distance):
    size = lax.axis_size(axis)
    return lax.ppermute(block, axis, [(i, (i + distance) % size) for i in range(size)])


def farther(block):
    size = lax.axis_size("stn")
    rest = lax.ppermute(block, "stn", [(i, (i + 1 if i % 2 == 0 else i + 3) % size) for i in range(size)])
    return shifted(block, "stn", 2), rest


def evenly(block):
    size = lax.axis_size("stn")
    ways = [(i, (i + 1 if i % 2 == 0 else i + 3) % size) for i in range(size) if i % 4 < 3]
    return shifted(block, "stn", 2), lax.ppermute(block, "stn", ways)


def relayed(two):
    return lax.ppermute(two, "stn", [(i, i + 1) for i in range(lax.axis_size("stn")) if i % 4 == 1])


def exchanged(block):
    return lax.ppermute(block, "stn", [(i, i ^ 1) for i in range(lax.axis_size("stn"))])


def paired(volts, fir_taps, place, correlated):
    frames = volts.shape[1]
    me = lax.axis_index("tm")
    sizes = [K2 // 2, K2 // 2]
    swap = [(0, 1), (1, 0)]
    edge = TAPS // 2
    last = frames // edge
    many, few = TAPS * H // LANES, edge * H // LANES
    volts, edge_frames, *fixed = prepare(volts, fir_taps, place, 2, (last - 1, 0), edge)
    visiting = lax.ppermute(edge_frames, "tm", swap)
    own_a, away_a = spectra(
        [(volts, TAPS, 0, 0, (0, 1)), (volts, TAPS, (0, 1), TAPS, 1)], TAPS, fixed, place, 2, sizes
    )
    got_a = lax.ppermute(away_a, "tm", swap)
    two_a, rest_a = farther(own_a)
    own_b, away_b = spectra(
        [(volts, TAPS, 0, 0, 1), (volts, TAPS, 1, TAPS, 1)], TAPS, fixed, place, 2, sizes, (1, 0), (own_a,)
    )
    own_c, away_c = spectra(
        [
            (volts, edge, (last - 2, 0), (0, edge), 1),
            (volts, edge, (last - 1, 1), (edge, 2 * edge), 1),
            (visiting, edge, 0, (2 * edge, 0), 1),
        ],
        edge, fixed, place, 2, sizes, 1, (own_b, two_a),
    )
    got_a, own_c, away_b, away_c, two_a = lax.optimization_barrier((got_a, own_c, away_b, away_c, two_a))
    two_g, rest_g = evenly(got_a)
    got_b = lax.ppermute(away_b, "tm", [(0, 1)])
    pair_a = exchanged(two_a)
    first = [(many, [(0, 0, 0)])]
    sums = correlated([own_a, pair_a, two_a, rest_a], first, None, False)
    got_b, away_c, sums = lax.optimization_barrier((got_b, away_c, sums))
    got_c = lax.ppermute(away_c, "tm", swap)
    piece_b = jnp.where(me == 0, own_b, got_b)
    two_b, rest_b = evenly(piece_b)
    pair_g, relay_g = exchanged(two_g), relayed(two_g)
    sums = correlated([got_a, pair_g, two_g, (rest_g, relay_g)], first, sums, False)
    piece_c = jnp.concatenate([own_c, got_c], axis=1)
    two_c, rest_c = farther(piece_c)
    pair_b, relay_b = exchanged(two_b), relayed(two_b)
    sums = correlated([piece_b, pair_b, two_b, (rest_b, relay_b)], first, sums, False)
    pair_c = exchanged(after(two_c, sums))
    return correlated([piece_c, pair_c, two_c, rest_c], [(few, [(0, 0, 0), (0, 0, few)])], sums, True)


def general(volts, fir_taps, place, correlated):
    groups = lax.axis_size("tm")
    frames = volts.shape[1]
    volts, edge_frames, *fixed = prepare(volts, fir_taps, place, groups, frames // TAPS - 1, TAPS)
    history = lax.ppermute(edge_frames, "tm", [(i, i + 1) for i in range(groups - 1)])
    parts = [(history, TAPS, 0, 0, 1)] + [(volts, TAPS, i, TAPS * (i + 1), 1) for i in range(frames // TAPS)]
    spectrum = spectra(parts, frames, fixed, place, groups, [K2])[0]
    spectrum = lax.all_to_all(spectrum, "tm", split_axis=0, concat_axis=0, tiled=True)
    two, rest = farther(spectrum)
    spots = [(0, K2 // groups * t, 0) for t in range(groups)]
    return correlated([spectrum, exchanged(two), two, rest], [(spectrum.shape[1], spots)], None, True)


def local(voltage, fir_taps):
    groups = lax.axis_size("tm")
    place = jnp.stack([lax.axis_index("tm"), lax.axis_index("stn") % 2]).astype(jnp.int32)
    scale = 1.0 / (groups * voltage.shape[1])

    def correlated(arrays, pieces, before, last, wait=(), cost=10**3):
        flat, spots_of = [], []
        for array in arrays:
            parts = array if isinstance(array, tuple) else (array,)
            spots_of.append(tuple(range(len(flat), len(flat) + len(parts))))
            flat += parts
        laid = [(tiles, [[(where, r, c) for _, r, c in spots] for where in spots_of]) for tiles, spots in pieces]
        return correlate(flat, laid, K2 // groups, place, scale, before, last, wait, cost)

    run = paired if groups == 2 else general
    return natural(run(stacked(voltage), fir_taps, place, correlated))


def solution(mesh):
    return jax.shard_map(
        local,
        mesh=mesh,
        in_specs=(P("stn", "tm", None, None), P()),
        out_specs=P(None, "stn", None, "tm"),
        check_vma=False,
    )
```

```python
import functools
import math

import jax
import jax.numpy as jnp
import numpy as np
from jax import lax
from jax.experimental import pallas as pl
from jax.experimental.pallas import tpu as pltpu
from jax.sharding import PartitionSpec as P

NCH = 4096
CHANS = 2048
TAPS = 16
VISITS = 4
H = 32
LANES = 128
ROWS = 2 * H
K2 = CHANS // H
STEP = 8
TILE = 16
PLACES = (0, (1, 3), 2, (3, 1))
MEMBERS = 4
PAD = 8
SUB = 8
BF16 = jnp.bfloat16
F32 = jnp.float32


def angles(rows, columns, modulus):
    turns = np.outer(rows, columns) % modulus
    return turns.astype(np.float64) * (2.0 * math.pi / modulus)


def stage_one_table():
    theta = angles(np.arange(H), np.arange(H), H)
    cosine, sine = np.cos(theta), np.sin(theta)
    table = np.zeros((2, H, H, 2))
    table[0, :, :, 0], table[0, :, :, 1] = cosine, sine
    table[1, :, :, 0], table[1, :, :, 1] = -sine, cosine
    return np.pad(table.reshape(ROWS, ROWS), ((0, 0), (0, 2 * LANES - ROWS)))


def turn_table():
    theta = angles(np.arange(H), np.arange(LANES), NCH)
    return np.concatenate([np.cos(theta), np.sin(theta)], axis=1)


def stage_two_table(groups):
    theta = angles(np.arange(K2), np.arange(LANES), LANES)
    cosine, sine = np.cos(theta) / math.sqrt(NCH), np.sin(theta) / math.sqrt(NCH)
    real = np.concatenate([cosine, sine], 1).reshape(groups, 1, K2 // groups, 2 * LANES)
    imag = np.concatenate([-sine, cosine], 1).reshape(groups, 1, K2 // groups, 2 * LANES)
    return np.concatenate([real, imag], 1).reshape(2 * K2, 2 * LANES)


def halves(value):
    high = value.astype(BF16)
    return high, (value - high.astype(F32)).astype(BF16)


def dot(left, right):
    return lax.dot_general(left, right, (((1,), (0,)), ((), ())), preferred_element_type=F32)


def dot_nt(left, right):
    return lax.dot_general(left, right, (((1,), (1,)), ((), ())), preferred_element_type=F32)


def value_of(number, group):
    if isinstance(number, int):
        return number
    return number[0] + (number[1] - number[0]) * group


def prepare_kernel(edge_block, swapped, place, volts_source, taps_source, table_source, turn_source, volts, edge, taps, one, two, turn, done, taps_ref, table_ref):
    count = edge.shape[1]
    start = pl.multiple_of(value_of(edge_block, place[0]) * count, count)
    copies = [
        pltpu.make_async_copy(taps_source, taps_ref, done.at[0]),
        pltpu.make_async_copy(table_source, table_ref, done.at[1]),
        pltpu.make_async_copy(volts_source.at[:, pl.ds(start, count)], edge, done.at[2]),
        pltpu.make_async_copy(volts_source, volts, done.at[3]),
        pltpu.make_async_copy(turn_source, turn, done.at[4]),
    ]
    for copy in copies:
        copy.start()
    copies[0].wait()
    copies[1].wait()
    for h in range(H):
        for half in range(TAPS // SUB):
            tile = taps_ref[pl.ds(half * SUB, SUB), pl.ds(h * LANES, LANES)]
            for r in range(2):
                taps[pl.ds(half * SUB * ROWS + 2 * h + r, SUB, stride=ROWS), :] = tile
    high, low = halves(table_ref[:ROWS, :ROWS])
    one[...] = jnp.concatenate([high, high, low], axis=1)
    start = pl.multiple_of(ROWS + place[0] * (2 * K2 * swapped), SUB)
    high, low = halves(table_ref[pl.ds(start, 2 * K2), :])
    two[0] = high
    two[1] = low
    for copy in copies[2:]:
        copy.wait()


def prepare(volts, fir_taps, place, groups, edge_block, edge_frames):
    signals, frames = volts.shape[:2]
    two = stage_two_table(groups)
    table = np.concatenate([stage_one_table(), two, np.roll(two, K2, axis=0)]).astype(np.float32)
    vmem = pl.BlockSpec(memory_space=pltpu.VMEM)
    return pl.pallas_call(
        functools.partial(prepare_kernel, edge_block, int(groups == 2)),
        grid_spec=pltpu.PrefetchScalarGridSpec(
            num_scalar_prefetch=1,
            grid=(),
            in_specs=[pl.BlockSpec(memory_space=pl.ANY)] * 4,
            out_specs=[vmem] * 6,
            scratch_shapes=[
                pltpu.SemaphoreType.DMA((5,)),
                pltpu.VMEM(fir_taps.shape, F32),
                pltpu.VMEM(table.shape, F32),
            ],
        ),
        out_shape=[
            jax.ShapeDtypeStruct((signals, frames, ROWS, LANES), BF16),
            jax.ShapeDtypeStruct((signals, edge_frames, ROWS, LANES), BF16),
            jax.ShapeDtypeStruct((TAPS * ROWS, LANES), F32),
            jax.ShapeDtypeStruct((ROWS, 3 * ROWS), BF16),
            jax.ShapeDtypeStruct((2, 2 * K2, 2 * LANES), BF16),
            jax.ShapeDtypeStruct((H, 2 * LANES), F32),
        ],
        compiler_params=pltpu.CompilerParams(vmem_limit_bytes=24 << 20),
    )(
        place,
        *[
            pltpu.with_memory_space_constraint(x, pltpu.HBM)
            for x in (volts, fir_taps, jnp.asarray(table), jnp.asarray(turn_table(), F32))
        ],
    )


def spectra_kernel(groups, parts, out_frames, run, place, *refs):
    part_refs, refs = refs[: len(parts)], refs[len(parts) :]
    taps, one, two, turn = refs[:4]
    outs, (ext, filtered, turned, staged) = refs[4:-4], refs[-4:]
    step, steps, members = pl.program_id(0), pl.num_programs(0), MEMBERS
    per_group = K2 // groups
    share = LANES // out_frames
    tiles = H // share
    pairs = tiles // 2
    frame_rows, row_rows = ROWS + PAD, tiles * TILE + PAD

    def load(member):
        signal = step * members + member
        for (frames, block, start, valid), ref in zip(parts, part_refs):
            first = value_of(block, place[0]) * frames
            start = value_of(start, place[0])
            valid = value_of(valid, place[0])

            def fill(ref=ref, frames=frames, first=first, start=start):
                for f in range(frames):
                    ext[member, start + f] = ref[signal, first + f].astype(F32)

            def clear(frames=frames, start=start):
                for f in range(frames):
                    ext[member, start + f] = jnp.zeros((ROWS, LANES), F32)

            if isinstance(valid, int):
                fill() if valid else clear()
            else:
                pl.when(valid == 1)(fill)
                pl.when(valid == 0)(clear)

    def filter_rows(member, q):
        rows = pl.ds(pl.multiple_of(q * SUB, SUB), SUB)
        tap = [taps[pl.ds(pl.multiple_of(m * ROWS + q * SUB, SUB), SUB), :] for m in range(TAPS)]
        for f in range(out_frames):
            total = tap[0] * ext[member, f + 1, rows]
            for m in range(1, TAPS):
                total = total + tap[m] * ext[member, f + 1 + m, rows]
            filtered[member, f, rows] = total

    def first_stage(member):
        cosine = turn[:, :LANES]
        sine = turn[:, LANES:]
        for g in range(out_frames // STEP):
            block = jnp.concatenate([filtered[member, g * STEP + f] for f in range(STEP)], axis=1)
            high, low = halves(block)
            first = dot(one[...], jnp.concatenate([high, low, high], axis=0))
            for f in range(STEP):
                real = first[:H, f * LANES : (f + 1) * LANES]
                imag = first[H:, f * LANES : (f + 1) * LANES]
                at = (g * STEP + f) * frame_rows
                turned[member, at : at + H, :] = real * cosine + imag * sine
                turned[member, at + H : at + ROWS, :] = imag * cosine - real * sine

    def second_stage(member, pair):
        rows = []
        for k1 in range(2 * pair * share, 2 * (pair + 1) * share):
            for f in range(0, out_frames, SUB):
                rows.append(
                    jnp.concatenate(
                        [turned[member, pl.ds(f * frame_rows + p * H + k1, SUB, stride=frame_rows), :] for p in range(2)],
                        axis=1,
                    )
                )
        high, low = halves(jnp.concatenate(rows, axis=0))
        spectrum = dot_nt(two[0], high) + dot_nt(two[1], high) + dot_nt(two[0], low)
        for k in range(2):
            for t in range(groups):
                for p in range(2):
                    for k2 in range(0, per_group, SUB):
                        row = (t * 2 + p) * per_group + k2
                        start = (t * per_group + k2) * row_rows + (2 * pair + k) * TILE + p * SUB
                        staged[pl.ds(start + step * members + member, SUB, stride=row_rows), :] = spectrum[
                            row : row + SUB, k * LANES : (k + 1) * LANES
                        ]

    def write():
        at = 0
        for out in outs:

            def write_row(k2, carry):
                for k in range(tiles):
                    start = pl.multiple_of((at + k2) * row_rows + k * TILE, PAD)
                    out[k2, k] = staged[pl.ds(start, TILE), :].astype(BF16)
                return carry

            lax.fori_loop(0, out.shape[0], write_row, 0, unroll=2)
            at += out.shape[0]

    def body():
        for member in range(members):
            load(member)

        def filter_one(index, carry):
            filter_rows(index // (ROWS // SUB), index % (ROWS // SUB))
            return carry

        lax.fori_loop(0, members * (ROWS // SUB), filter_one, 0)
        for member in range(members):
            first_stage(member)
        for member in range(members):
            for pair in range(pairs):
                second_stage(member, pair)

        pl.when(step == steps - 1)(write)

    if isinstance(run, int):
        body()
    else:
        pl.when(value_of(run, place[0]) == 1)(body)


def after(value, *others):
    return lax.optimization_barrier((value, *others))[0]


def spectra(parts, out_frames, fixed, place, groups, sizes, run=1, wait=(), cost=10**6):
    signals = parts[0][0].shape[0]
    place = after(place, *wait)
    tiles = H * out_frames // LANES
    shapes = [(n, tiles, TILE, LANES) for n in sizes]
    return pl.pallas_call(
        functools.partial(spectra_kernel, groups, tuple(part[1:] for part in parts), out_frames, run),
        grid_spec=pltpu.PrefetchScalarGridSpec(
            num_scalar_prefetch=1,
            grid=(signals // MEMBERS,),
            in_specs=[pl.BlockSpec(memory_space=pltpu.VMEM)] * (len(parts) + 4),
            out_specs=[pl.BlockSpec(shape, lambda s, place: (0, 0, 0, 0)) for shape in shapes],
            scratch_shapes=[
                pltpu.VMEM((MEMBERS, TAPS + out_frames, ROWS, LANES), F32),
                pltpu.VMEM((MEMBERS, out_frames, ROWS, LANES), F32),
                pltpu.VMEM((MEMBERS, out_frames * (ROWS + PAD), LANES), F32),
                pltpu.VMEM((K2 * (tiles * TILE + PAD), LANES), F32),
            ],
        ),
        out_shape=[jax.ShapeDtypeStruct(shape, BF16) for shape in shapes],
        compiler_params=pltpu.CompilerParams(vmem_limit_bytes=32 << 20),
        cost_estimate=pl.CostEstimate(flops=cost, bytes_accessed=0, transcendentals=0),
    )(place, *[part[0] for part in parts], *fixed)


def after(value, *others):
    return lax.optimization_barrier((value, *others))[0]


def correlate_kernel(pieces, per_group, scale, add, last, place, *refs):
    refs = list(refs)
    sums = refs.pop() if last else None
    out = refs.pop()
    before = refs.pop() if add else None
    if not last:
        sums = out
    half = per_group // 2
    lane = lax.broadcasted_iota(jnp.int32, (SUB, LANES), 1)
    first_tile = lane < LANES // 2
    real_lane = lane % TILE < SUB
    sign = jnp.where(real_lane, 1.0, -1.0).astype(F32)

    def fetch(spot, tile, k2, k1):
        arrays, row, column = spot
        values = [refs[array][row + tile * half + k2, column + k1] for array in arrays]
        return values[0] if len(values) == 1 else values[0] + values[1]

    for number, piece in enumerate(pieces):
        tiles, piece = piece
        share = H // tiles
        where = lax.broadcasted_iota(jnp.int32, (TILE, LANES), 1) // (LANES // share)

        def pair(index, carry):
            k2 = index // tiles
            k1 = index % tiles
            own, other = [], []
            for position in range(len(piece[0])):
                rows = []
                for tile in range(2):
                    a = fetch(piece[0][position], tile, k2, k1)
                    rows += [jnp.where(where == c, a, jnp.zeros_like(a)) for c in range(share)]
                own.append(jnp.concatenate(rows, axis=0))
                rows = []
                for tile in range(2):
                    for visit in range(VISITS):
                        rows.append(fetch(piece[visit][position], tile, k2, k1))
                other.append(jnp.concatenate(rows, axis=0))
            product = dot_nt(jnp.concatenate(own, axis=1), jnp.concatenate(other, axis=1))
            for c in range(share):
                value = []
                for p in range(2):
                    at = [((tile * share + c) * 2 + p) * SUB for tile in range(2)]
                    value.append(
                        jnp.where(first_tile, product[at[0] : at[0] + SUB], product[at[1] : at[1] + SUB])
                    )
                turned = jnp.where(
                    real_lane, pltpu.roll(value[1], LANES - SUB, 1), pltpu.roll(value[1], SUB, 1)
                )
                total = value[0] * sign + turned
                channel = k2 // 4 * LANES + k2 % 4 * H + k1 * share + c
                rows = pl.ds(pl.multiple_of(channel * SUB, SUB), SUB)
                if number:
                    total = total + sums[rows, :]
                elif add:
                    total = total + before[rows, :]
                sums[rows, :] = total
            return carry

        lax.fori_loop(0, half * tiles, pair, 0, unroll=16)
    if not last:
        return

    def finish(index, carry):
        block = index // SUB
        signal = index % SUB
        value = sums[pl.ds(block * LANES * SUB + signal, LANES, stride=SUB), :]
        value = jnp.transpose(value * scale)
        at = 0
        for tile in range(2):
            for visit in range(VISITS):
                for part in range(2):
                    out[part, signal, value_of(PLACES[visit], place[1]), tile * (half // 4) + block] = value[at : at + SUB]
                    at += SUB
        return carry

    lax.fori_loop(0, half // 4 * SUB, finish, 0)


def correlate(arrays, pieces, per_group, place, scale, before, last, wait=(), cost=10**3):
    signals = TILE // 2
    rows = per_group // 2 * H * SUB
    place = after(place, *wait)
    shape = (2, signals, VISITS, per_group // 4, SUB, LANES) if last else (rows, LANES)
    operands = list(arrays) + ([] if before is None else [before])
    vmem = pl.BlockSpec(memory_space=pltpu.VMEM)
    result = pl.pallas_call(
        functools.partial(correlate_kernel, pieces, per_group, scale, before is not None, last),
        grid_spec=pltpu.PrefetchScalarGridSpec(
            num_scalar_prefetch=1,
            grid=(),
            in_specs=[vmem] * len(operands),
            out_specs=vmem,
            scratch_shapes=[pltpu.VMEM((rows, LANES), F32)] if last else [],
        ),
        out_shape=jax.ShapeDtypeStruct(shape, F32),
        compiler_params=pltpu.CompilerParams(vmem_limit_bytes=24 << 20),
        input_output_aliases={} if before is None or last else {len(operands): 0},
        cost_estimate=pl.CostEstimate(flops=cost, bytes_accessed=0, transcendentals=0),
    )(place, *operands)
    return result if last else pltpu.with_memory_space_constraint(result, pltpu.VMEM)


def stacked(voltage):
    s, f = voltage.shape[:2]
    return voltage.reshape(s, f, 2, H, LANES).transpose(0, 1, 3, 2, 4).reshape(s, f, ROWS, LANES)


def natural(out):
    parts, s, visits, i, t, lanes = out.shape
    return out.transpose(0, 1, 2, 4, 3, 5).reshape(parts, s, visits * t, i * lanes)


def shifted(block, axis, distance):
    size = lax.axis_size(axis)
    return lax.ppermute(block, axis, [(i, (i + distance) % size) for i in range(size)])


def farther(block):
    size = lax.axis_size("stn")
    rest = lax.ppermute(block, "stn", [(i, (i + 1 if i % 2 == 0 else i + 3) % size) for i in range(size)])
    return shifted(block, "stn", 2), rest


def evenly(block):
    size = lax.axis_size("stn")
    ways = [(i, (i + 1 if i % 2 == 0 else i + 3) % size) for i in range(size) if i % 4 < 3]
    return shifted(block, "stn", 2), lax.ppermute(block, "stn", ways)


def relayed(two):
    return lax.ppermute(two, "stn", [(i, i + 1) for i in range(lax.axis_size("stn")) if i % 4 == 1])


def exchanged(block):
    return lax.ppermute(block, "stn", [(i, i ^ 1) for i in range(lax.axis_size("stn"))])


def paired(volts, fir_taps, place, correlated):
    frames = volts.shape[1]
    me = lax.axis_index("tm")
    sizes = [K2 // 2, K2 // 2]
    swap = [(0, 1), (1, 0)]
    edge = TAPS // 2
    last = frames // edge
    many, few = TAPS * H // LANES, edge * H // LANES
    volts, edge_frames, *fixed = prepare(volts, fir_taps, place, 2, (last - 1, 0), edge)
    visiting = lax.ppermute(edge_frames, "tm", swap)
    own_a, away_a = spectra(
        [(volts, TAPS, 0, 0, (0, 1)), (volts, TAPS, (0, 1), TAPS, 1)], TAPS, fixed, place, 2, sizes
    )
    got_a = lax.ppermute(away_a, "tm", swap)
    two_a, rest_a = farther(own_a)
    own_b, away_b = spectra(
        [(volts, TAPS, 0, 0, 1), (volts, TAPS, 1, TAPS, 1)], TAPS, fixed, place, 2, sizes, (1, 0), (own_a,)
    )
    own_c, away_c = spectra(
        [
            (volts, edge, (last - 2, 0), (0, edge), 1),
            (volts, edge, (last - 1, 1), (edge, 2 * edge), 1),
            (visiting, edge, 0, (2 * edge, 0), 1),
        ],
        edge, fixed, place, 2, sizes, 1, (own_b, two_a),
    )
    got_a, own_c, away_b, away_c, two_a = lax.optimization_barrier((got_a, own_c, away_b, away_c, two_a))
    two_g, rest_g = evenly(got_a)
    got_b = lax.ppermute(away_b, "tm", [(0, 1)])
    pair_a = exchanged(two_a)
    first = [(many, [(0, 0, 0)])]
    sums = correlated([own_a, pair_a, two_a, rest_a], first, None, False)
    got_b, away_c, sums = lax.optimization_barrier((got_b, away_c, sums))
    got_c = lax.ppermute(away_c, "tm", swap)
    piece_b = jnp.where(me == 0, own_b, got_b)
    two_b, rest_b = farther(piece_b)
    pair_g, relay_g = exchanged(two_g), relayed(two_g)
    sums = correlated([got_a, pair_g, two_g, (rest_g, relay_g)], first, sums, False)
    piece_c = jnp.concatenate([after(own_c, relay_g), got_c], axis=1)
    two_c, rest_c = farther(piece_c)
    pair_b = exchanged(two_b)
    sums = correlated([piece_b, pair_b, two_b, rest_b], first, sums, False)
    pair_c = exchanged(after(two_c, rest_c, sums))
    return correlated([piece_c, pair_c, two_c, rest_c], [(few, [(0, 0, 0), (0, 0, few)])], sums, True)


def general(volts, fir_taps, place, correlated):
    groups = lax.axis_size("tm")
    frames = volts.shape[1]
    volts, edge_frames, *fixed = prepare(volts, fir_taps, place, groups, frames // TAPS - 1, TAPS)
    history = lax.ppermute(edge_frames, "tm", [(i, i + 1) for i in range(groups - 1)])
    parts = [(history, TAPS, 0, 0, 1)] + [(volts, TAPS, i, TAPS * (i + 1), 1) for i in range(frames // TAPS)]
    spectrum = spectra(parts, frames, fixed, place, groups, [K2])[0]
    spectrum = lax.all_to_all(spectrum, "tm", split_axis=0, concat_axis=0, tiled=True)
    two, rest = farther(spectrum)
    spots = [(0, K2 // groups * t, 0) for t in range(groups)]
    return correlated([spectrum, exchanged(two), two, rest], [(spectrum.shape[1], spots)], None, True)


def local(voltage, fir_taps):
    groups = lax.axis_size("tm")
    place = jnp.stack([lax.axis_index("tm"), lax.axis_index("stn") % 2]).astype(jnp.int32)
    scale = 1.0 / (groups * voltage.shape[1])

    def correlated(arrays, pieces, before, last, wait=(), cost=10**3):
        flat, spots_of = [], []
        for array in arrays:
            parts = array if isinstance(array, tuple) else (array,)
            spots_of.append(tuple(range(len(flat), len(flat) + len(parts))))
            flat += parts
        laid = [(tiles, [[(where, r, c) for _, r, c in spots] for where in spots_of]) for tiles, spots in pieces]
        return correlate(flat, laid, K2 // groups, place, scale, before, last, wait, cost)

    run = paired if groups == 2 else general
    return natural(run(stacked(voltage), fir_taps, place, correlated))


def solution(mesh):
    return jax.shard_map(
        local,
        mesh=mesh,
        in_specs=(P("stn", "tm", None, None), P()),
        out_specs=P(None, "stn", None, "tm"),
        check_vma=False,
    )
```

```python
import functools
import math

import jax
import jax.numpy as jnp
import numpy as np
from jax import lax
from jax.experimental import pallas as pl
from jax.experimental.pallas import tpu as pltpu
from jax.sharding import PartitionSpec as P

NCH = 4096
CHANS = 2048
TAPS = 16
VISITS = 4
H = 32
LANES = 128
ROWS = 2 * H
K2 = CHANS // H
STEP = 8
TILE = 16
PLACES = (0, (1, 3), 2, (3, 1))
MEMBERS = 4
PAD = 8
SUB = 8
BF16 = jnp.bfloat16
F32 = jnp.float32


def angles(rows, columns, modulus):
    turns = np.outer(rows, columns) % modulus
    return turns.astype(np.float64) * (2.0 * math.pi / modulus)


def stage_one_table():
    theta = angles(np.arange(H), np.arange(H), H)
    cosine, sine = np.cos(theta), np.sin(theta)
    table = np.zeros((2, H, H, 2))
    table[0, :, :, 0], table[0, :, :, 1] = cosine, sine
    table[1, :, :, 0], table[1, :, :, 1] = -sine, cosine
    return np.pad(table.reshape(ROWS, ROWS), ((0, 0), (0, 2 * LANES - ROWS)))


def turn_table():
    theta = angles(np.arange(H), np.arange(LANES), NCH)
    return np.concatenate([np.cos(theta), np.sin(theta)], axis=1)


def stage_two_table(groups):
    theta = angles(np.arange(K2), np.arange(LANES), LANES)
    cosine, sine = np.cos(theta) / math.sqrt(NCH), np.sin(theta) / math.sqrt(NCH)
    real = np.concatenate([cosine, sine], 1).reshape(groups, 1, K2 // groups, 2 * LANES)
    imag = np.concatenate([-sine, cosine], 1).reshape(groups, 1, K2 // groups, 2 * LANES)
    return np.concatenate([real, imag], 1).reshape(2 * K2, 2 * LANES)


def halves(value):
    high = value.astype(BF16)
    return high, (value - high.astype(F32)).astype(BF16)


def dot(left, right):
    return lax.dot_general(left, right, (((1,), (0,)), ((), ())), preferred_element_type=F32)


def dot_nt(left, right):
    return lax.dot_general(left, right, (((1,), (1,)), ((), ())), preferred_element_type=F32)


def value_of(number, group):
    if isinstance(number, int):
        return number
    return number[0] + (number[1] - number[0]) * group


def prepare_kernel(edge_block, swapped, place, volts_source, taps_source, table_source, turn_source, volts, edge, taps, one, two, turn, done, taps_ref, table_ref):
    count = edge.shape[1]
    start = pl.multiple_of(value_of(edge_block, place[0]) * count, count)
    copies = [
        pltpu.make_async_copy(taps_source, taps_ref, done.at[0]),
        pltpu.make_async_copy(table_source, table_ref, done.at[1]),
        pltpu.make_async_copy(volts_source.at[:, pl.ds(start, count)], edge, done.at[2]),
        pltpu.make_async_copy(volts_source, volts, done.at[3]),
        pltpu.make_async_copy(turn_source, turn, done.at[4]),
    ]
    for copy in copies:
        copy.start()
    copies[0].wait()
    copies[1].wait()
    for h in range(H):
        for half in range(TAPS // SUB):
            tile = taps_ref[pl.ds(half * SUB, SUB), pl.ds(h * LANES, LANES)]
            for r in range(2):
                taps[pl.ds(half * SUB * ROWS + 2 * h + r, SUB, stride=ROWS), :] = tile
    high, low = halves(table_ref[:ROWS, :ROWS])
    one[...] = jnp.concatenate([high, high, low], axis=1)
    start = pl.multiple_of(ROWS + place[0] * (2 * K2 * swapped), SUB)
    high, low = halves(table_ref[pl.ds(start, 2 * K2), :])
    two[0] = high
    two[1] = low
    for copy in copies[2:]:
        copy.wait()


def prepare(volts, fir_taps, place, groups, edge_block, edge_frames):
    signals, frames = volts.shape[:2]
    two = stage_two_table(groups)
    table = np.concatenate([stage_one_table(), two, np.roll(two, K2, axis=0)]).astype(np.float32)
    vmem = pl.BlockSpec(memory_space=pltpu.VMEM)
    return pl.pallas_call(
        functools.partial(prepare_kernel, edge_block, int(groups == 2)),
        grid_spec=pltpu.PrefetchScalarGridSpec(
            num_scalar_prefetch=1,
            grid=(),
            in_specs=[pl.BlockSpec(memory_space=pl.ANY)] * 4,
            out_specs=[vmem] * 6,
            scratch_shapes=[
                pltpu.SemaphoreType.DMA((5,)),
                pltpu.VMEM(fir_taps.shape, F32),
                pltpu.VMEM(table.shape, F32),
            ],
        ),
        out_shape=[
            jax.ShapeDtypeStruct((signals, frames, ROWS, LANES), BF16),
            jax.ShapeDtypeStruct((signals, edge_frames, ROWS, LANES), BF16),
            jax.ShapeDtypeStruct((TAPS * ROWS, LANES), F32),
            jax.ShapeDtypeStruct((ROWS, 3 * ROWS), BF16),
            jax.ShapeDtypeStruct((2, 2 * K2, 2 * LANES), BF16),
            jax.ShapeDtypeStruct((H, 2 * LANES), F32),
        ],
        compiler_params=pltpu.CompilerParams(vmem_limit_bytes=24 << 20),
    )(
        place,
        *[
            pltpu.with_memory_space_constraint(x, pltpu.HBM)
            for x in (volts, fir_taps, jnp.asarray(table), jnp.asarray(turn_table(), F32))
        ],
    )


def spectra_kernel(groups, parts, out_frames, run, place, *refs):
    part_refs, refs = refs[: len(parts)], refs[len(parts) :]
    taps, one, two, turn = refs[:4]
    outs, (ext, filtered, turned, staged) = refs[4:-4], refs[-4:]
    step, steps, members = pl.program_id(0), pl.num_programs(0), MEMBERS
    per_group = K2 // groups
    share = LANES // out_frames
    tiles = H // share
    pairs = tiles // 2
    frame_rows, row_rows = ROWS + PAD, tiles * TILE + PAD

    def load(member):
        signal = step * members + member
        for (frames, block, start, valid), ref in zip(parts, part_refs):
            first = value_of(block, place[0]) * frames
            start = value_of(start, place[0])
            valid = value_of(valid, place[0])

            def fill(ref=ref, frames=frames, first=first, start=start):
                for f in range(frames):
                    ext[member, start + f] = ref[signal, first + f].astype(F32)

            def clear(frames=frames, start=start):
                for f in range(frames):
                    ext[member, start + f] = jnp.zeros((ROWS, LANES), F32)

            if isinstance(valid, int):
                fill() if valid else clear()
            else:
                pl.when(valid == 1)(fill)
                pl.when(valid == 0)(clear)

    def filter_rows(member, q):
        rows = pl.ds(pl.multiple_of(q * SUB, SUB), SUB)
        tap = [taps[pl.ds(pl.multiple_of(m * ROWS + q * SUB, SUB), SUB), :] for m in range(TAPS)]
        for f in range(out_frames):
            total = tap[0] * ext[member, f + 1, rows]
            for m in range(1, TAPS):
                total = total + tap[m] * ext[member, f + 1 + m, rows]
            filtered[member, f, rows] = total

    def first_stage(member):
        cosine = turn[:, :LANES]
        sine = turn[:, LANES:]
        for g in range(out_frames // STEP):
            block = jnp.concatenate([filtered[member, g * STEP + f] for f in range(STEP)], axis=1)
            high, low = halves(block)
            first = dot(one[...], jnp.concatenate([high, low, high], axis=0))
            for f in range(STEP):
                real = first[:H, f * LANES : (f + 1) * LANES]
                imag = first[H:, f * LANES : (f + 1) * LANES]
                at = (g * STEP + f) * frame_rows
                turned[member, at : at + H, :] = real * cosine + imag * sine
                turned[member, at + H : at + ROWS, :] = imag * cosine - real * sine

    def second_stage(member, pair):
        rows = []
        for k1 in range(2 * pair * share, 2 * (pair + 1) * share):
            for f in range(0, out_frames, SUB):
                rows.append(
                    jnp.concatenate(
                        [turned[member, pl.ds(f * frame_rows + p * H + k1, SUB, stride=frame_rows), :] for p in range(2)],
                        axis=1,
                    )
                )
        high, low = halves(jnp.concatenate(rows, axis=0))
        spectrum = dot_nt(two[0], high) + dot_nt(two[1], high) + dot_nt(two[0], low)
        for k in range(2):
            for t in range(groups):
                for p in range(2):
                    for k2 in range(0, per_group, SUB):
                        row = (t * 2 + p) * per_group + k2
                        start = (t * per_group + k2) * row_rows + (2 * pair + k) * TILE + p * SUB
                        staged[pl.ds(start + step * members + member, SUB, stride=row_rows), :] = spectrum[
                            row : row + SUB, k * LANES : (k + 1) * LANES
                        ]

    def write():
        at = 0
        for out in outs:

            def write_row(k2, carry):
                for k in range(tiles):
                    start = pl.multiple_of((at + k2) * row_rows + k * TILE, PAD)
                    out[k2, k] = staged[pl.ds(start, TILE), :].astype(BF16)
                return carry

            lax.fori_loop(0, out.shape[0], write_row, 0, unroll=2)
            at += out.shape[0]

    def body():
        for member in range(members):
            load(member)

        def filter_one(index, carry):
            filter_rows(index // (ROWS // SUB), index % (ROWS // SUB))
            return carry

        lax.fori_loop(0, members * (ROWS // SUB), filter_one, 0)
        for member in range(members):
            first_stage(member)
        for member in range(members):
            for pair in range(pairs):
                second_stage(member, pair)

        pl.when(step == steps - 1)(write)

    if isinstance(run, int):
        body()
    else:
        pl.when(value_of(run, place[0]) == 1)(body)


def after(value, *others):
    return lax.optimization_barrier((value, *others))[0]


def spectra(parts, out_frames, fixed, place, groups, sizes, run=1, wait=(), cost=10**6):
    signals = parts[0][0].shape[0]
    place = after(place, *wait)
    tiles = H * out_frames // LANES
    shapes = [(n, tiles, TILE, LANES) for n in sizes]
    return pl.pallas_call(
        functools.partial(spectra_kernel, groups, tuple(part[1:] for part in parts), out_frames, run),
        grid_spec=pltpu.PrefetchScalarGridSpec(
            num_scalar_prefetch=1,
            grid=(signals // MEMBERS,),
            in_specs=[pl.BlockSpec(memory_space=pltpu.VMEM)] * (len(parts) + 4),
            out_specs=[pl.BlockSpec(shape, lambda s, place: (0, 0, 0, 0)) for shape in shapes],
            scratch_shapes=[
                pltpu.VMEM((MEMBERS, TAPS + out_frames, ROWS, LANES), F32),
                pltpu.VMEM((MEMBERS, out_frames, ROWS, LANES), F32),
                pltpu.VMEM((MEMBERS, out_frames * (ROWS + PAD), LANES), F32),
                pltpu.VMEM((K2 * (tiles * TILE + PAD), LANES), F32),
            ],
        ),
        out_shape=[jax.ShapeDtypeStruct(shape, BF16) for shape in shapes],
        compiler_params=pltpu.CompilerParams(vmem_limit_bytes=32 << 20),
        cost_estimate=pl.CostEstimate(flops=cost, bytes_accessed=0, transcendentals=0),
    )(place, *[part[0] for part in parts], *fixed)


def after(value, *others):
    return lax.optimization_barrier((value, *others))[0]


def correlate_kernel(pieces, per_group, scale, add, last, place, *refs):
    refs = list(refs)
    sums = refs.pop() if last else None
    out = refs.pop()
    before = refs.pop() if add else None
    if not last:
        sums = out
    half = per_group // 2
    lane = lax.broadcasted_iota(jnp.int32, (SUB, LANES), 1)
    first_tile = lane < LANES // 2
    real_lane = lane % TILE < SUB
    sign = jnp.where(real_lane, 1.0, -1.0).astype(F32)

    def fetch(spot, tile, k2, k1):
        arrays, row, column = spot
        values = [refs[array][row + tile * half + k2, column + k1] for array in arrays]
        return values[0] if len(values) == 1 else values[0] + values[1]

    for number, piece in enumerate(pieces):
        tiles, piece = piece
        share = H // tiles
        where = lax.broadcasted_iota(jnp.int32, (TILE, LANES), 1) // (LANES // share)

        def pair(index, carry):
            k2 = index // tiles
            k1 = index % tiles
            own, other = [], []
            for position in range(len(piece[0])):
                rows = []
                for tile in range(2):
                    a = fetch(piece[0][position], tile, k2, k1)
                    rows += [jnp.where(where == c, a, jnp.zeros_like(a)) for c in range(share)]
                own.append(jnp.concatenate(rows, axis=0))
                rows = []
                for tile in range(2):
                    for visit in range(VISITS):
                        rows.append(fetch(piece[visit][position], tile, k2, k1))
                other.append(jnp.concatenate(rows, axis=0))
            product = dot_nt(jnp.concatenate(own, axis=1), jnp.concatenate(other, axis=1))
            for c in range(share):
                value = []
                for p in range(2):
                    at = [((tile * share + c) * 2 + p) * SUB for tile in range(2)]
                    value.append(
                        jnp.where(first_tile, product[at[0] : at[0] + SUB], product[at[1] : at[1] + SUB])
                    )
                turned = jnp.where(
                    real_lane, pltpu.roll(value[1], LANES - SUB, 1), pltpu.roll(value[1], SUB, 1)
                )
                total = value[0] * sign + turned
                channel = k2 // 4 * LANES + k2 % 4 * H + k1 * share + c
                rows = pl.ds(pl.multiple_of(channel * SUB, SUB), SUB)
                if number:
                    total = total + sums[rows, :]
                elif add:
                    total = total + before[rows, :]
                sums[rows, :] = total
            return carry

        lax.fori_loop(0, half * tiles, pair, 0, unroll=16)
    if not last:
        return

    def finish(index, carry):
        block = index // SUB
        signal = index % SUB
        value = sums[pl.ds(block * LANES * SUB + signal, LANES, stride=SUB), :]
        value = jnp.transpose(value * scale)
        at = 0
        for tile in range(2):
            for visit in range(VISITS):
                for part in range(2):
                    out[part, signal, value_of(PLACES[visit], place[1]), tile * (half // 4) + block] = value[at : at + SUB]
                    at += SUB
        return carry

    lax.fori_loop(0, half // 4 * SUB, finish, 0)


def correlate(arrays, pieces, per_group, place, scale, before, last, wait=(), cost=10**3):
    signals = TILE // 2
    rows = per_group // 2 * H * SUB
    place = after(place, *wait)
    shape = (2, signals, VISITS, per_group // 4, SUB, LANES) if last else (rows, LANES)
    operands = list(arrays) + ([] if before is None else [before])
    vmem = pl.BlockSpec(memory_space=pltpu.VMEM)
    result = pl.pallas_call(
        functools.partial(correlate_kernel, pieces, per_group, scale, before is not None, last),
        grid_spec=pltpu.PrefetchScalarGridSpec(
            num_scalar_prefetch=1,
            grid=(),
            in_specs=[vmem] * len(operands),
            out_specs=vmem,
            scratch_shapes=[pltpu.VMEM((rows, LANES), F32)] if last else [],
        ),
        out_shape=jax.ShapeDtypeStruct(shape, F32),
        compiler_params=pltpu.CompilerParams(vmem_limit_bytes=24 << 20),
        input_output_aliases={} if before is None or last else {len(operands): 0},
        cost_estimate=pl.CostEstimate(flops=cost, bytes_accessed=0, transcendentals=0),
    )(place, *operands)
    return result if last else pltpu.with_memory_space_constraint(result, pltpu.VMEM)


def stacked(voltage):
    s, f = voltage.shape[:2]
    return voltage.reshape(s, f, 2, H, LANES).transpose(0, 1, 3, 2, 4).reshape(s, f, ROWS, LANES)


def natural(out):
    parts, s, visits, i, t, lanes = out.shape
    return out.transpose(0, 1, 2, 4, 3, 5).reshape(parts, s, visits * t, i * lanes)


def shifted(block, axis, distance):
    size = lax.axis_size(axis)
    return lax.ppermute(block, axis, [(i, (i + distance) % size) for i in range(size)])


def farther(block):
    size = lax.axis_size("stn")
    rest = lax.ppermute(block, "stn", [(i, (i + 1 if i % 2 == 0 else i + 3) % size) for i in range(size)])
    return shifted(block, "stn", 2), rest


def evenly(block):
    size = lax.axis_size("stn")
    ways = [(i, (i + 1 if i % 2 == 0 else i + 3) % size) for i in range(size) if i % 4 < 3]
    return shifted(block, "stn", 2), lax.ppermute(block, "stn", ways)


def relayed(two):
    return lax.ppermute(two, "stn", [(i, i + 1) for i in range(lax.axis_size("stn")) if i % 4 == 1])


def exchanged(block):
    return lax.ppermute(block, "stn", [(i, i ^ 1) for i in range(lax.axis_size("stn"))])


def paired(volts, fir_taps, place, correlated):
    frames = volts.shape[1]
    me = lax.axis_index("tm")
    sizes = [K2 // 2, K2 // 2]
    swap = [(0, 1), (1, 0)]
    edge = TAPS // 2
    last = frames // edge
    many, few = TAPS * H // LANES, edge * H // LANES
    volts, edge_frames, *fixed = prepare(volts, fir_taps, place, 2, (last - 1, 0), edge)
    visiting = lax.ppermute(edge_frames, "tm", swap)
    own_a, away_a = spectra(
        [(volts, TAPS, 0, 0, (0, 1)), (volts, TAPS, (0, 1), TAPS, 1)], TAPS, fixed, place, 2, sizes
    )
    got_a = lax.ppermute(away_a, "tm", swap)
    two_a, rest_a = farther(own_a)
    own_b, away_b = spectra(
        [(volts, TAPS, 0, 0, 1), (volts, TAPS, 1, TAPS, 1)], TAPS, fixed, place, 2, sizes, (1, 0), (own_a,)
    )
    own_c, away_c = spectra(
        [
            (volts, edge, (last - 2, 0), (0, edge), 1),
            (volts, edge, (last - 1, 1), (edge, 2 * edge), 1),
            (visiting, edge, 0, (2 * edge, 0), 1),
        ],
        edge, fixed, place, 2, sizes, 1, (own_b, two_a),
    )
    got_a, own_c, away_b, away_c, two_a = lax.optimization_barrier((got_a, own_c, away_b, away_c, two_a))
    two_g, rest_g = evenly(got_a)
    got_b = lax.ppermute(away_b, "tm", [(0, 1)])
    pair_a = exchanged(two_a)
    first = [(many, [(0, 0, 0)])]
    sums = correlated([own_a, pair_a, two_a, rest_a], first, None, False)
    got_b, away_c, sums = lax.optimization_barrier((got_b, away_c, sums))
    got_c = lax.ppermute(away_c, "tm", swap)
    piece_b = jnp.where(me == 0, own_b, got_b)
    two_b, rest_b = farther(piece_b)
    pair_g, relay_g = exchanged(two_g), relayed(two_g)
    sums = correlated([got_a, pair_g, two_g, (rest_g, relay_g)], first, sums, False)
    piece_c = jnp.concatenate([own_c, got_c], axis=1)
    two_c, rest_c = farther(piece_c)
    pair_b = exchanged(two_b)
    sums = correlated([piece_b, pair_b, two_b, rest_b], first, sums, False)
    pair_c = exchanged(after(two_c, rest_c, sums))
    return correlated([piece_c, pair_c, two_c, rest_c], [(few, [(0, 0, 0), (0, 0, few)])], sums, True)


def general(volts, fir_taps, place, correlated):
    groups = lax.axis_size("tm")
    frames = volts.shape[1]
    volts, edge_frames, *fixed = prepare(volts, fir_taps, place, groups, frames // TAPS - 1, TAPS)
    history = lax.ppermute(edge_frames, "tm", [(i, i + 1) for i in range(groups - 1)])
    parts = [(history, TAPS, 0, 0, 1)] + [(volts, TAPS, i, TAPS * (i + 1), 1) for i in range(frames // TAPS)]
    spectrum = spectra(parts, frames, fixed, place, groups, [K2])[0]
    spectrum = lax.all_to_all(spectrum, "tm", split_axis=0, concat_axis=0, tiled=True)
    two, rest = farther(spectrum)
    spots = [(0, K2 // groups * t, 0) for t in range(groups)]
    return correlated([spectrum, exchanged(two), two, rest], [(spectrum.shape[1], spots)], None, True)


def local(voltage, fir_taps):
    groups = lax.axis_size("tm")
    place = jnp.stack([lax.axis_index("tm"), lax.axis_index("stn") % 2]).astype(jnp.int32)
    scale = 1.0 / (groups * voltage.shape[1])

    def correlated(arrays, pieces, before, last, wait=(), cost=10**3):
        flat, spots_of = [], []
        for array in arrays:
            parts = array if isinstance(array, tuple) else (array,)
            spots_of.append(tuple(range(len(flat), len(flat) + len(parts))))
            flat += parts
        laid = [(tiles, [[(where, r, c) for _, r, c in spots] for where in spots_of]) for tiles, spots in pieces]
        return correlate(flat, laid, K2 // groups, place, scale, before, last, wait, cost)

    run = paired if groups == 2 else general
    return natural(run(stacked(voltage), fir_taps, place, correlated))


def solution(mesh):
    return jax.shard_map(
        local,
        mesh=mesh,
        in_specs=(P("stn", "tm", None, None), P()),
        out_specs=P(None, "stn", None, "tm"),
        check_vma=False,
    )
```

```python
import functools
import math

import jax
import jax.numpy as jnp
import numpy as np
from jax import lax
from jax.experimental import pallas as pl
from jax.experimental.pallas import tpu as pltpu
from jax.sharding import PartitionSpec as P

NCH = 4096
CHANS = 2048
TAPS = 16
VISITS = 4
H = 32
LANES = 128
ROWS = 2 * H
K2 = CHANS // H
STEP = 8
TILE = 16
PLACES = (0, (1, 3), 2, (3, 1))
MEMBERS = 4
PAD = 8
SUB = 8
BF16 = jnp.bfloat16
F32 = jnp.float32


def angles(rows, columns, modulus):
    turns = np.outer(rows, columns) % modulus
    return turns.astype(np.float64) * (2.0 * math.pi / modulus)


def stage_one_table():
    theta = angles(np.arange(H), np.arange(H), H)
    cosine, sine = np.cos(theta), np.sin(theta)
    table = np.zeros((2, H, H, 2))
    table[0, :, :, 0], table[0, :, :, 1] = cosine, sine
    table[1, :, :, 0], table[1, :, :, 1] = -sine, cosine
    return np.pad(table.reshape(ROWS, ROWS), ((0, 0), (0, 2 * LANES - ROWS)))


def turn_table():
    theta = angles(np.arange(H), np.arange(LANES), NCH)
    return np.concatenate([np.cos(theta), np.sin(theta)], axis=1)


def stage_two_table(groups):
    theta = angles(np.arange(K2), np.arange(LANES), LANES)
    cosine, sine = np.cos(theta) / math.sqrt(NCH), np.sin(theta) / math.sqrt(NCH)
    real = np.concatenate([cosine, sine], 1).reshape(groups, 1, K2 // groups, 2 * LANES)
    imag = np.concatenate([-sine, cosine], 1).reshape(groups, 1, K2 // groups, 2 * LANES)
    return np.concatenate([real, imag], 1).reshape(2 * K2, 2 * LANES)


def halves(value):
    high = value.astype(BF16)
    return high, (value - high.astype(F32)).astype(BF16)


def dot(left, right):
    return lax.dot_general(left, right, (((1,), (0,)), ((), ())), preferred_element_type=F32)


def dot_nt(left, right):
    return lax.dot_general(left, right, (((1,), (1,)), ((), ())), preferred_element_type=F32)


def value_of(number, group):
    if isinstance(number, int):
        return number
    return number[0] + (number[1] - number[0]) * group


def prepare_kernel(edge_block, swapped, place, volts_source, taps_source, table_source, turn_source, volts, edge, taps, one, two, turn, done, taps_ref, table_ref):
    count = edge.shape[1]
    start = pl.multiple_of(value_of(edge_block, place[0]) * count, count)
    copies = [
        pltpu.make_async_copy(taps_source, taps_ref, done.at[0]),
        pltpu.make_async_copy(table_source, table_ref, done.at[1]),
        pltpu.make_async_copy(volts_source.at[:, pl.ds(start, count)], edge, done.at[2]),
        pltpu.make_async_copy(volts_source, volts, done.at[3]),
        pltpu.make_async_copy(turn_source, turn, done.at[4]),
    ]
    for copy in copies:
        copy.start()
    copies[0].wait()
    copies[1].wait()
    for h in range(H):
        for half in range(TAPS // SUB):
            tile = taps_ref[pl.ds(half * SUB, SUB), pl.ds(h * LANES, LANES)]
            for r in range(2):
                taps[pl.ds(half * SUB * ROWS + 2 * h + r, SUB, stride=ROWS), :] = tile
    high, low = halves(table_ref[:ROWS, :ROWS])
    one[...] = jnp.concatenate([high, high, low], axis=1)
    start = pl.multiple_of(ROWS + place[0] * (2 * K2 * swapped), SUB)
    high, low = halves(table_ref[pl.ds(start, 2 * K2), :])
    two[0] = high
    two[1] = low
    for copy in copies[2:]:
        copy.wait()


def prepare(volts, fir_taps, place, groups, edge_block, edge_frames):
    signals, frames = volts.shape[:2]
    two = stage_two_table(groups)
    table = np.concatenate([stage_one_table(), two, np.roll(two, K2, axis=0)]).astype(np.float32)
    vmem = pl.BlockSpec(memory_space=pltpu.VMEM)
    return pl.pallas_call(
        functools.partial(prepare_kernel, edge_block, int(groups == 2)),
        grid_spec=pltpu.PrefetchScalarGridSpec(
            num_scalar_prefetch=1,
            grid=(),
            in_specs=[pl.BlockSpec(memory_space=pl.ANY)] * 4,
            out_specs=[vmem] * 6,
            scratch_shapes=[
                pltpu.SemaphoreType.DMA((5,)),
                pltpu.VMEM(fir_taps.shape, F32),
                pltpu.VMEM(table.shape, F32),
            ],
        ),
        out_shape=[
            jax.ShapeDtypeStruct((signals, frames, ROWS, LANES), BF16),
            jax.ShapeDtypeStruct((signals, edge_frames, ROWS, LANES), BF16),
            jax.ShapeDtypeStruct((TAPS * ROWS, LANES), F32),
            jax.ShapeDtypeStruct((ROWS, 3 * ROWS), BF16),
            jax.ShapeDtypeStruct((2, 2 * K2, 2 * LANES), BF16),
            jax.ShapeDtypeStruct((H, 2 * LANES), F32),
        ],
        compiler_params=pltpu.CompilerParams(vmem_limit_bytes=24 << 20),
    )(
        place,
        *[
            pltpu.with_memory_space_constraint(x, pltpu.HBM)
            for x in (volts, fir_taps, jnp.asarray(table), jnp.asarray(turn_table(), F32))
        ],
    )


def spectra_kernel(groups, parts, out_frames, run, place, *refs):
    part_refs, refs = refs[: len(parts)], refs[len(parts) :]
    taps, one, two, turn = refs[:4]
    outs, (ext, filtered, turned, staged) = refs[4:-4], refs[-4:]
    step, steps, members = pl.program_id(0), pl.num_programs(0), MEMBERS
    per_group = K2 // groups
    share = LANES // out_frames
    tiles = H // share
    pairs = tiles // 2
    frame_rows, row_rows = ROWS + PAD, tiles * TILE + PAD

    def load(member):
        signal = step * members + member
        for (frames, block, start, valid), ref in zip(parts, part_refs):
            first = value_of(block, place[0]) * frames
            start = value_of(start, place[0])
            valid = value_of(valid, place[0])

            def fill(ref=ref, frames=frames, first=first, start=start):
                for f in range(frames):
                    ext[member, start + f] = ref[signal, first + f].astype(F32)

            def clear(frames=frames, start=start):
                for f in range(frames):
                    ext[member, start + f] = jnp.zeros((ROWS, LANES), F32)

            if isinstance(valid, int):
                fill() if valid else clear()
            else:
                pl.when(valid == 1)(fill)
                pl.when(valid == 0)(clear)

    def filter_rows(member, q):
        rows = pl.ds(pl.multiple_of(q * SUB, SUB), SUB)
        tap = [taps[pl.ds(pl.multiple_of(m * ROWS + q * SUB, SUB), SUB), :] for m in range(TAPS)]
        for f in range(out_frames):
            total = tap[0] * ext[member, f + 1, rows]
            for m in range(1, TAPS):
                total = total + tap[m] * ext[member, f + 1 + m, rows]
            filtered[member, f, rows] = total

    def first_stage(member):
        cosine = turn[:, :LANES]
        sine = turn[:, LANES:]
        for g in range(out_frames // STEP):
            block = jnp.concatenate([filtered[member, g * STEP + f] for f in range(STEP)], axis=1)
            high, low = halves(block)
            first = dot(one[...], jnp.concatenate([high, low, high], axis=0))
            for f in range(STEP):
                real = first[:H, f * LANES : (f + 1) * LANES]
                imag = first[H:, f * LANES : (f + 1) * LANES]
                at = (g * STEP + f) * frame_rows
                turned[member, at : at + H, :] = real * cosine + imag * sine
                turned[member, at + H : at + ROWS, :] = imag * cosine - real * sine

    def second_stage(member, pair):
        rows = []
        for k1 in range(2 * pair * share, 2 * (pair + 1) * share):
            for f in range(0, out_frames, SUB):
                rows.append(
                    jnp.concatenate(
                        [turned[member, pl.ds(f * frame_rows + p * H + k1, SUB, stride=frame_rows), :] for p in range(2)],
                        axis=1,
                    )
                )
        high, low = halves(jnp.concatenate(rows, axis=0))
        spectrum = dot_nt(two[0], high) + dot_nt(two[1], high) + dot_nt(two[0], low)
        for k in range(2):
            for t in range(groups):
                for p in range(2):
                    for k2 in range(0, per_group, SUB):
                        row = (t * 2 + p) * per_group + k2
                        start = (t * per_group + k2) * row_rows + (2 * pair + k) * TILE + p * SUB
                        staged[pl.ds(start + step * members + member, SUB, stride=row_rows), :] = spectrum[
                            row : row + SUB, k * LANES : (k + 1) * LANES
                        ]

    def write():
        at = 0
        for out in outs:

            def write_row(k2, carry):
                for k in range(tiles):
                    start = pl.multiple_of((at + k2) * row_rows + k * TILE, PAD)
                    out[k2, k] = staged[pl.ds(start, TILE), :].astype(BF16)
                return carry

            lax.fori_loop(0, out.shape[0], write_row, 0, unroll=2)
            at += out.shape[0]

    def body():
        for member in range(members):
            load(member)

        def filter_one(index, carry):
            filter_rows(index // (ROWS // SUB), index % (ROWS // SUB))
            return carry

        lax.fori_loop(0, members * (ROWS // SUB), filter_one, 0)
        for member in range(members):
            first_stage(member)
        for member in range(members):
            for pair in range(pairs):
                second_stage(member, pair)

        pl.when(step == steps - 1)(write)

    if isinstance(run, int):
        body()
    else:
        pl.when(value_of(run, place[0]) == 1)(body)


def after(value, *others):
    return lax.optimization_barrier((value, *others))[0]


def spectra(parts, out_frames, fixed, place, groups, sizes, run=1, wait=(), cost=10**6):
    signals = parts[0][0].shape[0]
    place = after(place, *wait)
    tiles = H * out_frames // LANES
    shapes = [(n, tiles, TILE, LANES) for n in sizes]
    return pl.pallas_call(
        functools.partial(spectra_kernel, groups, tuple(part[1:] for part in parts), out_frames, run),
        grid_spec=pltpu.PrefetchScalarGridSpec(
            num_scalar_prefetch=1,
            grid=(signals // MEMBERS,),
            in_specs=[pl.BlockSpec(memory_space=pltpu.VMEM)] * (len(parts) + 4),
            out_specs=[pl.BlockSpec(shape, lambda s, place: (0, 0, 0, 0)) for shape in shapes],
            scratch_shapes=[
                pltpu.VMEM((MEMBERS, TAPS + out_frames, ROWS, LANES), F32),
                pltpu.VMEM((MEMBERS, out_frames, ROWS, LANES), F32),
                pltpu.VMEM((MEMBERS, out_frames * (ROWS + PAD), LANES), F32),
                pltpu.VMEM((K2 * (tiles * TILE + PAD), LANES), F32),
            ],
        ),
        out_shape=[jax.ShapeDtypeStruct(shape, BF16) for shape in shapes],
        compiler_params=pltpu.CompilerParams(vmem_limit_bytes=32 << 20),
        cost_estimate=pl.CostEstimate(flops=cost, bytes_accessed=0, transcendentals=0),
    )(place, *[part[0] for part in parts], *fixed)


def after(value, *others):
    return lax.optimization_barrier((value, *others))[0]


def correlate_kernel(pieces, per_group, scale, add, last, place, *refs):
    refs = list(refs)
    sums = refs.pop() if last else None
    out = refs.pop()
    before = refs.pop() if add else None
    if not last:
        sums = out
    half = per_group // 2
    lane = lax.broadcasted_iota(jnp.int32, (SUB, LANES), 1)
    first_tile = lane < LANES // 2
    real_lane = lane % TILE < SUB
    sign = jnp.where(real_lane, 1.0, -1.0).astype(F32)

    def fetch(spot, tile, k2, k1):
        arrays, row, column = spot
        values = [refs[array][row + tile * half + k2, column + k1] for array in arrays]
        return values[0] if len(values) == 1 else values[0] + values[1]

    for number, piece in enumerate(pieces):
        tiles, piece = piece
        share = H // tiles
        where = lax.broadcasted_iota(jnp.int32, (TILE, LANES), 1) // (LANES // share)

        def pair(index, carry):
            k2 = index // tiles
            k1 = index % tiles
            own, other = [], []
            for position in range(len(piece[0])):
                rows = []
                for tile in range(2):
                    a = fetch(piece[0][position], tile, k2, k1)
                    rows += [jnp.where(where == c, a, jnp.zeros_like(a)) for c in range(share)]
                own.append(jnp.concatenate(rows, axis=0))
                rows = []
                for tile in range(2):
                    for visit in range(VISITS):
                        rows.append(fetch(piece[visit][position], tile, k2, k1))
                other.append(jnp.concatenate(rows, axis=0))
            product = dot_nt(jnp.concatenate(own, axis=1), jnp.concatenate(other, axis=1))
            for c in range(share):
                value = []
                for p in range(2):
                    at = [((tile * share + c) * 2 + p) * SUB for tile in range(2)]
                    value.append(
                        jnp.where(first_tile, product[at[0] : at[0] + SUB], product[at[1] : at[1] + SUB])
                    )
                turned = jnp.where(
                    real_lane, pltpu.roll(value[1], LANES - SUB, 1), pltpu.roll(value[1], SUB, 1)
                )
                total = value[0] * sign + turned
                channel = k2 // 4 * LANES + k2 % 4 * H + k1 * share + c
                rows = pl.ds(pl.multiple_of(channel * SUB, SUB), SUB)
                if number:
                    total = total + sums[rows, :]
                elif add:
                    total = total + before[rows, :]
                sums[rows, :] = total
            return carry

        lax.fori_loop(0, half * tiles, pair, 0, unroll=16)
    if not last:
        return

    def finish(index, carry):
        block = index // SUB
        signal = index % SUB
        value = sums[pl.ds(block * LANES * SUB + signal, LANES, stride=SUB), :]
        value = jnp.transpose(value * scale)
        at = 0
        for tile in range(2):
            for visit in range(VISITS):
                for part in range(2):
                    out[part, signal, value_of(PLACES[visit], place[1]), tile * (half // 4) + block] = value[at : at + SUB]
                    at += SUB
        return carry

    lax.fori_loop(0, half // 4 * SUB, finish, 0)


def correlate(arrays, pieces, per_group, place, scale, before, last, wait=(), cost=10**3):
    signals = TILE // 2
    rows = per_group // 2 * H * SUB
    place = after(place, *wait)
    shape = (2, signals, VISITS, per_group // 4, SUB, LANES) if last else (rows, LANES)
    operands = list(arrays) + ([] if before is None else [before])
    vmem = pl.BlockSpec(memory_space=pltpu.VMEM)
    result = pl.pallas_call(
        functools.partial(correlate_kernel, pieces, per_group, scale, before is not None, last),
        grid_spec=pltpu.PrefetchScalarGridSpec(
            num_scalar_prefetch=1,
            grid=(),
            in_specs=[vmem] * len(operands),
            out_specs=vmem,
            scratch_shapes=[pltpu.VMEM((rows, LANES), F32)] if last else [],
        ),
        out_shape=jax.ShapeDtypeStruct(shape, F32),
        compiler_params=pltpu.CompilerParams(vmem_limit_bytes=24 << 20),
        input_output_aliases={} if before is None or last else {len(operands): 0},
        cost_estimate=pl.CostEstimate(flops=cost, bytes_accessed=0, transcendentals=0),
    )(place, *operands)
    return result if last else pltpu.with_memory_space_constraint(result, pltpu.VMEM)


def stacked(voltage):
    s, f = voltage.shape[:2]
    return voltage.reshape(s, f, 2, H, LANES).transpose(0, 1, 3, 2, 4).reshape(s, f, ROWS, LANES)


def natural(out):
    parts, s, visits, i, t, lanes = out.shape
    return out.transpose(0, 1, 2, 4, 3, 5).reshape(parts, s, visits * t, i * lanes)


def shifted(block, axis, distance):
    size = lax.axis_size(axis)
    return lax.ppermute(block, axis, [(i, (i + distance) % size) for i in range(size)])


def farther(block):
    size = lax.axis_size("stn")
    rest = lax.ppermute(block, "stn", [(i, (i + 1 if i % 2 == 0 else i + 3) % size) for i in range(size)])
    return shifted(block, "stn", 2), rest


def evenly(block):
    size = lax.axis_size("stn")
    ways = [(i, (i + 1 if i % 2 == 0 else i + 3) % size) for i in range(size) if i % 4 < 3]
    return shifted(block, "stn", 2), lax.ppermute(block, "stn", ways)


def relayed(two):
    return lax.ppermute(two, "stn", [(i, i + 1) for i in range(lax.axis_size("stn")) if i % 4 == 1])


def exchanged(block):
    return lax.ppermute(block, "stn", [(i, i ^ 1) for i in range(lax.axis_size("stn"))])


def paired(volts, fir_taps, place, correlated):
    frames = volts.shape[1]
    me = lax.axis_index("tm")
    sizes = [K2 // 2, K2 // 2]
    swap = [(0, 1), (1, 0)]
    edge = TAPS // 2
    last = frames // edge
    many, few = TAPS * H // LANES, edge * H // LANES
    volts, edge_frames, *fixed = prepare(volts, fir_taps, place, 2, (last - 1, 0), edge)
    visiting = lax.ppermute(edge_frames, "tm", swap)
    own_a, away_a = spectra(
        [(volts, TAPS, 0, 0, (0, 1)), (volts, TAPS, (0, 1), TAPS, 1)], TAPS, fixed, place, 2, sizes
    )
    got_a = lax.ppermute(away_a, "tm", swap)
    two_a, rest_a = farther(own_a)
    own_b, away_b = spectra(
        [(volts, TAPS, 0, 0, 1), (volts, TAPS, 1, TAPS, 1)], TAPS, fixed, place, 2, sizes, (1, 0), (own_a,)
    )
    own_c, away_c = spectra(
        [
            (volts, edge, (last - 2, 0), (0, edge), 1),
            (volts, edge, (last - 1, 1), (edge, 2 * edge), 1),
            (visiting, edge, 0, (2 * edge, 0), 1),
        ],
        edge, fixed, place, 2, sizes, 1, (own_b, two_a),
    )
    got_a, own_c, away_b, away_c, two_a = lax.optimization_barrier((got_a, own_c, away_b, away_c, two_a))
    two_g, rest_g = evenly(got_a)
    got_c = lax.ppermute(away_c, "tm", swap)
    pair_a = exchanged(two_a)
    first = [(many, [(0, 0, 0)])]
    sums = correlated([own_a, pair_a, two_a, rest_a], first, None, False)
    got_c, away_b, sums = lax.optimization_barrier((got_c, away_b, sums))
    got_b = lax.ppermute(away_b, "tm", [(0, 1)])
    piece_c = jnp.concatenate([own_c, got_c], axis=1)
    two_c, rest_c = farther(piece_c)
    pair_g, relay_g = exchanged(two_g), relayed(two_g)
    sums = correlated([got_a, pair_g, two_g, (rest_g, relay_g)], first, sums, False)
    piece_b = jnp.where(me == 0, after(own_b, relay_g), got_b)
    two_b, rest_b = farther(piece_b)
    pair_c = exchanged(two_c)
    sums = correlated([piece_c, pair_c, two_c, rest_c], [(few, [(0, 0, 0), (0, 0, few)])], sums, False)
    pair_b = exchanged(after(two_b, rest_b, sums))
    return correlated([piece_b, pair_b, two_b, rest_b], first, sums, True)


def general(volts, fir_taps, place, correlated):
    groups = lax.axis_size("tm")
    frames = volts.shape[1]
    volts, edge_frames, *fixed = prepare(volts, fir_taps, place, groups, frames // TAPS - 1, TAPS)
    history = lax.ppermute(edge_frames, "tm", [(i, i + 1) for i in range(groups - 1)])
    parts = [(history, TAPS, 0, 0, 1)] + [(volts, TAPS, i, TAPS * (i + 1), 1) for i in range(frames // TAPS)]
    spectrum = spectra(parts, frames, fixed, place, groups, [K2])[0]
    spectrum = lax.all_to_all(spectrum, "tm", split_axis=0, concat_axis=0, tiled=True)
    two, rest = farther(spectrum)
    spots = [(0, K2 // groups * t, 0) for t in range(groups)]
    return correlated([spectrum, exchanged(two), two, rest], [(spectrum.shape[1], spots)], None, True)


def local(voltage, fir_taps):
    groups = lax.axis_size("tm")
    place = jnp.stack([lax.axis_index("tm"), lax.axis_index("stn") % 2]).astype(jnp.int32)
    scale = 1.0 / (groups * voltage.shape[1])

    def correlated(arrays, pieces, before, last, wait=(), cost=10**3):
        flat, spots_of = [], []
        for array in arrays:
            parts = array if isinstance(array, tuple) else (array,)
            spots_of.append(tuple(range(len(flat), len(flat) + len(parts))))
            flat += parts
        laid = [(tiles, [[(where, r, c) for _, r, c in spots] for where in spots_of]) for tiles, spots in pieces]
        return correlate(flat, laid, K2 // groups, place, scale, before, last, wait, cost)

    run = paired if groups == 2 else general
    return natural(run(stacked(voltage), fir_taps, place, correlated))


def solution(mesh):
    return jax.shard_map(
        local,
        mesh=mesh,
        in_specs=(P("stn", "tm", None, None), P()),
        out_specs=P(None, "stn", None, "tm"),
        check_vma=False,
    )
```

```python
import functools
import math

import jax
import jax.numpy as jnp
import numpy as np
from jax import lax
from jax.experimental import pallas as pl
from jax.experimental.pallas import tpu as pltpu
from jax.sharding import PartitionSpec as P

NCH = 4096
CHANS = 2048
TAPS = 16
VISITS = 4
H = 32
LANES = 128
ROWS = 2 * H
K2 = CHANS // H
STEP = 8
TILE = 16
PLACES = (0, (1, 3), 2, (3, 1))
MEMBERS = 4
PAD = 8
SUB = 8
BF16 = jnp.bfloat16
F32 = jnp.float32


def angles(rows, columns, modulus):
    turns = np.outer(rows, columns) % modulus
    return turns.astype(np.float64) * (2.0 * math.pi / modulus)


def stage_one_table():
    theta = angles(np.arange(H), np.arange(H), H)
    cosine, sine = np.cos(theta), np.sin(theta)
    table = np.zeros((2, H, H, 2))
    table[0, :, :, 0], table[0, :, :, 1] = cosine, sine
    table[1, :, :, 0], table[1, :, :, 1] = -sine, cosine
    return np.pad(table.reshape(ROWS, ROWS), ((0, 0), (0, 2 * LANES - ROWS)))


def turn_table():
    theta = angles(np.arange(H), np.arange(LANES), NCH)
    return np.concatenate([np.cos(theta), np.sin(theta)], axis=1)


def stage_two_table(groups):
    theta = angles(np.arange(K2), np.arange(LANES), LANES)
    cosine, sine = np.cos(theta) / math.sqrt(NCH), np.sin(theta) / math.sqrt(NCH)
    real = np.concatenate([cosine, sine], 1).reshape(groups, 1, K2 // groups, 2 * LANES)
    imag = np.concatenate([-sine, cosine], 1).reshape(groups, 1, K2 // groups, 2 * LANES)
    return np.concatenate([real, imag], 1).reshape(2 * K2, 2 * LANES)


def halves(value):
    high = value.astype(BF16)
    return high, (value - high.astype(F32)).astype(BF16)


def dot(left, right):
    return lax.dot_general(left, right, (((1,), (0,)), ((), ())), preferred_element_type=F32)


def dot_nt(left, right):
    return lax.dot_general(left, right, (((1,), (1,)), ((), ())), preferred_element_type=F32)


def value_of(number, group):
    if isinstance(number, int):
        return number
    return number[0] + (number[1] - number[0]) * group


def prepare_kernel(edge_block, swapped, place, volts_source, taps_source, table_source, turn_source, volts, edge, taps, one, two, turn, done, taps_ref, table_ref):
    count = edge.shape[1]
    start = pl.multiple_of(value_of(edge_block, place[0]) * count, count)
    copies = [
        pltpu.make_async_copy(taps_source, taps_ref, done.at[0]),
        pltpu.make_async_copy(table_source, table_ref, done.at[1]),
        pltpu.make_async_copy(volts_source.at[:, pl.ds(start, count)], edge, done.at[2]),
        pltpu.make_async_copy(volts_source, volts, done.at[3]),
        pltpu.make_async_copy(turn_source, turn, done.at[4]),
    ]
    for copy in copies:
        copy.start()
    copies[0].wait()
    copies[1].wait()
    for h in range(H):
        for half in range(TAPS // SUB):
            tile = taps_ref[pl.ds(half * SUB, SUB), pl.ds(h * LANES, LANES)]
            for r in range(2):
                taps[pl.ds(half * SUB * ROWS + 2 * h + r, SUB, stride=ROWS), :] = tile
    high, low = halves(table_ref[:ROWS, :ROWS])
    one[...] = jnp.concatenate([high, high, low], axis=1)
    start = pl.multiple_of(ROWS + place[0] * (2 * K2 * swapped), SUB)
    high, low = halves(table_ref[pl.ds(start, 2 * K2), :])
    two[0] = high
    two[1] = low
    for copy in copies[2:]:
        copy.wait()


def prepare(volts, fir_taps, place, groups, edge_block, edge_frames):
    signals, frames = volts.shape[:2]
    two = stage_two_table(groups)
    table = np.concatenate([stage_one_table(), two, np.roll(two, K2, axis=0)]).astype(np.float32)
    vmem = pl.BlockSpec(memory_space=pltpu.VMEM)
    return pl.pallas_call(
        functools.partial(prepare_kernel, edge_block, int(groups == 2)),
        grid_spec=pltpu.PrefetchScalarGridSpec(
            num_scalar_prefetch=1,
            grid=(),
            in_specs=[pl.BlockSpec(memory_space=pl.ANY)] * 4,
            out_specs=[vmem] * 6,
            scratch_shapes=[
                pltpu.SemaphoreType.DMA((5,)),
                pltpu.VMEM(fir_taps.shape, F32),
                pltpu.VMEM(table.shape, F32),
            ],
        ),
        out_shape=[
            jax.ShapeDtypeStruct((signals, frames, ROWS, LANES), BF16),
            jax.ShapeDtypeStruct((signals, edge_frames, ROWS, LANES), BF16),
            jax.ShapeDtypeStruct((TAPS * ROWS, LANES), F32),
            jax.ShapeDtypeStruct((ROWS, 3 * ROWS), BF16),
            jax.ShapeDtypeStruct((2, 2 * K2, 2 * LANES), BF16),
            jax.ShapeDtypeStruct((H, 2 * LANES), F32),
        ],
        compiler_params=pltpu.CompilerParams(vmem_limit_bytes=24 << 20),
    )(
        place,
        *[
            pltpu.with_memory_space_constraint(x, pltpu.HBM)
            for x in (volts, fir_taps, jnp.asarray(table), jnp.asarray(turn_table(), F32))
        ],
    )


def spectra_kernel(groups, parts, out_frames, run, place, *refs):
    part_refs, refs = refs[: len(parts)], refs[len(parts) :]
    taps, one, two, turn = refs[:4]
    outs, (ext, filtered, turned, staged) = refs[4:-4], refs[-4:]
    step, steps, members = pl.program_id(0), pl.num_programs(0), MEMBERS
    per_group = K2 // groups
    share = LANES // out_frames
    tiles = H // share
    pairs = tiles // 2
    frame_rows, row_rows = ROWS + PAD, tiles * TILE + PAD

    def load(member):
        signal = step * members + member
        for (frames, block, start, valid), ref in zip(parts, part_refs):
            first = value_of(block, place[0]) * frames
            start = value_of(start, place[0])
            valid = value_of(valid, place[0])

            def fill(ref=ref, frames=frames, first=first, start=start):
                for f in range(frames):
                    ext[member, start + f] = ref[signal, first + f].astype(F32)

            def clear(frames=frames, start=start):
                for f in range(frames):
                    ext[member, start + f] = jnp.zeros((ROWS, LANES), F32)

            if isinstance(valid, int):
                fill() if valid else clear()
            else:
                pl.when(valid == 1)(fill)
                pl.when(valid == 0)(clear)

    def filter_rows(member, q):
        rows = pl.ds(pl.multiple_of(q * SUB, SUB), SUB)
        tap = [taps[pl.ds(pl.multiple_of(m * ROWS + q * SUB, SUB), SUB), :] for m in range(TAPS)]
        for f in range(out_frames):
            total = tap[0] * ext[member, f + 1, rows]
            for m in range(1, TAPS):
                total = total + tap[m] * ext[member, f + 1 + m, rows]
            filtered[member, f, rows] = total

    def first_stage(member):
        cosine = turn[:, :LANES]
        sine = turn[:, LANES:]
        for g in range(out_frames // STEP):
            block = jnp.concatenate([filtered[member, g * STEP + f] for f in range(STEP)], axis=1)
            high, low = halves(block)
            first = dot(one[...], jnp.concatenate([high, low, high], axis=0))
            for f in range(STEP):
                real = first[:H, f * LANES : (f + 1) * LANES]
                imag = first[H:, f * LANES : (f + 1) * LANES]
                at = (g * STEP + f) * frame_rows
                turned[member, at : at + H, :] = real * cosine + imag * sine
                turned[member, at + H : at + ROWS, :] = imag * cosine - real * sine

    def second_stage(member, pair):
        rows = []
        for k1 in range(2 * pair * share, 2 * (pair + 1) * share):
            for f in range(0, out_frames, SUB):
                rows.append(
                    jnp.concatenate(
                        [turned[member, pl.ds(f * frame_rows + p * H + k1, SUB, stride=frame_rows), :] for p in range(2)],
                        axis=1,
                    )
                )
        high, low = halves(jnp.concatenate(rows, axis=0))
        spectrum = dot_nt(two[0], high) + dot_nt(two[1], high) + dot_nt(two[0], low)
        for k in range(2):
            for t in range(groups):
                for p in range(2):
                    for k2 in range(0, per_group, SUB):
                        row = (t * 2 + p) * per_group + k2
                        start = (t * per_group + k2) * row_rows + (2 * pair + k) * TILE + p * SUB
                        staged[pl.ds(start + step * members + member, SUB, stride=row_rows), :] = spectrum[
                            row : row + SUB, k * LANES : (k + 1) * LANES
                        ]

    def write():
        at = 0
        for out in outs:

            def write_row(k2, carry):
                for k in range(tiles):
                    start = pl.multiple_of((at + k2) * row_rows + k * TILE, PAD)
                    out[k2, k] = staged[pl.ds(start, TILE), :].astype(BF16)
                return carry

            lax.fori_loop(0, out.shape[0], write_row, 0, unroll=2)
            at += out.shape[0]

    def body():
        for member in range(members):
            load(member)

        def filter_one(index, carry):
            filter_rows(index // (ROWS // SUB), index % (ROWS // SUB))
            return carry

        lax.fori_loop(0, members * (ROWS // SUB), filter_one, 0)
        for member in range(members):
            first_stage(member)
        for member in range(members):
            for pair in range(pairs):
                second_stage(member, pair)

        pl.when(step == steps - 1)(write)

    if isinstance(run, int):
        body()
    else:
        pl.when(value_of(run, place[0]) == 1)(body)


def after(value, *others):
    return lax.optimization_barrier((value, *others))[0]


def spectra(parts, out_frames, fixed, place, groups, sizes, run=1, wait=(), cost=10**6):
    signals = parts[0][0].shape[0]
    place = after(place, *wait)
    tiles = H * out_frames // LANES
    shapes = [(n, tiles, TILE, LANES) for n in sizes]
    return pl.pallas_call(
        functools.partial(spectra_kernel, groups, tuple(part[1:] for part in parts), out_frames, run),
        grid_spec=pltpu.PrefetchScalarGridSpec(
            num_scalar_prefetch=1,
            grid=(signals // MEMBERS,),
            in_specs=[pl.BlockSpec(memory_space=pltpu.VMEM)] * (len(parts) + 4),
            out_specs=[pl.BlockSpec(shape, lambda s, place: (0, 0, 0, 0)) for shape in shapes],
            scratch_shapes=[
                pltpu.VMEM((MEMBERS, TAPS + out_frames, ROWS, LANES), F32),
                pltpu.VMEM((MEMBERS, out_frames, ROWS, LANES), F32),
                pltpu.VMEM((MEMBERS, out_frames * (ROWS + PAD), LANES), F32),
                pltpu.VMEM((K2 * (tiles * TILE + PAD), LANES), F32),
            ],
        ),
        out_shape=[jax.ShapeDtypeStruct(shape, BF16) for shape in shapes],
        compiler_params=pltpu.CompilerParams(vmem_limit_bytes=32 << 20),
        cost_estimate=pl.CostEstimate(flops=cost, bytes_accessed=0, transcendentals=0),
    )(place, *[part[0] for part in parts], *fixed)


def after(value, *others):
    return lax.optimization_barrier((value, *others))[0]


def correlate_kernel(pieces, per_group, scale, add, last, place, *refs):
    refs = list(refs)
    sums = refs.pop() if last else None
    out = refs.pop()
    before = refs.pop() if add else None
    if not last:
        sums = out
    half = per_group // 2
    lane = lax.broadcasted_iota(jnp.int32, (SUB, LANES), 1)
    first_tile = lane < LANES // 2
    real_lane = lane % TILE < SUB
    sign = jnp.where(real_lane, 1.0, -1.0).astype(F32)

    def fetch(spot, tile, k2, k1):
        arrays, row, column = spot
        values = [refs[array][row + tile * half + k2, column + k1] for array in arrays]
        return values[0] if len(values) == 1 else values[0] + values[1]

    for number, piece in enumerate(pieces):
        tiles, piece = piece
        share = H // tiles
        where = lax.broadcasted_iota(jnp.int32, (TILE, LANES), 1) // (LANES // share)

        def pair(index, carry):
            k2 = index // tiles
            k1 = index % tiles
            own, other = [], []
            for position in range(len(piece[0])):
                rows = []
                for tile in range(2):
                    a = fetch(piece[0][position], tile, k2, k1)
                    rows += [jnp.where(where == c, a, jnp.zeros_like(a)) for c in range(share)]
                own.append(jnp.concatenate(rows, axis=0))
                rows = []
                for tile in range(2):
                    for visit in range(VISITS):
                        rows.append(fetch(piece[visit][position], tile, k2, k1))
                other.append(jnp.concatenate(rows, axis=0))
            product = dot_nt(jnp.concatenate(own, axis=1), jnp.concatenate(other, axis=1))
            for c in range(share):
                value = []
                for p in range(2):
                    at = [((tile * share + c) * 2 + p) * SUB for tile in range(2)]
                    value.append(
                        jnp.where(first_tile, product[at[0] : at[0] + SUB], product[at[1] : at[1] + SUB])
                    )
                turned = jnp.where(
                    real_lane, pltpu.roll(value[1], LANES - SUB, 1), pltpu.roll(value[1], SUB, 1)
                )
                total = value[0] * sign + turned
                channel = k2 // 4 * LANES + k2 % 4 * H + k1 * share + c
                rows = pl.ds(pl.multiple_of(channel * SUB, SUB), SUB)
                if number:
                    total = total + sums[rows, :]
                elif add:
                    total = total + before[rows, :]
                sums[rows, :] = total
            return carry

        lax.fori_loop(0, half * tiles, pair, 0, unroll=32)
    if not last:
        return

    def finish(index, carry):
        block = index // SUB
        signal = index % SUB
        value = sums[pl.ds(block * LANES * SUB + signal, LANES, stride=SUB), :]
        value = jnp.transpose(value * scale)
        at = 0
        for tile in range(2):
            for visit in range(VISITS):
                for part in range(2):
                    out[part, signal, value_of(PLACES[visit], place[1]), tile * (half // 4) + block] = value[at : at + SUB]
                    at += SUB
        return carry

    lax.fori_loop(0, half // 4 * SUB, finish, 0, unroll=8)


def correlate(arrays, pieces, per_group, place, scale, before, last, wait=(), cost=10**3):
    signals = TILE // 2
    rows = per_group // 2 * H * SUB
    place = after(place, *wait)
    shape = (2, signals, VISITS, per_group // 4, SUB, LANES) if last else (rows, LANES)
    operands = list(arrays) + ([] if before is None else [before])
    vmem = pl.BlockSpec(memory_space=pltpu.VMEM)
    result = pl.pallas_call(
        functools.partial(correlate_kernel, pieces, per_group, scale, before is not None, last),
        grid_spec=pltpu.PrefetchScalarGridSpec(
            num_scalar_prefetch=1,
            grid=(),
            in_specs=[vmem] * len(operands),
            out_specs=vmem,
            scratch_shapes=[pltpu.VMEM((rows, LANES), F32)] if last else [],
        ),
        out_shape=jax.ShapeDtypeStruct(shape, F32),
        compiler_params=pltpu.CompilerParams(vmem_limit_bytes=24 << 20),
        input_output_aliases={} if before is None or last else {len(operands): 0},
        cost_estimate=pl.CostEstimate(flops=cost, bytes_accessed=0, transcendentals=0),
    )(place, *operands)
    return result if last else pltpu.with_memory_space_constraint(result, pltpu.VMEM)


def stacked(voltage):
    s, f = voltage.shape[:2]
    return voltage.reshape(s, f, 2, H, LANES).transpose(0, 1, 3, 2, 4).reshape(s, f, ROWS, LANES)


def natural(out):
    parts, s, visits, i, t, lanes = out.shape
    return out.transpose(0, 1, 2, 4, 3, 5).reshape(parts, s, visits * t, i * lanes)


def shifted(block, axis, distance):
    size = lax.axis_size(axis)
    return lax.ppermute(block, axis, [(i, (i + distance) % size) for i in range(size)])


def farther(block):
    size = lax.axis_size("stn")
    rest = lax.ppermute(block, "stn", [(i, (i + 1 if i % 2 == 0 else i + 3) % size) for i in range(size)])
    return shifted(block, "stn", 2), rest


def evenly(block):
    size = lax.axis_size("stn")
    ways = [(i, (i + 1 if i % 2 == 0 else i + 3) % size) for i in range(size) if i % 4 < 3]
    return shifted(block, "stn", 2), lax.ppermute(block, "stn", ways)


def relayed(two):
    return lax.ppermute(two, "stn", [(i, i + 1) for i in range(lax.axis_size("stn")) if i % 4 == 1])


def exchanged(block):
    return lax.ppermute(block, "stn", [(i, i ^ 1) for i in range(lax.axis_size("stn"))])


def paired(volts, fir_taps, place, correlated):
    frames = volts.shape[1]
    me = lax.axis_index("tm")
    sizes = [K2 // 2, K2 // 2]
    swap = [(0, 1), (1, 0)]
    edge = TAPS // 2
    last = frames // edge
    many, few = TAPS * H // LANES, edge * H // LANES
    volts, edge_frames, *fixed = prepare(volts, fir_taps, place, 2, (last - 1, 0), edge)
    visiting = lax.ppermute(edge_frames, "tm", swap)
    own_a, away_a = spectra(
        [(volts, TAPS, 0, 0, (0, 1)), (volts, TAPS, (0, 1), TAPS, 1)], TAPS, fixed, place, 2, sizes
    )
    got_a = lax.ppermute(away_a, "tm", swap)
    two_a, rest_a = farther(own_a)
    own_b, away_b = spectra(
        [(volts, TAPS, 0, 0, 1), (volts, TAPS, 1, TAPS, 1)], TAPS, fixed, place, 2, sizes, (1, 0), (own_a,)
    )
    own_c, away_c = spectra(
        [
            (volts, edge, (last - 2, 0), (0, edge), 1),
            (volts, edge, (last - 1, 1), (edge, 2 * edge), 1),
            (visiting, edge, 0, (2 * edge, 0), 1),
        ],
        edge, fixed, place, 2, sizes, 1, (own_b, two_a),
    )
    got_a, own_c, away_b, away_c, two_a = lax.optimization_barrier((got_a, own_c, away_b, away_c, two_a))
    two_g, rest_g = evenly(got_a)
    got_b = lax.ppermute(away_b, "tm", [(0, 1)])
    pair_a = exchanged(two_a)
    first = [(many, [(0, 0, 0)])]
    sums = correlated([own_a, pair_a, two_a, rest_a], first, None, False)
    got_b, away_c, sums = lax.optimization_barrier((got_b, away_c, sums))
    got_c = lax.ppermute(away_c, "tm", swap)
    piece_b = jnp.where(me == 0, own_b, got_b)
    two_b, rest_b = farther(piece_b)
    pair_g, relay_g = exchanged(two_g), relayed(two_g)
    sums = correlated([got_a, pair_g, two_g, (rest_g, relay_g)], first, sums, False)
    piece_c = jnp.concatenate([own_c, got_c], axis=1)
    two_c, rest_c = farther(piece_c)
    pair_b = exchanged(two_b)
    sums = correlated([piece_b, pair_b, two_b, rest_b], first, sums, False)
    pair_c = exchanged(after(two_c, rest_c, sums))
    return correlated([piece_c, pair_c, two_c, rest_c], [(few, [(0, 0, 0), (0, 0, few)])], sums, True)


def general(volts, fir_taps, place, correlated):
    groups = lax.axis_size("tm")
    frames = volts.shape[1]
    volts, edge_frames, *fixed = prepare(volts, fir_taps, place, groups, frames // TAPS - 1, TAPS)
    history = lax.ppermute(edge_frames, "tm", [(i, i + 1) for i in range(groups - 1)])
    parts = [(history, TAPS, 0, 0, 1)] + [(volts, TAPS, i, TAPS * (i + 1), 1) for i in range(frames // TAPS)]
    spectrum = spectra(parts, frames, fixed, place, groups, [K2])[0]
    spectrum = lax.all_to_all(spectrum, "tm", split_axis=0, concat_axis=0, tiled=True)
    two, rest = farther(spectrum)
    spots = [(0, K2 // groups * t, 0) for t in range(groups)]
    return correlated([spectrum, exchanged(two), two, rest], [(spectrum.shape[1], spots)], None, True)


def local(voltage, fir_taps):
    groups = lax.axis_size("tm")
    place = jnp.stack([lax.axis_index("tm"), lax.axis_index("stn") % 2]).astype(jnp.int32)
    scale = 1.0 / (groups * voltage.shape[1])

    def correlated(arrays, pieces, before, last, wait=(), cost=10**3):
        flat, spots_of = [], []
        for array in arrays:
            parts = array if isinstance(array, tuple) else (array,)
            spots_of.append(tuple(range(len(flat), len(flat) + len(parts))))
            flat += parts
        laid = [(tiles, [[(where, r, c) for _, r, c in spots] for where in spots_of]) for tiles, spots in pieces]
        return correlate(flat, laid, K2 // groups, place, scale, before, last, wait, cost)

    run = paired if groups == 2 else general
    return natural(run(stacked(voltage), fir_taps, place, correlated))


def solution(mesh):
    return jax.shard_map(
        local,
        mesh=mesh,
        in_specs=(P("stn", "tm", None, None), P()),
        out_specs=P(None, "stn", None, "tm"),
        check_vma=False,
    )
```

```python
import functools
import math

import jax
import jax.numpy as jnp
import numpy as np
from jax import lax
from jax.experimental import pallas as pl
from jax.experimental.pallas import tpu as pltpu
from jax.sharding import PartitionSpec as P

NCH = 4096
CHANS = 2048
TAPS = 16
VISITS = 4
H = 32
LANES = 128
ROWS = 2 * H
K2 = CHANS // H
STEP = 8
TILE = 16
PLACES = (0, (1, 3), 2, (3, 1))
MEMBERS = 4
PAD = 8
SUB = 8
BF16 = jnp.bfloat16
F32 = jnp.float32


def angles(rows, columns, modulus):
    turns = np.outer(rows, columns) % modulus
    return turns.astype(np.float64) * (2.0 * math.pi / modulus)


def stage_one_table():
    theta = angles(np.arange(H), np.arange(H), H)
    cosine, sine = np.cos(theta), np.sin(theta)
    table = np.zeros((2, H, H, 2))
    table[0, :, :, 0], table[0, :, :, 1] = cosine, sine
    table[1, :, :, 0], table[1, :, :, 1] = -sine, cosine
    return np.pad(table.reshape(ROWS, ROWS), ((0, 0), (0, 2 * LANES - ROWS)))


def turn_table():
    theta = angles(np.arange(H), np.arange(LANES), NCH)
    return np.concatenate([np.cos(theta), np.sin(theta)], axis=1)


def stage_two_table(groups):
    theta = angles(np.arange(K2), np.arange(LANES), LANES)
    cosine, sine = np.cos(theta) / math.sqrt(NCH), np.sin(theta) / math.sqrt(NCH)
    real = np.concatenate([cosine, sine], 1).reshape(groups, 1, K2 // groups, 2 * LANES)
    imag = np.concatenate([-sine, cosine], 1).reshape(groups, 1, K2 // groups, 2 * LANES)
    return np.concatenate([real, imag], 1).reshape(2 * K2, 2 * LANES)


def halves(value):
    high = value.astype(BF16)
    return high, (value - high.astype(F32)).astype(BF16)


def dot(left, right):
    return lax.dot_general(left, right, (((1,), (0,)), ((), ())), preferred_element_type=F32)


def dot_nt(left, right):
    return lax.dot_general(left, right, (((1,), (1,)), ((), ())), preferred_element_type=F32)


def value_of(number, group):
    if isinstance(number, int):
        return number
    return number[0] + (number[1] - number[0]) * group


def prepare_kernel(edge_block, swapped, place, volts_source, taps_source, table_source, turn_source, volts, edge, taps, one, two, turn, done, taps_ref, table_ref):
    count = edge.shape[1]
    start = pl.multiple_of(value_of(edge_block, place[0]) * count, count)
    copies = [
        pltpu.make_async_copy(taps_source, taps_ref, done.at[0]),
        pltpu.make_async_copy(table_source, table_ref, done.at[1]),
        pltpu.make_async_copy(volts_source.at[:, pl.ds(start, count)], edge, done.at[2]),
        pltpu.make_async_copy(volts_source, volts, done.at[3]),
        pltpu.make_async_copy(turn_source, turn, done.at[4]),
    ]
    for copy in copies:
        copy.start()
    copies[0].wait()
    copies[1].wait()
    for h in range(H):
        for half in range(TAPS // SUB):
            tile = taps_ref[pl.ds(half * SUB, SUB), pl.ds(h * LANES, LANES)]
            for r in range(2):
                taps[pl.ds(half * SUB * ROWS + 2 * h + r, SUB, stride=ROWS), :] = tile
    high, low = halves(table_ref[:ROWS, :ROWS])
    one[...] = jnp.concatenate([high, high, low], axis=1)
    start = pl.multiple_of(ROWS + place[0] * (2 * K2 * swapped), SUB)
    high, low = halves(table_ref[pl.ds(start, 2 * K2), :])
    two[0] = high
    two[1] = low
    for copy in copies[2:]:
        copy.wait()


def prepare(volts, fir_taps, place, groups, edge_block, edge_frames):
    signals, frames = volts.shape[:2]
    two = stage_two_table(groups)
    table = np.concatenate([stage_one_table(), two, np.roll(two, K2, axis=0)]).astype(np.float32)
    vmem = pl.BlockSpec(memory_space=pltpu.VMEM)
    return pl.pallas_call(
        functools.partial(prepare_kernel, edge_block, int(groups == 2)),
        grid_spec=pltpu.PrefetchScalarGridSpec(
            num_scalar_prefetch=1,
            grid=(),
            in_specs=[pl.BlockSpec(memory_space=pl.ANY)] * 4,
            out_specs=[vmem] * 6,
            scratch_shapes=[
                pltpu.SemaphoreType.DMA((5,)),
                pltpu.VMEM(fir_taps.shape, F32),
                pltpu.VMEM(table.shape, F32),
            ],
        ),
        out_shape=[
            jax.ShapeDtypeStruct((signals, frames, ROWS, LANES), BF16),
            jax.ShapeDtypeStruct((signals, edge_frames, ROWS, LANES), BF16),
            jax.ShapeDtypeStruct((TAPS * ROWS, LANES), F32),
            jax.ShapeDtypeStruct((ROWS, 3 * ROWS), BF16),
            jax.ShapeDtypeStruct((2, 2 * K2, 2 * LANES), BF16),
            jax.ShapeDtypeStruct((H, 2 * LANES), F32),
        ],
        compiler_params=pltpu.CompilerParams(vmem_limit_bytes=24 << 20),
    )(
        place,
        *[
            pltpu.with_memory_space_constraint(x, pltpu.HBM)
            for x in (volts, fir_taps, jnp.asarray(table), jnp.asarray(turn_table(), F32))
        ],
    )


def spectra_kernel(groups, parts, out_frames, run, place, *refs):
    part_refs, refs = refs[: len(parts)], refs[len(parts) :]
    taps, one, two, turn = refs[:4]
    outs, (ext, filtered, turned, staged) = refs[4:-4], refs[-4:]
    step, steps, members = pl.program_id(0), pl.num_programs(0), MEMBERS
    per_group = K2 // groups
    share = LANES // out_frames
    tiles = H // share
    pairs = tiles // 2
    frame_rows, row_rows = ROWS + PAD, tiles * TILE + PAD

    def load(member):
        signal = step * members + member
        for (frames, block, start, valid), ref in zip(parts, part_refs):
            first = value_of(block, place[0]) * frames
            start = value_of(start, place[0])
            valid = value_of(valid, place[0])

            def fill(ref=ref, frames=frames, first=first, start=start):
                for f in range(frames):
                    ext[member, start + f] = ref[signal, first + f].astype(F32)

            def clear(frames=frames, start=start):
                for f in range(frames):
                    ext[member, start + f] = jnp.zeros((ROWS, LANES), F32)

            if isinstance(valid, int):
                fill() if valid else clear()
            else:
                pl.when(valid == 1)(fill)
                pl.when(valid == 0)(clear)

    def filter_rows(member, q):
        rows = pl.ds(pl.multiple_of(q * SUB, SUB), SUB)
        tap = [taps[pl.ds(pl.multiple_of(m * ROWS + q * SUB, SUB), SUB), :] for m in range(TAPS)]
        for f in range(out_frames):
            total = tap[0] * ext[member, f + 1, rows]
            for m in range(1, TAPS):
                total = total + tap[m] * ext[member, f + 1 + m, rows]
            filtered[member, f, rows] = total

    def first_stage(member):
        cosine = turn[:, :LANES]
        sine = turn[:, LANES:]
        for g in range(out_frames // STEP):
            block = jnp.concatenate([filtered[member, g * STEP + f] for f in range(STEP)], axis=1)
            high, low = halves(block)
            first = dot(one[...], jnp.concatenate([high, low, high], axis=0))
            for f in range(STEP):
                real = first[:H, f * LANES : (f + 1) * LANES]
                imag = first[H:, f * LANES : (f + 1) * LANES]
                at = (g * STEP + f) * frame_rows
                turned[member, at : at + H, :] = real * cosine + imag * sine
                turned[member, at + H : at + ROWS, :] = imag * cosine - real * sine

    def second_stage(member, pair):
        rows = []
        for k1 in range(2 * pair * share, 2 * (pair + 1) * share):
            for f in range(0, out_frames, SUB):
                rows.append(
                    jnp.concatenate(
                        [turned[member, pl.ds(f * frame_rows + p * H + k1, SUB, stride=frame_rows), :] for p in range(2)],
                        axis=1,
                    )
                )
        high, low = halves(jnp.concatenate(rows, axis=0))
        spectrum = dot_nt(two[0], high) + dot_nt(two[1], high) + dot_nt(two[0], low)
        for k in range(2):
            for t in range(groups):
                for p in range(2):
                    for k2 in range(0, per_group, SUB):
                        row = (t * 2 + p) * per_group + k2
                        start = (t * per_group + k2) * row_rows + (2 * pair + k) * TILE + p * SUB
                        staged[pl.ds(start + step * members + member, SUB, stride=row_rows), :] = spectrum[
                            row : row + SUB, k * LANES : (k + 1) * LANES
                        ]

    def write():
        at = 0
        for out in outs:

            def write_row(k2, carry):
                for k in range(tiles):
                    start = pl.multiple_of((at + k2) * row_rows + k * TILE, PAD)
                    out[k2, k] = staged[pl.ds(start, TILE), :].astype(BF16)
                return carry

            lax.fori_loop(0, out.shape[0], write_row, 0, unroll=2)
            at += out.shape[0]

    def body():
        for member in range(members):
            load(member)

        def filter_one(index, carry):
            filter_rows(index // (ROWS // SUB), index % (ROWS // SUB))
            return carry

        lax.fori_loop(0, members * (ROWS // SUB), filter_one, 0)
        for member in range(members):
            first_stage(member)
        for member in range(members):
            for pair in range(pairs):
                second_stage(member, pair)

        pl.when(step == steps - 1)(write)

    if isinstance(run, int):
        body()
    else:
        pl.when(value_of(run, place[0]) == 1)(body)


def after(value, *others):
    return lax.optimization_barrier((value, *others))[0]


def spectra(parts, out_frames, fixed, place, groups, sizes, run=1, wait=(), cost=10**6):
    signals = parts[0][0].shape[0]
    place = after(place, *wait)
    tiles = H * out_frames // LANES
    shapes = [(n, tiles, TILE, LANES) for n in sizes]
    return pl.pallas_call(
        functools.partial(spectra_kernel, groups, tuple(part[1:] for part in parts), out_frames, run),
        grid_spec=pltpu.PrefetchScalarGridSpec(
            num_scalar_prefetch=1,
            grid=(signals // MEMBERS,),
            in_specs=[pl.BlockSpec(memory_space=pltpu.VMEM)] * (len(parts) + 4),
            out_specs=[pl.BlockSpec(shape, lambda s, place: (0, 0, 0, 0)) for shape in shapes],
            scratch_shapes=[
                pltpu.VMEM((MEMBERS, TAPS + out_frames, ROWS, LANES), F32),
                pltpu.VMEM((MEMBERS, out_frames, ROWS, LANES), F32),
                pltpu.VMEM((MEMBERS, out_frames * (ROWS + PAD), LANES), F32),
                pltpu.VMEM((K2 * (tiles * TILE + PAD), LANES), F32),
            ],
        ),
        out_shape=[jax.ShapeDtypeStruct(shape, BF16) for shape in shapes],
        compiler_params=pltpu.CompilerParams(vmem_limit_bytes=32 << 20),
        cost_estimate=pl.CostEstimate(flops=cost, bytes_accessed=0, transcendentals=0),
    )(place, *[part[0] for part in parts], *fixed)


def after(value, *others):
    return lax.optimization_barrier((value, *others))[0]


def correlate_kernel(pieces, per_group, scale, add, last, place, *refs):
    refs = list(refs)
    sums = refs.pop() if last else None
    out = refs.pop()
    before = refs.pop() if add else None
    if not last:
        sums = out
    half = per_group // 2
    lane = lax.broadcasted_iota(jnp.int32, (SUB, LANES), 1)
    first_tile = lane < LANES // 2
    real_lane = lane % TILE < SUB
    sign = jnp.where(real_lane, 1.0, -1.0).astype(F32)

    def fetch(spot, tile, k2, k1):
        arrays, row, column = spot
        values = [refs[array][row + tile * half + k2, column + k1] for array in arrays]
        return values[0] if len(values) == 1 else values[0] + values[1]

    for number, piece in enumerate(pieces):
        tiles, piece = piece
        share = H // tiles
        where = lax.broadcasted_iota(jnp.int32, (TILE, LANES), 1) // (LANES // share)

        def pair(index, carry):
            k2 = index // tiles
            k1 = index % tiles
            own, other = [], []
            for position in range(len(piece[0])):
                rows = []
                for tile in range(2):
                    a = fetch(piece[0][position], tile, k2, k1)
                    rows += [jnp.where(where == c, a, jnp.zeros_like(a)) for c in range(share)]
                own.append(jnp.concatenate(rows, axis=0))
                rows = []
                for tile in range(2):
                    for visit in range(VISITS):
                        rows.append(fetch(piece[visit][position], tile, k2, k1))
                other.append(jnp.concatenate(rows, axis=0))
            product = dot_nt(jnp.concatenate(own, axis=1), jnp.concatenate(other, axis=1))
            for c in range(share):
                value = []
                for p in range(2):
                    at = [((tile * share + c) * 2 + p) * SUB for tile in range(2)]
                    value.append(
                        jnp.where(first_tile, product[at[0] : at[0] + SUB], product[at[1] : at[1] + SUB])
                    )
                turned = jnp.where(
                    real_lane, pltpu.roll(value[1], LANES - SUB, 1), pltpu.roll(value[1], SUB, 1)
                )
                total = value[0] * sign + turned
                channel = k2 // 4 * LANES + k2 % 4 * H + k1 * share + c
                rows = pl.ds(pl.multiple_of(channel * SUB, SUB), SUB)
                if number:
                    total = total + sums[rows, :]
                elif add:
                    total = total + before[rows, :]
                sums[rows, :] = total
            return carry

        lax.fori_loop(0, half * tiles, pair, 0, unroll=32)
    if not last:
        return

    def finish(index, carry):
        block = index // SUB
        signal = index % SUB
        value = sums[pl.ds(block * LANES * SUB + signal, LANES, stride=SUB), :]
        value = jnp.transpose(value * scale)
        at = 0
        for tile in range(2):
            for visit in range(VISITS):
                for part in range(2):
                    out[part, signal, value_of(PLACES[visit], place[1]), tile * (half // 4) + block] = value[at : at + SUB]
                    at += SUB
        return carry

    lax.fori_loop(0, half // 4 * SUB, finish, 0, unroll=8)


def correlate(arrays, pieces, per_group, place, scale, before, last, wait=(), cost=10**3):
    signals = TILE // 2
    rows = per_group // 2 * H * SUB
    place = after(place, *wait)
    shape = (2, signals, VISITS, per_group // 4, SUB, LANES) if last else (rows, LANES)
    operands = list(arrays) + ([] if before is None else [before])
    vmem = pl.BlockSpec(memory_space=pltpu.VMEM)
    result = pl.pallas_call(
        functools.partial(correlate_kernel, pieces, per_group, scale, before is not None, last),
        grid_spec=pltpu.PrefetchScalarGridSpec(
            num_scalar_prefetch=1,
            grid=(),
            in_specs=[vmem] * len(operands),
            out_specs=vmem,
            scratch_shapes=[pltpu.VMEM((rows, LANES), F32)] if last else [],
        ),
        out_shape=jax.ShapeDtypeStruct(shape, F32),
        compiler_params=pltpu.CompilerParams(vmem_limit_bytes=24 << 20),
        input_output_aliases={} if before is None or last else {len(operands): 0},
        cost_estimate=pl.CostEstimate(flops=cost, bytes_accessed=0, transcendentals=0),
    )(place, *operands)
    return result if last else pltpu.with_memory_space_constraint(result, pltpu.VMEM)


def stacked(voltage):
    s, f = voltage.shape[:2]
    return voltage.reshape(s, f, 2, H, LANES).transpose(0, 1, 3, 2, 4).reshape(s, f, ROWS, LANES)


def natural(out):
    parts, s, visits, i, t, lanes = out.shape
    return out.transpose(0, 1, 2, 4, 3, 5).reshape(parts, s, visits * t, i * lanes)


def shifted(block, axis, distance):
    size = lax.axis_size(axis)
    return lax.ppermute(block, axis, [(i, (i + distance) % size) for i in range(size)])


def farther(block):
    size = lax.axis_size("stn")
    rest = lax.ppermute(block, "stn", [(i, (i + 1 if i % 2 == 0 else i + 3) % size) for i in range(size)])
    return shifted(block, "stn", 2), rest


def evenly(block):
    size = lax.axis_size("stn")
    ways = [(i, (i + 1 if i % 2 == 0 else i + 3) % size) for i in range(size) if i % 4 < 3]
    return shifted(block, "stn", 2), lax.ppermute(block, "stn", ways)


def relayed(two):
    return lax.ppermute(two, "stn", [(i, i + 1) for i in range(lax.axis_size("stn")) if i % 4 == 1])


def exchanged(block):
    return lax.ppermute(block, "stn", [(i, i ^ 1) for i in range(lax.axis_size("stn"))])


def paired(volts, fir_taps, place, correlated):
    frames = volts.shape[1]
    me = lax.axis_index("tm")
    sizes = [K2 // 2, K2 // 2]
    swap = [(0, 1), (1, 0)]
    edge = TAPS // 2
    last = frames // edge
    many, few = TAPS * H // LANES, edge * H // LANES
    volts, edge_frames, *fixed = prepare(volts, fir_taps, place, 2, (last - 1, 0), edge)
    visiting = lax.ppermute(edge_frames, "tm", swap)
    own_a, away_a = spectra(
        [(volts, TAPS, 0, 0, (0, 1)), (volts, TAPS, (0, 1), TAPS, 1)], TAPS, fixed, place, 2, sizes
    )
    got_a = lax.ppermute(away_a, "tm", swap)
    two_a, rest_a = farther(own_a)
    own_b, away_b = spectra(
        [(volts, TAPS, 0, 0, 1), (volts, TAPS, 1, TAPS, 1)], TAPS, fixed, place, 2, sizes, (1, 0), (own_a,)
    )
    own_c, away_c = spectra(
        [
            (volts, edge, (last - 2, 0), (0, edge), 1),
            (volts, edge, (last - 1, 1), (edge, 2 * edge), 1),
            (visiting, edge, 0, (2 * edge, 0), 1),
        ],
        edge, fixed, place, 2, sizes, 1, (own_b, two_a),
    )
    got_a, own_c, away_b, away_c, two_a = lax.optimization_barrier((got_a, own_c, away_b, away_c, two_a))
    two_g, rest_g = evenly(got_a)
    got_b = lax.ppermute(away_b, "tm", [(0, 1)])
    pair_a = exchanged(two_a)
    first = [(many, [(0, 0, 0)])]
    sums = correlated([own_a, pair_a, two_a, rest_a], first, None, False)
    got_b, away_c, sums = lax.optimization_barrier((got_b, away_c, sums))
    got_c = lax.ppermute(away_c, "tm", swap)
    piece_b = jnp.where(me == 0, own_b, got_b)
    two_b, rest_b = farther(piece_b)
    pair_g, relay_g = exchanged(two_g), relayed(two_g)
    sums = correlated([got_a, pair_g, two_g, (rest_g, relay_g)], first, sums, False)
    piece_c = jnp.concatenate([own_c, got_c], axis=1)
    two_c, rest_c = evenly(piece_c)
    pair_b = exchanged(two_b)
    sums = correlated([piece_b, pair_b, two_b, rest_b], first, sums, False)
    two_c = after(two_c, rest_c, sums)
    pair_c, relay_c = exchanged(two_c), relayed(two_c)
    return correlated([piece_c, pair_c, two_c, (rest_c, relay_c)], [(few, [(0, 0, 0), (0, 0, few)])], sums, True)


def general(volts, fir_taps, place, correlated):
    groups = lax.axis_size("tm")
    frames = volts.shape[1]
    volts, edge_frames, *fixed = prepare(volts, fir_taps, place, groups, frames // TAPS - 1, TAPS)
    history = lax.ppermute(edge_frames, "tm", [(i, i + 1) for i in range(groups - 1)])
    parts = [(history, TAPS, 0, 0, 1)] + [(volts, TAPS, i, TAPS * (i + 1), 1) for i in range(frames // TAPS)]
    spectrum = spectra(parts, frames, fixed, place, groups, [K2])[0]
    spectrum = lax.all_to_all(spectrum, "tm", split_axis=0, concat_axis=0, tiled=True)
    two, rest = farther(spectrum)
    spots = [(0, K2 // groups * t, 0) for t in range(groups)]
    return correlated([spectrum, exchanged(two), two, rest], [(spectrum.shape[1], spots)], None, True)


def local(voltage, fir_taps):
    groups = lax.axis_size("tm")
    place = jnp.stack([lax.axis_index("tm"), lax.axis_index("stn") % 2]).astype(jnp.int32)
    scale = 1.0 / (groups * voltage.shape[1])

    def correlated(arrays, pieces, before, last, wait=(), cost=10**3):
        flat, spots_of = [], []
        for array in arrays:
            parts = array if isinstance(array, tuple) else (array,)
            spots_of.append(tuple(range(len(flat), len(flat) + len(parts))))
            flat += parts
        laid = [(tiles, [[(where, r, c) for _, r, c in spots] for where in spots_of]) for tiles, spots in pieces]
        return correlate(flat, laid, K2 // groups, place, scale, before, last, wait, cost)

    run = paired if groups == 2 else general
    return natural(run(stacked(voltage), fir_taps, place, correlated))


def solution(mesh):
    return jax.shard_map(
        local,
        mesh=mesh,
        in_specs=(P("stn", "tm", None, None), P()),
        out_specs=P(None, "stn", None, "tm"),
        check_vma=False,
    )
```

```python
import functools
import math

import jax
import jax.numpy as jnp
import numpy as np
from jax import lax
from jax.experimental import pallas as pl
from jax.experimental.pallas import tpu as pltpu
from jax.sharding import PartitionSpec as P

NCH = 4096
CHANS = 2048
TAPS = 16
VISITS = 4
H = 32
LANES = 128
ROWS = 2 * H
K2 = CHANS // H
STEP = 8
TILE = 16
PLACES = (0, (1, 3), 2, (3, 1))
MEMBERS = 4
PAD = 8
SUB = 8
BF16 = jnp.bfloat16
F32 = jnp.float32


def angles(rows, columns, modulus):
    turns = np.outer(rows, columns) % modulus
    return turns.astype(np.float64) * (2.0 * math.pi / modulus)


def stage_one_table():
    theta = angles(np.arange(H), np.arange(H), H)
    cosine, sine = np.cos(theta), np.sin(theta)
    table = np.zeros((2, H, H, 2))
    table[0, :, :, 0], table[0, :, :, 1] = cosine, sine
    table[1, :, :, 0], table[1, :, :, 1] = -sine, cosine
    return np.pad(table.reshape(ROWS, ROWS), ((0, 0), (0, 2 * LANES - ROWS)))


def turn_table():
    theta = angles(np.arange(H), np.arange(LANES), NCH)
    return np.concatenate([np.cos(theta), np.sin(theta)], axis=1)


def stage_two_table(groups):
    theta = angles(np.arange(K2), np.arange(LANES), LANES)
    cosine, sine = np.cos(theta) / math.sqrt(NCH), np.sin(theta) / math.sqrt(NCH)
    real = np.concatenate([cosine, sine], 1).reshape(groups, 1, K2 // groups, 2 * LANES)
    imag = np.concatenate([-sine, cosine], 1).reshape(groups, 1, K2 // groups, 2 * LANES)
    return np.concatenate([real, imag], 1).reshape(2 * K2, 2 * LANES)


def halves(value):
    high = value.astype(BF16)
    return high, (value - high.astype(F32)).astype(BF16)


def dot(left, right):
    return lax.dot_general(left, right, (((1,), (0,)), ((), ())), preferred_element_type=F32)


def dot_nt(left, right):
    return lax.dot_general(left, right, (((1,), (1,)), ((), ())), preferred_element_type=F32)


def value_of(number, group):
    if isinstance(number, int):
        return number
    return number[0] + (number[1] - number[0]) * group


def prepare_kernel(edge_block, swapped, place, volts_source, taps_source, table_source, turn_source, volts, edge, taps, one, two, turn, done, taps_ref, table_ref):
    count = edge.shape[1]
    start = pl.multiple_of(value_of(edge_block, place[0]) * count, count)
    copies = [
        pltpu.make_async_copy(taps_source, taps_ref, done.at[0]),
        pltpu.make_async_copy(table_source, table_ref, done.at[1]),
        pltpu.make_async_copy(volts_source.at[:, pl.ds(start, count)], edge, done.at[2]),
        pltpu.make_async_copy(volts_source, volts, done.at[3]),
        pltpu.make_async_copy(turn_source, turn, done.at[4]),
    ]
    for copy in copies:
        copy.start()
    copies[0].wait()
    copies[1].wait()
    for h in range(H):
        for half in range(TAPS // SUB):
            tile = taps_ref[pl.ds(half * SUB, SUB), pl.ds(h * LANES, LANES)]
            for r in range(2):
                taps[pl.ds(half * SUB * ROWS + 2 * h + r, SUB, stride=ROWS), :] = tile
    high, low = halves(table_ref[:ROWS, :ROWS])
    one[...] = jnp.concatenate([high, high, low], axis=1)
    start = pl.multiple_of(ROWS + place[0] * (2 * K2 * swapped), SUB)
    high, low = halves(table_ref[pl.ds(start, 2 * K2), :])
    two[0] = high
    two[1] = low
    for copy in copies[2:]:
        copy.wait()


def prepare(volts, fir_taps, place, groups, edge_block, edge_frames):
    signals, frames = volts.shape[:2]
    two = stage_two_table(groups)
    table = np.concatenate([stage_one_table(), two, np.roll(two, K2, axis=0)]).astype(np.float32)
    vmem = pl.BlockSpec(memory_space=pltpu.VMEM)
    return pl.pallas_call(
        functools.partial(prepare_kernel, edge_block, int(groups == 2)),
        grid_spec=pltpu.PrefetchScalarGridSpec(
            num_scalar_prefetch=1,
            grid=(),
            in_specs=[pl.BlockSpec(memory_space=pl.ANY)] * 4,
            out_specs=[vmem] * 6,
            scratch_shapes=[
                pltpu.SemaphoreType.DMA((5,)),
                pltpu.VMEM(fir_taps.shape, F32),
                pltpu.VMEM(table.shape, F32),
            ],
        ),
        out_shape=[
            jax.ShapeDtypeStruct((signals, frames, ROWS, LANES), BF16),
            jax.ShapeDtypeStruct((signals, edge_frames, ROWS, LANES), BF16),
            jax.ShapeDtypeStruct((TAPS * ROWS, LANES), F32),
            jax.ShapeDtypeStruct((ROWS, 3 * ROWS), BF16),
            jax.ShapeDtypeStruct((2, 2 * K2, 2 * LANES), BF16),
            jax.ShapeDtypeStruct((H, 2 * LANES), F32),
        ],
        compiler_params=pltpu.CompilerParams(vmem_limit_bytes=24 << 20),
    )(
        place,
        *[
            pltpu.with_memory_space_constraint(x, pltpu.HBM)
            for x in (volts, fir_taps, jnp.asarray(table), jnp.asarray(turn_table(), F32))
        ],
    )


def spectra_kernel(groups, parts, out_frames, run, place, *refs):
    part_refs, refs = refs[: len(parts)], refs[len(parts) :]
    taps, one, two, turn = refs[:4]
    outs, (ext, filtered, turned, staged) = refs[4:-4], refs[-4:]
    step, steps, members = pl.program_id(0), pl.num_programs(0), MEMBERS
    per_group = K2 // groups
    share = LANES // out_frames
    tiles = H // share
    pairs = tiles // 2
    frame_rows, row_rows = ROWS + PAD, tiles * TILE + PAD

    def load(member):
        signal = step * members + member
        for (frames, block, start, valid), ref in zip(parts, part_refs):
            first = value_of(block, place[0]) * frames
            start = value_of(start, place[0])
            valid = value_of(valid, place[0])

            def fill(ref=ref, frames=frames, first=first, start=start):
                for f in range(frames):
                    ext[member, start + f] = ref[signal, first + f].astype(F32)

            def clear(frames=frames, start=start):
                for f in range(frames):
                    ext[member, start + f] = jnp.zeros((ROWS, LANES), F32)

            if isinstance(valid, int):
                fill() if valid else clear()
            else:
                pl.when(valid == 1)(fill)
                pl.when(valid == 0)(clear)

    def filter_rows(member, q):
        rows = pl.ds(pl.multiple_of(q * SUB, SUB), SUB)
        tap = [taps[pl.ds(pl.multiple_of(m * ROWS + q * SUB, SUB), SUB), :] for m in range(TAPS)]
        for f in range(out_frames):
            total = tap[0] * ext[member, f + 1, rows]
            for m in range(1, TAPS):
                total = total + tap[m] * ext[member, f + 1 + m, rows]
            filtered[member, f, rows] = total

    def first_stage(member):
        cosine = turn[:, :LANES]
        sine = turn[:, LANES:]
        for g in range(out_frames // STEP):
            block = jnp.concatenate([filtered[member, g * STEP + f] for f in range(STEP)], axis=1)
            high, low = halves(block)
            first = dot(one[...], jnp.concatenate([high, low, high], axis=0))
            for f in range(STEP):
                real = first[:H, f * LANES : (f + 1) * LANES]
                imag = first[H:, f * LANES : (f + 1) * LANES]
                at = (g * STEP + f) * frame_rows
                turned[member, at : at + H, :] = real * cosine + imag * sine
                turned[member, at + H : at + ROWS, :] = imag * cosine - real * sine

    def second_stage(member, pair):
        rows = []
        for k1 in range(2 * pair * share, 2 * (pair + 1) * share):
            for f in range(0, out_frames, SUB):
                rows.append(
                    jnp.concatenate(
                        [turned[member, pl.ds(f * frame_rows + p * H + k1, SUB, stride=frame_rows), :] for p in range(2)],
                        axis=1,
                    )
                )
        high, low = halves(jnp.concatenate(rows, axis=0))
        spectrum = dot_nt(two[0], high) + dot_nt(two[1], high) + dot_nt(two[0], low)
        for k in range(2):
            for t in range(groups):
                for p in range(2):
                    for k2 in range(0, per_group, SUB):
                        row = (t * 2 + p) * per_group + k2
                        start = (t * per_group + k2) * row_rows + (2 * pair + k) * TILE + p * SUB
                        staged[pl.ds(start + step * members + member, SUB, stride=row_rows), :] = spectrum[
                            row : row + SUB, k * LANES : (k + 1) * LANES
                        ]

    def write():
        at = 0
        for out in outs:

            def write_row(k2, carry):
                for k in range(tiles):
                    start = pl.multiple_of((at + k2) * row_rows + k * TILE, PAD)
                    out[k2, k] = staged[pl.ds(start, TILE), :].astype(BF16)
                return carry

            lax.fori_loop(0, out.shape[0], write_row, 0, unroll=2)
            at += out.shape[0]

    def body():
        for member in range(members):
            load(member)

        def filter_one(index, carry):
            filter_rows(index // (ROWS // SUB), index % (ROWS // SUB))
            return carry

        lax.fori_loop(0, members * (ROWS // SUB), filter_one, 0)
        for member in range(members):
            first_stage(member)
        for member in range(members):
            for pair in range(pairs):
                second_stage(member, pair)

        pl.when(step == steps - 1)(write)

    if isinstance(run, int):
        body()
    else:
        pl.when(value_of(run, place[0]) == 1)(body)


def after(value, *others):
    return lax.optimization_barrier((value, *others))[0]


def spectra(parts, out_frames, fixed, place, groups, sizes, run=1, wait=(), cost=10**6):
    signals = parts[0][0].shape[0]
    place = after(place, *wait)
    tiles = H * out_frames // LANES
    shapes = [(n, tiles, TILE, LANES) for n in sizes]
    return pl.pallas_call(
        functools.partial(spectra_kernel, groups, tuple(part[1:] for part in parts), out_frames, run),
        grid_spec=pltpu.PrefetchScalarGridSpec(
            num_scalar_prefetch=1,
            grid=(signals // MEMBERS,),
            in_specs=[pl.BlockSpec(memory_space=pltpu.VMEM)] * (len(parts) + 4),
            out_specs=[pl.BlockSpec(shape, lambda s, place: (0, 0, 0, 0)) for shape in shapes],
            scratch_shapes=[
                pltpu.VMEM((MEMBERS, TAPS + out_frames, ROWS, LANES), F32),
                pltpu.VMEM((MEMBERS, out_frames, ROWS, LANES), F32),
                pltpu.VMEM((MEMBERS, out_frames * (ROWS + PAD), LANES), F32),
                pltpu.VMEM((K2 * (tiles * TILE + PAD), LANES), F32),
            ],
        ),
        out_shape=[jax.ShapeDtypeStruct(shape, BF16) for shape in shapes],
        compiler_params=pltpu.CompilerParams(vmem_limit_bytes=32 << 20),
        cost_estimate=pl.CostEstimate(flops=cost, bytes_accessed=0, transcendentals=0),
    )(place, *[part[0] for part in parts], *fixed)


def after(value, *others):
    return lax.optimization_barrier((value, *others))[0]


def correlate_kernel(pieces, per_group, scale, add, last, place, *refs):
    refs = list(refs)
    sums = refs.pop() if last else None
    out = refs.pop()
    before = refs.pop() if add else None
    if not last:
        sums = out
    half = per_group // 2
    lane = lax.broadcasted_iota(jnp.int32, (SUB, LANES), 1)
    first_tile = lane < LANES // 2
    real_lane = lane % TILE < SUB
    sign = jnp.where(real_lane, 1.0, -1.0).astype(F32)

    def fetch(spot, tile, k2, k1):
        arrays, row, column = spot
        values = [refs[array][row + tile * half + k2, column + k1] for array in arrays]
        return values[0] if len(values) == 1 else values[0] + values[1]

    for number, piece in enumerate(pieces):
        tiles, piece = piece
        share = H // tiles
        where = lax.broadcasted_iota(jnp.int32, (TILE, LANES), 1) // (LANES // share)

        def pair(index, carry):
            k2 = index // tiles
            k1 = index % tiles
            own, other = [], []
            for position in range(len(piece[0])):
                rows = []
                for tile in range(2):
                    a = fetch(piece[0][position], tile, k2, k1)
                    rows += [jnp.where(where == c, a, jnp.zeros_like(a)) for c in range(share)]
                own.append(jnp.concatenate(rows, axis=0))
                rows = []
                for tile in range(2):
                    for visit in range(VISITS):
                        rows.append(fetch(piece[visit][position], tile, k2, k1))
                other.append(jnp.concatenate(rows, axis=0))
            product = dot_nt(jnp.concatenate(own, axis=1), jnp.concatenate(other, axis=1))
            for c in range(share):
                value = []
                for p in range(2):
                    at = [((tile * share + c) * 2 + p) * SUB for tile in range(2)]
                    value.append(
                        jnp.where(first_tile, product[at[0] : at[0] + SUB], product[at[1] : at[1] + SUB])
                    )
                turned = jnp.where(
                    real_lane, pltpu.roll(value[1], LANES - SUB, 1), pltpu.roll(value[1], SUB, 1)
                )
                total = value[0] * sign + turned
                channel = k2 // 4 * LANES + k2 % 4 * H + k1 * share + c
                rows = pl.ds(pl.multiple_of(channel * SUB, SUB), SUB)
                if number:
                    total = total + sums[rows, :]
                elif add:
                    total = total + before[rows, :]
                sums[rows, :] = total
            return carry

        lax.fori_loop(0, half * tiles, pair, 0, unroll=32)
    if not last:
        return

    def finish(index, carry):
        block = index // SUB
        signal = index % SUB
        value = sums[pl.ds(block * LANES * SUB + signal, LANES, stride=SUB), :]
        value = jnp.transpose(value * scale)
        at = 0
        for tile in range(2):
            for visit in range(VISITS):
                for part in range(2):
                    out[part, signal, value_of(PLACES[visit], place[1]), tile * (half // 4) + block] = value[at : at + SUB]
                    at += SUB
        return carry

    lax.fori_loop(0, half // 4 * SUB, finish, 0, unroll=8)


def correlate(arrays, pieces, per_group, place, scale, before, last, wait=(), cost=10**3):
    signals = TILE // 2
    rows = per_group // 2 * H * SUB
    place = after(place, *wait)
    shape = (2, signals, VISITS, per_group // 4, SUB, LANES) if last else (rows, LANES)
    operands = list(arrays) + ([] if before is None else [before])
    vmem = pl.BlockSpec(memory_space=pltpu.VMEM)
    result = pl.pallas_call(
        functools.partial(correlate_kernel, pieces, per_group, scale, before is not None, last),
        grid_spec=pltpu.PrefetchScalarGridSpec(
            num_scalar_prefetch=1,
            grid=(),
            in_specs=[vmem] * len(operands),
            out_specs=vmem,
            scratch_shapes=[pltpu.VMEM((rows, LANES), F32)] if last else [],
        ),
        out_shape=jax.ShapeDtypeStruct(shape, F32),
        compiler_params=pltpu.CompilerParams(vmem_limit_bytes=24 << 20),
        input_output_aliases={} if before is None or last else {len(operands): 0},
        cost_estimate=pl.CostEstimate(flops=cost, bytes_accessed=0, transcendentals=0),
    )(place, *operands)
    return result if last else pltpu.with_memory_space_constraint(result, pltpu.VMEM)


def stacked(voltage):
    s, f = voltage.shape[:2]
    return voltage.reshape(s, f, 2, H, LANES).transpose(0, 1, 3, 2, 4).reshape(s, f, ROWS, LANES)


def natural(out):
    parts, s, visits, i, t, lanes = out.shape
    return out.transpose(0, 1, 2, 4, 3, 5).reshape(parts, s, visits * t, i * lanes)


def shifted(block, axis, distance):
    size = lax.axis_size(axis)
    return lax.ppermute(block, axis, [(i, (i + distance) % size) for i in range(size)])


def farther(block):
    size = lax.axis_size("stn")
    rest = lax.ppermute(block, "stn", [(i, (i + 1 if i % 2 == 0 else i + 3) % size) for i in range(size)])
    return shifted(block, "stn", 2), rest


def evenly(block):
    size = lax.axis_size("stn")
    ways = [(i, (i + 1 if i % 2 == 0 else i + 3) % size) for i in range(size) if i % 4 < 3]
    return shifted(block, "stn", 2), lax.ppermute(block, "stn", ways)


def relayed(two):
    return lax.ppermute(two, "stn", [(i, i + 1) for i in range(lax.axis_size("stn")) if i % 4 == 1])


def exchanged(block):
    return lax.ppermute(block, "stn", [(i, i ^ 1) for i in range(lax.axis_size("stn"))])


def paired(volts, fir_taps, place, correlated):
    frames = volts.shape[1]
    me = lax.axis_index("tm")
    sizes = [K2 // 2, K2 // 2]
    swap = [(0, 1), (1, 0)]
    edge = TAPS // 2
    last = frames // edge
    many, few = TAPS * H // LANES, edge * H // LANES
    volts, edge_frames, *fixed = prepare(volts, fir_taps, place, 2, (last - 1, 0), edge)
    visiting = lax.ppermute(edge_frames, "tm", swap)
    own_a, away_a = spectra(
        [(volts, TAPS, 0, 0, (0, 1)), (volts, TAPS, (0, 1), TAPS, 1)], TAPS, fixed, place, 2, sizes
    )
    got_a = lax.ppermute(away_a, "tm", swap)
    two_a, rest_a = farther(own_a)
    own_b, away_b = spectra(
        [(volts, TAPS, 0, 0, 1), (volts, TAPS, 1, TAPS, 1)], TAPS, fixed, place, 2, sizes, (1, 0), (own_a,)
    )
    own_c, away_c = spectra(
        [
            (volts, edge, (last - 2, 0), (0, edge), 1),
            (volts, edge, (last - 1, 1), (edge, 2 * edge), 1),
            (visiting, edge, 0, (2 * edge, 0), 1),
        ],
        edge, fixed, place, 2, sizes, 1, (own_b, two_a),
    )
    got_a, own_c, away_b, away_c, two_a = lax.optimization_barrier((got_a, own_c, away_b, away_c, two_a))
    two_g, rest_g = evenly(got_a)
    got_b = lax.ppermute(away_b, "tm", [(0, 1)])
    pair_a = exchanged(two_a)
    first = [(many, [(0, 0, 0)])]
    sums = correlated([own_a, pair_a, two_a, rest_a], first, None, False)
    got_b, away_c, sums = lax.optimization_barrier((got_b, away_c, sums))
    got_c = lax.ppermute(away_c, "tm", swap)
    piece_b = jnp.where(me == 0, own_b, got_b)
    two_b, rest_b = evenly(piece_b)
    pair_g, relay_g = exchanged(two_g), relayed(two_g)
    sums = correlated([got_a, pair_g, two_g, (rest_g, relay_g)], first, sums, False)
    piece_c = jnp.concatenate([own_c, got_c], axis=1)
    two_c, rest_c = farther(piece_c)
    pair_b, relay_b = exchanged(two_b), relayed(two_b)
    pair_c = exchanged(after(two_c, rest_c, sums))
    sums = correlated([piece_b, pair_b, two_b, (rest_b, relay_b)], first, sums, False, (), 6 * 10**9)
    return correlated([piece_c, pair_c, two_c, rest_c], [(few, [(0, 0, 0), (0, 0, few)])], sums, True)


def general(volts, fir_taps, place, correlated):
    groups = lax.axis_size("tm")
    frames = volts.shape[1]
    volts, edge_frames, *fixed = prepare(volts, fir_taps, place, groups, frames // TAPS - 1, TAPS)
    history = lax.ppermute(edge_frames, "tm", [(i, i + 1) for i in range(groups - 1)])
    parts = [(history, TAPS, 0, 0, 1)] + [(volts, TAPS, i, TAPS * (i + 1), 1) for i in range(frames // TAPS)]
    spectrum = spectra(parts, frames, fixed, place, groups, [K2])[0]
    spectrum = lax.all_to_all(spectrum, "tm", split_axis=0, concat_axis=0, tiled=True)
    two, rest = farther(spectrum)
    spots = [(0, K2 // groups * t, 0) for t in range(groups)]
    return correlated([spectrum, exchanged(two), two, rest], [(spectrum.shape[1], spots)], None, True)


def local(voltage, fir_taps):
    groups = lax.axis_size("tm")
    place = jnp.stack([lax.axis_index("tm"), lax.axis_index("stn") % 2]).astype(jnp.int32)
    scale = 1.0 / (groups * voltage.shape[1])

    def correlated(arrays, pieces, before, last, wait=(), cost=10**3):
        flat, spots_of = [], []
        for array in arrays:
            parts = array if isinstance(array, tuple) else (array,)
            spots_of.append(tuple(range(len(flat), len(flat) + len(parts))))
            flat += parts
        laid = [(tiles, [[(where, r, c) for _, r, c in spots] for where in spots_of]) for tiles, spots in pieces]
        return correlate(flat, laid, K2 // groups, place, scale, before, last, wait, cost)

    run = paired if groups == 2 else general
    return natural(run(stacked(voltage), fir_taps, place, correlated))


def solution(mesh):
    return jax.shard_map(
        local,
        mesh=mesh,
        in_specs=(P("stn", "tm", None, None), P()),
        out_specs=P(None, "stn", None, "tm"),
        check_vma=False,
    )
```

```python
import functools
import math

import jax
import jax.numpy as jnp
import numpy as np
from jax import lax
from jax.experimental import pallas as pl
from jax.experimental.pallas import tpu as pltpu
from jax.sharding import PartitionSpec as P

NCH = 4096
CHANS = 2048
TAPS = 16
VISITS = 4
H = 32
LANES = 128
ROWS = 2 * H
K2 = CHANS // H
STEP = 8
TILE = 16
PLACES = (0, (1, 3), 2, (3, 1))
MEMBERS = 4
PAD = 8
SUB = 8
BF16 = jnp.bfloat16
F32 = jnp.float32


def angles(rows, columns, modulus):
    turns = np.outer(rows, columns) % modulus
    return turns.astype(np.float64) * (2.0 * math.pi / modulus)


def stage_one_table():
    theta = angles(np.arange(H), np.arange(H), H)
    cosine, sine = np.cos(theta), np.sin(theta)
    table = np.zeros((2, H, H, 2))
    table[0, :, :, 0], table[0, :, :, 1] = cosine, sine
    table[1, :, :, 0], table[1, :, :, 1] = -sine, cosine
    return np.pad(table.reshape(ROWS, ROWS), ((0, 0), (0, 2 * LANES - ROWS)))


def turn_table():
    theta = angles(np.arange(H), np.arange(LANES), NCH)
    return np.concatenate([np.cos(theta), np.sin(theta)], axis=1)


def stage_two_table(groups):
    theta = angles(np.arange(K2), np.arange(LANES), LANES)
    cosine, sine = np.cos(theta) / math.sqrt(NCH), np.sin(theta) / math.sqrt(NCH)
    real = np.concatenate([cosine, sine], 1).reshape(groups, 1, K2 // groups, 2 * LANES)
    imag = np.concatenate([-sine, cosine], 1).reshape(groups, 1, K2 // groups, 2 * LANES)
    return np.concatenate([real, imag], 1).reshape(2 * K2, 2 * LANES)


def halves(value):
    high = value.astype(BF16)
    return high, (value - high.astype(F32)).astype(BF16)


def dot(left, right):
    return lax.dot_general(left, right, (((1,), (0,)), ((), ())), preferred_element_type=F32)


def dot_nt(left, right):
    return lax.dot_general(left, right, (((1,), (1,)), ((), ())), preferred_element_type=F32)


def value_of(number, group):
    if isinstance(number, int):
        return number
    return number[0] + (number[1] - number[0]) * group


def prepare_kernel(edge_block, swapped, place, volts_source, taps_source, table_source, turn_source, volts, edge, taps, one, two, turn, done, taps_ref, table_ref):
    count = edge.shape[1]
    start = pl.multiple_of(value_of(edge_block, place[0]) * count, count)
    copies = [
        pltpu.make_async_copy(taps_source, taps_ref, done.at[0]),
        pltpu.make_async_copy(table_source, table_ref, done.at[1]),
        pltpu.make_async_copy(volts_source.at[:, pl.ds(start, count)], edge, done.at[2]),
        pltpu.make_async_copy(volts_source, volts, done.at[3]),
        pltpu.make_async_copy(turn_source, turn, done.at[4]),
    ]
    for copy in copies:
        copy.start()
    copies[0].wait()
    copies[1].wait()
    for h in range(H):
        for half in range(TAPS // SUB):
            tile = taps_ref[pl.ds(half * SUB, SUB), pl.ds(h * LANES, LANES)]
            for r in range(2):
                taps[pl.ds(half * SUB * ROWS + 2 * h + r, SUB, stride=ROWS), :] = tile
    high, low = halves(table_ref[:ROWS, :ROWS])
    one[...] = jnp.concatenate([high, high, low], axis=1)
    start = pl.multiple_of(ROWS + place[0] * (2 * K2 * swapped), SUB)
    high, low = halves(table_ref[pl.ds(start, 2 * K2), :])
    two[0] = high
    two[1] = low
    for copy in copies[2:]:
        copy.wait()


def prepare(volts, fir_taps, place, groups, edge_block, edge_frames):
    signals, frames = volts.shape[:2]
    two = stage_two_table(groups)
    table = np.concatenate([stage_one_table(), two, np.roll(two, K2, axis=0)]).astype(np.float32)
    vmem = pl.BlockSpec(memory_space=pltpu.VMEM)
    return pl.pallas_call(
        functools.partial(prepare_kernel, edge_block, int(groups == 2)),
        grid_spec=pltpu.PrefetchScalarGridSpec(
            num_scalar_prefetch=1,
            grid=(),
            in_specs=[pl.BlockSpec(memory_space=pl.ANY)] * 4,
            out_specs=[vmem] * 6,
            scratch_shapes=[
                pltpu.SemaphoreType.DMA((5,)),
                pltpu.VMEM(fir_taps.shape, F32),
                pltpu.VMEM(table.shape, F32),
            ],
        ),
        out_shape=[
            jax.ShapeDtypeStruct((signals, frames, ROWS, LANES), BF16),
            jax.ShapeDtypeStruct((signals, edge_frames, ROWS, LANES), BF16),
            jax.ShapeDtypeStruct((TAPS * ROWS, LANES), F32),
            jax.ShapeDtypeStruct((ROWS, 3 * ROWS), BF16),
            jax.ShapeDtypeStruct((2, 2 * K2, 2 * LANES), BF16),
            jax.ShapeDtypeStruct((H, 2 * LANES), F32),
        ],
        compiler_params=pltpu.CompilerParams(vmem_limit_bytes=24 << 20),
    )(
        place,
        *[
            pltpu.with_memory_space_constraint(x, pltpu.HBM)
            for x in (volts, fir_taps, jnp.asarray(table), jnp.asarray(turn_table(), F32))
        ],
    )


def spectra_kernel(groups, parts, out_frames, run, place, *refs):
    part_refs, refs = refs[: len(parts)], refs[len(parts) :]
    taps, one, two, turn = refs[:4]
    outs, (ext, filtered, turned, staged) = refs[4:-4], refs[-4:]
    step, steps, members = pl.program_id(0), pl.num_programs(0), MEMBERS
    per_group = K2 // groups
    share = LANES // out_frames
    tiles = H // share
    pairs = tiles // 2
    frame_rows, row_rows = ROWS + PAD, tiles * TILE + PAD

    def load(member):
        signal = step * members + member
        for (frames, block, start, valid), ref in zip(parts, part_refs):
            first = value_of(block, place[0]) * frames
            start = value_of(start, place[0])
            valid = value_of(valid, place[0])

            def fill(ref=ref, frames=frames, first=first, start=start):
                for f in range(frames):
                    ext[member, start + f] = ref[signal, first + f].astype(F32)

            def clear(frames=frames, start=start):
                for f in range(frames):
                    ext[member, start + f] = jnp.zeros((ROWS, LANES), F32)

            if isinstance(valid, int):
                fill() if valid else clear()
            else:
                pl.when(valid == 1)(fill)
                pl.when(valid == 0)(clear)

    def filter_rows(member, q):
        rows = pl.ds(pl.multiple_of(q * SUB, SUB), SUB)
        tap = [taps[pl.ds(pl.multiple_of(m * ROWS + q * SUB, SUB), SUB), :] for m in range(TAPS)]
        for f in range(out_frames):
            total = tap[0] * ext[member, f + 1, rows]
            for m in range(1, TAPS):
                total = total + tap[m] * ext[member, f + 1 + m, rows]
            filtered[member, f, rows] = total

    def first_stage(member):
        cosine = turn[:, :LANES]
        sine = turn[:, LANES:]
        for g in range(out_frames // STEP):
            block = jnp.concatenate([filtered[member, g * STEP + f] for f in range(STEP)], axis=1)
            high, low = halves(block)
            first = dot(one[...], jnp.concatenate([high, low, high], axis=0))
            for f in range(STEP):
                real = first[:H, f * LANES : (f + 1) * LANES]
                imag = first[H:, f * LANES : (f + 1) * LANES]
                at = (g * STEP + f) * frame_rows
                turned[member, at : at + H, :] = real * cosine + imag * sine
                turned[member, at + H : at + ROWS, :] = imag * cosine - real * sine

    def second_stage(member, pair):
        rows = []
        for k1 in range(2 * pair * share, 2 * (pair + 1) * share):
            for f in range(0, out_frames, SUB):
                rows.append(
                    jnp.concatenate(
                        [turned[member, pl.ds(f * frame_rows + p * H + k1, SUB, stride=frame_rows), :] for p in range(2)],
                        axis=1,
                    )
                )
        high, low = halves(jnp.concatenate(rows, axis=0))
        spectrum = dot_nt(two[0], high) + dot_nt(two[1], high) + dot_nt(two[0], low)
        for k in range(2):
            for t in range(groups):
                for p in range(2):
                    for k2 in range(0, per_group, SUB):
                        row = (t * 2 + p) * per_group + k2
                        start = (t * per_group + k2) * row_rows + (2 * pair + k) * TILE + p * SUB
                        staged[pl.ds(start + step * members + member, SUB, stride=row_rows), :] = spectrum[
                            row : row + SUB, k * LANES : (k + 1) * LANES
                        ]

    def write():
        at = 0
        for out in outs:

            def write_row(k2, carry):
                for k in range(tiles):
                    start = pl.multiple_of((at + k2) * row_rows + k * TILE, PAD)
                    out[k2, k] = staged[pl.ds(start, TILE), :].astype(BF16)
                return carry

            lax.fori_loop(0, out.shape[0], write_row, 0, unroll=2)
            at += out.shape[0]

    def body():
        for member in range(members):
            load(member)

        def filter_one(index, carry):
            filter_rows(index // (ROWS // SUB), index % (ROWS // SUB))
            return carry

        lax.fori_loop(0, members * (ROWS // SUB), filter_one, 0)
        for member in range(members):
            first_stage(member)
        for member in range(members):
            for pair in range(pairs):
                second_stage(member, pair)

        pl.when(step == steps - 1)(write)

    if isinstance(run, int):
        body()
    else:
        pl.when(value_of(run, place[0]) == 1)(body)


def after(value, *others):
    return lax.optimization_barrier((value, *others))[0]


def spectra(parts, out_frames, fixed, place, groups, sizes, run=1, wait=(), cost=10**6):
    signals = parts[0][0].shape[0]
    place = after(place, *wait)
    tiles = H * out_frames // LANES
    shapes = [(n, tiles, TILE, LANES) for n in sizes]
    return pl.pallas_call(
        functools.partial(spectra_kernel, groups, tuple(part[1:] for part in parts), out_frames, run),
        grid_spec=pltpu.PrefetchScalarGridSpec(
            num_scalar_prefetch=1,
            grid=(signals // MEMBERS,),
            in_specs=[pl.BlockSpec(memory_space=pltpu.VMEM)] * (len(parts) + 4),
            out_specs=[pl.BlockSpec(shape, lambda s, place: (0, 0, 0, 0)) for shape in shapes],
            scratch_shapes=[
                pltpu.VMEM((MEMBERS, TAPS + out_frames, ROWS, LANES), F32),
                pltpu.VMEM((MEMBERS, out_frames, ROWS, LANES), F32),
                pltpu.VMEM((MEMBERS, out_frames * (ROWS + PAD), LANES), F32),
                pltpu.VMEM((K2 * (tiles * TILE + PAD), LANES), F32),
            ],
        ),
        out_shape=[jax.ShapeDtypeStruct(shape, BF16) for shape in shapes],
        compiler_params=pltpu.CompilerParams(vmem_limit_bytes=32 << 20),
        cost_estimate=pl.CostEstimate(flops=cost, bytes_accessed=0, transcendentals=0),
    )(place, *[part[0] for part in parts], *fixed)


def after(value, *others):
    return lax.optimization_barrier((value, *others))[0]


def correlate_kernel(pieces, per_group, scale, add, last, place, *refs):
    refs = list(refs)
    sums = refs.pop() if last else None
    out = refs.pop()
    before = refs.pop() if add else None
    if not last:
        sums = out
    half = per_group // 2
    lane = lax.broadcasted_iota(jnp.int32, (SUB, LANES), 1)
    first_tile = lane < LANES // 2
    real_lane = lane % TILE < SUB
    sign = jnp.where(real_lane, 1.0, -1.0).astype(F32)

    def fetch(spot, tile, k2, k1):
        arrays, row, column = spot
        values = [refs[array][row + tile * half + k2, column + k1] for array in arrays]
        return values[0] if len(values) == 1 else values[0] + values[1]

    for number, piece in enumerate(pieces):
        tiles, piece = piece
        share = H // tiles
        where = lax.broadcasted_iota(jnp.int32, (TILE, LANES), 1) // (LANES // share)

        def pair(index, carry):
            k2 = index // tiles
            k1 = index % tiles
            own, other = [], []
            for position in range(len(piece[0])):
                rows = []
                for tile in range(2):
                    a = fetch(piece[0][position], tile, k2, k1)
                    rows += [jnp.where(where == c, a, jnp.zeros_like(a)) for c in range(share)]
                own.append(jnp.concatenate(rows, axis=0))
                rows = []
                for tile in range(2):
                    for visit in range(VISITS):
                        rows.append(fetch(piece[visit][position], tile, k2, k1))
                other.append(jnp.concatenate(rows, axis=0))
            product = dot_nt(jnp.concatenate(own, axis=1), jnp.concatenate(other, axis=1))
            for c in range(share):
                value = []
                for p in range(2):
                    at = [((tile * share + c) * 2 + p) * SUB for tile in range(2)]
                    value.append(
                        jnp.where(first_tile, product[at[0] : at[0] + SUB], product[at[1] : at[1] + SUB])
                    )
                turned = jnp.where(
                    real_lane, pltpu.roll(value[1], LANES - SUB, 1), pltpu.roll(value[1], SUB, 1)
                )
                total = value[0] * sign + turned
                channel = k2 // 4 * LANES + k2 % 4 * H + k1 * share + c
                rows = pl.ds(pl.multiple_of(channel * SUB, SUB), SUB)
                if number:
                    total = total + sums[rows, :]
                elif add:
                    total = total + before[rows, :]
                sums[rows, :] = total
            return carry

        lax.fori_loop(0, half * tiles, pair, 0, unroll=32)
    if not last:
        return

    def finish(index, carry):
        block = index // SUB
        signal = index % SUB
        value = sums[pl.ds(block * LANES * SUB + signal, LANES, stride=SUB), :]
        value = jnp.transpose(value * scale)
        at = 0
        for tile in range(2):
            for visit in range(VISITS):
                for part in range(2):
                    out[part, signal, value_of(PLACES[visit], place[1]), tile * (half // 4) + block] = value[at : at + SUB]
                    at += SUB
        return carry

    lax.fori_loop(0, half // 4 * SUB, finish, 0, unroll=8)


def correlate(arrays, pieces, per_group, place, scale, before, last, wait=(), cost=10**3):
    signals = TILE // 2
    rows = per_group // 2 * H * SUB
    place = after(place, *wait)
    shape = (2, signals, VISITS, per_group // 4, SUB, LANES) if last else (rows, LANES)
    operands = list(arrays) + ([] if before is None else [before])
    vmem = pl.BlockSpec(memory_space=pltpu.VMEM)
    result = pl.pallas_call(
        functools.partial(correlate_kernel, pieces, per_group, scale, before is not None, last),
        grid_spec=pltpu.PrefetchScalarGridSpec(
            num_scalar_prefetch=1,
            grid=(),
            in_specs=[vmem] * len(operands),
            out_specs=vmem,
            scratch_shapes=[pltpu.VMEM((rows, LANES), F32)] if last else [],
        ),
        out_shape=jax.ShapeDtypeStruct(shape, F32),
        compiler_params=pltpu.CompilerParams(vmem_limit_bytes=24 << 20),
        input_output_aliases={} if before is None or last else {len(operands): 0},
        cost_estimate=pl.CostEstimate(flops=cost, bytes_accessed=0, transcendentals=0),
    )(place, *operands)
    return result if last else pltpu.with_memory_space_constraint(result, pltpu.VMEM)


def stacked(voltage):
    s, f = voltage.shape[:2]
    return voltage.reshape(s, f, 2, H, LANES).transpose(0, 1, 3, 2, 4).reshape(s, f, ROWS, LANES)


def natural(out):
    parts, s, visits, i, t, lanes = out.shape
    return out.transpose(0, 1, 2, 4, 3, 5).reshape(parts, s, visits * t, i * lanes)


def shifted(block, axis, distance):
    size = lax.axis_size(axis)
    return lax.ppermute(block, axis, [(i, (i + distance) % size) for i in range(size)])


def farther(block):
    size = lax.axis_size("stn")
    rest = lax.ppermute(block, "stn", [(i, (i + 1 if i % 2 == 0 else i + 3) % size) for i in range(size)])
    return shifted(block, "stn", 2), rest


def evenly(block):
    size = lax.axis_size("stn")
    ways = [(i, (i + 1 if i % 2 == 0 else i + 3) % size) for i in range(size) if i % 4 < 3]
    return shifted(block, "stn", 2), lax.ppermute(block, "stn", ways)


def relayed(two):
    return lax.ppermute(two, "stn", [(i, i + 1) for i in range(lax.axis_size("stn")) if i % 4 == 1])


def exchanged(block):
    return lax.ppermute(block, "stn", [(i, i ^ 1) for i in range(lax.axis_size("stn"))])


def paired(volts, fir_taps, place, correlated):
    frames = volts.shape[1]
    me = lax.axis_index("tm")
    sizes = [K2 // 2, K2 // 2]
    swap = [(0, 1), (1, 0)]
    edge = TAPS // 2
    last = frames // edge
    many, few = TAPS * H // LANES, edge * H // LANES
    volts, edge_frames, *fixed = prepare(volts, fir_taps, place, 2, (last - 1, 0), edge)
    visiting = lax.ppermute(edge_frames, "tm", swap)
    own_a, away_a = spectra(
        [(volts, TAPS, 0, 0, (0, 1)), (volts, TAPS, (0, 1), TAPS, 1)], TAPS, fixed, place, 2, sizes
    )
    got_a = lax.ppermute(away_a, "tm", swap)
    two_a, rest_a = farther(own_a)
    own_b, away_b = spectra(
        [(volts, TAPS, 0, 0, 1), (volts, TAPS, 1, TAPS, 1)], TAPS, fixed, place, 2, sizes, (1, 0), (own_a,)
    )
    own_c, away_c = spectra(
        [
            (volts, edge, (last - 2, 0), (0, edge), 1),
            (volts, edge, (last - 1, 1), (edge, 2 * edge), 1),
            (visiting, edge, 0, (2 * edge, 0), 1),
        ],
        edge, fixed, place, 2, sizes, 1, (own_b, two_a),
    )
    got_a, own_c, away_b, away_c, two_a = lax.optimization_barrier((got_a, own_c, away_b, away_c, two_a))
    two_g, rest_g = evenly(got_a)
    got_b = lax.ppermute(away_b, "tm", [(0, 1)])
    pair_a = exchanged(two_a)
    first = [(many, [(0, 0, 0)])]
    sums = correlated([own_a, pair_a, two_a, rest_a], first, None, False)
    got_b, away_c, sums = lax.optimization_barrier((got_b, away_c, sums))
    got_c = lax.ppermute(away_c, "tm", swap)
    piece_b = jnp.where(me == 0, own_b, got_b)
    two_b, rest_b = farther(piece_b)
    pair_g, relay_g = exchanged(two_g), relayed(two_g)
    sums = correlated([got_a, pair_g, two_g, (rest_g, relay_g)], first, sums, False)
    piece_c = jnp.concatenate([own_c, got_c], axis=1)
    two_c, rest_c = farther(piece_c)
    pair_b = exchanged(two_b)
    sums = correlated([piece_b, pair_b, two_b, rest_b], first, sums, False)
    rest_c, two_c, sums = lax.optimization_barrier((rest_c, two_c, sums))
    pair_c = exchanged(two_c)
    return correlated([piece_c, pair_c, two_c, rest_c], [(few, [(0, 0, 0), (0, 0, few)])], sums, True)


def general(volts, fir_taps, place, correlated):
    groups = lax.axis_size("tm")
    frames = volts.shape[1]
    volts, edge_frames, *fixed = prepare(volts, fir_taps, place, groups, frames // TAPS - 1, TAPS)
    history = lax.ppermute(edge_frames, "tm", [(i, i + 1) for i in range(groups - 1)])
    parts = [(history, TAPS, 0, 0, 1)] + [(volts, TAPS, i, TAPS * (i + 1), 1) for i in range(frames // TAPS)]
    spectrum = spectra(parts, frames, fixed, place, groups, [K2])[0]
    spectrum = lax.all_to_all(spectrum, "tm", split_axis=0, concat_axis=0, tiled=True)
    two, rest = farther(spectrum)
    spots = [(0, K2 // groups * t, 0) for t in range(groups)]
    return correlated([spectrum, exchanged(two), two, rest], [(spectrum.shape[1], spots)], None, True)


def local(voltage, fir_taps):
    groups = lax.axis_size("tm")
    place = jnp.stack([lax.axis_index("tm"), lax.axis_index("stn") % 2]).astype(jnp.int32)
    scale = 1.0 / (groups * voltage.shape[1])

    def correlated(arrays, pieces, before, last, wait=(), cost=10**3):
        flat, spots_of = [], []
        for array in arrays:
            parts = array if isinstance(array, tuple) else (array,)
            spots_of.append(tuple(range(len(flat), len(flat) + len(parts))))
            flat += parts
        laid = [(tiles, [[(where, r, c) for _, r, c in spots] for where in spots_of]) for tiles, spots in pieces]
        return correlate(flat, laid, K2 // groups, place, scale, before, last, wait, cost)

    run = paired if groups == 2 else general
    return natural(run(stacked(voltage), fir_taps, place, correlated))


def solution(mesh):
    return jax.shard_map(
        local,
        mesh=mesh,
        in_specs=(P("stn", "tm", None, None), P()),
        out_specs=P(None, "stn", None, "tm"),
        check_vma=False,
    )
```

```python
import functools
import math

import jax
import jax.numpy as jnp
import numpy as np
from jax import lax
from jax.experimental import pallas as pl
from jax.experimental.pallas import tpu as pltpu
from jax.sharding import PartitionSpec as P

NCH = 4096
CHANS = 2048
TAPS = 16
VISITS = 4
H = 32
LANES = 128
ROWS = 2 * H
K2 = CHANS // H
STEP = 8
TILE = 16
PLACES = (0, (1, 3), 2, (3, 1))
MEMBERS = 4
PAD = 8
SUB = 8
BF16 = jnp.bfloat16
F32 = jnp.float32


def angles(rows, columns, modulus):
    turns = np.outer(rows, columns) % modulus
    return turns.astype(np.float64) * (2.0 * math.pi / modulus)


def stage_one_table():
    theta = angles(np.arange(H), np.arange(H), H)
    cosine, sine = np.cos(theta), np.sin(theta)
    table = np.zeros((2, H, H, 2))
    table[0, :, :, 0], table[0, :, :, 1] = cosine, sine
    table[1, :, :, 0], table[1, :, :, 1] = -sine, cosine
    return np.pad(table.reshape(ROWS, ROWS), ((0, 0), (0, 2 * LANES - ROWS)))


def turn_table():
    theta = angles(np.arange(H), np.arange(LANES), NCH)
    return np.concatenate([np.cos(theta), np.sin(theta)], axis=1)


def stage_two_table(groups):
    theta = angles(np.arange(K2), np.arange(LANES), LANES)
    cosine, sine = np.cos(theta) / math.sqrt(NCH), np.sin(theta) / math.sqrt(NCH)
    real = np.concatenate([cosine, sine], 1).reshape(groups, 1, K2 // groups, 2 * LANES)
    imag = np.concatenate([-sine, cosine], 1).reshape(groups, 1, K2 // groups, 2 * LANES)
    return np.concatenate([real, imag], 1).reshape(2 * K2, 2 * LANES)


def halves(value):
    high = value.astype(BF16)
    return high, (value - high.astype(F32)).astype(BF16)


def dot(left, right):
    return lax.dot_general(left, right, (((1,), (0,)), ((), ())), preferred_element_type=F32)


def dot_nt(left, right):
    return lax.dot_general(left, right, (((1,), (1,)), ((), ())), preferred_element_type=F32)


def value_of(number, group):
    if isinstance(number, int):
        return number
    return number[0] + (number[1] - number[0]) * group


def cut_kernel(edge_block, place, source, edge, done):
    count = edge.shape[1]
    start = pl.multiple_of(value_of(edge_block, place[0]) * count, count)
    copy = pltpu.make_async_copy(source.at[:, pl.ds(start, count)], edge, done)
    copy.start()
    copy.wait()


def cut(volts, place, edge_block, edge_frames):
    return pl.pallas_call(
        functools.partial(cut_kernel, edge_block),
        grid_spec=pltpu.PrefetchScalarGridSpec(
            num_scalar_prefetch=1,
            grid=(),
            in_specs=[pl.BlockSpec(memory_space=pl.ANY)],
            out_specs=pl.BlockSpec(memory_space=pltpu.VMEM),
            scratch_shapes=[pltpu.SemaphoreType.DMA],
        ),
        out_shape=jax.ShapeDtypeStruct((volts.shape[0], edge_frames, ROWS, LANES), BF16),
        compiler_params=pltpu.CompilerParams(vmem_limit_bytes=24 << 20),
    )(place, pltpu.with_memory_space_constraint(volts, pltpu.HBM))


def prepare_kernel(swapped, place, volts_source, taps_source, table_source, turn_source, volts, taps, one, two, turn, done, taps_ref, table_ref):
    copies = [
        pltpu.make_async_copy(taps_source, taps_ref, done.at[0]),
        pltpu.make_async_copy(table_source, table_ref, done.at[1]),
        pltpu.make_async_copy(volts_source, volts, done.at[2]),
        pltpu.make_async_copy(turn_source, turn, done.at[3]),
    ]
    for copy in copies:
        copy.start()
    copies[0].wait()
    copies[1].wait()
    for h in range(H):
        for half in range(TAPS // SUB):
            tile = taps_ref[pl.ds(half * SUB, SUB), pl.ds(h * LANES, LANES)]
            for r in range(2):
                taps[pl.ds(half * SUB * ROWS + 2 * h + r, SUB, stride=ROWS), :] = tile
    high, low = halves(table_ref[:ROWS, :ROWS])
    one[...] = jnp.concatenate([high, high, low], axis=1)
    start = pl.multiple_of(ROWS + place[0] * (2 * K2 * swapped), SUB)
    high, low = halves(table_ref[pl.ds(start, 2 * K2), :])
    two[0] = high
    two[1] = low
    for copy in copies[2:]:
        copy.wait()


def prepare(volts, fir_taps, place, groups):
    signals, frames = volts.shape[:2]
    two = stage_two_table(groups)
    table = np.concatenate([stage_one_table(), two, np.roll(two, K2, axis=0)]).astype(np.float32)
    vmem = pl.BlockSpec(memory_space=pltpu.VMEM)
    return pl.pallas_call(
        functools.partial(prepare_kernel, int(groups == 2)),
        grid_spec=pltpu.PrefetchScalarGridSpec(
            num_scalar_prefetch=1,
            grid=(),
            in_specs=[pl.BlockSpec(memory_space=pl.ANY)] * 4,
            out_specs=[vmem] * 5,
            scratch_shapes=[
                pltpu.SemaphoreType.DMA((4,)),
                pltpu.VMEM(fir_taps.shape, F32),
                pltpu.VMEM(table.shape, F32),
            ],
        ),
        out_shape=[
            jax.ShapeDtypeStruct((signals, frames, ROWS, LANES), BF16),
            jax.ShapeDtypeStruct((TAPS * ROWS, LANES), F32),
            jax.ShapeDtypeStruct((ROWS, 3 * ROWS), BF16),
            jax.ShapeDtypeStruct((2, 2 * K2, 2 * LANES), BF16),
            jax.ShapeDtypeStruct((H, 2 * LANES), F32),
        ],
        compiler_params=pltpu.CompilerParams(vmem_limit_bytes=24 << 20),
    )(
        place,
        *[
            pltpu.with_memory_space_constraint(x, pltpu.HBM)
            for x in (volts, fir_taps, jnp.asarray(table), jnp.asarray(turn_table(), F32))
        ],
    )


def spectra_kernel(groups, parts, out_frames, run, place, *refs):
    part_refs, refs = refs[: len(parts)], refs[len(parts) :]
    taps, one, two, turn = refs[:4]
    outs, (ext, filtered, turned, staged) = refs[4:-4], refs[-4:]
    step, steps, members = pl.program_id(0), pl.num_programs(0), MEMBERS
    per_group = K2 // groups
    share = LANES // out_frames
    tiles = H // share
    pairs = tiles // 2
    frame_rows, row_rows = ROWS + PAD, tiles * TILE + PAD

    def load(member):
        signal = step * members + member
        for (frames, block, start, valid), ref in zip(parts, part_refs):
            first = value_of(block, place[0]) * frames
            start = value_of(start, place[0])
            valid = value_of(valid, place[0])

            def fill(ref=ref, frames=frames, first=first, start=start):
                for f in range(frames):
                    ext[member, start + f] = ref[signal, first + f].astype(F32)

            def clear(frames=frames, start=start):
                for f in range(frames):
                    ext[member, start + f] = jnp.zeros((ROWS, LANES), F32)

            if isinstance(valid, int):
                fill() if valid else clear()
            else:
                pl.when(valid == 1)(fill)
                pl.when(valid == 0)(clear)

    def filter_rows(member, q):
        rows = pl.ds(pl.multiple_of(q * SUB, SUB), SUB)
        tap = [taps[pl.ds(pl.multiple_of(m * ROWS + q * SUB, SUB), SUB), :] for m in range(TAPS)]
        for f in range(out_frames):
            total = tap[0] * ext[member, f + 1, rows]
            for m in range(1, TAPS):
                total = total + tap[m] * ext[member, f + 1 + m, rows]
            filtered[member, f, rows] = total

    def first_stage(member):
        cosine = turn[:, :LANES]
        sine = turn[:, LANES:]
        for g in range(out_frames // STEP):
            block = jnp.concatenate([filtered[member, g * STEP + f] for f in range(STEP)], axis=1)
            high, low = halves(block)
            first = dot(one[...], jnp.concatenate([high, low, high], axis=0))
            for f in range(STEP):
                real = first[:H, f * LANES : (f + 1) * LANES]
                imag = first[H:, f * LANES : (f + 1) * LANES]
                at = (g * STEP + f) * frame_rows
                turned[member, at : at + H, :] = real * cosine + imag * sine
                turned[member, at + H : at + ROWS, :] = imag * cosine - real * sine

    def second_stage(member, pair):
        rows = []
        for k1 in range(2 * pair * share, 2 * (pair + 1) * share):
            for f in range(0, out_frames, SUB):
                rows.append(
                    jnp.concatenate(
                        [turned[member, pl.ds(f * frame_rows + p * H + k1, SUB, stride=frame_rows), :] for p in range(2)],
                        axis=1,
                    )
                )
        high, low = halves(jnp.concatenate(rows, axis=0))
        spectrum = dot_nt(two[0], high) + dot_nt(two[1], high) + dot_nt(two[0], low)
        for k in range(2):
            for t in range(groups):
                for p in range(2):
                    for k2 in range(0, per_group, SUB):
                        row = (t * 2 + p) * per_group + k2
                        start = (t * per_group + k2) * row_rows + (2 * pair + k) * TILE + p * SUB
                        staged[pl.ds(start + step * members + member, SUB, stride=row_rows), :] = spectrum[
                            row : row + SUB, k * LANES : (k + 1) * LANES
                        ]

    def write():
        at = 0
        for out in outs:

            def write_row(k2, carry):
                for k in range(tiles):
                    start = pl.multiple_of((at + k2) * row_rows + k * TILE, PAD)
                    out[k2, k] = staged[pl.ds(start, TILE), :].astype(BF16)
                return carry

            lax.fori_loop(0, out.shape[0], write_row, 0, unroll=2)
            at += out.shape[0]

    def body():
        for member in range(members):
            load(member)

        def filter_one(index, carry):
            filter_rows(index // (ROWS // SUB), index % (ROWS // SUB))
            return carry

        lax.fori_loop(0, members * (ROWS // SUB), filter_one, 0)
        for member in range(members):
            first_stage(member)
        for member in range(members):
            for pair in range(pairs):
                second_stage(member, pair)

        pl.when(step == steps - 1)(write)

    if isinstance(run, int):
        body()
    else:
        pl.when(value_of(run, place[0]) == 1)(body)


def after(value, *others):
    return lax.optimization_barrier((value, *others))[0]


def spectra(parts, out_frames, fixed, place, groups, sizes, run=1, wait=(), cost=10**6):
    signals = parts[0][0].shape[0]
    place = after(place, *wait)
    tiles = H * out_frames // LANES
    shapes = [(n, tiles, TILE, LANES) for n in sizes]
    return pl.pallas_call(
        functools.partial(spectra_kernel, groups, tuple(part[1:] for part in parts), out_frames, run),
        grid_spec=pltpu.PrefetchScalarGridSpec(
            num_scalar_prefetch=1,
            grid=(signals // MEMBERS,),
            in_specs=[pl.BlockSpec(memory_space=pltpu.VMEM)] * (len(parts) + 4),
            out_specs=[pl.BlockSpec(shape, lambda s, place: (0, 0, 0, 0)) for shape in shapes],
            scratch_shapes=[
                pltpu.VMEM((MEMBERS, TAPS + out_frames, ROWS, LANES), F32),
                pltpu.VMEM((MEMBERS, out_frames, ROWS, LANES), F32),
                pltpu.VMEM((MEMBERS, out_frames * (ROWS + PAD), LANES), F32),
                pltpu.VMEM((K2 * (tiles * TILE + PAD), LANES), F32),
            ],
        ),
        out_shape=[jax.ShapeDtypeStruct(shape, BF16) for shape in shapes],
        compiler_params=pltpu.CompilerParams(vmem_limit_bytes=32 << 20),
        cost_estimate=pl.CostEstimate(flops=cost, bytes_accessed=0, transcendentals=0),
    )(place, *[part[0] for part in parts], *fixed)


def after(value, *others):
    return lax.optimization_barrier((value, *others))[0]


def correlate_kernel(pieces, per_group, scale, add, last, place, *refs):
    refs = list(refs)
    sums = refs.pop() if last else None
    out = refs.pop()
    before = refs.pop() if add else None
    if not last:
        sums = out
    half = per_group // 2
    lane = lax.broadcasted_iota(jnp.int32, (SUB, LANES), 1)
    first_tile = lane < LANES // 2
    real_lane = lane % TILE < SUB
    sign = jnp.where(real_lane, 1.0, -1.0).astype(F32)

    def fetch(spot, tile, k2, k1):
        arrays, row, column = spot
        values = [refs[array][row + tile * half + k2, column + k1] for array in arrays]
        return values[0] if len(values) == 1 else values[0] + values[1]

    for number, piece in enumerate(pieces):
        tiles, piece = piece
        share = H // tiles
        where = lax.broadcasted_iota(jnp.int32, (TILE, LANES), 1) // (LANES // share)

        def pair(index, carry):
            k2 = index // tiles
            k1 = index % tiles
            own, other = [], []
            for position in range(len(piece[0])):
                rows = []
                for tile in range(2):
                    a = fetch(piece[0][position], tile, k2, k1)
                    rows += [jnp.where(where == c, a, jnp.zeros_like(a)) for c in range(share)]
                own.append(jnp.concatenate(rows, axis=0))
                rows = []
                for tile in range(2):
                    for visit in range(VISITS):
                        rows.append(fetch(piece[visit][position], tile, k2, k1))
                other.append(jnp.concatenate(rows, axis=0))
            product = dot_nt(jnp.concatenate(own, axis=1), jnp.concatenate(other, axis=1))
            for c in range(share):
                value = []
                for p in range(2):
                    at = [((tile * share + c) * 2 + p) * SUB for tile in range(2)]
                    value.append(
                        jnp.where(first_tile, product[at[0] : at[0] + SUB], product[at[1] : at[1] + SUB])
                    )
                turned = jnp.where(
                    real_lane, pltpu.roll(value[1], LANES - SUB, 1), pltpu.roll(value[1], SUB, 1)
                )
                total = value[0] * sign + turned
                channel = k2 // 4 * LANES + k2 % 4 * H + k1 * share + c
                rows = pl.ds(pl.multiple_of(channel * SUB, SUB), SUB)
                if number:
                    total = total + sums[rows, :]
                elif add:
                    total = total + before[rows, :]
                sums[rows, :] = total
            return carry

        lax.fori_loop(0, half * tiles, pair, 0, unroll=32)
    if not last:
        return

    def finish(index, carry):
        block = index // SUB
        signal = index % SUB
        value = sums[pl.ds(block * LANES * SUB + signal, LANES, stride=SUB), :]
        value = jnp.transpose(value * scale)
        at = 0
        for tile in range(2):
            for visit in range(VISITS):
                for part in range(2):
                    out[part, signal, value_of(PLACES[visit], place[1]), tile * (half // 4) + block] = value[at : at + SUB]
                    at += SUB
        return carry

    lax.fori_loop(0, half // 4 * SUB, finish, 0, unroll=8)


def correlate(arrays, pieces, per_group, place, scale, before, last, wait=(), cost=10**3):
    signals = TILE // 2
    rows = per_group // 2 * H * SUB
    place = after(place, *wait)
    shape = (2, signals, VISITS, per_group // 4, SUB, LANES) if last else (rows, LANES)
    operands = list(arrays) + ([] if before is None else [before])
    vmem = pl.BlockSpec(memory_space=pltpu.VMEM)
    result = pl.pallas_call(
        functools.partial(correlate_kernel, pieces, per_group, scale, before is not None, last),
        grid_spec=pltpu.PrefetchScalarGridSpec(
            num_scalar_prefetch=1,
            grid=(),
            in_specs=[vmem] * len(operands),
            out_specs=vmem,
            scratch_shapes=[pltpu.VMEM((rows, LANES), F32)] if last else [],
        ),
        out_shape=jax.ShapeDtypeStruct(shape, F32),
        compiler_params=pltpu.CompilerParams(vmem_limit_bytes=24 << 20),
        input_output_aliases={} if before is None or last else {len(operands): 0},
        cost_estimate=pl.CostEstimate(flops=cost, bytes_accessed=0, transcendentals=0),
    )(place, *operands)
    return result if last else pltpu.with_memory_space_constraint(result, pltpu.VMEM)


def stacked(voltage):
    s, f = voltage.shape[:2]
    return voltage.reshape(s, f, 2, H, LANES).transpose(0, 1, 3, 2, 4).reshape(s, f, ROWS, LANES)


def natural(out):
    parts, s, visits, i, t, lanes = out.shape
    return out.transpose(0, 1, 2, 4, 3, 5).reshape(parts, s, visits * t, i * lanes)


def shifted(block, axis, distance):
    size = lax.axis_size(axis)
    return lax.ppermute(block, axis, [(i, (i + distance) % size) for i in range(size)])


def farther(block):
    size = lax.axis_size("stn")
    rest = lax.ppermute(block, "stn", [(i, (i + 1 if i % 2 == 0 else i + 3) % size) for i in range(size)])
    return shifted(block, "stn", 2), rest


def evenly(block):
    size = lax.axis_size("stn")
    ways = [(i, (i + 1 if i % 2 == 0 else i + 3) % size) for i in range(size) if i % 4 < 3]
    return shifted(block, "stn", 2), lax.ppermute(block, "stn", ways)


def relayed(two):
    return lax.ppermute(two, "stn", [(i, i + 1) for i in range(lax.axis_size("stn")) if i % 4 == 1])


def exchanged(block):
    return lax.ppermute(block, "stn", [(i, i ^ 1) for i in range(lax.axis_size("stn"))])


def paired(volts, fir_taps, place, correlated):
    frames = volts.shape[1]
    me = lax.axis_index("tm")
    sizes = [K2 // 2, K2 // 2]
    swap = [(0, 1), (1, 0)]
    edge = TAPS // 2
    last = frames // edge
    many, few = TAPS * H // LANES, edge * H // LANES
    edge_frames = cut(volts, place, (last - 1, 0), edge)
    visiting = lax.ppermute(edge_frames, "tm", swap)
    volts, *fixed = prepare(volts, fir_taps, after(place, edge_frames), 2)
    own_a, away_a = spectra(
        [(volts, TAPS, 0, 0, (0, 1)), (volts, TAPS, (0, 1), TAPS, 1)], TAPS, fixed, place, 2, sizes
    )
    got_a = lax.ppermute(away_a, "tm", swap)
    two_a, rest_a = farther(own_a)
    own_b, away_b = spectra(
        [(volts, TAPS, 0, 0, 1), (volts, TAPS, 1, TAPS, 1)], TAPS, fixed, place, 2, sizes, (1, 0), (own_a,)
    )
    own_c, away_c = spectra(
        [
            (volts, edge, (last - 2, 0), (0, edge), 1),
            (volts, edge, (last - 1, 1), (edge, 2 * edge), 1),
            (visiting, edge, 0, (2 * edge, 0), 1),
        ],
        edge, fixed, place, 2, sizes, 1, (own_b, two_a),
    )
    got_a, own_c, away_b, away_c, two_a = lax.optimization_barrier((got_a, own_c, away_b, away_c, two_a))
    two_g, rest_g = evenly(got_a)
    got_b = lax.ppermute(away_b, "tm", [(0, 1)])
    pair_a = exchanged(two_a)
    first = [(many, [(0, 0, 0)])]
    sums = correlated([own_a, pair_a, two_a, rest_a], first, None, False)
    got_b, away_c, sums = lax.optimization_barrier((got_b, away_c, sums))
    got_c = lax.ppermute(away_c, "tm", swap)
    piece_b = jnp.where(me == 0, own_b, got_b)
    two_b, rest_b = farther(piece_b)
    pair_g, relay_g = exchanged(two_g), relayed(two_g)
    sums = correlated([got_a, pair_g, two_g, (rest_g, relay_g)], first, sums, False)
    piece_c = jnp.concatenate([own_c, got_c], axis=1)
    two_c, rest_c = farther(piece_c)
    pair_b = exchanged(two_b)
    sums = correlated([piece_b, pair_b, two_b, rest_b], first, sums, False)
    rest_c, two_c, sums = lax.optimization_barrier((rest_c, two_c, sums))
    pair_c = exchanged(two_c)
    return correlated([piece_c, pair_c, two_c, rest_c], [(few, [(0, 0, 0), (0, 0, few)])], sums, True)


def general(volts, fir_taps, place, correlated):
    groups = lax.axis_size("tm")
    frames = volts.shape[1]
    edge_frames = cut(volts, place, frames // TAPS - 1, TAPS)
    volts, *fixed = prepare(volts, fir_taps, place, groups)
    history = lax.ppermute(edge_frames, "tm", [(i, i + 1) for i in range(groups - 1)])
    parts = [(history, TAPS, 0, 0, 1)] + [(volts, TAPS, i, TAPS * (i + 1), 1) for i in range(frames // TAPS)]
    spectrum = spectra(parts, frames, fixed, place, groups, [K2])[0]
    spectrum = lax.all_to_all(spectrum, "tm", split_axis=0, concat_axis=0, tiled=True)
    two, rest = farther(spectrum)
    spots = [(0, K2 // groups * t, 0) for t in range(groups)]
    return correlated([spectrum, exchanged(two), two, rest], [(spectrum.shape[1], spots)], None, True)


def local(voltage, fir_taps):
    groups = lax.axis_size("tm")
    place = jnp.stack([lax.axis_index("tm"), lax.axis_index("stn") % 2]).astype(jnp.int32)
    scale = 1.0 / (groups * voltage.shape[1])

    def correlated(arrays, pieces, before, last, wait=(), cost=10**3):
        flat, spots_of = [], []
        for array in arrays:
            parts = array if isinstance(array, tuple) else (array,)
            spots_of.append(tuple(range(len(flat), len(flat) + len(parts))))
            flat += parts
        laid = [(tiles, [[(where, r, c) for _, r, c in spots] for where in spots_of]) for tiles, spots in pieces]
        return correlate(flat, laid, K2 // groups, place, scale, before, last, wait, cost)

    run = paired if groups == 2 else general
    return natural(run(stacked(voltage), fir_taps, place, correlated))


def solution(mesh):
    return jax.shard_map(
        local,
        mesh=mesh,
        in_specs=(P("stn", "tm", None, None), P()),
        out_specs=P(None, "stn", None, "tm"),
        check_vma=False,
    )
```

```python
import functools
import math

import jax
import jax.numpy as jnp
import numpy as np
from jax import lax
from jax.experimental import pallas as pl
from jax.experimental.pallas import tpu as pltpu
from jax.sharding import PartitionSpec as P

NCH = 4096
CHANS = 2048
TAPS = 16
VISITS = 4
H = 32
LANES = 128
ROWS = 2 * H
K2 = CHANS // H
STEP = 8
TILE = 16
PLACES = (0, (1, 3), 2, (3, 1))
MEMBERS = 4
PAD = 8
SUB = 8
BF16 = jnp.bfloat16
F32 = jnp.float32


def angles(rows, columns, modulus):
    turns = np.outer(rows, columns) % modulus
    return turns.astype(np.float64) * (2.0 * math.pi / modulus)


def stage_one_table():
    theta = angles(np.arange(H), np.arange(H), H)
    cosine, sine = np.cos(theta), np.sin(theta)
    table = np.zeros((2, H, H, 2))
    table[0, :, :, 0], table[0, :, :, 1] = cosine, sine
    table[1, :, :, 0], table[1, :, :, 1] = -sine, cosine
    return np.pad(table.reshape(ROWS, ROWS), ((0, 0), (0, 2 * LANES - ROWS)))


def turn_table():
    theta = angles(np.arange(H), np.arange(LANES), NCH)
    return np.concatenate([np.cos(theta), np.sin(theta)], axis=1)


def stage_two_table(groups):
    theta = angles(np.arange(K2), np.arange(LANES), LANES)
    cosine, sine = np.cos(theta) / math.sqrt(NCH), np.sin(theta) / math.sqrt(NCH)
    real = np.concatenate([cosine, sine], 1).reshape(groups, 1, K2 // groups, 2 * LANES)
    imag = np.concatenate([-sine, cosine], 1).reshape(groups, 1, K2 // groups, 2 * LANES)
    return np.concatenate([real, imag], 1).reshape(2 * K2, 2 * LANES)


def halves(value):
    high = value.astype(BF16)
    return high, (value - high.astype(F32)).astype(BF16)


def dot(left, right):
    return lax.dot_general(left, right, (((1,), (0,)), ((), ())), preferred_element_type=F32)


def dot_nt(left, right):
    return lax.dot_general(left, right, (((1,), (1,)), ((), ())), preferred_element_type=F32)


def value_of(number, group):
    if isinstance(number, int):
        return number
    return number[0] + (number[1] - number[0]) * group


def prepare_kernel(edge_block, swapped, place, volts_source, taps_source, table_source, turn_source, volts, edge, taps, one, two, turn, done, taps_ref, table_ref):
    count = edge.shape[1]
    start = pl.multiple_of(value_of(edge_block, place[0]) * count, count)
    copies = [
        pltpu.make_async_copy(taps_source, taps_ref, done.at[0]),
        pltpu.make_async_copy(table_source, table_ref, done.at[1]),
        pltpu.make_async_copy(volts_source.at[:, pl.ds(start, count)], edge, done.at[2]),
        pltpu.make_async_copy(volts_source, volts, done.at[3]),
        pltpu.make_async_copy(turn_source, turn, done.at[4]),
    ]
    for copy in copies:
        copy.start()
    copies[0].wait()
    copies[1].wait()
    for h in range(H):
        for half in range(TAPS // SUB):
            tile = taps_ref[pl.ds(half * SUB, SUB), pl.ds(h * LANES, LANES)]
            for r in range(2):
                taps[pl.ds(half * SUB * ROWS + 2 * h + r, SUB, stride=ROWS), :] = tile
    high, low = halves(table_ref[:ROWS, :ROWS])
    one[...] = jnp.concatenate([high, high, low], axis=1)
    start = pl.multiple_of(ROWS + place[0] * (2 * K2 * swapped), SUB)
    high, low = halves(table_ref[pl.ds(start, 2 * K2), :])
    two[0] = high
    two[1] = low
    for copy in copies[2:]:
        copy.wait()


def prepare(volts, fir_taps, place, groups, edge_block, edge_frames):
    signals, frames = volts.shape[:2]
    two = stage_two_table(groups)
    table = np.concatenate([stage_one_table(), two, np.roll(two, K2, axis=0)]).astype(np.float32)
    vmem = pl.BlockSpec(memory_space=pltpu.VMEM)
    return pl.pallas_call(
        functools.partial(prepare_kernel, edge_block, int(groups == 2)),
        grid_spec=pltpu.PrefetchScalarGridSpec(
            num_scalar_prefetch=1,
            grid=(),
            in_specs=[pl.BlockSpec(memory_space=pl.ANY)] * 4,
            out_specs=[vmem] * 6,
            scratch_shapes=[
                pltpu.SemaphoreType.DMA((5,)),
                pltpu.VMEM(fir_taps.shape, F32),
                pltpu.VMEM(table.shape, F32),
            ],
        ),
        out_shape=[
            jax.ShapeDtypeStruct((signals, frames, ROWS, LANES), BF16),
            jax.ShapeDtypeStruct((signals, edge_frames, ROWS, LANES), BF16),
            jax.ShapeDtypeStruct(((TAPS + 1) * ROWS, LANES), F32),
            jax.ShapeDtypeStruct((ROWS, 3 * ROWS), BF16),
            jax.ShapeDtypeStruct((2, 2 * K2, 2 * LANES), BF16),
            jax.ShapeDtypeStruct((H, 2 * LANES), F32),
        ],
        compiler_params=pltpu.CompilerParams(vmem_limit_bytes=24 << 20),
    )(
        place,
        *[
            pltpu.with_memory_space_constraint(x, pltpu.HBM)
            for x in (volts, fir_taps, jnp.asarray(table), jnp.asarray(turn_table(), F32))
        ],
    )


def spectra_kernel(groups, parts, out_frames, run, place, *refs):
    part_refs, refs = refs[: len(parts)], refs[len(parts) :]
    taps, one, two, turn = refs[:4]
    outs, (ext, filtered, turned, staged) = refs[4:-4], refs[-4:]
    step, steps, members = pl.program_id(0), pl.num_programs(0), MEMBERS
    per_group = K2 // groups
    share = LANES // out_frames
    tiles = H // share
    pairs = tiles // 2
    frame_rows, row_rows = ROWS + PAD, tiles * TILE + PAD

    def load(member):
        signal = step * members + member
        for (frames, block, start, valid), ref in zip(parts, part_refs):
            first = value_of(block, place[0]) * frames
            start = value_of(start, place[0])
            valid = value_of(valid, place[0])

            def fill(ref=ref, frames=frames, first=first, start=start):
                for f in range(frames):
                    ext[member, start + f] = ref[signal, first + f].astype(F32)

            def clear(frames=frames, start=start):
                for f in range(frames):
                    ext[member, start + f] = jnp.zeros((ROWS, LANES), F32)

            if isinstance(valid, int):
                fill() if valid else clear()
            else:
                pl.when(valid == 1)(fill)
                pl.when(valid == 0)(clear)

    def filter_rows(member, q):
        rows = pl.ds(pl.multiple_of(q * SUB, SUB), SUB)
        tap = [taps[pl.ds(pl.multiple_of(m * ROWS + q * SUB, SUB), SUB), :] for m in range(TAPS)]
        for f in range(out_frames):
            total = tap[0] * ext[member, f + 1, rows]
            for m in range(1, TAPS):
                total = total + tap[m] * ext[member, f + 1 + m, rows]
            filtered[member, f, rows] = total

    def first_stage(member):
        cosine = turn[:, :LANES]
        sine = turn[:, LANES:]
        for g in range(out_frames // STEP):
            block = jnp.concatenate([filtered[member, g * STEP + f] for f in range(STEP)], axis=1)
            high, low = halves(block)
            first = dot(one[...], jnp.concatenate([high, low, high], axis=0))
            for f in range(STEP):
                real = first[:H, f * LANES : (f + 1) * LANES]
                imag = first[H:, f * LANES : (f + 1) * LANES]
                at = (g * STEP + f) * frame_rows
                turned[member, at : at + H, :] = real * cosine + imag * sine
                turned[member, at + H : at + ROWS, :] = imag * cosine - real * sine

    def second_stage(member, pair):
        rows = []
        for k1 in range(2 * pair * share, 2 * (pair + 1) * share):
            for f in range(0, out_frames, SUB):
                rows.append(
                    jnp.concatenate(
                        [turned[member, pl.ds(f * frame_rows + p * H + k1, SUB, stride=frame_rows), :] for p in range(2)],
                        axis=1,
                    )
                )
        high, low = halves(jnp.concatenate(rows, axis=0))
        spectrum = dot_nt(two[0], high) + dot_nt(two[1], high) + dot_nt(two[0], low)
        for k in range(2):
            for t in range(groups):
                for p in range(2):
                    for k2 in range(0, per_group, SUB):
                        row = (t * 2 + p) * per_group + k2
                        start = (t * per_group + k2) * row_rows + (2 * pair + k) * TILE + p * SUB
                        staged[pl.ds(start + step * members + member, SUB, stride=row_rows), :] = spectrum[
                            row : row + SUB, k * LANES : (k + 1) * LANES
                        ]

    def write():
        at = 0
        for out in outs:

            def write_row(k2, carry):
                for k in range(tiles):
                    start = pl.multiple_of((at + k2) * row_rows + k * TILE, PAD)
                    out[k2, k] = staged[pl.ds(start, TILE), :].astype(BF16)
                return carry

            lax.fori_loop(0, out.shape[0], write_row, 0, unroll=2)
            at += out.shape[0]

    def body():
        for member in range(members):
            load(member)

        def filter_one(index, carry):
            filter_rows(index // (ROWS // SUB), index % (ROWS // SUB))
            return carry

        lax.fori_loop(0, members * (ROWS // SUB), filter_one, 0)
        for member in range(members):
            first_stage(member)
        for member in range(members):
            for pair in range(pairs):
                second_stage(member, pair)

        pl.when(step == steps - 1)(write)

    if isinstance(run, int):
        body()
    else:
        pl.when(value_of(run, place[0]) == 1)(body)


def after(value, *others):
    return lax.optimization_barrier((value, *others))[0]


def spectra(parts, out_frames, fixed, place, groups, sizes, run=1, wait=(), cost=10**6):
    signals = parts[0][0].shape[0]
    place = after(place, *wait)
    tiles = H * out_frames // LANES
    shapes = [(n, tiles, TILE, LANES) for n in sizes]
    return pl.pallas_call(
        functools.partial(spectra_kernel, groups, tuple(part[1:] for part in parts), out_frames, run),
        grid_spec=pltpu.PrefetchScalarGridSpec(
            num_scalar_prefetch=1,
            grid=(signals // MEMBERS,),
            in_specs=[pl.BlockSpec(memory_space=pltpu.VMEM)] * (len(parts) + 4),
            out_specs=[pl.BlockSpec(shape, lambda s, place: (0, 0, 0, 0)) for shape in shapes],
            scratch_shapes=[
                pltpu.VMEM((MEMBERS, TAPS + out_frames, ROWS, LANES), F32),
                pltpu.VMEM((MEMBERS, out_frames, ROWS, LANES), F32),
                pltpu.VMEM((MEMBERS, (out_frames + 1) * (ROWS + PAD), LANES), F32),
                pltpu.VMEM(((K2 + 1) * (tiles * TILE + PAD), LANES), F32),
            ],
        ),
        out_shape=[jax.ShapeDtypeStruct(shape, BF16) for shape in shapes],
        compiler_params=pltpu.CompilerParams(vmem_limit_bytes=32 << 20),
        cost_estimate=pl.CostEstimate(flops=cost, bytes_accessed=0, transcendentals=0),
    )(place, *[part[0] for part in parts], *fixed)


def after(value, *others):
    return lax.optimization_barrier((value, *others))[0]


def correlate_kernel(pieces, per_group, scale, add, last, place, *refs):
    refs = list(refs)
    sums = refs.pop() if last else None
    out = refs.pop()
    before = refs.pop() if add else None
    if not last:
        sums = out
    half = per_group // 2
    lane = lax.broadcasted_iota(jnp.int32, (SUB, LANES), 1)
    first_tile = lane < LANES // 2
    real_lane = lane % TILE < SUB
    sign = jnp.where(real_lane, 1.0, -1.0).astype(F32)

    def fetch(spot, tile, k2, k1):
        arrays, row, column = spot
        values = [refs[array][row + tile * half + k2, column + k1] for array in arrays]
        return values[0] if len(values) == 1 else values[0] + values[1]

    for number, piece in enumerate(pieces):
        tiles, piece = piece
        share = H // tiles
        where = lax.broadcasted_iota(jnp.int32, (TILE, LANES), 1) // (LANES // share)

        def pair(index, carry):
            k2 = index // tiles
            k1 = index % tiles
            own, other = [], []
            for position in range(len(piece[0])):
                rows = []
                for tile in range(2):
                    a = fetch(piece[0][position], tile, k2, k1)
                    rows += [jnp.where(where == c, a, jnp.zeros_like(a)) for c in range(share)]
                own.append(jnp.concatenate(rows, axis=0))
                rows = []
                for tile in range(2):
                    for visit in range(VISITS):
                        rows.append(fetch(piece[visit][position], tile, k2, k1))
                other.append(jnp.concatenate(rows, axis=0))
            product = dot_nt(jnp.concatenate(own, axis=1), jnp.concatenate(other, axis=1))
            for c in range(share):
                value = []
                for p in range(2):
                    at = [((tile * share + c) * 2 + p) * SUB for tile in range(2)]
                    value.append(
                        jnp.where(first_tile, product[at[0] : at[0] + SUB], product[at[1] : at[1] + SUB])
                    )
                turned = jnp.where(
                    real_lane, pltpu.roll(value[1], LANES - SUB, 1), pltpu.roll(value[1], SUB, 1)
                )
                total = value[0] * sign + turned
                channel = k2 // 4 * LANES + k2 % 4 * H + k1 * share + c
                rows = pl.ds(pl.multiple_of(channel * SUB, SUB), SUB)
                if number:
                    total = total + sums[rows, :]
                elif add:
                    total = total + before[rows, :]
                sums[rows, :] = total
            return carry

        lax.fori_loop(0, half * tiles, pair, 0, unroll=32)
    if not last:
        return

    def finish(index, carry):
        block = index // SUB
        signal = index % SUB
        value = sums[pl.ds(block * LANES * SUB + signal, LANES, stride=SUB), :]
        value = jnp.transpose(value * scale)
        at = 0
        for tile in range(2):
            for visit in range(VISITS):
                for part in range(2):
                    out[part, signal, value_of(PLACES[visit], place[1]), tile * (half // 4) + block] = value[at : at + SUB]
                    at += SUB
        return carry

    lax.fori_loop(0, half // 4 * SUB, finish, 0, unroll=8)


def correlate(arrays, pieces, per_group, place, scale, before, last, wait=(), cost=10**3):
    signals = TILE // 2
    rows = per_group // 2 * H * SUB + SUB
    place = after(place, *wait)
    shape = (2, signals, VISITS, per_group // 4, SUB, LANES) if last else (rows, LANES)
    operands = list(arrays) + ([] if before is None else [before])
    vmem = pl.BlockSpec(memory_space=pltpu.VMEM)
    result = pl.pallas_call(
        functools.partial(correlate_kernel, pieces, per_group, scale, before is not None, last),
        grid_spec=pltpu.PrefetchScalarGridSpec(
            num_scalar_prefetch=1,
            grid=(),
            in_specs=[vmem] * len(operands),
            out_specs=vmem,
            scratch_shapes=[pltpu.VMEM((rows, LANES), F32)] if last else [],
        ),
        out_shape=jax.ShapeDtypeStruct(shape, F32),
        compiler_params=pltpu.CompilerParams(vmem_limit_bytes=24 << 20),
        input_output_aliases={} if before is None or last else {len(operands): 0},
        cost_estimate=pl.CostEstimate(flops=cost, bytes_accessed=0, transcendentals=0),
    )(place, *operands)
    return result if last else pltpu.with_memory_space_constraint(result, pltpu.VMEM)


def stacked(voltage):
    s, f = voltage.shape[:2]
    return voltage.reshape(s, f, 2, H, LANES).transpose(0, 1, 3, 2, 4).reshape(s, f, ROWS, LANES)


def natural(out):
    parts, s, visits, i, t, lanes = out.shape
    return out.transpose(0, 1, 2, 4, 3, 5).reshape(parts, s, visits * t, i * lanes)


def shifted(block, axis, distance):
    size = lax.axis_size(axis)
    return lax.ppermute(block, axis, [(i, (i + distance) % size) for i in range(size)])


def farther(block):
    size = lax.axis_size("stn")
    rest = lax.ppermute(block, "stn", [(i, (i + 1 if i % 2 == 0 else i + 3) % size) for i in range(size)])
    return shifted(block, "stn", 2), rest


def evenly(block):
    size = lax.axis_size("stn")
    ways = [(i, (i + 1 if i % 2 == 0 else i + 3) % size) for i in range(size) if i % 4 < 3]
    return shifted(block, "stn", 2), lax.ppermute(block, "stn", ways)


def relayed(two):
    return lax.ppermute(two, "stn", [(i, i + 1) for i in range(lax.axis_size("stn")) if i % 4 == 1])


def exchanged(block):
    return lax.ppermute(block, "stn", [(i, i ^ 1) for i in range(lax.axis_size("stn"))])


def paired(volts, fir_taps, place, correlated):
    frames = volts.shape[1]
    me = lax.axis_index("tm")
    sizes = [K2 // 2, K2 // 2]
    swap = [(0, 1), (1, 0)]
    edge = TAPS // 2
    last = frames // edge
    many, few = TAPS * H // LANES, edge * H // LANES
    volts, edge_frames, *fixed = prepare(volts, fir_taps, place, 2, (last - 1, 0), edge)
    visiting = lax.ppermute(edge_frames, "tm", swap)
    own_a, away_a = spectra(
        [(volts, TAPS, 0, 0, (0, 1)), (volts, TAPS, (0, 1), TAPS, 1)], TAPS, fixed, place, 2, sizes
    )
    got_a = lax.ppermute(away_a, "tm", swap)
    two_a, rest_a = farther(own_a)
    own_b, away_b = spectra(
        [(volts, TAPS, 0, 0, 1), (volts, TAPS, 1, TAPS, 1)], TAPS, fixed, place, 2, sizes, (1, 0), (own_a,)
    )
    own_c, away_c = spectra(
        [
            (volts, edge, (last - 2, 0), (0, edge), 1),
            (volts, edge, (last - 1, 1), (edge, 2 * edge), 1),
            (visiting, edge, 0, (2 * edge, 0), 1),
        ],
        edge, fixed, place, 2, sizes, 1, (own_b, two_a),
    )
    got_a, own_c, away_b, away_c, two_a = lax.optimization_barrier((got_a, own_c, away_b, away_c, two_a))
    two_g, rest_g = evenly(got_a)
    got_b = lax.ppermute(away_b, "tm", [(0, 1)])
    pair_a = exchanged(two_a)
    first = [(many, [(0, 0, 0)])]
    sums = correlated([own_a, pair_a, two_a, rest_a], first, None, False)
    got_b, away_c, sums = lax.optimization_barrier((got_b, away_c, sums))
    got_c = lax.ppermute(away_c, "tm", swap)
    piece_b = jnp.where(me == 0, own_b, got_b)
    two_b, rest_b = farther(piece_b)
    pair_g, relay_g = exchanged(two_g), relayed(two_g)
    sums = correlated([got_a, pair_g, two_g, (rest_g, relay_g)], first, sums, False)
    piece_c = jnp.concatenate([own_c, got_c], axis=1)
    two_c, rest_c = farther(piece_c)
    pair_b = exchanged(two_b)
    sums = correlated([piece_b, pair_b, two_b, rest_b], first, sums, False)
    rest_c, two_c, sums = lax.optimization_barrier((rest_c, two_c, sums))
    pair_c = exchanged(two_c)
    return correlated([piece_c, pair_c, two_c, rest_c], [(few, [(0, 0, 0), (0, 0, few)])], sums, True)


def general(volts, fir_taps, place, correlated):
    groups = lax.axis_size("tm")
    frames = volts.shape[1]
    volts, edge_frames, *fixed = prepare(volts, fir_taps, place, groups, frames // TAPS - 1, TAPS)
    history = lax.ppermute(edge_frames, "tm", [(i, i + 1) for i in range(groups - 1)])
    parts = [(history, TAPS, 0, 0, 1)] + [(volts, TAPS, i, TAPS * (i + 1), 1) for i in range(frames // TAPS)]
    spectrum = spectra(parts, frames, fixed, place, groups, [K2])[0]
    spectrum = lax.all_to_all(spectrum, "tm", split_axis=0, concat_axis=0, tiled=True)
    two, rest = farther(spectrum)
    spots = [(0, K2 // groups * t, 0) for t in range(groups)]
    return correlated([spectrum, exchanged(two), two, rest], [(spectrum.shape[1], spots)], None, True)


def local(voltage, fir_taps):
    groups = lax.axis_size("tm")
    place = jnp.stack([lax.axis_index("tm"), lax.axis_index("stn") % 2]).astype(jnp.int32)
    scale = 1.0 / (groups * voltage.shape[1])

    def correlated(arrays, pieces, before, last, wait=(), cost=10**3):
        flat, spots_of = [], []
        for array in arrays:
            parts = array if isinstance(array, tuple) else (array,)
            spots_of.append(tuple(range(len(flat), len(flat) + len(parts))))
            flat += parts
        laid = [(tiles, [[(where, r, c) for _, r, c in spots] for where in spots_of]) for tiles, spots in pieces]
        return correlate(flat, laid, K2 // groups, place, scale, before, last, wait, cost)

    run = paired if groups == 2 else general
    return natural(run(stacked(voltage), fir_taps, place, correlated))


def solution(mesh):
    return jax.shard_map(
        local,
        mesh=mesh,
        in_specs=(P("stn", "tm", None, None), P()),
        out_specs=P(None, "stn", None, "tm"),
        check_vma=False,
    )
```

```python
import functools
import math

import jax
import jax.numpy as jnp
import numpy as np
from jax import lax
from jax.experimental import pallas as pl
from jax.experimental.pallas import tpu as pltpu
from jax.sharding import PartitionSpec as P

NCH = 4096
CHANS = 2048
TAPS = 16
VISITS = 4
H = 32
LANES = 128
ROWS = 2 * H
K2 = CHANS // H
STEP = 8
TILE = 16
PLACES = (0, (1, 3), 2, (3, 1))
MEMBERS = 4
PAD = 8
SUB = 8
BF16 = jnp.bfloat16
F32 = jnp.float32


def angles(rows, columns, modulus):
    turns = np.outer(rows, columns) % modulus
    return turns.astype(np.float64) * (2.0 * math.pi / modulus)


def stage_one_table():
    theta = angles(np.arange(H), np.arange(H), H)
    cosine, sine = np.cos(theta), np.sin(theta)
    table = np.zeros((2, H, H, 2))
    table[0, :, :, 0], table[0, :, :, 1] = cosine, sine
    table[1, :, :, 0], table[1, :, :, 1] = -sine, cosine
    return np.pad(table.reshape(ROWS, ROWS), ((0, 0), (0, 2 * LANES - ROWS)))


def turn_table():
    theta = angles(np.arange(H), np.arange(LANES), NCH)
    return np.concatenate([np.cos(theta), np.sin(theta)], axis=1)


def stage_two_table(groups):
    theta = angles(np.arange(K2), np.arange(LANES), LANES)
    cosine, sine = np.cos(theta) / math.sqrt(NCH), np.sin(theta) / math.sqrt(NCH)
    real = np.concatenate([cosine, sine], 1).reshape(groups, 1, K2 // groups, 2 * LANES)
    imag = np.concatenate([-sine, cosine], 1).reshape(groups, 1, K2 // groups, 2 * LANES)
    return np.concatenate([real, imag], 1).reshape(2 * K2, 2 * LANES)


def halves(value):
    high = value.astype(BF16)
    return high, (value - high.astype(F32)).astype(BF16)


def dot(left, right):
    return lax.dot_general(left, right, (((1,), (0,)), ((), ())), preferred_element_type=F32)


def dot_nt(left, right):
    return lax.dot_general(left, right, (((1,), (1,)), ((), ())), preferred_element_type=F32)


def value_of(number, group):
    if isinstance(number, int):
        return number
    return number[0] + (number[1] - number[0]) * group


def prepare_kernel(edge_block, swapped, place, volts_source, taps_source, table_source, turn_source, volts, edge, taps, one, two, turn, done, taps_ref, table_ref):
    count = edge.shape[1]
    start = pl.multiple_of(value_of(edge_block, place[0]) * count, count)
    copies = [
        pltpu.make_async_copy(taps_source, taps_ref, done.at[0]),
        pltpu.make_async_copy(table_source, table_ref, done.at[1]),
        pltpu.make_async_copy(volts_source.at[:, pl.ds(start, count)], edge, done.at[2]),
        pltpu.make_async_copy(volts_source, volts, done.at[3]),
        pltpu.make_async_copy(turn_source, turn, done.at[4]),
    ]
    for copy in copies:
        copy.start()
    copies[0].wait()
    copies[1].wait()
    for h in range(H):
        for half in range(TAPS // SUB):
            tile = taps_ref[pl.ds(half * SUB, SUB), pl.ds(h * LANES, LANES)]
            for r in range(2):
                taps[pl.ds(half * SUB * ROWS + 2 * h + r, SUB, stride=ROWS), :] = tile
    high, low = halves(table_ref[:ROWS, :ROWS])
    one[...] = jnp.concatenate([high, high, low], axis=1)
    start = pl.multiple_of(ROWS + place[0] * (2 * K2 * swapped), SUB)
    high, low = halves(table_ref[pl.ds(start, 2 * K2), :])
    two[0] = high
    two[1] = low
    for copy in copies[2:]:
        copy.wait()


def prepare(volts, fir_taps, place, groups, edge_block, edge_frames):
    signals, frames = volts.shape[:2]
    two = stage_two_table(groups)
    table = np.concatenate([stage_one_table(), two, np.roll(two, K2, axis=0)]).astype(np.float32)
    vmem = pl.BlockSpec(memory_space=pltpu.VMEM)
    return pl.pallas_call(
        functools.partial(prepare_kernel, edge_block, int(groups == 2)),
        grid_spec=pltpu.PrefetchScalarGridSpec(
            num_scalar_prefetch=1,
            grid=(),
            in_specs=[pl.BlockSpec(memory_space=pl.ANY)] * 4,
            out_specs=[vmem] * 6,
            scratch_shapes=[
                pltpu.SemaphoreType.DMA((5,)),
                pltpu.VMEM(fir_taps.shape, F32),
                pltpu.VMEM(table.shape, F32),
            ],
        ),
        out_shape=[
            jax.ShapeDtypeStruct((signals, frames, ROWS, LANES), BF16),
            jax.ShapeDtypeStruct((signals, edge_frames, ROWS, LANES), BF16),
            jax.ShapeDtypeStruct(((TAPS + 1) * ROWS, LANES), F32),
            jax.ShapeDtypeStruct((ROWS, 3 * ROWS), BF16),
            jax.ShapeDtypeStruct((2, 2 * K2, 2 * LANES), BF16),
            jax.ShapeDtypeStruct((H, 2 * LANES), F32),
        ],
        compiler_params=pltpu.CompilerParams(vmem_limit_bytes=24 << 20),
    )(
        place,
        *[
            pltpu.with_memory_space_constraint(x, pltpu.HBM)
            for x in (volts, fir_taps, jnp.asarray(table), jnp.asarray(turn_table(), F32))
        ],
    )


def spectra_kernel(groups, parts, out_frames, run, place, *refs):
    part_refs, refs = refs[: len(parts)], refs[len(parts) :]
    taps, one, two, turn = refs[:4]
    outs, (ext, filtered, turned, staged) = refs[4:-4], refs[-4:]
    step, steps, members = pl.program_id(0), pl.num_programs(0), MEMBERS
    per_group = K2 // groups
    share = LANES // out_frames
    tiles = H // share
    pairs = tiles // 2
    frame_rows, row_rows = ROWS + PAD, tiles * TILE + PAD

    def load(member):
        signal = step * members + member
        for (frames, block, start, valid), ref in zip(parts, part_refs):
            first = value_of(block, place[0]) * frames
            start = value_of(start, place[0])
            valid = value_of(valid, place[0])

            def fill(ref=ref, frames=frames, first=first, start=start):
                for f in range(frames):
                    ext[member, start + f] = ref[signal, first + f].astype(F32)

            def clear(frames=frames, start=start):
                for f in range(frames):
                    ext[member, start + f] = jnp.zeros((ROWS, LANES), F32)

            if isinstance(valid, int):
                fill() if valid else clear()
            else:
                pl.when(valid == 1)(fill)
                pl.when(valid == 0)(clear)

    def filter_rows(member, q):
        rows = pl.ds(pl.multiple_of(q * SUB, SUB), SUB)
        tap = [taps[pl.ds(pl.multiple_of(m * ROWS + q * SUB, SUB), SUB), :] for m in range(TAPS)]
        for f in range(out_frames):
            total = tap[0] * ext[member, f + 1, rows]
            for m in range(1, TAPS):
                total = total + tap[m] * ext[member, f + 1 + m, rows]
            filtered[member, f, rows] = total

    def first_stage(member):
        cosine = turn[:, :LANES]
        sine = turn[:, LANES:]
        for g in range(out_frames // STEP):
            block = jnp.concatenate([filtered[member, g * STEP + f] for f in range(STEP)], axis=1)
            high, low = halves(block)
            first = dot(one[...], jnp.concatenate([high, low, high], axis=0))
            for f in range(STEP):
                real = first[:H, f * LANES : (f + 1) * LANES]
                imag = first[H:, f * LANES : (f + 1) * LANES]
                at = (g * STEP + f) * frame_rows
                turned[member, at : at + H, :] = real * cosine + imag * sine
                turned[member, at + H : at + ROWS, :] = imag * cosine - real * sine

    def second_stage(member, pair):
        rows = []
        for k1 in range(2 * pair * share, 2 * (pair + 1) * share):
            for f in range(0, out_frames, SUB):
                rows.append(
                    jnp.concatenate(
                        [turned[member, pl.ds(f * frame_rows + p * H + k1, SUB, stride=frame_rows), :] for p in range(2)],
                        axis=1,
                    )
                )
        high, low = halves(jnp.concatenate(rows, axis=0))
        spectrum = dot_nt(two[0], high) + dot_nt(two[1], high) + dot_nt(two[0], low)
        for k in range(2):
            for t in range(groups):
                for p in range(2):
                    for k2 in range(0, per_group, SUB):
                        row = (t * 2 + p) * per_group + k2
                        start = (t * per_group + k2) * row_rows + (2 * pair + k) * TILE + p * SUB
                        staged[pl.ds(start + step * members + member, SUB, stride=row_rows), :] = spectrum[
                            row : row + SUB, k * LANES : (k + 1) * LANES
                        ]

    def write():
        at = 0
        for out in outs:

            def write_row(k2, carry):
                for k in range(tiles):
                    start = pl.multiple_of((at + k2) * row_rows + k * TILE, PAD)
                    out[k2, k] = staged[pl.ds(start, TILE), :].astype(BF16)
                return carry

            lax.fori_loop(0, out.shape[0], write_row, 0, unroll=2)
            at += out.shape[0]

    def body():
        for member in range(members):
            load(member)

        def filter_one(index, carry):
            filter_rows(index // (ROWS // SUB), index % (ROWS // SUB))
            return carry

        lax.fori_loop(0, members * (ROWS // SUB), filter_one, 0)
        for member in range(members):
            first_stage(member)
        for member in range(members):
            for pair in range(pairs):
                second_stage(member, pair)

        pl.when(step == steps - 1)(write)

    if isinstance(run, int):
        body()
    else:
        pl.when(value_of(run, place[0]) == 1)(body)


def after(value, *others):
    return lax.optimization_barrier((value, *others))[0]


def spectra(parts, out_frames, fixed, place, groups, sizes, run=1, wait=(), cost=10**6):
    signals = parts[0][0].shape[0]
    place = after(place, *wait)
    tiles = H * out_frames // LANES
    shapes = [(n, tiles, TILE, LANES) for n in sizes]
    return pl.pallas_call(
        functools.partial(spectra_kernel, groups, tuple(part[1:] for part in parts), out_frames, run),
        grid_spec=pltpu.PrefetchScalarGridSpec(
            num_scalar_prefetch=1,
            grid=(signals // MEMBERS,),
            in_specs=[pl.BlockSpec(memory_space=pltpu.VMEM)] * (len(parts) + 4),
            out_specs=[pl.BlockSpec(shape, lambda s, place: (0, 0, 0, 0)) for shape in shapes],
            scratch_shapes=[
                pltpu.VMEM((MEMBERS, TAPS + out_frames, ROWS, LANES), F32),
                pltpu.VMEM((MEMBERS, out_frames, ROWS, LANES), F32),
                pltpu.VMEM((MEMBERS, (out_frames + 1) * (ROWS + PAD), LANES), F32),
                pltpu.VMEM(((K2 + 1) * (tiles * TILE + PAD), LANES), F32),
            ],
        ),
        out_shape=[jax.ShapeDtypeStruct(shape, BF16) for shape in shapes],
        compiler_params=pltpu.CompilerParams(vmem_limit_bytes=32 << 20),
        cost_estimate=pl.CostEstimate(flops=cost, bytes_accessed=0, transcendentals=0),
    )(place, *[part[0] for part in parts], *fixed)


def after(value, *others):
    return lax.optimization_barrier((value, *others))[0]


def correlate_kernel(pieces, per_group, scale, add, last, place, *refs):
    refs = list(refs)
    sums = refs.pop() if last else None
    out = refs.pop()
    before = refs.pop() if add else None
    if not last:
        sums = out
    half = per_group // 2
    lane = lax.broadcasted_iota(jnp.int32, (SUB, LANES), 1)
    first_tile = lane < LANES // 2
    real_lane = lane % TILE < SUB
    sign = jnp.where(real_lane, 1.0, -1.0).astype(F32)

    def fetch(spot, tile, k2, k1):
        arrays, row, column = spot
        values = [refs[array][row + tile * half + k2, column + k1] for array in arrays]
        return values[0] if len(values) == 1 else values[0] + values[1]

    for number, piece in enumerate(pieces):
        tiles, piece = piece
        share = H // tiles
        where = lax.broadcasted_iota(jnp.int32, (TILE, LANES), 1) // (LANES // share)

        def pair(index, carry):
            k2 = index // tiles
            k1 = index % tiles
            own, other = [], []
            for position in range(len(piece[0])):
                rows = []
                for tile in range(2):
                    a = fetch(piece[0][position], tile, k2, k1)
                    rows += [jnp.where(where == c, a, jnp.zeros_like(a)) for c in range(share)]
                own.append(jnp.concatenate(rows, axis=0))
                rows = []
                for tile in range(2):
                    for visit in range(VISITS):
                        rows.append(fetch(piece[visit][position], tile, k2, k1))
                other.append(jnp.concatenate(rows, axis=0))
            product = dot_nt(jnp.concatenate(own, axis=1), jnp.concatenate(other, axis=1))
            for c in range(share):
                value = []
                for p in range(2):
                    at = [((tile * share + c) * 2 + p) * SUB for tile in range(2)]
                    value.append(
                        jnp.where(first_tile, product[at[0] : at[0] + SUB], product[at[1] : at[1] + SUB])
                    )
                turned = jnp.where(
                    real_lane, pltpu.roll(value[1], LANES - SUB, 1), pltpu.roll(value[1], SUB, 1)
                )
                total = value[0] * sign + turned
                channel = k2 // 4 * LANES + k2 % 4 * H + k1 * share + c
                rows = pl.ds(pl.multiple_of(channel * SUB, SUB), SUB)
                if number:
                    total = total + sums[rows, :]
                elif add:
                    total = total + before[rows, :]
                sums[rows, :] = total
            return carry

        lax.fori_loop(0, half * tiles, pair, 0, unroll=32)
    if not last:
        return

    def finish(index, carry):
        block = index // SUB
        signal = index % SUB
        value = sums[pl.ds(block * LANES * SUB + signal, LANES, stride=SUB), :]
        value = jnp.transpose(value * scale)
        at = 0
        for tile in range(2):
            for visit in range(VISITS):
                for part in range(2):
                    out[part, signal, value_of(PLACES[visit], place[1]), tile * (half // 4) + block] = value[at : at + SUB]
                    at += SUB
        return carry

    lax.fori_loop(0, half // 4 * SUB, finish, 0, unroll=8)


def correlate(arrays, pieces, per_group, place, scale, before, last, wait=(), cost=10**3):
    signals = TILE // 2
    rows = per_group // 2 * H * SUB + SUB
    place = after(place, *wait)
    shape = (2, signals, VISITS, per_group // 4, SUB, LANES) if last else (rows, LANES)
    operands = list(arrays) + ([] if before is None else [before])
    vmem = pl.BlockSpec(memory_space=pltpu.VMEM)
    result = pl.pallas_call(
        functools.partial(correlate_kernel, pieces, per_group, scale, before is not None, last),
        grid_spec=pltpu.PrefetchScalarGridSpec(
            num_scalar_prefetch=1,
            grid=(),
            in_specs=[vmem] * len(operands),
            out_specs=vmem,
            scratch_shapes=[pltpu.VMEM((rows, LANES), F32)] if last else [],
        ),
        out_shape=jax.ShapeDtypeStruct(shape, F32),
        compiler_params=pltpu.CompilerParams(vmem_limit_bytes=24 << 20),
        input_output_aliases={} if before is None or last else {len(operands): 0},
        cost_estimate=pl.CostEstimate(flops=cost, bytes_accessed=0, transcendentals=0),
    )(place, *operands)
    return result if last else pltpu.with_memory_space_constraint(result, pltpu.VMEM)


def stacked(voltage):
    s, f = voltage.shape[:2]
    return voltage.reshape(s, f, 2, H, LANES).transpose(0, 1, 3, 2, 4).reshape(s, f, ROWS, LANES)


def natural(out):
    parts, s, visits, i, t, lanes = out.shape
    return out.transpose(0, 1, 2, 4, 3, 5).reshape(parts, s, visits * t, i * lanes)


def shifted(block, axis, distance):
    size = lax.axis_size(axis)
    return lax.ppermute(block, axis, [(i, (i + distance) % size) for i in range(size)])


def farther(block):
    size = lax.axis_size("stn")
    rest = lax.ppermute(block, "stn", [(i, (i + 1 if i % 2 == 0 else i + 3) % size) for i in range(size)])
    return shifted(block, "stn", 2), rest


def exchanged(block):
    return lax.ppermute(block, "stn", [(i, i ^ 1) for i in range(lax.axis_size("stn"))])


def paired(volts, fir_taps, place, correlated):
    frames = volts.shape[1]
    me = lax.axis_index("tm")
    sizes = [K2 // 2, K2 // 2]
    swap = [(0, 1), (1, 0)]
    edge = TAPS // 2
    last = frames // edge
    many, few = TAPS * H // LANES, edge * H // LANES
    volts, edge_frames, *fixed = prepare(volts, fir_taps, place, 2, (last - 1, 0), edge)
    visiting = lax.ppermute(edge_frames, "tm", swap)
    own_a, away_a = spectra(
        [(volts, TAPS, 0, 0, (0, 1)), (volts, TAPS, (0, 1), TAPS, 1)], TAPS, fixed, place, 2, sizes
    )
    got_a = lax.ppermute(away_a, "tm", swap)
    two_a, rest_a = farther(own_a)
    own_b, away_b = spectra(
        [(volts, TAPS, 0, 0, 1), (volts, TAPS, 1, TAPS, 1)], TAPS, fixed, place, 2, sizes, (1, 0), (own_a,)
    )
    own_c, away_c = spectra(
        [
            (volts, edge, (last - 2, 0), (0, edge), 1),
            (volts, edge, (last - 1, 1), (edge, 2 * edge), 1),
            (visiting, edge, 0, (2 * edge, 0), 1),
        ],
        edge, fixed, place, 2, sizes, 1, (own_b, two_a),
    )
    got_a, own_c, away_b, away_c, two_a = lax.optimization_barrier((got_a, own_c, away_b, away_c, two_a))
    two_g, rest_g = farther(got_a)
    got_b = lax.ppermute(away_b, "tm", [(0, 1)])
    pair_a = exchanged(two_a)
    first = [(many, [(0, 0, 0)])]
    sums = correlated([own_a, pair_a, two_a, rest_a], first, None, False)
    got_b, away_c, sums = lax.optimization_barrier((got_b, away_c, sums))
    got_c = lax.ppermute(away_c, "tm", swap)
    piece_b = jnp.where(me == 0, own_b, got_b)
    two_b, rest_b = farther(piece_b)
    pair_g = exchanged(two_g)
    sums = correlated([got_a, pair_g, two_g, rest_g], first, sums, False)
    piece_c = jnp.concatenate([own_c, got_c], axis=1)
    two_c, rest_c = farther(piece_c)
    pair_b = exchanged(two_b)
    sums = correlated([piece_b, pair_b, two_b, rest_b], first, sums, False)
    rest_c, two_c, sums = lax.optimization_barrier((rest_c, two_c, sums))
    pair_c = exchanged(two_c)
    return correlated([piece_c, pair_c, two_c, rest_c], [(few, [(0, 0, 0), (0, 0, few)])], sums, True)


def general(volts, fir_taps, place, correlated):
    groups = lax.axis_size("tm")
    frames = volts.shape[1]
    volts, edge_frames, *fixed = prepare(volts, fir_taps, place, groups, frames // TAPS - 1, TAPS)
    history = lax.ppermute(edge_frames, "tm", [(i, i + 1) for i in range(groups - 1)])
    parts = [(history, TAPS, 0, 0, 1)] + [(volts, TAPS, i, TAPS * (i + 1), 1) for i in range(frames // TAPS)]
    spectrum = spectra(parts, frames, fixed, place, groups, [K2])[0]
    spectrum = lax.all_to_all(spectrum, "tm", split_axis=0, concat_axis=0, tiled=True)
    two, rest = farther(spectrum)
    spots = [(0, K2 // groups * t, 0) for t in range(groups)]
    return correlated([spectrum, exchanged(two), two, rest], [(spectrum.shape[1], spots)], None, True)


def local(voltage, fir_taps):
    groups = lax.axis_size("tm")
    place = jnp.stack([lax.axis_index("tm"), lax.axis_index("stn") % 2]).astype(jnp.int32)
    scale = 1.0 / (groups * voltage.shape[1])

    def correlated(arrays, pieces, before, last, wait=(), cost=10**3):
        flat, spots_of = [], []
        for array in arrays:
            parts = array if isinstance(array, tuple) else (array,)
            spots_of.append(tuple(range(len(flat), len(flat) + len(parts))))
            flat += parts
        laid = [(tiles, [[(where, r, c) for _, r, c in spots] for where in spots_of]) for tiles, spots in pieces]
        return correlate(flat, laid, K2 // groups, place, scale, before, last, wait, cost)

    run = paired if groups == 2 else general
    return natural(run(stacked(voltage), fir_taps, place, correlated))


def solution(mesh):
    return jax.shard_map(
        local,
        mesh=mesh,
        in_specs=(P("stn", "tm", None, None), P()),
        out_specs=P(None, "stn", None, "tm"),
        check_vma=False,
    )
```
